512 devices in a mesh: span: 32 (over y_lo, z, core), wrap: 4 (over y_hi), normal: 4 (over x).
Axes of the slice: x: 4, y: 8 (y_hi: 4, y_lo: 2; y = y_hi * 2 + y_lo), z: 8, core: 2. Of those that a mesh axis runs over, the one named last changes fastest.
Arguments:
- flow_state: float32 [5, 256, 64, 512], P(None, 'span', 'wrap', 'normal'), may hold values from -6 to 6
- inv_volume: float32 [256, 64, 512], P('span', 'wrap', 'normal'), may hold values from 0.5 to 2
- flux_jacobians: float32 [3, 5, 5], replicated, may hold values from -2.5 to 2.5
- area: float32 [256, 64], P('span', 'wrap'), may hold values from 0.5 to 2
- station_map: int32 [256, 64], P('span', 'wrap'), may hold values from 0 to 127, as said below
- contact: int32 [128], replicated, may hold values from 0 to 2
- bending: float32 [128], replicated, may hold values from 50 to 400
- mass: float32 [128], replicated, may hold values from 0.25 to 1.75
- hardening: float32 [128], replicated, may hold values from 2 to 12
- disp_old: float32 [128], replicated, may hold values from -2 to 2
- vel_old: float32 [128], replicated, may hold values from -6 to 6
Outputs:
- flow_next: float32 [5, 256, 64, 512], P(None, 'span', 'wrap', 'normal')
- deflection: float32 [128], replicated
The draws below stay inside these ranges and needn't reach their ends.
Inputs may be any that keep to these rules, and one draw needn't show every extreme that they name: `station_map`: each face's station differs by at most one from floor(i * 128 / 256) for its span index i.
All inputs are finite; a program needn't handle non-finite values.
Results may differ from the reference program's by a relative error of at most 0.0001.
Values sent between devices are 32-bit elements; how exact they have to be, the bound alone decides.
A program may use at most 64 MiB of HBM per device.

```python
import math
import jax
import jax.numpy as jnp
from jax import lax

VARS = 5
STATIONS = 128
NEWTON = 3
NS = 256
NW = 64
NN = 512


def draw_station_map(key, part):
    key = jax.random.fold_in(key, 1)
    rows = jnp.arange(NS, dtype=jnp.int32)
    nominal = rows * STATIONS // NS
    jitter = jax.random.randint(key, (NS, NW), -1, 2, dtype=jnp.int32)
    return jnp.clip(nominal[:, None] + jitter, 0, STATIONS - 1).astype(jnp.int32)


def wall_layer(span_low, wave):
    span_pos = jnp.arange(NS, dtype=jnp.float32) / max(NS - 1, 1)
    profile = span_low + span_pos
    turning = 2.0 * jnp.pi * jnp.arange(NW, dtype=jnp.float32) / NW
    beside_all = 1.0 + wave * jnp.cos(turning)
    decay = jnp.exp(-jnp.arange(NN, dtype=jnp.float32) / 8.0)
    return profile[:, None, None] * beside_all[None, :, None] * decay[None, None, :]


def draw_flow_state(key, part):
    key = jax.random.fold_in(key, 2)
    noise = jnp.clip(jax.random.normal(key, (VARS, NS, NW, NN), jnp.float32), -2.5, 2.5)
    offset = wall_layer(0.5, 0.0)
    first = noise[:1] + offset[None]
    return jnp.concatenate([first, noise[1:]], axis=0).astype(jnp.float32)


def place_ends(result, stream_key, least, high):
    longest = result.shape.index(max(result.shape))
    spots = []
    for shift in (0, 1):
        where = [jax.random.randint(jax.random.fold_in(stream_key, axis), (), 0, length) for axis, length in enumerate(result.shape)]
        where[longest] = (where[longest] + shift) % result.shape[longest]
        spots.append(tuple(where))
    return result.at[spots[0]].set(least).at[spots[1]].set(high)


def level_of(own_key, extent, split, low, top_value):
    factor_of, own = 1.0, jax.random.fold_in(own_key, 6)
    for dim, blocks in split:
        heights = jnp.exp(jax.random.uniform(jax.random.fold_in(own, dim), (blocks,), jnp.float32, low / len(split), top_value / len(split)))
        factor_of = factor_of * jnp.repeat(heights, extent[dim] // blocks).reshape([-1 if axis == dim else 1 for axis in range(len(extent))])
    return factor_of


def normal_values(key, extent, width, reach, held_as=jnp.bfloat16):
    result = jax.random.normal(key, extent, jnp.float32) * width
    return jnp.minimum(jnp.maximum(result, -reach), reach).astype(held_as)


def setup_inputs(seed: int = 0) -> dict:
    seeds = jax.random.split(jax.random.key(seed), 12)
    return {
        "flow_state": draw_flow_state(jax.random.fold_in(seeds[11], 71), 0),
        "inv_volume": jnp.clip(jnp.exp(math.log(2.0) - 1.3862944 * jax.random.uniform(seeds[1], (NS, NW, NN), jnp.float32) ** level_of(seeds[1], (NS, NW, NN), ((0, 32), (1, 4), (2, 4)), -0.2, 0.2)), 0.5, 2.0),
        "flux_jacobians": normal_values(seeds[2], (3, VARS, VARS), VARS ** -0.5, 2.5, jnp.float32),
        "area": jnp.clip(jnp.exp(math.log(2.0) - 1.3862944 * jax.random.uniform(seeds[3], (NS, NW), jnp.float32) ** level_of(seeds[3], (NS, NW), ((0, 32), (1, 4)), -0.2, 0.2)), 0.5, 2.0),
        "station_map": draw_station_map(jax.random.fold_in(seeds[11], 71), 0),
        "contact": place_ends(jax.random.randint(seeds[5], (STATIONS,), 0, 3), jax.random.fold_in(seeds[5], 1), 0, 2).astype(jnp.int32),
        "bending": jnp.clip(jnp.exp(jax.random.uniform(seeds[6], (STATIONS,), jnp.float32, math.log(50.0), math.log(400.0))), 50.0, 400.0),
        "mass": jnp.clip(1.0 + 0.15 * jax.random.normal(seeds[7], (STATIONS,), jnp.float32), 0.25, 1.75),
        "hardening": jnp.clip(jnp.exp(jax.random.uniform(seeds[8], (STATIONS,), jnp.float32, math.log(2.0), math.log(12.0))), 2.0, 12.0),
        "disp_old": normal_values(seeds[9], (STATIONS,), 0.5, 2.0, jnp.float32),
        "vel_old": normal_values(seeds[10], (STATIONS,), 2.0, 6.0, jnp.float32),
    }


DT_FLOW = 0.2
DISSIPATION = 0.03
DT_BEAM = 0.2
STOP_GAP = 0.5
CONTACT_STIFF = 40.0

def window(field, axis_dim, offset):
    picks = [slice(None)]
    for other in (1, 2, 3):
        length = field.shape[other] - 4
        start = 2 + (offset if other == axis_dim else 0)
        picks.append(slice(start, start + length))
    return field[tuple(picks)]

def rates(padded, flux_jacobians, volume):
    summed = jnp.zeros(window(padded, 1, 0).shape, jnp.float32)
    for axis_dim in (1, 2, 3):
        fluxes = jnp.einsum('uv,vabc->uabc', flux_jacobians[axis_dim - 1], padded, precision=lax.Precision.HIGHEST)
        deriv = (-window(fluxes, axis_dim, 2) + 8.0 * window(fluxes, axis_dim, 1) - 8.0 * window(fluxes, axis_dim, -1) + window(fluxes, axis_dim, -2)) / 12.0
        smooth = window(padded, axis_dim, 2) - 4.0 * window(padded, axis_dim, 1) + 6.0 * window(padded, axis_dim, 0) - 4.0 * window(padded, axis_dim, -1) + window(padded, axis_dim, -2)
        summed = summed - deriv - DISSIPATION * smooth
    return volume * summed

def pad_field(field):
    spanned = jnp.pad(field, ((0, 0), (2, 2), (0, 0), (0, 0)))
    wrapped = jnp.pad(spanned, ((0, 0), (0, 0), (2, 2), (0, 0)), mode='wrap')
    mirror = jnp.flip(wrapped[..., :2], axis=3)
    zeroes = jnp.zeros(wrapped.shape[:3] + (2,), jnp.float32)
    return jnp.concatenate([mirror, wrapped, zeroes], axis=3)

def stiffness_matrix(bending):
    count = bending.shape[0]
    rows = lax.broadcasted_iota(jnp.int32, (count, count), 0)
    cols = lax.broadcasted_iota(jnp.int32, (count, count), 1)
    second = (cols == rows - 1).astype(jnp.float32) - 2.0 * (cols == rows).astype(jnp.float32) + (cols == rows + 1).astype(jnp.float32)
    return jnp.dot(second.T, bending[:, None] * second, precision=lax.Precision.HIGHEST)

def beam_step(loads, contact, bending, mass, hardening, disp_old, vel_old):
    stiffness = stiffness_matrix(bending)
    disp = disp_old
    touching = (contact > 0).astype(jnp.float32)
    for newton_step in range(NEWTON):
        accel = 2.0 * (disp - disp_old - DT_BEAM * vel_old) / (DT_BEAM * DT_BEAM)
        stop_force = jnp.where(contact == 1, CONTACT_STIFF * (disp - STOP_GAP), jnp.where(contact == 2, CONTACT_STIFF * (disp + STOP_GAP), 0.0))
        elastic = jnp.dot(stiffness, disp, precision=lax.Precision.HIGHEST)
        resid = mass * accel + elastic + hardening * disp * disp * disp + stop_force - loads
        diagonal = 2.0 * mass / (DT_BEAM * DT_BEAM) + 3.0 * hardening * disp * disp + CONTACT_STIFF * touching
        jacobian = stiffness + jnp.diag(diagonal)
        factor = jnp.linalg.cholesky(jacobian)
        update = jax.scipy.linalg.cho_solve((factor, True), resid)
        disp = disp - update
    return disp

def reference(flow_state, inv_volume, flux_jacobians, area, station_map, contact, bending, mass, hardening, disp_old, vel_old):
    flow_mid = flow_state + DT_FLOW * rates(pad_field(flow_state), flux_jacobians, inv_volume)
    flow_next = 0.5 * (flow_state + flow_mid + DT_FLOW * rates(pad_field(flow_mid), flux_jacobians, inv_volume))
    weighted = (area * flow_next[0, :, :, 0]).reshape(-1)
    loads = jax.ops.segment_sum(weighted, station_map.reshape(-1), num_segments=STATIONS)
    deflection = beam_step(loads, contact, bending, mass, hardening, disp_old, vel_old)
    return (flow_next, deflection)
```

```python
import functools

import jax
import jax.numpy as jnp
from jax import lax
from jax.experimental import pallas as pl
from jax.experimental.pallas import tpu as pltpu
from jax.sharding import PartitionSpec as P

MESH = pl.DeviceIdType.MESH
VARS = 5
STATIONS = 128
NEWTON = 3
DT_FLOW = 0.2
DISSIPATION = 0.03
DT_BEAM = 0.2
STOP_GAP = 0.5
CONTACT_STIFF = 40.0
SPAN, WRAP, LANES = 8, 16, 128
TOP = 8


def lane_of(shape):
    return lax.broadcasted_iota(jnp.int32, shape, len(shape) - 1)


def roll(x, shift):
    return pltpu.roll(x, shift % LANES if isinstance(shift, int) else shift, 1)


def factor(be, bo, diag_e, diag_o):
    lane = lane_of((1, LANES))
    half = LANES // 2
    valid, inner = lane < half, lane < half - 1
    bo_prev, be_next = roll(bo, 1), roll(be, -1)
    p = jnp.where(valid, 4.0 * be + bo_prev + bo + diag_e, 1.0)
    q = jnp.where(valid, -2.0 * (be + bo), 0.0)
    r = jnp.where(valid, 4.0 * bo + be + be_next + diag_o, 1.0)
    c11 = jnp.where(inner, bo, 0.0)
    c12 = jnp.zeros_like(bo)
    c21 = jnp.where(inner, -2.0 * (bo + be_next), 0.0)
    c22 = jnp.where(inner, be_next, 0.0)
    a11, a12, a21, a22 = roll(c11, 1), roll(c21, 1), c12, roll(c22, 1)
    levels = []
    step = 1
    while step < half:
        inv = 1.0 / (p * r - q * q)
        w11, w12, w22 = r * inv, -q * inv, p * inv
        u11, u12 = c11 * w11 + c21 * w12, c11 * w12 + c21 * w22
        u21, u22 = c12 * w11 + c22 * w12, c12 * w12 + c22 * w22
        d11, d12 = a11 * w11 + a21 * w12, a11 * w12 + a21 * w22
        d21, d22 = a12 * w11 + a22 * w12, a12 * w12 + a22 * w22
        levels.append((step, u11, u12, u21, u22, d11, d12, d21, d22))
        p = p - roll(u11 * c11 + u12 * c21, step) - roll(d11 * a11 + d12 * a21, -step)
        q = q - roll(u11 * c12 + u12 * c22, step) - roll(d11 * a12 + d12 * a22, -step)
        r = r - roll(u21 * c12 + u22 * c22, step) - roll(d21 * a12 + d22 * a22, -step)
        if 2 * step < half:
            n11, n12 = -(d11 * c11 + d12 * c21), -(d11 * c12 + d12 * c22)
            n21, n22 = -(d21 * c11 + d22 * c21), -(d21 * c12 + d22 * c22)
            c11, c12 = roll(n11, -step), roll(n12, -step)
            c21, c22 = roll(n21, -step), roll(n22, -step)
            a11, a12 = roll(n11, step), roll(n21, step)
            a21, a22 = roll(n12, step), roll(n22, step)
        step *= 2
    inv = 1.0 / (p * r - q * q)
    return levels, (r * inv, -q * inv, p * inv)


def substitute(factors, e, o):
    levels, (w11, w12, w22) = factors
    for step, u11, u12, u21, u22, d11, d12, d21, d22 in levels:
        e, o = (
            e - roll(u11 * e + u12 * o, step) - roll(d11 * e + d12 * o, -step),
            o - roll(u21 * e + u22 * o, step) - roll(d21 * e + d22 * o, -step),
        )
    return w11 * e + w12 * o, w12 * e + w22 * o


def right_side(fe, fo, he, ho, ue, uo):
    return fe + 2.0 * he * ue * ue * ue, fo + 2.0 * ho * uo * uo * uo


def halves(x):
    valid = lane_of((1, LANES)) < LANES // 2
    return jnp.where(valid, x, 0.0), jnp.where(valid, roll(x, LANES // 2), 0.0)


def pack_plane(packed, cells, s):
    slot = lane_of((8, LANES)) // 4
    new = []
    for v in range(VARS):
        have = packed[v]
        for t in range(2):
            k = 2 * s + t
            have = jnp.where(slot == k, roll(cells[v][t], 4 * k + 2), have)
        new.append(have)
    return tuple(new)


def edge_terms(normal, n_norm, own, left, right, jac, corr):
    lane = lane_of((8, LANES))
    place = lane % 4
    ends, smooths = [], []
    for v in range(VARS):
        mine = own[v]
        mirror = jnp.where(place == 0, roll(mine, -3), roll(mine, -1))
        low = jnp.where(normal == 0, mirror, left[v])
        high = jnp.where(normal == n_norm - 1, 0.0, right[v])
        delta = jnp.where(place < 2, roll(high - mine, -2), roll(low - mine, 2))
        near = jnp.where(place == 1, roll(delta, 1), jnp.where(place == 2, roll(delta, -1), 0.0))
        end = delta - 8.0 * near
        ends.append(jnp.where(place < 2, -end, end))
        smooths.append(delta - 4.0 * near)
    for u in range(VARS):
        total = -DISSIPATION * smooths[u]
        for v in range(VARS):
            total = total + jac[50 + 5 * u + v] * ends[v]
        corr[u] = total


def plane_rates(field, s, jac, corr):
    lane = lane_of((8, LANES))
    edge = (lane < 2) | (lane >= LANES - 2)
    cells, grads, smooths = [], [[], [], []], []
    for v in range(VARS):

        def at(ds, dw):
            return field[v, s + (2 + ds), TOP + dw : TOP + dw + WRAP, :]

        c = at(0, 0)
        reads = [
            [at(k, 0) for k in (-2, -1, 1, 2)],
            [at(0, k) for k in (-2, -1, 1, 2)],
            [roll(c, -k) for k in (-2, -1, 1, 2)],
        ]
        near, far = None, None
        for d, (m2, m1, p1, p2) in enumerate(reads):
            grads[d].append(((m2 - p2) + 8.0 * (p1 - m1)).reshape(2, 8, LANES))
            near = (m1 + p1) if near is None else near + (m1 + p1)
            far = (m2 + p2) if far is None else far + (m2 + p2)
        smooths.append((-DISSIPATION * (far - 4.0 * near + 18.0 * c)).reshape(2, 8, LANES))
        cells.append(c.reshape(2, 8, LANES))
    rates = []
    for u in range(VARS):
        total = smooths[u]
        for d in range(3):
            for v in range(VARS):
                total = total + jac[25 * d + 5 * u + v][None] * grads[d][v]
        ends = corr[u]
        fix = [
            jnp.where(edge, roll(ends, (2 * LANES - 2 - 4 * (2 * s + t)) % LANES), 0.0)
            for t in range(2)
        ]
        rates.append(total + jnp.stack(fix))
    return cells, rates


def kernel(
    n_span,
    n_wrap,
    n_norm,
    flow_hbm,
    volume_hbm,
    jac_smem,
    area_hbm,
    map_hbm,
    contact_hbm,
    bending_hbm,
    mass_hbm,
    hardening_hbm,
    disp_hbm,
    vel_hbm,
    out_hbm,
    state_ref,
    field1,
    field2,
    volume,
    wall_send,
    wall_recv,
    edges,
    corr,
    jac,
    result,
    faces,
    area,
    stations,
    contact_v,
    beam_v,
    loads_a,
    loads_b,
    tally,
    local_sem,
    send_sem,
    recv_sem,
    group_sem,
):
    span, wrap, normal = lax.axis_index("span"), lax.axis_index("wrap"), lax.axis_index("normal")
    rows = 2
    cols = n_span // rows
    row, col = span // cols, span % cols

    inputs = [
        (flow_hbm, field1.at[:, 2 : 2 + SPAN, TOP : TOP + WRAP, :]),
        (volume_hbm, volume),
        (area_hbm, area),
        (map_hbm, stations),
        (contact_hbm, contact_v),
        (bending_hbm, beam_v.at[0]),
        (mass_hbm, beam_v.at[1]),
        (hardening_hbm, beam_v.at[2]),
        (disp_hbm, beam_v.at[3]),
        (vel_hbm, beam_v.at[4]),
    ]
    reads = [pltpu.make_async_copy(a, b, local_sem.at[i]) for i, (a, b) in enumerate(inputs)]
    for read in reads:
        read.start()

    def turned(index, by, count):
        return (index + (by + count)) % count

    span_at = {by: turned(span, by, n_span) for by in (-1, 1)}
    wrap_at = [turned(wrap, by, n_wrap) for by in range(n_wrap)]
    norm_at = {by: turned(normal, by, n_norm) for by in (-1, 1)}
    row_at = [turned(row, by, rows) for by in range(rows)]
    col_at = [turned(col, by, cols) for by in range(cols)]
    sides = [
        (span_at[-1], wrap, normal),
        (span_at[1], wrap, normal),
        (span, wrap_at[n_wrap - 1], normal),
        (span, wrap_at[1], normal),
        (span, wrap, norm_at[-1]),
        (span, wrap, norm_at[1]),
    ]
    barrier = pltpu.get_barrier_semaphore()

    def greet(target):
        pl.semaphore_signal(barrier, inc=1, device_id=target, device_id_type=MESH)

    for side in sides:
        greet(side)
    for a in range(rows):
        for b in range(n_wrap):
            source = (row_at[-a % rows] * cols + col, wrap_at[-b % n_wrap], 0)
            if a == 0 and b == 0:

                @pl.when(normal != 0)
                def _():
                    greet(source)

            else:
                greet(source)
    for k in range(1, cols):
        greet((row * cols + col_at[-k % cols], wrap, normal))

    for d in range(3):
        for u in range(VARS):
            for v in range(VARS):
                scaled = jac_smem[u, d, v] * (-1.0 / 12.0)
                jac[25 * d + 5 * u + v] = jnp.full((8, LANES), scaled, jnp.float32)

    def copy(src, dst, slot, target):
        return pltpu.make_async_remote_copy(
            src_ref=src,
            dst_ref=dst,
            send_sem=send_sem.at[slot],
            recv_sem=recv_sem.at[slot],
            device_id=target,
            device_id_type=MESH,
        )

    def stage_copies(stage, field):
        cells = pl.ds(TOP, WRAP)
        base = 6 * stage
        pairs = [
            (field.at[:, 2:4, cells, :], field.at[:, 2 + SPAN : 4 + SPAN, cells, :]),
            (field.at[:, SPAN : 2 + SPAN, cells, :], field.at[:, 0:2, cells, :]),
            (wall_send.at[stage, 0], wall_recv.at[stage, 0]),
            (wall_send.at[stage, 1], wall_recv.at[stage, 1]),
            (edges.at[stage, 0], edges.at[stage, 2]),
            (edges.at[stage, 0], edges.at[stage, 1]),
        ]
        return [copy(src, dst, base + i, sides[i]) for i, (src, dst) in enumerate(pairs)]

    def stage_wrap_rows(stage, field):
        for v in range(VARS):
            for r in range(2):
                wall_send[stage, 0, v, r] = field[v, 2 : 2 + SPAN, TOP + r, :]
                wall_send[stage, 1, v, r] = field[v, 2 : 2 + SPAN, TOP + WRAP - 2 + r, :]

    def stage_arrive(stage, field):
        zeros = jnp.zeros((VARS, 2, WRAP, LANES), jnp.float32)

        @pl.when(span == 0)
        def _():
            field[:, 0:2, TOP : TOP + WRAP, :] = zeros

        @pl.when(span == n_span - 1)
        def _():
            field[:, 2 + SPAN : 4 + SPAN, TOP : TOP + WRAP, :] = zeros

        for v in range(VARS):
            for r in range(2):
                field[v, 2 : 2 + SPAN, TOP + WRAP + r, :] = wall_recv[stage, 0, v, r]
                field[v, 2 : 2 + SPAN, TOP - 2 + r, :] = wall_recv[stage, 1, v, r]
        edge_terms(
            normal, n_norm, edges.at[stage, 0], edges.at[stage, 1], edges.at[stage, 2], jac, corr
        )

    empty = tuple(jnp.zeros((8, LANES), jnp.float32) for _ in range(VARS))

    reads[0].wait()
    stage_wrap_rows(0, field1)

    def pack_first(s, packed):
        cells = [
            field1[v, s + 2, TOP : TOP + WRAP, :].reshape(2, 8, LANES) for v in range(VARS)
        ]
        return pack_plane(packed, cells, s)

    packed = lax.fori_loop(0, SPAN, pack_first, empty, unroll=True)
    for v in range(VARS):
        edges[0, 0, v] = packed[v]

    at_wall = (n_norm - normal) // n_norm
    pl.semaphore_wait(barrier, 5 + cols + at_wall * (rows * n_wrap * n_norm - 1))

    first = stage_copies(0, field1)
    for one in first:
        one.start()

    for read in reads[1:]:
        read.wait()
    lane = lane_of((8, LANES))
    held = jnp.where(lane < LANES // 2, 2 * lane, 2 * lane - (LANES - 1))
    for j in range(WRAP):
        weight = jnp.broadcast_to(area[:, j : j + 1], (8, LANES))
        where = jnp.broadcast_to(stations[:, j : j + 1], (8, LANES))
        faces[j] = jnp.where(where == held, weight, 0.0)

    for one in first:
        one.wait_recv()
    stage_arrive(0, field1)

    def first_plane(s, packed):
        cells, rates = plane_rates(field1, s, jac, corr)
        scale = DT_FLOW * volume[s].reshape(2, 8, LANES)
        mids = [cells[u] + scale * rates[u] for u in range(VARS)]
        for u in range(VARS):
            field2[u, s + 2, TOP : TOP + WRAP, :] = mids[u].reshape(WRAP, LANES)
        return pack_plane(packed, mids, s)

    packed = lax.fori_loop(0, SPAN, first_plane, empty)
    for v in range(VARS):
        edges[1, 0, v] = packed[v]

    stage_wrap_rows(1, field2)
    second = stage_copies(1, field2)
    for one in second:
        one.start()
    for one in second:
        one.wait_recv()
    stage_arrive(1, field2)

    def second_plane(s, carry):
        cells, rates = plane_rates(field2, s, jac, corr)
        scale = DT_FLOW * volume[s].reshape(2, 8, LANES)
        for u in range(VARS):
            start = field1[u, s + 2, TOP : TOP + WRAP, :].reshape(2, 8, LANES)
            after = 0.5 * (start + cells[u] + scale * rates[u])
            result[u, s] = after.reshape(WRAP, LANES)
        return carry

    lax.fori_loop(0, SPAN, second_plane, 0)

    def group_copy(buffer, slot, which, target):
        return pltpu.make_async_remote_copy(
            src_ref=buffer.at[0],
            dst_ref=buffer.at[slot],
            send_sem=group_sem.at[2 * which],
            recv_sem=group_sem.at[2 * which + 1],
            device_id=target,
            device_id_type=MESH,
        )

    def take(ref, which):
        pltpu.make_async_copy(ref, ref, group_sem.at[which]).wait()

    count_a = rows * n_wrap

    @pl.when(normal == 0)
    def _():
        partial = jnp.zeros((8, LANES), jnp.float32)
        for j in range(WRAP):
            beside = result[0, :, j, :]
            partial = partial + faces[j] * jnp.broadcast_to(beside[:, 0:1], (8, LANES))
        loads_a[0] = partial
        for a in range(rows):
            for b in range(n_wrap):
                for c in range(n_norm):
                    if a or b or c:
                        target = (row_at[a] * cols + col, wrap_at[b], c)
                        group_copy(loads_a, a * n_wrap + b, 0, target).start()

    write = pltpu.make_async_copy(result, out_hbm, local_sem.at[len(inputs)])
    write.start()

    def permuted(x):
        full = jnp.broadcast_to(x, (8, LANES))
        return jnp.take_along_axis(full, held, axis=1)[0:1]

    bending, mass, hardening, disp, vel = [permuted(beam_v[i]) for i in range(5)]
    contact = permuted(contact_v[...])
    inertia = 2.0 * mass / (DT_BEAM * DT_BEAM)
    pull = CONTACT_STIFF * STOP_GAP
    push = jnp.where(contact == 1, pull, jnp.where(contact == 2, -pull, 0.0))
    steady = inertia * (disp + DT_BEAM * vel) + push
    base = inertia + jnp.where(contact > 0, CONTACT_STIFF, 0.0)
    be, bo = halves(bending)
    he, ho = halves(hardening)
    ge, go = halves(base)
    ue, uo = halves(disp)
    fe, fo = halves(steady)
    factors = factor(be, bo, ge + 3.0 * he * ue * ue, go + 3.0 * ho * uo * uo)

    @pl.when(normal == 0)
    def _():
        take(loads_a.at[1:], 1)

    @pl.when(normal != 0)
    def _():
        take(loads_a, 1)

    total = None
    for y in range(count_a):
        a = (row + (rows - y // n_wrap)) % rows
        b = (wrap + (n_wrap - y % n_wrap)) % n_wrap
        term = loads_a[a * n_wrap + b]
        total = term if total is None else total + term
    loads_b[0] = total
    for k in range(1, cols):
        group_copy(loads_b, k, 1, (row * cols + col_at[k], wrap, normal)).start()
    take(loads_b.at[1:], 3)
    total = None
    for z in range(cols):
        term = loads_b[(col + (cols - z)) % cols]
        total = term if total is None else total + term
    loads = jnp.sum(total, axis=0, keepdims=True)

    le, lo = halves(loads)
    fe, fo = fe + le, fo + lo
    ue, uo = substitute(factors, *right_side(fe, fo, he, ho, ue, uo))
    for i, x in enumerate((be, bo, ge, go, he, ho, fe, fo, ue, uo)):
        state_ref[i : i + 1, :] = x

    for one in first + second:
        one.wait_send()

    @pl.when(normal == 0)
    def _():
        take(tally, 0)

    take(loads_b.at[1:], 2)
    write.wait()


def beam_kernel(state_ref, flow_hbm, out_hbm, defl_ref, sem):
    write = pltpu.make_async_copy(flow_hbm, out_hbm, sem)
    write.start()
    be, bo, ge, go, he, ho, fe, fo, ue, uo = [state_ref[i : i + 1, :] for i in range(10)]
    for _ in range(NEWTON - 1):
        factors = factor(be, bo, ge + 3.0 * he * ue * ue, go + 3.0 * ho * uo * uo)
        ue, uo = substitute(factors, *right_side(fe, fo, he, ho, ue, uo))
    both = jnp.where(lane_of((1, LANES)) < LANES // 2, ue, roll(uo, LANES // 2))
    lane = lane_of((8, LANES))
    back = (lane % 2) * (LANES // 2) + lane // 2
    full = jnp.broadcast_to(both, (8, LANES))
    defl_ref[...] = jnp.take_along_axis(full, back, axis=1)[0:1]
    write.wait()


def solution(mesh):
    n_span, n_wrap, n_norm = (mesh.shape[axis] for axis in ("span", "wrap", "normal"))
    cols, ys = n_span // 2, 2 * n_wrap
    f32 = jnp.float32

    def step(
        flow_state,
        inv_volume,
        flux_jacobians,
        area,
        station_map,
        contact,
        bending,
        mass,
        hardening,
        disp_old,
        vel_old,
    ):
        vectors = [
            x.reshape(1, STATIONS) for x in (contact, bending, mass, hardening, disp_old, vel_old)
        ]
        hbm = pl.BlockSpec(memory_space=pltpu.HBM)
        flow_next, state = pl.pallas_call(
            functools.partial(kernel, n_span, n_wrap, n_norm),
            out_shape=(
                jax.ShapeDtypeStruct(flow_state.shape, f32),
                jax.ShapeDtypeStruct((16, LANES), f32),
            ),
            in_specs=[hbm, hbm, pl.BlockSpec(memory_space=pltpu.SMEM)] + [hbm] * 8,
            out_specs=(hbm, pl.BlockSpec(memory_space=pltpu.VMEM)),
            scratch_shapes=[
                pltpu.VMEM((VARS, SPAN + 4, WRAP + 16, LANES), f32),
                pltpu.VMEM((VARS, SPAN + 4, WRAP + 16, LANES), f32),
                pltpu.VMEM((SPAN, WRAP, LANES), f32),
                pltpu.VMEM((2, 2, VARS, 2, SPAN, LANES), f32),
                pltpu.VMEM((2, 2, VARS, 2, SPAN, LANES), f32),
                pltpu.VMEM((2, 3, VARS, 8, LANES), f32),
                pltpu.VMEM((VARS, 8, LANES), f32),
                pltpu.VMEM((75, 8, LANES), f32),
                pltpu.VMEM((VARS, SPAN, WRAP, LANES), f32),
                pltpu.VMEM((WRAP, 8, LANES), f32),
                pltpu.VMEM((SPAN, WRAP), f32),
                pltpu.VMEM((SPAN, WRAP), jnp.int32),
                pltpu.VMEM((1, STATIONS), jnp.int32),
                pltpu.VMEM((5, 1, STATIONS), f32),
                pltpu.VMEM((ys, 8, LANES), f32),
                pltpu.VMEM((cols, 8, LANES), f32),
                pltpu.VMEM((ys * n_norm - 1, 8, LANES), f32),
                pltpu.SemaphoreType.DMA((11,)),
                pltpu.SemaphoreType.DMA((12,)),
                pltpu.SemaphoreType.DMA((12,)),
                pltpu.SemaphoreType.DMA((4,)),
            ],
            compiler_params=pltpu.CompilerParams(
                collective_id=0, has_side_effects=True, vmem_limit_bytes=60 * 1024 * 1024
            ),
            cost_estimate=pl.CostEstimate(
                flops=10_000_000, bytes_accessed=1_000_000, transcendentals=0
            ),
        )(flow_state, inv_volume, flux_jacobians.transpose(1, 0, 2), area, station_map, *vectors)
        flow_next, deflection = pl.pallas_call(
            beam_kernel,
            out_shape=(
                jax.ShapeDtypeStruct(flow_state.shape, f32),
                jax.ShapeDtypeStruct((1, STATIONS), f32),
            ),
            in_specs=[pl.BlockSpec(memory_space=pltpu.VMEM), hbm],
            out_specs=(hbm, pl.BlockSpec(memory_space=pltpu.VMEM)),
            scratch_shapes=[pltpu.SemaphoreType.DMA(())],
            compiler_params=pltpu.CompilerParams(vmem_limit_bytes=60 * 1024 * 1024),
        )(state, flow_next)
        return flow_next, deflection.reshape(STATIONS)

    placed = (
        P(None, "span", "wrap", "normal"),
        P("span", "wrap", "normal"),
        P(),
        P("span", "wrap"),
        P("span", "wrap"),
    ) + (P(),) * 6
    return jax.shard_map(
        step,
        mesh=mesh,
        in_specs=placed,
        out_specs=(P(None, "span", "wrap", "normal"), P()),
        check_vma=False,
    )
```

```python
import functools

import jax
import jax.numpy as jnp
from jax import lax
from jax.experimental import pallas as pl
from jax.experimental.pallas import tpu as pltpu
from jax.sharding import PartitionSpec as P

MESH = pl.DeviceIdType.MESH
VARS = 5
STATIONS = 128
NEWTON = 3
DT_FLOW = 0.2
DISSIPATION = 0.03
DT_BEAM = 0.2
STOP_GAP = 0.5
CONTACT_STIFF = 40.0
SPAN, WRAP, LANES = 8, 16, 128
TOP = 8


def lane_of(shape):
    return lax.broadcasted_iota(jnp.int32, shape, len(shape) - 1)


def roll(x, shift):
    return pltpu.roll(x, shift % LANES if isinstance(shift, int) else shift, 1)


def factor(be, bo, diag_e, diag_o):
    lane = lane_of((1, LANES))
    half = LANES // 2
    valid, inner = lane < half, lane < half - 1
    bo_prev, be_next = roll(bo, 1), roll(be, -1)
    p = jnp.where(valid, 4.0 * be + bo_prev + bo + diag_e, 1.0)
    q = jnp.where(valid, -2.0 * (be + bo), 0.0)
    r = jnp.where(valid, 4.0 * bo + be + be_next + diag_o, 1.0)
    c11 = jnp.where(inner, bo, 0.0)
    c12 = jnp.zeros_like(bo)
    c21 = jnp.where(inner, -2.0 * (bo + be_next), 0.0)
    c22 = jnp.where(inner, be_next, 0.0)
    a11, a12, a21, a22 = roll(c11, 1), roll(c21, 1), c12, roll(c22, 1)
    levels = []
    step = 1
    while step < half:
        inv = 1.0 / (p * r - q * q)
        w11, w12, w22 = r * inv, -q * inv, p * inv
        u11, u12 = c11 * w11 + c21 * w12, c11 * w12 + c21 * w22
        u21, u22 = c12 * w11 + c22 * w12, c12 * w12 + c22 * w22
        d11, d12 = a11 * w11 + a21 * w12, a11 * w12 + a21 * w22
        d21, d22 = a12 * w11 + a22 * w12, a12 * w12 + a22 * w22
        levels.append((step, u11, u12, u21, u22, d11, d12, d21, d22))
        p = p - roll(u11 * c11 + u12 * c21, step) - roll(d11 * a11 + d12 * a21, -step)
        q = q - roll(u11 * c12 + u12 * c22, step) - roll(d11 * a12 + d12 * a22, -step)
        r = r - roll(u21 * c12 + u22 * c22, step) - roll(d21 * a12 + d22 * a22, -step)
        if 2 * step < half:
            n11, n12 = -(d11 * c11 + d12 * c21), -(d11 * c12 + d12 * c22)
            n21, n22 = -(d21 * c11 + d22 * c21), -(d21 * c12 + d22 * c22)
            c11, c12 = roll(n11, -step), roll(n12, -step)
            c21, c22 = roll(n21, -step), roll(n22, -step)
            a11, a12 = roll(n11, step), roll(n21, step)
            a21, a22 = roll(n12, step), roll(n22, step)
        step *= 2
    inv = 1.0 / (p * r - q * q)
    return levels, (r * inv, -q * inv, p * inv)


def substitute(factors, e, o):
    levels, (w11, w12, w22) = factors
    for step, u11, u12, u21, u22, d11, d12, d21, d22 in levels:
        e, o = (
            e - roll(u11 * e + u12 * o, step) - roll(d11 * e + d12 * o, -step),
            o - roll(u21 * e + u22 * o, step) - roll(d21 * e + d22 * o, -step),
        )
    return w11 * e + w12 * o, w12 * e + w22 * o


def right_side(fe, fo, he, ho, ue, uo):
    return fe + 2.0 * he * ue * ue * ue, fo + 2.0 * ho * uo * uo * uo


def halves(x):
    valid = lane_of((1, LANES)) < LANES // 2
    return jnp.where(valid, x, 0.0), jnp.where(valid, roll(x, LANES // 2), 0.0)


def pack_plane(packed, cells, s):
    slot = lane_of((8, LANES)) // 4
    new = []
    for v in range(VARS):
        have = packed[v]
        for t in range(2):
            k = 2 * s + t
            have = jnp.where(slot == k, roll(cells[v][t], 4 * k + 2), have)
        new.append(have)
    return tuple(new)


def edge_terms(normal, n_norm, own, left, right, jac, corr):
    lane = lane_of((8, LANES))
    place = lane % 4
    ends, smooths = [], []
    for v in range(VARS):
        mine = own[v]
        mirror = jnp.where(place == 0, roll(mine, -3), roll(mine, -1))
        low = jnp.where(normal == 0, mirror, left[v])
        high = jnp.where(normal == n_norm - 1, 0.0, right[v])
        delta = jnp.where(place < 2, roll(high - mine, -2), roll(low - mine, 2))
        near = jnp.where(place == 1, roll(delta, 1), jnp.where(place == 2, roll(delta, -1), 0.0))
        end = delta - 8.0 * near
        ends.append(jnp.where(place < 2, -end, end))
        smooths.append(delta - 4.0 * near)
    for u in range(VARS):
        total = -DISSIPATION * smooths[u]
        for v in range(VARS):
            total = total + jac[50 + 5 * u + v] * ends[v]
        corr[u] = total


def plane_rates(field, s, jac, corr):
    lane = lane_of((8, LANES))
    edge = (lane < 2) | (lane >= LANES - 2)
    cells, grads, smooths = [], [[], [], []], []
    for v in range(VARS):

        def at(ds, dw):
            return field[v, s + (2 + ds), TOP + dw : TOP + dw + WRAP, :]

        c = at(0, 0)
        reads = [
            [at(k, 0) for k in (-2, -1, 1, 2)],
            [at(0, k) for k in (-2, -1, 1, 2)],
            [roll(c, -k) for k in (-2, -1, 1, 2)],
        ]
        near, far = None, None
        for d, (m2, m1, p1, p2) in enumerate(reads):
            grads[d].append(((m2 - p2) + 8.0 * (p1 - m1)).reshape(2, 8, LANES))
            near = (m1 + p1) if near is None else near + (m1 + p1)
            far = (m2 + p2) if far is None else far + (m2 + p2)
        smooths.append((-DISSIPATION * (far - 4.0 * near + 18.0 * c)).reshape(2, 8, LANES))
        cells.append(c.reshape(2, 8, LANES))
    rates = []
    for u in range(VARS):
        total = smooths[u]
        for d in range(3):
            for v in range(VARS):
                total = total + jac[25 * d + 5 * u + v][None] * grads[d][v]
        ends = corr[u]
        fix = [
            jnp.where(edge, roll(ends, (2 * LANES - 2 - 4 * (2 * s + t)) % LANES), 0.0)
            for t in range(2)
        ]
        rates.append(total + jnp.stack(fix))
    return cells, rates


def pack_wall(field, volume, packed):
    group = lane_of((8, LANES)) // 8
    for v in range(VARS + 1):
        for t in range(2):
            have = jnp.zeros((8, LANES), jnp.float32)
            for s in range(SPAN):
                if v < VARS:
                    tile = field[v, s + 2, TOP + 8 * t : TOP + 8 * t + 8, :]
                else:
                    tile = volume[s, 8 * t : 8 * t + 8, :]
                have = jnp.where(group == s + 4, roll(tile, 8 * (s + 4) + 2), have)
            packed[v, 8 * t : 8 * t + 8, :] = have


def mirrored(x):
    place = lane_of(x.shape) % 8
    return jnp.where(place == 0, roll(x, -3), jnp.where(place == 1, roll(x, -1), x))


def wall_rates(layer, top, rows, wanted, jac):
    cells, grads, smooths = [], [[], [], []], []
    shape = (rows // 8, 8, LANES)
    for v in range(VARS):
        c = layer[v, top : top + rows, :]
        reads = [
            [roll(c, -8 * k) for k in (-2, -1, 1, 2)],
            [layer[v, top + k : top + k + rows, :] for k in (-2, -1, 1, 2)],
            [roll(c, -k) for k in (-2, -1, 1, 2)],
        ]
        near, far = None, None
        for d, (m2, m1, p1, p2) in enumerate(reads):
            grads[d].append(((m2 - p2) + 8.0 * (p1 - m1)).reshape(shape))
            near = (m1 + p1) if near is None else near + (m1 + p1)
            far = (m2 + p2) if far is None else far + (m2 + p2)
        smooths.append((-DISSIPATION * (far - 4.0 * near + 18.0 * c)).reshape(shape))
        cells.append(c)
    rates = []
    for u in range(wanted):
        total = smooths[u]
        for d in range(3):
            for v in range(VARS):
                total = total + jac[25 * d + 5 * u + v][None] * grads[d][v]
        rates.append(total.reshape(rows, LANES))
    return cells, rates


def wall_loads(span, n_span, packed, beside, corner, layer, mid, faces, jac):
    group = lane_of((8, LANES)) // 8
    first, last = span == 0, span == n_span - 1
    for v in range(VARS + 1):
        tiles = [
            (corner[0, v], beside[2, v, 0:8], corner[1, v]),
            (beside[0, v, 0:8], packed[v, 0:8], beside[1, v, 0:8]),
            (beside[0, v, 8:16], packed[v, 8:16], beside[1, v, 8:16]),
            (corner[2, v], beside[3, v, 0:8], corner[3, v]),
        ]
        for t, (left, centre, right) in enumerate(tiles):
            left = jnp.where(first, 0.0, roll(left, LANES // 2))
            right = jnp.where(last, 0.0, roll(right, LANES // 2))
            whole = jnp.where(group < 4, left, jnp.where(group >= 12, right, centre))
            layer[v, 8 * t : 8 * t + 8, :] = mirrored(whole)
    span_group = lane_of((24, LANES)) // 8
    outside = (first & (span_group < 4)) | (last & (span_group >= 12))
    cells, rates = wall_rates(layer, 4, 24, VARS, jac)
    scale = DT_FLOW * layer[VARS, 4:28, :]
    for u in range(VARS):
        mid[u] = mirrored(jnp.where(outside, 0.0, cells[u] + scale * rates[u]))
    cells, rates = wall_rates(mid, 4, 16, 1, jac)
    scale = DT_FLOW * layer[VARS, 8:24, :]
    after = 0.5 * (layer[0, 8:24, :] + cells[0] + scale * rates[0])
    total = jnp.zeros((WRAP, LANES), jnp.float32)
    for s in range(SPAN):
        at = 8 * (s + 4) + 2
        total = total + faces[s] * jnp.broadcast_to(after[:, at : at + 1], (WRAP, LANES))
    return total[0:8] + total[8:16]


def kernel(
    n_span,
    n_wrap,
    n_norm,
    flow_hbm,
    volume_hbm,
    jac_smem,
    area_hbm,
    map_hbm,
    contact_hbm,
    bending_hbm,
    mass_hbm,
    hardening_hbm,
    disp_hbm,
    vel_hbm,
    out_hbm,
    state_ref,
    field1,
    field2,
    volume,
    wall_send,
    wall_recv,
    edges,
    corr,
    jac,
    result,
    faces,
    area,
    stations,
    contact_v,
    beam_v,
    loads_a,
    loads_b,
    tally,
    wall_packed,
    wall_beside,
    wall_corner,
    wall_layer,
    wall_mid,
    local_sem,
    send_sem,
    recv_sem,
    group_sem,
    wide_send_sem,
    wide_recv_sem,
):
    span, wrap, normal = lax.axis_index("span"), lax.axis_index("wrap"), lax.axis_index("normal")
    rows = 2
    cols = n_span // rows
    row, col = span // cols, span % cols

    inputs = [
        (flow_hbm, field1.at[:, 2 : 2 + SPAN, TOP : TOP + WRAP, :]),
        (volume_hbm, volume),
        (area_hbm, area),
        (map_hbm, stations),
        (contact_hbm, contact_v),
        (bending_hbm, beam_v.at[0]),
        (mass_hbm, beam_v.at[1]),
        (hardening_hbm, beam_v.at[2]),
        (disp_hbm, beam_v.at[3]),
        (vel_hbm, beam_v.at[4]),
    ]
    reads = [pltpu.make_async_copy(a, b, local_sem.at[i]) for i, (a, b) in enumerate(inputs)]
    for read in reads:
        read.start()

    def turned(index, by, count):
        return (index + (by + count)) % count

    span_at = {by: turned(span, by, n_span) for by in (-1, 1)}
    wrap_at = [turned(wrap, by, n_wrap) for by in range(n_wrap)]
    norm_at = {by: turned(normal, by, n_norm) for by in (-1, 1)}
    row_at = [turned(row, by, rows) for by in range(rows)]
    col_at = [turned(col, by, cols) for by in range(cols)]
    sides = [
        (span_at[-1], wrap, normal),
        (span_at[1], wrap, normal),
        (span, wrap_at[n_wrap - 1], normal),
        (span, wrap_at[1], normal),
        (span, wrap, norm_at[-1]),
        (span, wrap, norm_at[1]),
    ]
    barrier = pltpu.get_barrier_semaphore()

    def greet(target):
        pl.semaphore_signal(barrier, inc=1, device_id=target, device_id_type=MESH)

    corners = [(span_at[i], wrap_at[j], normal) for j in (n_wrap - 1, 1) for i in (-1, 1)]

    for side in sides:
        greet(side)

    @pl.when(normal == 0)
    def _():
        for one in corners:
            greet(one)

    for a in range(rows):
        for b in range(n_wrap):
            source = (row_at[-a % rows] * cols + col, wrap_at[-b % n_wrap], 0)
            if a == 0 and b == 0:

                @pl.when(normal != 0)
                def _():
                    greet(source)

            else:
                greet(source)
    for k in range(1, cols):
        greet((row * cols + col_at[-k % cols], wrap, normal))

    for d in range(3):
        for u in range(VARS):
            for v in range(VARS):
                scaled = jac_smem[u, d, v] * (-1.0 / 12.0)
                jac[25 * d + 5 * u + v] = jnp.full((8, LANES), scaled, jnp.float32)

    def copy(src, dst, slot, target):
        return pltpu.make_async_remote_copy(
            src_ref=src,
            dst_ref=dst,
            send_sem=send_sem.at[slot],
            recv_sem=recv_sem.at[slot],
            device_id=target,
            device_id_type=MESH,
        )

    def stage_copies(stage, field):
        cells = pl.ds(TOP, WRAP)
        base = 6 * stage
        pairs = [
            (field.at[:, 2:4, cells, :], field.at[:, 2 + SPAN : 4 + SPAN, cells, :]),
            (field.at[:, SPAN : 2 + SPAN, cells, :], field.at[:, 0:2, cells, :]),
            (wall_send.at[stage, 0], wall_recv.at[stage, 0]),
            (wall_send.at[stage, 1], wall_recv.at[stage, 1]),
            (edges.at[stage, 0], edges.at[stage, 2]),
            (edges.at[stage, 0], edges.at[stage, 1]),
        ]
        return [copy(src, dst, base + i, sides[i]) for i, (src, dst) in enumerate(pairs)]

    def stage_wrap_rows(stage, field):
        for v in range(VARS):
            for r in range(2):
                wall_send[stage, 0, v, r] = field[v, 2 : 2 + SPAN, TOP + r, :]
                wall_send[stage, 1, v, r] = field[v, 2 : 2 + SPAN, TOP + WRAP - 2 + r, :]

    def stage_arrive(stage, field):
        zeros = jnp.zeros((VARS, 2, WRAP, LANES), jnp.float32)

        @pl.when(span == 0)
        def _():
            field[:, 0:2, TOP : TOP + WRAP, :] = zeros

        @pl.when(span == n_span - 1)
        def _():
            field[:, 2 + SPAN : 4 + SPAN, TOP : TOP + WRAP, :] = zeros

        for v in range(VARS):
            for r in range(2):
                field[v, 2 : 2 + SPAN, TOP + WRAP + r, :] = wall_recv[stage, 0, v, r]
                field[v, 2 : 2 + SPAN, TOP - 2 + r, :] = wall_recv[stage, 1, v, r]
        edge_terms(
            normal, n_norm, edges.at[stage, 0], edges.at[stage, 1], edges.at[stage, 2], jac, corr
        )

    whole, low, high = pl.ds(0, WRAP), pl.ds(0, 8), pl.ds(8, 8)
    wide = []
    for i, (target, part, land) in enumerate(
        [
            (sides[0], whole, wall_beside.at[1]),
            (sides[1], whole, wall_beside.at[0]),
            (sides[2], low, wall_beside.at[3, :, low]),
            (sides[3], high, wall_beside.at[2, :, low]),
            (corners[0], low, wall_corner.at[3]),
            (corners[1], low, wall_corner.at[2]),
            (corners[2], high, wall_corner.at[1]),
            (corners[3], high, wall_corner.at[0]),
        ]
    ):
        wide.append(
            pltpu.make_async_remote_copy(
                src_ref=wall_packed.at[:, part],
                dst_ref=land,
                send_sem=wide_send_sem.at[i],
                recv_sem=wide_recv_sem.at[i],
                device_id=target,
                device_id_type=MESH,
            )
        )

    empty = tuple(jnp.zeros((8, LANES), jnp.float32) for _ in range(VARS))

    reads[0].wait()
    reads[1].wait()

    @pl.when(normal == 0)
    def _():
        pack_wall(field1, volume, wall_packed)

    stage_wrap_rows(0, field1)

    def pack_first(s, packed):
        cells = [
            field1[v, s + 2, TOP : TOP + WRAP, :].reshape(2, 8, LANES) for v in range(VARS)
        ]
        return pack_plane(packed, cells, s)

    packed = lax.fori_loop(0, SPAN, pack_first, empty, unroll=True)
    for v in range(VARS):
        edges[0, 0, v] = packed[v]

    at_wall = (n_norm - normal) // n_norm
    pl.semaphore_wait(barrier, 5 + cols + at_wall * (rows * n_wrap * n_norm + 3))

    @pl.when(normal == 0)
    def _():
        for one in wide:
            one.start()

    first = stage_copies(0, field1)
    for one in first:
        one.start()

    for read in reads[2:]:
        read.wait()
    lane = lane_of((8, LANES))
    held = jnp.where(lane < LANES // 2, 2 * lane, 2 * lane - (LANES - 1))

    def group_copy(buffer, slot, which, target):
        return pltpu.make_async_remote_copy(
            src_ref=buffer.at[0],
            dst_ref=buffer.at[slot],
            send_sem=group_sem.at[2 * which],
            recv_sem=group_sem.at[2 * which + 1],
            device_id=target,
            device_id_type=MESH,
        )

    def take(ref, which):
        pltpu.make_async_copy(ref, ref, group_sem.at[which]).wait()

    def permuted(x):
        full = jnp.broadcast_to(x, (8, LANES))
        return jnp.take_along_axis(full, held, axis=1)[0:1]

    bending, mass, hardening, disp, vel = [permuted(beam_v[i]) for i in range(5)]
    contact = permuted(contact_v[...])
    inertia = 2.0 * mass / (DT_BEAM * DT_BEAM)
    pull = CONTACT_STIFF * STOP_GAP
    push = jnp.where(contact == 1, pull, jnp.where(contact == 2, -pull, 0.0))
    steady = inertia * (disp + DT_BEAM * vel) + push
    base = inertia + jnp.where(contact > 0, CONTACT_STIFF, 0.0)
    be, bo = halves(bending)
    he, ho = halves(hardening)
    ge, go = halves(base)
    ue, uo = halves(disp)
    fe, fo = halves(steady)
    factors = factor(be, bo, ge + 3.0 * he * ue * ue, go + 3.0 * ho * uo * uo)

    @pl.when(normal == 0)
    def _():
        row_id = lax.broadcasted_iota(jnp.int32, (WRAP, WRAP), 0)
        same = (row_id == lane_of((WRAP, WRAP))).astype(jnp.float32)

        def turned_over(x):
            return lax.dot_general(
                same, x, (((1,), (1,)), ((), ())), precision=lax.Precision.HIGHEST
            )

        weights = turned_over(area[...])
        places = turned_over(stations[...].astype(jnp.float32))
        aims = jnp.broadcast_to(held[0:1], (WRAP, LANES)).astype(jnp.float32)
        for s in range(SPAN):
            weight = jnp.broadcast_to(weights[:, s : s + 1], (WRAP, LANES))
            place = jnp.broadcast_to(places[:, s : s + 1], (WRAP, LANES))
            faces[s] = jnp.where(place == aims, weight, 0.0)
        for one in wide:
            one.wait_recv()
        loads_a[0] = wall_loads(
            span,
            n_span,
            wall_packed,
            wall_beside,
            wall_corner,
            wall_layer,
            wall_mid,
            faces,
            jac,
        )
        for a in range(rows):
            for b in range(n_wrap):
                for c in range(n_norm):
                    if a or b or c:
                        target = (row_at[a] * cols + col, wrap_at[b], c)
                        group_copy(loads_a, a * n_wrap + b, 0, target).start()

    for one in first:
        one.wait_recv()
    stage_arrive(0, field1)

    def first_plane(s, packed):
        cells, rates = plane_rates(field1, s, jac, corr)
        scale = DT_FLOW * volume[s].reshape(2, 8, LANES)
        mids = [cells[u] + scale * rates[u] for u in range(VARS)]
        for u in range(VARS):
            field2[u, s + 2, TOP : TOP + WRAP, :] = mids[u].reshape(WRAP, LANES)
        return pack_plane(packed, mids, s)

    packed = lax.fori_loop(0, SPAN, first_plane, empty)
    for v in range(VARS):
        edges[1, 0, v] = packed[v]

    stage_wrap_rows(1, field2)
    second = stage_copies(1, field2)
    for one in second:
        one.start()
    @pl.when(normal == 0)
    def _():
        take(loads_a.at[1:], 1)

    @pl.when(normal != 0)
    def _():
        take(loads_a, 1)

    count_a = rows * n_wrap
    total = None
    for y in range(count_a):
        a = (row + (rows - y // n_wrap)) % rows
        b = (wrap + (n_wrap - y % n_wrap)) % n_wrap
        term = loads_a[a * n_wrap + b]
        total = term if total is None else total + term
    loads_b[0] = total
    for k in range(1, cols):
        group_copy(loads_b, k, 1, (row * cols + col_at[k], wrap, normal)).start()
    for one in second:
        one.wait_recv()
    stage_arrive(1, field2)

    def second_plane(s, carry):
        cells, rates = plane_rates(field2, s, jac, corr)
        scale = DT_FLOW * volume[s].reshape(2, 8, LANES)
        for u in range(VARS):
            start = field1[u, s + 2, TOP : TOP + WRAP, :].reshape(2, 8, LANES)
            after = 0.5 * (start + cells[u] + scale * rates[u])
            result[u, s] = after.reshape(WRAP, LANES)
        return carry

    lax.fori_loop(0, SPAN, second_plane, 0)

    write = pltpu.make_async_copy(result, out_hbm, local_sem.at[len(inputs)])
    write.start()

    take(loads_b.at[1:], 3)
    total = None
    for z in range(cols):
        term = loads_b[(col + (cols - z)) % cols]
        total = term if total is None else total + term
    loads = jnp.sum(total, axis=0, keepdims=True)

    le, lo = halves(loads)
    fe, fo = fe + le, fo + lo
    ue, uo = substitute(factors, *right_side(fe, fo, he, ho, ue, uo))
    for i, x in enumerate((be, bo, ge, go, he, ho, fe, fo, ue, uo)):
        state_ref[i : i + 1, :] = x

    for one in first + second:
        one.wait_send()

    @pl.when(normal == 0)
    def _():
        for one in wide:
            one.wait_send()
        take(tally, 0)

    take(loads_b.at[1:], 2)
    write.wait()


def beam_kernel(state_ref, flow_hbm, out_hbm, defl_ref, held, read_sem, write_sem):
    def each(src, dst, sem):
        return [pltpu.make_async_copy(src.at[v], dst.at[v], sem.at[v]) for v in range(VARS)]

    reads, writes = each(flow_hbm, held, read_sem), each(held, out_hbm, write_sem)
    for read in reads:
        read.start()
    for read, write in zip(reads, writes):
        read.wait()
        write.start()
    be, bo, ge, go, he, ho, fe, fo, ue, uo = [state_ref[i : i + 1, :] for i in range(10)]
    for _ in range(NEWTON - 1):
        factors = factor(be, bo, ge + 3.0 * he * ue * ue, go + 3.0 * ho * uo * uo)
        ue, uo = substitute(factors, *right_side(fe, fo, he, ho, ue, uo))
    both = jnp.where(lane_of((1, LANES)) < LANES // 2, ue, roll(uo, LANES // 2))
    lane = lane_of((8, LANES))
    back = (lane % 2) * (LANES // 2) + lane // 2
    full = jnp.broadcast_to(both, (8, LANES))
    defl_ref[...] = jnp.take_along_axis(full, back, axis=1)[0:1]
    for write in writes:
        write.wait()


def solution(mesh):
    n_span, n_wrap, n_norm = (mesh.shape[axis] for axis in ("span", "wrap", "normal"))
    cols, ys = n_span // 2, 2 * n_wrap
    f32 = jnp.float32

    def step(
        flow_state,
        inv_volume,
        flux_jacobians,
        area,
        station_map,
        contact,
        bending,
        mass,
        hardening,
        disp_old,
        vel_old,
    ):
        vectors = [
            x.reshape(1, STATIONS) for x in (contact, bending, mass, hardening, disp_old, vel_old)
        ]
        hbm = pl.BlockSpec(memory_space=pltpu.HBM)
        flow_next, state = pl.pallas_call(
            functools.partial(kernel, n_span, n_wrap, n_norm),
            out_shape=(
                jax.ShapeDtypeStruct(flow_state.shape, f32),
                jax.ShapeDtypeStruct((16, LANES), f32),
            ),
            in_specs=[hbm, hbm, pl.BlockSpec(memory_space=pltpu.SMEM)] + [hbm] * 8,
            out_specs=(hbm, pl.BlockSpec(memory_space=pltpu.VMEM)),
            scratch_shapes=[
                pltpu.VMEM((VARS, SPAN + 4, WRAP + 16, LANES), f32),
                pltpu.VMEM((VARS, SPAN + 4, WRAP + 16, LANES), f32),
                pltpu.VMEM((SPAN, WRAP, LANES), f32),
                pltpu.VMEM((2, 2, VARS, 2, SPAN, LANES), f32),
                pltpu.VMEM((2, 2, VARS, 2, SPAN, LANES), f32),
                pltpu.VMEM((2, 3, VARS, 8, LANES), f32),
                pltpu.VMEM((VARS, 8, LANES), f32),
                pltpu.VMEM((75, 8, LANES), f32),
                pltpu.VMEM((VARS, SPAN, WRAP, LANES), f32),
                pltpu.VMEM((SPAN, WRAP, LANES), f32),
                pltpu.VMEM((SPAN, WRAP), f32),
                pltpu.VMEM((SPAN, WRAP), jnp.int32),
                pltpu.VMEM((1, STATIONS), jnp.int32),
                pltpu.VMEM((5, 1, STATIONS), f32),
                pltpu.VMEM((ys, 8, LANES), f32),
                pltpu.VMEM((cols, 8, LANES), f32),
                pltpu.VMEM((ys * n_norm - 1, 8, LANES), f32),
                pltpu.VMEM((VARS + 1, WRAP, LANES), f32),
                pltpu.VMEM((4, VARS + 1, WRAP, LANES), f32),
                pltpu.VMEM((4, VARS + 1, 8, LANES), f32),
                pltpu.VMEM((VARS + 1, WRAP + 16, LANES), f32),
                pltpu.VMEM((VARS, 24, LANES), f32),
                pltpu.SemaphoreType.DMA((11,)),
                pltpu.SemaphoreType.DMA((12,)),
                pltpu.SemaphoreType.DMA((12,)),
                pltpu.SemaphoreType.DMA((4,)),
                pltpu.SemaphoreType.DMA((8,)),
                pltpu.SemaphoreType.DMA((8,)),
            ],
            compiler_params=pltpu.CompilerParams(
                collective_id=0, has_side_effects=True, vmem_limit_bytes=60 * 1024 * 1024
            ),
            cost_estimate=pl.CostEstimate(
                flops=10_000_000, bytes_accessed=1_000_000, transcendentals=0
            ),
        )(flow_state, inv_volume, flux_jacobians.transpose(1, 0, 2), area, station_map, *vectors)
        flow_next, deflection = pl.pallas_call(
            beam_kernel,
            out_shape=(
                jax.ShapeDtypeStruct(flow_state.shape, f32),
                jax.ShapeDtypeStruct((1, STATIONS), f32),
            ),
            in_specs=[pl.BlockSpec(memory_space=pltpu.VMEM), hbm],
            out_specs=(hbm, pl.BlockSpec(memory_space=pltpu.VMEM)),
            scratch_shapes=[
                pltpu.VMEM((VARS, SPAN, WRAP, LANES), f32),
                pltpu.SemaphoreType.DMA((VARS,)),
                pltpu.SemaphoreType.DMA((VARS,)),
            ],
            compiler_params=pltpu.CompilerParams(vmem_limit_bytes=60 * 1024 * 1024),
        )(state, flow_next)
        return flow_next, deflection.reshape(STATIONS)

    placed = (
        P(None, "span", "wrap", "normal"),
        P("span", "wrap", "normal"),
        P(),
        P("span", "wrap"),
        P("span", "wrap"),
    ) + (P(),) * 6
    return jax.shard_map(
        step,
        mesh=mesh,
        in_specs=placed,
        out_specs=(P(None, "span", "wrap", "normal"), P()),
        check_vma=False,
    )
```

```python
import functools

import jax
import jax.numpy as jnp
from jax import lax
from jax.experimental import pallas as pl
from jax.experimental.pallas import tpu as pltpu
from jax.sharding import PartitionSpec as P

MESH = pl.DeviceIdType.MESH
VARS = 5
STATIONS = 128
NEWTON = 3
DT_FLOW = 0.2
DISSIPATION = 0.03
DT_BEAM = 0.2
STOP_GAP = 0.5
CONTACT_STIFF = 40.0
SPAN, WRAP, LANES = 8, 16, 128
TOP = 8


def lane_of(shape):
    return lax.broadcasted_iota(jnp.int32, shape, len(shape) - 1)


def roll(x, shift):
    return pltpu.roll(x, shift % LANES if isinstance(shift, int) else shift, 1)


def factor(be, bo, diag_e, diag_o):
    lane = lane_of((1, LANES))
    half = LANES // 2
    valid, inner = lane < half, lane < half - 1
    bo_prev, be_next = roll(bo, 1), roll(be, -1)
    p = jnp.where(valid, 4.0 * be + bo_prev + bo + diag_e, 1.0)
    q = jnp.where(valid, -2.0 * (be + bo), 0.0)
    r = jnp.where(valid, 4.0 * bo + be + be_next + diag_o, 1.0)
    c11 = jnp.where(inner, bo, 0.0)
    c12 = jnp.zeros_like(bo)
    c21 = jnp.where(inner, -2.0 * (bo + be_next), 0.0)
    c22 = jnp.where(inner, be_next, 0.0)
    a11, a12, a21, a22 = roll(c11, 1), roll(c21, 1), c12, roll(c22, 1)
    levels = []
    step = 1
    while step < half:
        inv = 1.0 / (p * r - q * q)
        w11, w12, w22 = r * inv, -q * inv, p * inv
        u11, u12 = c11 * w11 + c21 * w12, c11 * w12 + c21 * w22
        u21, u22 = c12 * w11 + c22 * w12, c12 * w12 + c22 * w22
        d11, d12 = a11 * w11 + a21 * w12, a11 * w12 + a21 * w22
        d21, d22 = a12 * w11 + a22 * w12, a12 * w12 + a22 * w22
        levels.append((step, u11, u12, u21, u22, d11, d12, d21, d22))
        p = p - roll(u11 * c11 + u12 * c21, step) - roll(d11 * a11 + d12 * a21, -step)
        q = q - roll(u11 * c12 + u12 * c22, step) - roll(d11 * a12 + d12 * a22, -step)
        r = r - roll(u21 * c12 + u22 * c22, step) - roll(d21 * a12 + d22 * a22, -step)
        if 2 * step < half:
            n11, n12 = -(d11 * c11 + d12 * c21), -(d11 * c12 + d12 * c22)
            n21, n22 = -(d21 * c11 + d22 * c21), -(d21 * c12 + d22 * c22)
            c11, c12 = roll(n11, -step), roll(n12, -step)
            c21, c22 = roll(n21, -step), roll(n22, -step)
            a11, a12 = roll(n11, step), roll(n21, step)
            a21, a22 = roll(n12, step), roll(n22, step)
        step *= 2
    inv = 1.0 / (p * r - q * q)
    return levels, (r * inv, -q * inv, p * inv)


def substitute(factors, e, o):
    levels, (w11, w12, w22) = factors
    for step, u11, u12, u21, u22, d11, d12, d21, d22 in levels:
        e, o = (
            e - roll(u11 * e + u12 * o, step) - roll(d11 * e + d12 * o, -step),
            o - roll(u21 * e + u22 * o, step) - roll(d21 * e + d22 * o, -step),
        )
    return w11 * e + w12 * o, w12 * e + w22 * o


def right_side(fe, fo, he, ho, ue, uo):
    return fe + 2.0 * he * ue * ue * ue, fo + 2.0 * ho * uo * uo * uo


def halves(x):
    valid = lane_of((1, LANES)) < LANES // 2
    return jnp.where(valid, x, 0.0), jnp.where(valid, roll(x, LANES // 2), 0.0)


def pack_plane(packed, cells, s):
    slot = lane_of((8, LANES)) // 4
    new = []
    for v in range(VARS):
        have = packed[v]
        for t in range(2):
            k = 2 * s + t
            have = jnp.where(slot == k, roll(cells[v][t], 4 * k + 2), have)
        new.append(have)
    return tuple(new)


def edge_terms(normal, n_norm, own, left, right, jac, corr):
    lane = lane_of((8, LANES))
    place = lane % 4
    ends, smooths = [], []
    for v in range(VARS):
        mine = own[v]
        mirror = jnp.where(place == 0, roll(mine, -3), roll(mine, -1))
        low = jnp.where(normal == 0, mirror, left[v])
        high = jnp.where(normal == n_norm - 1, 0.0, right[v])
        delta = jnp.where(place < 2, roll(high - mine, -2), roll(low - mine, 2))
        near = jnp.where(place == 1, roll(delta, 1), jnp.where(place == 2, roll(delta, -1), 0.0))
        end = delta - 8.0 * near
        ends.append(jnp.where(place < 2, -end, end))
        smooths.append(delta - 4.0 * near)
    for u in range(VARS):
        total = -DISSIPATION * smooths[u]
        for v in range(VARS):
            total = total + jac[50 + 5 * u + v] * ends[v]
        corr[u] = total


def plane_rates(field, s, jac, corr):
    lane = lane_of((8, LANES))
    edge = (lane < 2) | (lane >= LANES - 2)
    cells, grads, smooths = [], [[], [], []], []
    for v in range(VARS):

        def at(ds, dw):
            return field[v, s + (2 + ds), TOP + dw : TOP + dw + WRAP, :]

        c = at(0, 0)
        reads = [
            [at(k, 0) for k in (-2, -1, 1, 2)],
            [at(0, k) for k in (-2, -1, 1, 2)],
            [roll(c, -k) for k in (-2, -1, 1, 2)],
        ]
        near, far = None, None
        for d, (m2, m1, p1, p2) in enumerate(reads):
            grads[d].append(((m2 - p2) + 8.0 * (p1 - m1)).reshape(2, 8, LANES))
            near = (m1 + p1) if near is None else near + (m1 + p1)
            far = (m2 + p2) if far is None else far + (m2 + p2)
        smooths.append((-DISSIPATION * (far - 4.0 * near + 18.0 * c)).reshape(2, 8, LANES))
        cells.append(c.reshape(2, 8, LANES))
    rates = []
    for u in range(VARS):
        total = smooths[u]
        for d in range(3):
            for v in range(VARS):
                total = total + jac[25 * d + 5 * u + v][None] * grads[d][v]
        ends = corr[u]
        fix = [
            jnp.where(edge, roll(ends, (2 * LANES - 2 - 4 * (2 * s + t)) % LANES), 0.0)
            for t in range(2)
        ]
        rates.append(total + jnp.stack(fix))
    return cells, rates


def pack_wall(field, volume, packed):
    group = lane_of((8, LANES)) // 8
    for v in range(VARS + 1):
        for t in range(2):
            have = jnp.zeros((8, LANES), jnp.float32)
            for s in range(SPAN):
                if v < VARS:
                    tile = field[v, s + 2, TOP + 8 * t : TOP + 8 * t + 8, :]
                else:
                    tile = volume[s, 8 * t : 8 * t + 8, :]
                have = jnp.where(group == s + 4, roll(tile, 8 * (s + 4) + 2), have)
            packed[v, 8 * t : 8 * t + 8, :] = have


def pair_wall(packed, pairs, edge, tip):
    lane, row = lane_of((8, LANES)), lax.broadcasted_iota(jnp.int32, (8, LANES), 0)
    own = (lane >= LANES // 4) & (lane < 3 * LANES // 4)
    for p in range(3):
        for t in range(2):
            rows = slice(8 * t, 8 * t + 8)
            pairs[p, rows, :] = jnp.where(own, packed[p, rows, :], roll(packed[p + 3, rows, :], 64))
    for t in range(2):
        a, b, c = (pairs[p, 8 * t : 8 * t + 8, :] for p in range(3))
        four = row < 4
        edge[t, 0] = jnp.where(four, a if t == 0 else pltpu.roll(a, 4, 0), b if t else pltpu.roll(b, 4, 0))
        edge[t, 1] = c
        at = 6 * t
        tip[t] = jnp.where(
            row < 2,
            turn_rows(a, -at),
            jnp.where(four, turn_rows(b, 2 - at), turn_rows(c, 4 - at)),
        )


def turn_rows(x, by):
    return pltpu.roll(x, by % 8, 0) if by % 8 else x


def mirrored(x):
    place = lane_of(x.shape) % 8
    return jnp.where(place == 0, roll(x, -3), jnp.where(place == 1, roll(x, -1), x))


def wall_rates(layer, top, rows, wanted, jac):
    cells, grads, smooths = [], [[], [], []], []
    shape = (rows // 8, 8, LANES)
    for v in range(VARS):
        c = layer[v, top : top + rows, :]
        reads = [
            [roll(c, -8 * k) for k in (-2, -1, 1, 2)],
            [layer[v, top + k : top + k + rows, :] for k in (-2, -1, 1, 2)],
            [roll(c, -k) for k in (-2, -1, 1, 2)],
        ]
        near, far = None, None
        for d, (m2, m1, p1, p2) in enumerate(reads):
            grads[d].append(((m2 - p2) + 8.0 * (p1 - m1)).reshape(shape))
            near = (m1 + p1) if near is None else near + (m1 + p1)
            far = (m2 + p2) if far is None else far + (m2 + p2)
        smooths.append((-DISSIPATION * (far - 4.0 * near + 18.0 * c)).reshape(shape))
        cells.append(c)
    rates = []
    for u in range(wanted):
        total = smooths[u]
        for d in range(3):
            for v in range(VARS):
                total = total + jac[25 * d + 5 * u + v][None] * grads[d][v]
        rates.append(total.reshape(rows, LANES))
    return cells, rates


def wall_loads(span, n_span, packed, beside, edges, tips, layer, mid, faces, jac):
    group = lane_of((8, LANES)) // 8
    first, last = span == 0, span == n_span - 1

    def swing(x, when):
        return roll(x, LANES // 2) if when else x

    for v in range(VARS + 1):
        p, upper = v % 3, v >= 3
        low_edge = edges[0, 1] if p == 2 else turn_rows(edges[0, 0], 4 - 4 * p)
        high_edge = edges[1, 1] if p == 2 else turn_rows(edges[1, 0], 4 * p)
        tiles = [
            (turn_rows(tips[0], 6 - 2 * p), swing(low_edge, upper), turn_rows(tips[1], 6 - 2 * p)),
            (beside[0, p, 0:8], packed[v, 0:8], beside[1, p, 0:8]),
            (beside[0, p, 8:16], packed[v, 8:16], beside[1, p, 8:16]),
            (turn_rows(tips[2], -2 * p), swing(high_edge, upper), turn_rows(tips[3], -2 * p)),
        ]
        for t, (left, centre, right) in enumerate(tiles):
            left = jnp.where(first, 0.0, swing(left, not upper))
            right = jnp.where(last, 0.0, swing(right, not upper))
            whole = jnp.where(group < 4, left, jnp.where(group >= 12, right, centre))
            layer[v, 8 * t : 8 * t + 8, :] = mirrored(whole)
    span_group = lane_of((24, LANES)) // 8
    outside = (first & (span_group < 4)) | (last & (span_group >= 12))
    cells, rates = wall_rates(layer, 4, 24, VARS, jac)
    scale = DT_FLOW * layer[VARS, 4:28, :]
    for u in range(VARS):
        mid[u] = mirrored(jnp.where(outside, 0.0, cells[u] + scale * rates[u]))
    cells, rates = wall_rates(mid, 4, 16, 1, jac)
    scale = DT_FLOW * layer[VARS, 8:24, :]
    after = 0.5 * (layer[0, 8:24, :] + cells[0] + scale * rates[0])
    total = jnp.zeros((WRAP, LANES), jnp.float32)
    for s in range(SPAN):
        at = 8 * (s + 4) + 2
        total = total + faces[s] * jnp.broadcast_to(after[:, at : at + 1], (WRAP, LANES))
    return jnp.sum(total, axis=0, keepdims=True)


def kernel(
    n_span,
    n_wrap,
    n_norm,
    flow_hbm,
    volume_hbm,
    jac_hbm,
    area_hbm,
    map_hbm,
    contact_hbm,
    bending_hbm,
    mass_hbm,
    hardening_hbm,
    disp_hbm,
    vel_hbm,
    result,
    defl_ref,
    field1,
    field2,
    volume,
    wall_send,
    wall_recv,
    edges,
    corr,
    jac,
    faces,
    area,
    stations,
    contact_v,
    beam_v,
    jac_held,
    loads_a,
    loads_b,
    loads_c,
    tally,
    wall_packed,
    wall_pairs,
    wall_beside,
    edge_put,
    edge_got,
    tip_put,
    tip_got,
    wall_layer,
    wall_mid,
    local_sem,
    send_sem,
    recv_sem,
    group_sem,
    wide_send_sem,
    wide_recv_sem,
):
    span, wrap, normal = lax.axis_index("span"), lax.axis_index("wrap"), lax.axis_index("normal")
    rows = 2
    cols = n_span // rows
    row, col = lax.div(span, cols), lax.rem(span, cols)
    zs, cores = cols // 2, 2
    z, core = lax.div(col, cores), lax.rem(col, cores)
    y_own = row * n_wrap + wrap

    inputs = [
        (flow_hbm, field1.at[:, 2 : 2 + SPAN, TOP : TOP + WRAP, :]),
        (volume_hbm, volume),
        (area_hbm, area),
        (map_hbm, stations),
        (contact_hbm, contact_v),
        (bending_hbm, beam_v.at[0]),
        (mass_hbm, beam_v.at[1]),
        (hardening_hbm, beam_v.at[2]),
        (disp_hbm, beam_v.at[3]),
        (vel_hbm, beam_v.at[4]),
        (jac_hbm, jac_held),
    ]
    reads = [pltpu.make_async_copy(a, b, local_sem.at[i]) for i, (a, b) in enumerate(inputs)]
    for read in reads:
        read.start()

    def turned(index, by, count):
        return lax.rem(index + (by + count), count)

    span_at = {by: turned(span, by, n_span) for by in (-1, 1)}
    wrap_at = [turned(wrap, by, n_wrap) for by in range(n_wrap)]
    norm_at = {by: turned(normal, by, n_norm) for by in (-1, 1)}
    row_at = [turned(row, by, rows) for by in range(rows)]
    z_at = [turned(z, by, zs) for by in range(zs)]
    core_at = [core, turned(core, 1, cores)]
    sides = [
        (span_at[-1], wrap, normal),
        (span_at[1], wrap, normal),
        (span, wrap_at[n_wrap - 1], normal),
        (span, wrap_at[1], normal),
        (span, wrap, norm_at[-1]),
        (span, wrap, norm_at[1]),
    ]
    barrier = pltpu.get_barrier_semaphore()

    def greet(target):
        pl.semaphore_signal(barrier, inc=1, device_id=target, device_id_type=MESH)

    corners = [(span_at[i], wrap_at[j], normal) for j in (n_wrap - 1, 1) for i in (-1, 1)]

    for side in sides:
        greet(side)

    def device(y, z, core, x):
        return (y[0] * cols + z * cores + core, y[1], x)

    here = (row, wrap)
    y_at = [(row_at[a], wrap_at[b]) for a in range(rows) for b in range(n_wrap)]
    beside_y = (1, n_wrap - 1)

    @pl.when(normal == 0)
    def _():
        for one in corners:
            greet(one)
        for k in range(1, len(y_at)):
            if k not in beside_y:
                greet(device(y_at[k], z, core, 0))
        for k in range(1, zs):
            greet(device(here, z_at[k], core, 0))

    @pl.when(normal != 0)
    def _():
        for k in range(cores):
            greet(device(here, z, core_at[k], 0))

    def copy(src, dst, slot, target):
        return pltpu.make_async_remote_copy(
            src_ref=src,
            dst_ref=dst,
            send_sem=send_sem.at[slot],
            recv_sem=recv_sem.at[slot],
            device_id=target,
            device_id_type=MESH,
        )

    def stage_copies(stage, field):
        cells = pl.ds(TOP, WRAP)
        base = 6 * stage
        pairs = [
            (field.at[:, 2:4, cells, :], field.at[:, 2 + SPAN : 4 + SPAN, cells, :]),
            (field.at[:, SPAN : 2 + SPAN, cells, :], field.at[:, 0:2, cells, :]),
            (wall_send.at[stage, 0], wall_recv.at[stage, 0]),
            (wall_send.at[stage, 1], wall_recv.at[stage, 1]),
            (edges.at[stage, 0], edges.at[stage, 2]),
            (edges.at[stage, 0], edges.at[stage, 1]),
        ]
        return [copy(src, dst, base + i, sides[i]) for i, (src, dst) in enumerate(pairs)]

    def stage_wrap_rows(stage, field):
        for v in range(VARS):
            for r in range(2):
                wall_send[stage, 0, v, r] = field[v, 2 : 2 + SPAN, TOP + r, :]
                wall_send[stage, 1, v, r] = field[v, 2 : 2 + SPAN, TOP + WRAP - 2 + r, :]

    def stage_arrive(stage, field):
        zeros = jnp.zeros((VARS, 2, WRAP, LANES), jnp.float32)

        @pl.when(span == 0)
        def _():
            field[:, 0:2, TOP : TOP + WRAP, :] = zeros

        @pl.when(span == n_span - 1)
        def _():
            field[:, 2 + SPAN : 4 + SPAN, TOP : TOP + WRAP, :] = zeros

        for v in range(VARS):
            for r in range(2):
                field[v, 2 : 2 + SPAN, TOP + WRAP + r, :] = wall_recv[stage, 0, v, r]
                field[v, 2 : 2 + SPAN, TOP - 2 + r, :] = wall_recv[stage, 1, v, r]
        edge_terms(
            normal, n_norm, edges.at[stage, 0], edges.at[stage, 1], edges.at[stage, 2], jac, corr
        )

    wide = []
    for i, (src, dst, target) in enumerate(
        [
            (tip_put.at[0], tip_got.at[3], corners[0]),
            (tip_put.at[0], tip_got.at[2], corners[1]),
            (tip_put.at[1], tip_got.at[1], corners[2]),
            (tip_put.at[1], tip_got.at[0], corners[3]),
            (edge_put.at[0], edge_got.at[1], sides[2]),
            (edge_put.at[1], edge_got.at[0], sides[3]),
            (wall_pairs, wall_beside.at[1], sides[0]),
            (wall_pairs, wall_beside.at[0], sides[1]),
        ]
    ):
        wide.append(
            pltpu.make_async_remote_copy(
                src_ref=src,
                dst_ref=dst,
                send_sem=wide_send_sem.at[i],
                recv_sem=wide_recv_sem.at[i],
                device_id=target,
                device_id_type=MESH,
            )
        )

    empty = tuple(jnp.zeros((8, LANES), jnp.float32) for _ in range(VARS))

    reads[0].wait()
    reads[1].wait()

    @pl.when(normal == 0)
    def _():
        pack_wall(field1, volume, wall_packed)
        pair_wall(wall_packed, wall_pairs, edge_put, tip_put)

    at_wall = lax.div(n_norm - normal, n_norm)
    wall_peers = 4 + (len(y_at) - 1 - len(set(beside_y))) + (zs - 1) + cores * (n_norm - 1)
    pl.semaphore_wait(barrier, 6 + at_wall * wall_peers)

    @pl.when(normal == 0)
    def _():
        for one in wide:
            one.start()

    stage_wrap_rows(0, field1)

    def pack_first(s, packed):
        cells = [
            field1[v, s + 2, TOP : TOP + WRAP, :].reshape(2, 8, LANES) for v in range(VARS)
        ]
        return pack_plane(packed, cells, s)

    packed = lax.fori_loop(0, SPAN, pack_first, empty, unroll=True)
    for v in range(VARS):
        edges[0, 0, v] = packed[v]

    first = stage_copies(0, field1)
    for one in first:
        one.start()

    for read in reads[2:]:
        read.wait()
    for d in range(3):
        for u in range(VARS):
            for v in range(VARS):
                scaled = jac_held[u, d, v] * (-1.0 / 12.0)
                jac[25 * d + 5 * u + v] = jnp.full((8, LANES), scaled, jnp.float32)
    lane = lane_of((8, LANES))
    held = jnp.where(lane < LANES // 2, 2 * lane, 2 * lane - (LANES - 1))

    def group_copy(buffer, own, which, target):
        return pltpu.make_async_remote_copy(
            src_ref=buffer.at[own],
            dst_ref=buffer.at[own],
            send_sem=group_sem.at[2 * which],
            recv_sem=group_sem.at[2 * which + 1],
            device_id=target,
            device_id_type=MESH,
        )

    def added(ref):
        terms = [ref[i] for i in range(ref.shape[0])]
        while len(terms) > 1:
            terms = [sum(terms[i + 1 : i + 2], terms[i]) for i in range(0, len(terms), 2)]
        return terms[0]

    def take(ref, which):
        pltpu.make_async_copy(ref, ref, group_sem.at[which]).wait()

    def permuted(x):
        full = jnp.broadcast_to(x, (8, LANES))
        return jnp.take_along_axis(full, held, axis=1)[0:1]

    bending, mass, hardening, disp, vel = [permuted(beam_v[i]) for i in range(5)]
    contact = permuted(contact_v[...])
    inertia = 2.0 * mass / (DT_BEAM * DT_BEAM)
    pull = CONTACT_STIFF * STOP_GAP
    push = jnp.where(contact == 1, pull, jnp.where(contact == 2, -pull, 0.0))
    steady = inertia * (disp + DT_BEAM * vel) + push
    base = inertia + jnp.where(contact > 0, CONTACT_STIFF, 0.0)
    be, bo = halves(bending)
    he, ho = halves(hardening)
    ge, go = halves(base)
    ue, uo = halves(disp)
    fe, fo = halves(steady)
    factors = factor(be, bo, ge + 3.0 * he * ue * ue, go + 3.0 * ho * uo * uo)

    @pl.when(normal == 0)
    def _():
        row_id = lax.broadcasted_iota(jnp.int32, (WRAP, WRAP), 0)
        same = (row_id == lane_of((WRAP, WRAP))).astype(jnp.float32)

        def turned_over(x):
            return lax.dot_general(
                same, x, (((1,), (1,)), ((), ())), precision=lax.Precision.HIGHEST
            )

        weights = turned_over(area[...])
        places = turned_over(stations[...].astype(jnp.float32))
        aims = jnp.broadcast_to(held[0:1], (WRAP, LANES)).astype(jnp.float32)
        for s in range(SPAN):
            weight = jnp.broadcast_to(weights[:, s : s + 1], (WRAP, LANES))
            place = jnp.broadcast_to(places[:, s : s + 1], (WRAP, LANES))
            faces[s] = jnp.where(place == aims, weight, 0.0)
        for one in wide:
            one.wait_recv()
        loads_a[y_own] = wall_loads(
            span,
            n_span,
            wall_packed,
            wall_beside,
            edge_got,
            tip_got,
            wall_layer,
            wall_mid,
            faces,
            jac,
        )
        for k in range(1, len(y_at)):
            group_copy(loads_a, y_own, 0, device(y_at[k], z, core, 0)).start()

    for one in first:
        one.wait_recv()
    stage_arrive(0, field1)

    def first_plane(s, packed):
        cells, rates = plane_rates(field1, s, jac, corr)
        scale = DT_FLOW * volume[s].reshape(2, 8, LANES)
        mids = [cells[u] + scale * rates[u] for u in range(VARS)]
        for u in range(VARS):
            field2[u, s + 2, TOP : TOP + WRAP, :] = mids[u].reshape(WRAP, LANES)
        return pack_plane(packed, mids, s)

    packed = lax.fori_loop(0, SPAN, first_plane, empty)
    for v in range(VARS):
        edges[1, 0, v] = packed[v]

    stage_wrap_rows(1, field2)
    second = stage_copies(1, field2)
    for one in second:
        one.start()
    @pl.when(normal == 0)
    def _():
        take(loads_a.at[1:], 1)
        loads_b[z] = added(loads_a)
        for k in range(1, zs):
            group_copy(loads_b, z, 1, device(here, z_at[k], core, 0)).start()
        if zs > 1:
            take(loads_b.at[1:], 3)
        loads_c[core] = added(loads_b)
        for x in range(n_norm - 1, -1, -1):
            for k in range(cores):
                if x or k:
                    group_copy(loads_c, core, 2, device(here, z, core_at[k], x)).start()

    for one in second:
        one.wait_recv()
    stage_arrive(1, field2)

    def second_plane(s, carry):
        cells, rates = plane_rates(field2, s, jac, corr)
        scale = DT_FLOW * volume[s].reshape(2, 8, LANES)
        for u in range(VARS):
            start = field1[u, s + 2, TOP : TOP + WRAP, :].reshape(2, 8, LANES)
            after = 0.5 * (start + cells[u] + scale * rates[u])
            result[u, s] = after.reshape(WRAP, LANES)
        return carry

    lax.fori_loop(0, SPAN, second_plane, 0)

    for one in first + second:
        one.wait_send()

    @pl.when(normal == 0)
    def _():
        for one in wide:
            one.wait_send()
        take(loads_a.at[1:], 0)
        if zs > 1:
            take(loads_b.at[1:], 2)
        take(tally, 4)

    @pl.when(normal == 0)
    def _():
        take(loads_c.at[1:], 5)

    @pl.when(normal != 0)
    def _():
        take(loads_c, 5)

    loads = added(loads_c)

    le, lo = halves(loads)
    fe, fo = fe + le, fo + lo
    for newton_step in range(NEWTON):
        if newton_step:
            factors = factor(be, bo, ge + 3.0 * he * ue * ue, go + 3.0 * ho * uo * uo)
        ue, uo = substitute(factors, *right_side(fe, fo, he, ho, ue, uo))
    both = jnp.where(lane_of((1, LANES)) < LANES // 2, ue, roll(uo, LANES // 2))
    back = (lane % 2) * (LANES // 2) + lane // 2
    full = jnp.broadcast_to(both, (8, LANES))
    defl_ref[...] = jnp.take_along_axis(full, back, axis=1)[0:1]


def hand_out(flow_ref, defl_ref, flow_out, defl_out, sem):
    copies = [
        pltpu.make_async_copy(flow_ref, flow_out, sem.at[0]),
        pltpu.make_async_copy(defl_ref, defl_out, sem.at[1]),
    ]
    for one in copies:
        one.start()
    for one in copies:
        one.wait()


def solution(mesh):
    n_span, n_wrap, n_norm = (mesh.shape[axis] for axis in ("span", "wrap", "normal"))
    zs, ys = n_span // 4, 2 * n_wrap
    f32 = jnp.float32

    def step(
        flow_state,
        inv_volume,
        flux_jacobians,
        area,
        station_map,
        contact,
        bending,
        mass,
        hardening,
        disp_old,
        vel_old,
    ):
        vectors = [
            x.reshape(1, STATIONS) for x in (contact, bending, mass, hardening, disp_old, vel_old)
        ]
        hbm, vmem = (pl.BlockSpec(memory_space=space) for space in (pltpu.HBM, pltpu.VMEM))
        operands = [flow_state, inv_volume, flux_jacobians.transpose(1, 0, 2), area, station_map]
        operands = [pltpu.with_memory_space_constraint(x, pltpu.HBM) for x in operands + vectors]
        flow_next, deflection = pl.pallas_call(
            functools.partial(kernel, n_span, n_wrap, n_norm),
            out_shape=(
                pltpu.VMEM(flow_state.shape, f32),
                pltpu.VMEM((1, STATIONS), f32),
            ),
            in_specs=[hbm] * len(operands),
            out_specs=(vmem, vmem),
            scratch_shapes=[
                pltpu.VMEM((VARS, SPAN + 4, WRAP + 16, LANES), f32),
                pltpu.VMEM((VARS, SPAN + 4, WRAP + 16, LANES), f32),
                pltpu.VMEM((SPAN, WRAP, LANES), f32),
                pltpu.VMEM((2, 2, VARS, 2, SPAN, LANES), f32),
                pltpu.VMEM((2, 2, VARS, 2, SPAN, LANES), f32),
                pltpu.VMEM((2, 3, VARS, 8, LANES), f32),
                pltpu.VMEM((VARS, 8, LANES), f32),
                pltpu.VMEM((75, 8, LANES), f32),
                pltpu.VMEM((SPAN, WRAP, LANES), f32),
                pltpu.VMEM((SPAN, WRAP), f32),
                pltpu.VMEM((SPAN, WRAP), jnp.int32),
                pltpu.VMEM((1, STATIONS), jnp.int32),
                pltpu.VMEM((5, 1, STATIONS), f32),
                pltpu.SMEM((VARS, 3, VARS), f32),
                pltpu.VMEM((ys, 1, LANES), f32),
                pltpu.VMEM((zs, 1, LANES), f32),
                pltpu.VMEM((2, 1, LANES), f32),
                pltpu.VMEM((2 * n_norm - 1, 1, LANES), f32),
                pltpu.VMEM((VARS + 1, WRAP, LANES), f32),
                pltpu.VMEM((3, WRAP, LANES), f32),
                pltpu.VMEM((2, 3, WRAP, LANES), f32),
                pltpu.VMEM((2, 2, 8, LANES), f32),
                pltpu.VMEM((2, 2, 8, LANES), f32),
                pltpu.VMEM((2, 8, LANES), f32),
                pltpu.VMEM((4, 8, LANES), f32),
                pltpu.VMEM((VARS + 1, WRAP + 16, LANES), f32),
                pltpu.VMEM((VARS, 24, LANES), f32),
                pltpu.SemaphoreType.DMA((11,)),
                pltpu.SemaphoreType.DMA((12,)),
                pltpu.SemaphoreType.DMA((12,)),
                pltpu.SemaphoreType.DMA((6,)),
                pltpu.SemaphoreType.DMA((8,)),
                pltpu.SemaphoreType.DMA((8,)),
            ],
            compiler_params=pltpu.CompilerParams(
                collective_id=0, has_side_effects=True, vmem_limit_bytes=32 * 1024 * 1024
            ),
            cost_estimate=pl.CostEstimate(
                flops=10_000_000, bytes_accessed=1_000_000, transcendentals=0
            ),
        )(*operands)
        flow_next, deflection = pl.pallas_call(
            hand_out,
            out_shape=(
                jax.ShapeDtypeStruct(flow_state.shape, f32),
                jax.ShapeDtypeStruct((1, STATIONS), f32),
            ),
            in_specs=(vmem, vmem),
            out_specs=(hbm, hbm),
            scratch_shapes=[pltpu.SemaphoreType.DMA((2,))],
        )(
            pltpu.with_memory_space_constraint(flow_next, pltpu.VMEM),
            pltpu.with_memory_space_constraint(deflection, pltpu.VMEM),
        )
        return flow_next, deflection.reshape(STATIONS)

    placed = (
        P(None, "span", "wrap", "normal"),
        P("span", "wrap", "normal"),
        P(),
        P("span", "wrap"),
        P("span", "wrap"),
    ) + (P(),) * 6
    return jax.shard_map(
        step,
        mesh=mesh,
        in_specs=placed,
        out_specs=(P(None, "span", "wrap", "normal"), P()),
        check_vma=False,
    )
```

```python
import functools

import jax
import jax.numpy as jnp
from jax import lax
from jax.experimental import pallas as pl
from jax.experimental.pallas import tpu as pltpu
from jax.sharding import PartitionSpec as P

MESH = pl.DeviceIdType.MESH
VARS = 5
STATIONS = 128
NEWTON = 3
DT_FLOW = 0.2
DISSIPATION = 0.03
DT_BEAM = 0.2
STOP_GAP = 0.5
CONTACT_STIFF = 40.0
SPAN, WRAP, LANES = 8, 16, 128
TOP = 8


def lane_of(shape):
    return lax.broadcasted_iota(jnp.int32, shape, len(shape) - 1)


def roll(x, shift):
    return pltpu.roll(x, shift % LANES if isinstance(shift, int) else shift, 1)


def factor(be, bo, diag_e, diag_o):
    lane = lane_of((1, LANES))
    half = LANES // 2
    valid, inner = lane < half, lane < half - 1
    bo_prev, be_next = roll(bo, 1), roll(be, -1)
    p = jnp.where(valid, 4.0 * be + bo_prev + bo + diag_e, 1.0)
    q = jnp.where(valid, -2.0 * (be + bo), 0.0)
    r = jnp.where(valid, 4.0 * bo + be + be_next + diag_o, 1.0)
    c11 = jnp.where(inner, bo, 0.0)
    c12 = jnp.zeros_like(bo)
    c21 = jnp.where(inner, -2.0 * (bo + be_next), 0.0)
    c22 = jnp.where(inner, be_next, 0.0)
    a11, a12, a21, a22 = roll(c11, 1), roll(c21, 1), c12, roll(c22, 1)
    levels = []
    step = 1
    while step < half:
        inv = 1.0 / (p * r - q * q)
        u11, u12 = c11 * r - c21 * q, c21 * p - c11 * q
        u21, u22 = c12 * r - c22 * q, c22 * p - c12 * q
        d11, d12 = a11 * r - a21 * q, a21 * p - a11 * q
        d21, d22 = a12 * r - a22 * q, a22 * p - a12 * q
        levels.append((step, inv, u11, u12, u21, u22, d11, d12, d21, d22))
        up = [
            (u11 * c11 + u12 * c21) * inv,
            (u11 * c12 + u12 * c22) * inv,
            (u21 * c12 + u22 * c22) * inv,
        ]
        down = [
            (d11 * a11 + d12 * a21) * inv,
            (d11 * a12 + d12 * a22) * inv,
            (d21 * a12 + d22 * a22) * inv,
        ]
        p = p - (roll(up[0], step) + roll(down[0], -step))
        q = q - (roll(up[1], step) + roll(down[1], -step))
        r = r - (roll(up[2], step) + roll(down[2], -step))
        if 2 * step < half:
            n11, n12 = -(d11 * c11 + d12 * c21) * inv, -(d11 * c12 + d12 * c22) * inv
            n21, n22 = -(d21 * c11 + d22 * c21) * inv, -(d21 * c12 + d22 * c22) * inv
            c11, c12 = roll(n11, -step), roll(n12, -step)
            c21, c22 = roll(n21, -step), roll(n22, -step)
            a11, a12 = roll(n11, step), roll(n21, step)
            a21, a22 = roll(n12, step), roll(n22, step)
        step *= 2
    return levels, (1.0 / (p * r - q * q), p, q, r)


def substitute(factors, e, o):
    levels, (inv, p, q, r) = factors
    for step, scale, u11, u12, u21, u22, d11, d12, d21, d22 in levels:
        e, o = (
            e - (roll((u11 * e + u12 * o) * scale, step) + roll((d11 * e + d12 * o) * scale, -step)),
            o - (roll((u21 * e + u22 * o) * scale, step) + roll((d21 * e + d22 * o) * scale, -step)),
        )
    return (r * e - q * o) * inv, (p * o - q * e) * inv


def right_side(fe, fo, he, ho, ue, uo):
    return fe + 2.0 * he * ue * ue * ue, fo + 2.0 * ho * uo * uo * uo


def halves(x):
    valid = lane_of((1, LANES)) < LANES // 2
    return jnp.where(valid, x, 0.0), jnp.where(valid, roll(x, LANES // 2), 0.0)


def ring(by, count):
    return min(by, count - by)


def pack_plane(packed, cells, s):
    slot = lane_of((8, LANES)) // 4
    new = []
    for v in range(VARS):
        have = packed[v]
        for t in range(2):
            k = 2 * s + t
            have = jnp.where(slot == k, roll(cells[v][t], 4 * k + 2), have)
        new.append(have)
    return tuple(new)


def edge_terms(normal, n_norm, own, left, right, jac, corr):
    lane = lane_of((8, LANES))
    place = lane % 4
    ends, smooths = [], []
    for v in range(VARS):
        mine = own[v]
        mirror = jnp.where(place == 0, roll(mine, -3), roll(mine, -1))
        low = jnp.where(normal == 0, mirror, left[v])
        high = jnp.where(normal == n_norm - 1, 0.0, right[v])
        delta = jnp.where(place < 2, roll(high - mine, -2), roll(low - mine, 2))
        near = jnp.where(place == 1, roll(delta, 1), jnp.where(place == 2, roll(delta, -1), 0.0))
        end = delta - 8.0 * near
        ends.append(jnp.where(place < 2, -end, end))
        smooths.append(delta - 4.0 * near)
    for u in range(VARS):
        total = -DISSIPATION * smooths[u]
        for v in range(VARS):
            total = total + jac[50 + 5 * u + v] * ends[v]
        corr[u] = total


def plane_rates(field, s, jac, corr):
    lane = lane_of((8, LANES))
    edge = (lane < 2) | (lane >= LANES - 2)
    cells, grads, smooths = [], [[], [], []], []
    for v in range(VARS):

        def at(ds, dw):
            return field[v, s + (2 + ds), TOP + dw : TOP + dw + WRAP, :]

        c = at(0, 0)
        reads = [
            [at(k, 0) for k in (-2, -1, 1, 2)],
            [at(0, k) for k in (-2, -1, 1, 2)],
            [roll(c, -k) for k in (-2, -1, 1, 2)],
        ]
        near, far = None, None
        for d, (m2, m1, p1, p2) in enumerate(reads):
            grads[d].append(((m2 - p2) + 8.0 * (p1 - m1)).reshape(2, 8, LANES))
            near = (m1 + p1) if near is None else near + (m1 + p1)
            far = (m2 + p2) if far is None else far + (m2 + p2)
        smooths.append((-DISSIPATION * (far - 4.0 * near + 18.0 * c)).reshape(2, 8, LANES))
        cells.append(c.reshape(2, 8, LANES))
    rates = []
    for u in range(VARS):
        total = smooths[u]
        for d in range(3):
            for v in range(VARS):
                total = total + jac[25 * d + 5 * u + v][None] * grads[d][v]
        ends = corr[u]
        fix = [
            jnp.where(edge, roll(ends, (2 * LANES - 2 - 4 * (2 * s + t)) % LANES), 0.0)
            for t in range(2)
        ]
        rates.append(total + jnp.stack(fix))
    return cells, rates


def pack_wall(field, volume, packed):
    group = lane_of((8, LANES)) // 8
    for v in range(VARS + 1):
        for t in range(2):
            have = jnp.zeros((8, LANES), jnp.float32)
            for s in range(SPAN):
                if v < VARS:
                    tile = field[v, s + 2, TOP + 8 * t : TOP + 8 * t + 8, :]
                else:
                    tile = volume[s, 8 * t : 8 * t + 8, :]
                have = jnp.where(group == s + 4, roll(tile, 8 * (s + 4) + 2), have)
            packed[v, 8 * t : 8 * t + 8, :] = mirrored(have)


def pair_wall(packed, pairs, edge, tip):
    lane, row = lane_of((8, LANES)), lax.broadcasted_iota(jnp.int32, (8, LANES), 0)
    own = (lane >= LANES // 4) & (lane < 3 * LANES // 4)
    for p in range(3):
        for t in range(2):
            rows = slice(8 * t, 8 * t + 8)
            pairs[p, rows, :] = jnp.where(own, packed[p, rows, :], roll(packed[p + 3, rows, :], 64))
    for t in range(2):
        a, b, c = (pairs[p, 8 * t : 8 * t + 8, :] for p in range(3))
        four = row < 4
        edge[t, 0] = jnp.where(four, a if t == 0 else pltpu.roll(a, 4, 0), b if t else pltpu.roll(b, 4, 0))
        edge[t, 1] = c
        at = 6 * t
        tip[t] = jnp.where(
            row < 2,
            turn_rows(a, -at),
            jnp.where(four, turn_rows(b, 2 - at), turn_rows(c, 4 - at)),
        )


def turn_rows(x, by):
    return pltpu.roll(x, by % 8, 0) if by % 8 else x


def mirrored(x):
    place = lane_of(x.shape) % 8
    return jnp.where(place == 0, roll(x, -3), jnp.where(place == 1, roll(x, -1), x))


def wall_rates(layer, top, rows, wanted, jac, at_wall):
    cells, grads, smooths = [], [[], [], []], []
    shape = (rows // 8, 8, LANES)
    for v in range(VARS):
        c = layer[v, top : top + rows, :]
        reads = [
            [roll(c, -8 * k) for k in (-2, -1, 1, 2)],
            [layer[v, top + k : top + k + rows, :] for k in (-2, -1, 1, 2)],
        ]
        if at_wall:
            p1, p2 = roll(c, -1), roll(c, -2)
            reads.append([p1, c, p1, p2])
        else:
            reads.append([roll(c, -k) for k in (-2, -1, 1, 2)])
        near, far = None, None
        for d, (m2, m1, p1, p2) in enumerate(reads):
            grads[d].append(((m2 - p2) + 8.0 * (p1 - m1)).reshape(shape))
            near = (m1 + p1) if near is None else near + (m1 + p1)
            far = (m2 + p2) if far is None else far + (m2 + p2)
        smooths.append((-DISSIPATION * (far - 4.0 * near + 18.0 * c)).reshape(shape))
        cells.append(c)
    rates = []
    for u in range(wanted):
        total = smooths[u]
        for d in range(3):
            for v in range(VARS):
                total = total + jac[25 * d + 5 * u + v][None] * grads[d][v]
        rates.append(total.reshape(rows, LANES))
    return cells, rates


def wall_loads(span, n_span, packed, beside, edges, tips, layer, mid, faces, jac):
    group = lane_of((8, LANES)) // 8
    first, last = span == 0, span == n_span - 1

    def swing(x, when):
        return roll(x, LANES // 2) if when else x

    for v in range(VARS + 1):
        p, upper = v % 3, v >= 3
        low_edge = edges[0, 1] if p == 2 else turn_rows(edges[0, 0], 4 - 4 * p)
        high_edge = edges[1, 1] if p == 2 else turn_rows(edges[1, 0], 4 * p)
        tiles = [
            (turn_rows(tips[0], 6 - 2 * p), swing(low_edge, upper), turn_rows(tips[1], 6 - 2 * p)),
            (beside[0, p, 0:8], packed[v, 0:8], beside[1, p, 0:8]),
            (beside[0, p, 8:16], packed[v, 8:16], beside[1, p, 8:16]),
            (turn_rows(tips[2], -2 * p), swing(high_edge, upper), turn_rows(tips[3], -2 * p)),
        ]
        for t, (left, centre, right) in enumerate(tiles):
            left = jnp.where(first, 0.0, swing(left, not upper))
            right = jnp.where(last, 0.0, swing(right, not upper))
            whole = jnp.where(group < 4, left, jnp.where(group >= 12, right, centre))
            layer[v, 8 * t : 8 * t + 8, :] = whole
    span_group = lane_of((24, LANES)) // 8
    outside = (first & (span_group < 4)) | (last & (span_group >= 12))
    cells, rates = wall_rates(layer, 4, 24, VARS, jac, False)
    scale = DT_FLOW * layer[VARS, 4:28, :]
    for u in range(VARS):
        mid[u] = jnp.where(outside, 0.0, cells[u] + scale * rates[u])
    cells, rates = wall_rates(mid, 4, 16, 1, jac, True)
    scale = DT_FLOW * layer[VARS, 8:24, :]
    after = 0.5 * (layer[0, 8:24, :] + cells[0] + scale * rates[0])
    total = jnp.zeros((WRAP, LANES), jnp.float32)
    for s in range(SPAN):
        at = 8 * (s + 4) + 2
        total = total + faces[s] * jnp.broadcast_to(after[:, at : at + 1], (WRAP, LANES))
    return jnp.sum(total, axis=0, keepdims=True)


def kernel(
    n_span,
    n_wrap,
    n_norm,
    flow_hbm,
    volume_hbm,
    jac_hbm,
    area_hbm,
    map_hbm,
    contact_hbm,
    bending_hbm,
    mass_hbm,
    hardening_hbm,
    disp_hbm,
    vel_hbm,
    result,
    defl_ref,
    field1,
    field2,
    volume,
    wall_send,
    wall_recv,
    edges,
    corr,
    jac,
    faces,
    area,
    stations,
    contact_v,
    beam_v,
    jac_held,
    loads_a,
    loads_b,
    loads_c,
    tally,
    wall_packed,
    wall_pairs,
    wall_beside,
    edge_put,
    edge_got,
    tip_put,
    tip_got,
    wall_layer,
    wall_mid,
    local_sem,
    send_sem,
    recv_sem,
    group_sem,
    wide_send_sem,
    wide_recv_sem,
):
    span, wrap, normal = lax.axis_index("span"), lax.axis_index("wrap"), lax.axis_index("normal")
    rows = 2
    cols = n_span // rows
    row, col = lax.div(span, cols), lax.rem(span, cols)
    zs, cores = cols // 2, 2
    z, core = lax.div(col, cores), lax.rem(col, cores)
    y_own = row * n_wrap + wrap

    inputs = [
        (flow_hbm, field1.at[:, 2 : 2 + SPAN, TOP : TOP + WRAP, :]),
        (volume_hbm, volume),
        (area_hbm, area),
        (map_hbm, stations),
        (contact_hbm, contact_v),
        (bending_hbm, beam_v.at[0]),
        (mass_hbm, beam_v.at[1]),
        (hardening_hbm, beam_v.at[2]),
        (disp_hbm, beam_v.at[3]),
        (vel_hbm, beam_v.at[4]),
        (jac_hbm, jac_held),
    ]
    reads = [pltpu.make_async_copy(a, b, local_sem.at[i]) for i, (a, b) in enumerate(inputs)]
    for read in reads[:2]:
        read.start()

    def turned(index, by, count):
        return lax.rem(index + (by + count), count)

    span_at = {by: turned(span, by, n_span) for by in (-1, 1)}
    wrap_at = [turned(wrap, by, n_wrap) for by in range(n_wrap)]
    norm_at = {by: turned(normal, by, n_norm) for by in (-1, 1)}
    row_at = [turned(row, by, rows) for by in range(rows)]
    z_at = [turned(z, by, zs) for by in range(zs)]
    core_at = [core, turned(core, 1, cores)]
    sides = [
        (span_at[-1], wrap, normal),
        (span_at[1], wrap, normal),
        (span, wrap_at[n_wrap - 1], normal),
        (span, wrap_at[1], normal),
        (span, wrap, norm_at[-1]),
        (span, wrap, norm_at[1]),
    ]
    barrier = pltpu.get_barrier_semaphore()

    def greet(target):
        pl.semaphore_signal(barrier, inc=1, device_id=target, device_id_type=MESH)

    corners = [(span_at[i], wrap_at[j], normal) for j in (n_wrap - 1, 1) for i in (-1, 1)]
    for side in sides:
        greet(side)

    def device(y, z, core, x):
        return (y[0] * cols + z * cores + core, y[1], x)

    here = (row, wrap)
    y_at = [(row_at[a], wrap_at[b]) for a in range(rows) for b in range(n_wrap)]
    y_far = sorted(range(1, rows * n_wrap), key=lambda k: -ring(2 * (k % n_wrap) + k // n_wrap, 2 * n_wrap))
    z_far = sorted(range(1, zs), key=lambda k: -ring(k, zs))
    beside_y = (1, n_wrap - 1)

    @pl.when(normal == 0)
    def _():
        for one in corners:
            greet(one)
        for k in y_far:
            if k not in beside_y:
                greet(device(y_at[k], z, core, 0))
        for k in z_far:
            greet(device(here, z_at[k], core, 0))

    @pl.when(normal != 0)
    def _():
        for k in range(cores):
            greet(device(here, z, core_at[k], 0))

    def copy(src, dst, slot, target):
        return pltpu.make_async_remote_copy(
            src_ref=src,
            dst_ref=dst,
            send_sem=send_sem.at[slot],
            recv_sem=recv_sem.at[slot],
            device_id=target,
            device_id_type=MESH,
        )

    def stage_copies(stage, field):
        cells = pl.ds(TOP, WRAP)
        base = 6 * stage
        pairs = [
            (field.at[:, 2:4, cells, :], field.at[:, 2 + SPAN : 4 + SPAN, cells, :]),
            (field.at[:, SPAN : 2 + SPAN, cells, :], field.at[:, 0:2, cells, :]),
            (wall_send.at[stage, 0], wall_recv.at[stage, 0]),
            (wall_send.at[stage, 1], wall_recv.at[stage, 1]),
            (edges.at[stage, 0], edges.at[stage, 2]),
            (edges.at[stage, 0], edges.at[stage, 1]),
        ]
        return [copy(src, dst, base + i, sides[i]) for i, (src, dst) in enumerate(pairs)]

    def stage_wrap_rows(stage, field):
        for v in range(VARS):
            for r in range(2):
                wall_send[stage, 0, v, r] = field[v, 2 : 2 + SPAN, TOP + r, :]
                wall_send[stage, 1, v, r] = field[v, 2 : 2 + SPAN, TOP + WRAP - 2 + r, :]

    def stage_arrive(stage, field):
        zeros = jnp.zeros((VARS, 2, WRAP, LANES), jnp.float32)

        @pl.when(span == 0)
        def _():
            field[:, 0:2, TOP : TOP + WRAP, :] = zeros

        @pl.when(span == n_span - 1)
        def _():
            field[:, 2 + SPAN : 4 + SPAN, TOP : TOP + WRAP, :] = zeros

        for v in range(VARS):
            for r in range(2):
                field[v, 2 : 2 + SPAN, TOP + WRAP + r, :] = wall_recv[stage, 0, v, r]
                field[v, 2 : 2 + SPAN, TOP - 2 + r, :] = wall_recv[stage, 1, v, r]
        edge_terms(
            normal, n_norm, edges.at[stage, 0], edges.at[stage, 1], edges.at[stage, 2], jac, corr
        )

    wide = []
    for i, (src, dst, target) in enumerate(
        [
            (tip_put.at[0], tip_got.at[3], corners[0]),
            (tip_put.at[0], tip_got.at[2], corners[1]),
            (tip_put.at[1], tip_got.at[1], corners[2]),
            (tip_put.at[1], tip_got.at[0], corners[3]),
            (edge_put.at[0], edge_got.at[1], sides[2]),
            (edge_put.at[1], edge_got.at[0], sides[3]),
            (wall_pairs, wall_beside.at[1], sides[0]),
            (wall_pairs, wall_beside.at[0], sides[1]),
        ]
    ):
        wide.append(
            pltpu.make_async_remote_copy(
                src_ref=src,
                dst_ref=dst,
                send_sem=wide_send_sem.at[i],
                recv_sem=wide_recv_sem.at[i],
                device_id=target,
                device_id_type=MESH,
            )
        )

    empty = tuple(jnp.zeros((8, LANES), jnp.float32) for _ in range(VARS))

    reads[0].wait()
    reads[1].wait()

    @pl.when(normal == 0)
    def _():
        pack_wall(field1, volume, wall_packed)
        pair_wall(wall_packed, wall_pairs, edge_put, tip_put)

    at_wall = lax.div(n_norm - normal, n_norm)
    wall_peers = 4 + (len(y_at) - 1 - len(set(beside_y))) + (zs - 1) + cores * (n_norm - 1)
    pl.semaphore_wait(barrier, 6 + at_wall * wall_peers)

    @pl.when(normal == 0)
    def _():
        for one in wide:
            one.start()

    for read in reads[2:]:
        read.start()
    stage_wrap_rows(0, field1)

    def pack_first(s, packed):
        cells = [
            field1[v, s + 2, TOP : TOP + WRAP, :].reshape(2, 8, LANES) for v in range(VARS)
        ]
        return pack_plane(packed, cells, s)

    packed = lax.fori_loop(0, SPAN, pack_first, empty, unroll=True)
    for v in range(VARS):
        edges[0, 0, v] = packed[v]

    first = stage_copies(0, field1)
    for one in first:
        one.start()

    for read in reads[2:]:
        read.wait()
    for d in range(3):
        for u in range(VARS):
            for v in range(VARS):
                scaled = jac_held[u, d, v] * (-1.0 / 12.0)
                jac[25 * d + 5 * u + v] = jnp.full((8, LANES), scaled, jnp.float32)
    lane = lane_of((8, LANES))
    held = jnp.where(lane < LANES // 2, 2 * lane, 2 * lane - (LANES - 1))

    def group_copy(buffer, own, which, target):
        return pltpu.make_async_remote_copy(
            src_ref=buffer.at[own],
            dst_ref=buffer.at[own],
            send_sem=group_sem.at[2 * which],
            recv_sem=group_sem.at[2 * which + 1],
            device_id=target,
            device_id_type=MESH,
        )

    def added(ref):
        terms = [ref[i] for i in range(ref.shape[0])]
        while len(terms) > 1:
            terms = [sum(terms[i + 1 : i + 2], terms[i]) for i in range(0, len(terms), 2)]
        return terms[0]

    def take(ref, which):
        pltpu.make_async_copy(ref, ref, group_sem.at[which]).wait()

    def permuted(x):
        full = jnp.broadcast_to(x, (8, LANES))
        return jnp.take_along_axis(full, held, axis=1)[0:1]

    bending, mass, hardening, disp, vel = [permuted(beam_v[i]) for i in range(5)]
    contact = permuted(contact_v[...])
    inertia = 2.0 * mass / (DT_BEAM * DT_BEAM)
    pull = CONTACT_STIFF * STOP_GAP
    push = jnp.where(contact == 1, pull, jnp.where(contact == 2, -pull, 0.0))
    steady = inertia * (disp + DT_BEAM * vel) + push
    base = inertia + jnp.where(contact > 0, CONTACT_STIFF, 0.0)
    be, bo = halves(bending)
    he, ho = halves(hardening)
    ge, go = halves(base)
    ue, uo = halves(disp)
    fe, fo = halves(steady)
    factors = factor(be, bo, ge + 3.0 * he * ue * ue, go + 3.0 * ho * uo * uo)

    @pl.when(normal == 0)
    def _():
        row_id = lax.broadcasted_iota(jnp.int32, (WRAP, WRAP), 0)
        same = (row_id == lane_of((WRAP, WRAP))).astype(jnp.float32)

        def turned_over(x):
            return lax.dot_general(
                same, x, (((1,), (1,)), ((), ())), precision=lax.Precision.HIGHEST
            )

        weights = turned_over(area[...])
        places = turned_over(stations[...].astype(jnp.float32))
        aims = jnp.broadcast_to(held[0:1], (WRAP, LANES)).astype(jnp.float32)
        for s in range(SPAN):
            weight = jnp.broadcast_to(weights[:, s : s + 1], (WRAP, LANES))
            place = jnp.broadcast_to(places[:, s : s + 1], (WRAP, LANES))
            faces[s] = jnp.where(place == aims, weight, 0.0)
        for one in wide:
            one.wait_recv()
        loads_a[y_own] = wall_loads(
            span,
            n_span,
            wall_packed,
            wall_beside,
            edge_got,
            tip_got,
            wall_layer,
            wall_mid,
            faces,
            jac,
        )
        for k in y_far:
            group_copy(loads_a, y_own, 0, device(y_at[k], z, core, 0)).start()

    for one in first:
        one.wait_recv()
    stage_arrive(0, field1)

    def first_plane(s, packed):
        cells, rates = plane_rates(field1, s, jac, corr)
        scale = DT_FLOW * volume[s].reshape(2, 8, LANES)
        mids = [cells[u] + scale * rates[u] for u in range(VARS)]
        for u in range(VARS):
            field2[u, s + 2, TOP : TOP + WRAP, :] = mids[u].reshape(WRAP, LANES)
        return pack_plane(packed, mids, s)

    packed = lax.fori_loop(0, SPAN, first_plane, empty)
    for v in range(VARS):
        edges[1, 0, v] = packed[v]

    stage_wrap_rows(1, field2)
    second = stage_copies(1, field2)
    for one in second:
        one.start()
    @pl.when(normal == 0)
    def _():
        take(loads_a.at[1:], 1)
        loads_b[z] = added(loads_a)
        for k in z_far:
            group_copy(loads_b, z, 1, device(here, z_at[k], core, 0)).start()
        if zs > 1:
            take(loads_b.at[1:], 3)
        loads_c[core] = added(loads_b)
        for x in sorted(range(n_norm), key=lambda x: -ring(x, n_norm)):
            for k in range(cores):
                if x or k:
                    group_copy(loads_c, core, 2, device(here, z, core_at[k], x)).start()

    for one in second:
        one.wait_recv()
    stage_arrive(1, field2)

    def second_plane(s, carry):
        cells, rates = plane_rates(field2, s, jac, corr)
        scale = DT_FLOW * volume[s].reshape(2, 8, LANES)
        for u in range(VARS):
            start = field1[u, s + 2, TOP : TOP + WRAP, :].reshape(2, 8, LANES)
            after = 0.5 * (start + cells[u] + scale * rates[u])
            result[u, s] = after.reshape(WRAP, LANES)
        return carry

    lax.fori_loop(0, SPAN, second_plane, 0)

    for one in first + second:
        one.wait_send()

    @pl.when(normal == 0)
    def _():
        for one in wide:
            one.wait_send()
        take(loads_a.at[1:], 0)
        if zs > 1:
            take(loads_b.at[1:], 2)
        take(tally, 4)

    @pl.when(normal == 0)
    def _():
        take(loads_c.at[1:], 5)

    @pl.when(normal != 0)
    def _():
        take(loads_c, 5)

    loads = added(loads_c)

    le, lo = halves(loads)
    fe, fo = fe + le, fo + lo
    for newton_step in range(NEWTON):
        if newton_step:
            factors = factor(be, bo, ge + 3.0 * he * ue * ue, go + 3.0 * ho * uo * uo)
        ue, uo = substitute(factors, *right_side(fe, fo, he, ho, ue, uo))
    both = jnp.where(lane_of((1, LANES)) < LANES // 2, ue, roll(uo, LANES // 2))
    back = (lane % 2) * (LANES // 2) + lane // 2
    full = jnp.broadcast_to(both, (8, LANES))
    defl_ref[...] = jnp.take_along_axis(full, back, axis=1)[0:1]


def hand_out(flow_ref, defl_ref, flow_out, defl_out, sem):
    copies = [
        pltpu.make_async_copy(flow_ref, flow_out, sem.at[0]),
        pltpu.make_async_copy(defl_ref, defl_out, sem.at[1]),
    ]
    for one in copies:
        one.start()
    for one in copies:
        one.wait()


def solution(mesh):
    n_span, n_wrap, n_norm = (mesh.shape[axis] for axis in ("span", "wrap", "normal"))
    zs, ys = n_span // 4, 2 * n_wrap
    f32 = jnp.float32

    def step(
        flow_state,
        inv_volume,
        flux_jacobians,
        area,
        station_map,
        contact,
        bending,
        mass,
        hardening,
        disp_old,
        vel_old,
    ):
        vectors = [
            x.reshape(1, STATIONS) for x in (contact, bending, mass, hardening, disp_old, vel_old)
        ]
        hbm, vmem = (pl.BlockSpec(memory_space=space) for space in (pltpu.HBM, pltpu.VMEM))
        operands = [flow_state, inv_volume, flux_jacobians.transpose(1, 0, 2), area, station_map]
        operands = [pltpu.with_memory_space_constraint(x, pltpu.HBM) for x in operands + vectors]
        flow_next, deflection = pl.pallas_call(
            functools.partial(kernel, n_span, n_wrap, n_norm),
            out_shape=(
                pltpu.VMEM(flow_state.shape, f32),
                pltpu.VMEM((1, STATIONS), f32),
            ),
            in_specs=[hbm] * len(operands),
            out_specs=(vmem, vmem),
            scratch_shapes=[
                pltpu.VMEM((VARS, SPAN + 4, WRAP + 16, LANES), f32),
                pltpu.VMEM((VARS, SPAN + 4, WRAP + 16, LANES), f32),
                pltpu.VMEM((SPAN, WRAP, LANES), f32),
                pltpu.VMEM((2, 2, VARS, 2, SPAN, LANES), f32),
                pltpu.VMEM((2, 2, VARS, 2, SPAN, LANES), f32),
                pltpu.VMEM((2, 3, VARS, 8, LANES), f32),
                pltpu.VMEM((VARS, 8, LANES), f32),
                pltpu.VMEM((75, 8, LANES), f32),
                pltpu.VMEM((SPAN, WRAP, LANES), f32),
                pltpu.VMEM((SPAN, WRAP), f32),
                pltpu.VMEM((SPAN, WRAP), jnp.int32),
                pltpu.VMEM((1, STATIONS), jnp.int32),
                pltpu.VMEM((5, 1, STATIONS), f32),
                pltpu.SMEM((VARS, 3, VARS), f32),
                pltpu.VMEM((ys, 1, LANES), f32),
                pltpu.VMEM((zs, 1, LANES), f32),
                pltpu.VMEM((2, 1, LANES), f32),
                pltpu.VMEM((2 * n_norm - 1, 1, LANES), f32),
                pltpu.VMEM((VARS + 1, WRAP, LANES), f32),
                pltpu.VMEM((3, WRAP, LANES), f32),
                pltpu.VMEM((2, 3, WRAP, LANES), f32),
                pltpu.VMEM((2, 2, 8, LANES), f32),
                pltpu.VMEM((2, 2, 8, LANES), f32),
                pltpu.VMEM((2, 8, LANES), f32),
                pltpu.VMEM((4, 8, LANES), f32),
                pltpu.VMEM((VARS + 1, WRAP + 16, LANES), f32),
                pltpu.VMEM((VARS, 24, LANES), f32),
                pltpu.SemaphoreType.DMA((11,)),
                pltpu.SemaphoreType.DMA((12,)),
                pltpu.SemaphoreType.DMA((12,)),
                pltpu.SemaphoreType.DMA((6,)),
                pltpu.SemaphoreType.DMA((8,)),
                pltpu.SemaphoreType.DMA((8,)),
            ],
            compiler_params=pltpu.CompilerParams(
                collective_id=0, has_side_effects=True, vmem_limit_bytes=32 * 1024 * 1024
            ),
            cost_estimate=pl.CostEstimate(
                flops=10_000_000, bytes_accessed=1_000_000, transcendentals=0
            ),
        )(*operands)
        flow_next, deflection = pl.pallas_call(
            hand_out,
            out_shape=(
                jax.ShapeDtypeStruct(flow_state.shape, f32),
                jax.ShapeDtypeStruct((1, STATIONS), f32),
            ),
            in_specs=(vmem, vmem),
            out_specs=(hbm, hbm),
            scratch_shapes=[pltpu.SemaphoreType.DMA((2,))],
        )(
            pltpu.with_memory_space_constraint(flow_next, pltpu.VMEM),
            pltpu.with_memory_space_constraint(deflection, pltpu.VMEM),
        )
        return flow_next, deflection.reshape(STATIONS)

    placed = (
        P(None, "span", "wrap", "normal"),
        P("span", "wrap", "normal"),
        P(),
        P("span", "wrap"),
        P("span", "wrap"),
    ) + (P(),) * 6
    return jax.shard_map(
        step,
        mesh=mesh,
        in_specs=placed,
        out_specs=(P(None, "span", "wrap", "normal"), P()),
        check_vma=False,
    )
```

```python
import functools

import jax
import jax.numpy as jnp
from jax import lax
from jax.experimental import pallas as pl
from jax.experimental.pallas import tpu as pltpu
from jax.sharding import PartitionSpec as P

MESH = pl.DeviceIdType.MESH
VARS = 5
STATIONS = 128
NEWTON = 3
DT_FLOW = 0.2
DISSIPATION = 0.03
DT_BEAM = 0.2
STOP_GAP = 0.5
CONTACT_STIFF = 40.0
SPAN, WRAP, LANES = 8, 16, 128
TOP = 8


def lane_of(shape):
    return lax.broadcasted_iota(jnp.int32, shape, len(shape) - 1)


def roll(x, shift):
    return pltpu.roll(x, shift % LANES if isinstance(shift, int) else shift, 1)


def factor(be, bo, diag_e, diag_o):
    lane = lane_of((1, LANES))
    half = LANES // 2
    valid, inner = lane < half, lane < half - 1
    bo_prev, be_next = roll(bo, 1), roll(be, -1)
    p = jnp.where(valid, 4.0 * be + bo_prev + bo + diag_e, 1.0)
    q = jnp.where(valid, -2.0 * (be + bo), 0.0)
    r = jnp.where(valid, 4.0 * bo + be + be_next + diag_o, 1.0)
    c11 = jnp.where(inner, bo, 0.0)
    c12 = jnp.zeros_like(bo)
    c21 = jnp.where(inner, -2.0 * (bo + be_next), 0.0)
    c22 = jnp.where(inner, be_next, 0.0)
    a11, a12, a21, a22 = roll(c11, 1), roll(c21, 1), c12, roll(c22, 1)
    levels = []
    step = 1
    while step < half:
        inv = 1.0 / (p * r - q * q)
        u11, u12 = c11 * r - c21 * q, c21 * p - c11 * q
        u21, u22 = c12 * r - c22 * q, c22 * p - c12 * q
        d11, d12 = a11 * r - a21 * q, a21 * p - a11 * q
        d21, d22 = a12 * r - a22 * q, a22 * p - a12 * q
        levels.append((step, inv, u11, u12, u21, u22, d11, d12, d21, d22))
        up = [
            (u11 * c11 + u12 * c21) * inv,
            (u11 * c12 + u12 * c22) * inv,
            (u21 * c12 + u22 * c22) * inv,
        ]
        down = [
            (d11 * a11 + d12 * a21) * inv,
            (d11 * a12 + d12 * a22) * inv,
            (d21 * a12 + d22 * a22) * inv,
        ]
        p = p - (roll(up[0], step) + roll(down[0], -step))
        q = q - (roll(up[1], step) + roll(down[1], -step))
        r = r - (roll(up[2], step) + roll(down[2], -step))
        if 2 * step < half:
            n11, n12 = -(d11 * c11 + d12 * c21) * inv, -(d11 * c12 + d12 * c22) * inv
            n21, n22 = -(d21 * c11 + d22 * c21) * inv, -(d21 * c12 + d22 * c22) * inv
            c11, c12 = roll(n11, -step), roll(n12, -step)
            c21, c22 = roll(n21, -step), roll(n22, -step)
            a11, a12 = roll(n11, step), roll(n21, step)
            a21, a22 = roll(n12, step), roll(n22, step)
        step *= 2
    return levels, (1.0 / (p * r - q * q), p, q, r)


def substitute(factors, e, o):
    levels, (inv, p, q, r) = factors
    for step, scale, u11, u12, u21, u22, d11, d12, d21, d22 in levels:
        e, o = (
            e - (roll((u11 * e + u12 * o) * scale, step) + roll((d11 * e + d12 * o) * scale, -step)),
            o - (roll((u21 * e + u22 * o) * scale, step) + roll((d21 * e + d22 * o) * scale, -step)),
        )
    return (r * e - q * o) * inv, (p * o - q * e) * inv


def right_side(fe, fo, he, ho, ue, uo):
    return fe + 2.0 * he * ue * ue * ue, fo + 2.0 * ho * uo * uo * uo


def halves(x):
    valid = lane_of((1, LANES)) < LANES // 2
    return jnp.where(valid, x, 0.0), jnp.where(valid, roll(x, LANES // 2), 0.0)


def ring(by, count):
    return min(by, count - by)


def pack_plane(packed, cells, s):
    slot = lane_of((8, LANES)) // 4
    new = []
    for v in range(VARS):
        have = packed[v]
        for t in range(2):
            k = 2 * s + t
            have = jnp.where(slot == k, roll(cells[v][t], 4 * k + 2), have)
        new.append(have)
    return tuple(new)


def edge_terms(normal, n_norm, own, left, right, jac, corr):
    lane = lane_of((8, LANES))
    place = lane % 4
    ends, smooths = [], []
    for v in range(VARS):
        mine = own[v]
        mirror = jnp.where(place == 0, roll(mine, -3), roll(mine, -1))
        low = jnp.where(normal == 0, mirror, left[v])
        high = jnp.where(normal == n_norm - 1, 0.0, right[v])
        delta = jnp.where(place < 2, roll(high - mine, -2), roll(low - mine, 2))
        near = jnp.where(place == 1, roll(delta, 1), jnp.where(place == 2, roll(delta, -1), 0.0))
        end = delta - 8.0 * near
        ends.append(jnp.where(place < 2, -end, end))
        smooths.append(delta - 4.0 * near)
    for u in range(VARS):
        total = -DISSIPATION * smooths[u]
        for v in range(VARS):
            total = total + jac[50 + 5 * u + v] * ends[v]
        corr[u] = total


def plane_rates(field, s, jac):
    cells, grads, smooths = [], [[], [], []], []
    for v in range(VARS):

        def at(ds, dw):
            return field[v, s + (2 + ds), TOP + dw : TOP + dw + WRAP, :]

        c = at(0, 0)
        reads = [
            [at(k, 0) for k in (-2, -1, 1, 2)],
            [at(0, k) for k in (-2, -1, 1, 2)],
            [roll(c, -k) for k in (-2, -1, 1, 2)],
        ]
        near, far = None, None
        for d, (m2, m1, p1, p2) in enumerate(reads):
            grads[d].append(((m2 - p2) + 8.0 * (p1 - m1)).reshape(2, 8, LANES))
            near = (m1 + p1) if near is None else near + (m1 + p1)
            far = (m2 + p2) if far is None else far + (m2 + p2)
        smooths.append((-DISSIPATION * (far - 4.0 * near + 18.0 * c)).reshape(2, 8, LANES))
        cells.append(c.reshape(2, 8, LANES))
    rates = []
    for u in range(VARS):
        total = smooths[u]
        for d in range(3):
            for v in range(VARS):
                total = total + jac[25 * d + 5 * u + v][None] * grads[d][v]
        rates.append(total)
    return cells, rates


def ghost_rates(direction, low, first, second, jac, shape):
    outer, inner = [], []
    for v in range(VARS):
        a, b = first(v), second(v)
        if low:
            outer.append((a - 8.0 * b, a - 4.0 * b))
            inner.append((b, b))
        else:
            outer.append((8.0 * a - b, b - 4.0 * a))
            inner.append((-a, a))
    fixes = []
    for layer in (outer, inner):
        grads = [g.reshape(shape) for g, _ in layer]
        layer_fixes = []
        for u in range(VARS):
            total = -DISSIPATION * layer[u][1].reshape(shape)
            for v in range(VARS):
                total = total + jac[25 * direction + 5 * u + v][None] * grads[v]
            layer_fixes.append(total)
        fixes.append(layer_fixes)
    return fixes


def add_ghosts(span, n_span, planes, rows, corr, jac, volume, factor_of, at_plane, at_row, at_cells, done):
    for low in (True, False):
        gone = span == (0 if low else n_span - 1)
        side = 0 if low else 1

        def ghost(layer):
            return lambda v: jnp.where(gone, 0.0, planes[side, v, layer])

        fixes = ghost_rates(0, low, ghost(0), ghost(1), jac, (2, 8, LANES))
        for s, fix in zip((0, 1) if low else (SPAN - 1, SPAN - 2), fixes):
            scale = factor_of * volume[s]
            for u in range(VARS):
                at_plane(u, s, scale * fix[u].reshape(WRAP, LANES))
    for low in (True, False):
        side = 1 if low else 0

        def ghost(layer):
            return lambda v: rows[side, v, layer]

        fixes = ghost_rates(1, low, ghost(0), ghost(1), jac, (1, 8, LANES))
        for r, fix in zip((0, 1) if low else (WRAP - 1, WRAP - 2), fixes):
            scale = factor_of * volume[:, r, :]
            for u in range(VARS):
                at_row(u, r, scale * fix[u].reshape(8, LANES))
    lane = lane_of((8, LANES))
    edge = (lane < 2) | (lane >= LANES - 2)

    def columns(s, carry):
        scale = factor_of * volume[s].reshape(2, 8, LANES)
        cells = []
        for u in range(VARS):
            ends = corr[u]
            fix = [
                jnp.where(edge, roll(ends, (2 * LANES - 2 - 4 * (2 * s + t)) % LANES), 0.0)
                for t in range(2)
            ]
            cells.append(at_cells(u, s, scale * jnp.stack(fix)))
        return done(carry, cells, s)

    return columns


def pack_wall(field, volume, packed):
    group = lane_of((8, LANES)) // 8
    for v in range(VARS + 1):
        for t in range(2):
            have = jnp.zeros((8, LANES), jnp.float32)
            for s in range(SPAN):
                if v < VARS:
                    tile = field[v, s + 2, TOP + 8 * t : TOP + 8 * t + 8, :]
                else:
                    tile = volume[s, 8 * t : 8 * t + 8, :]
                have = jnp.where(group == s + 4, roll(tile, 8 * (s + 4) + 2), have)
            packed[v, 8 * t : 8 * t + 8, :] = mirrored(have)


def pair_wall(packed, pairs, edge, tip):
    lane, row = lane_of((8, LANES)), lax.broadcasted_iota(jnp.int32, (8, LANES), 0)
    own = (lane >= LANES // 4) & (lane < 3 * LANES // 4)
    for p in range(3):
        for t in range(2):
            rows = slice(8 * t, 8 * t + 8)
            pairs[p, rows, :] = jnp.where(own, packed[p, rows, :], roll(packed[p + 3, rows, :], 64))
    for t in range(2):
        a, b, c = (pairs[p, 8 * t : 8 * t + 8, :] for p in range(3))
        four = row < 4
        edge[t, 0] = jnp.where(four, a if t == 0 else pltpu.roll(a, 4, 0), b if t else pltpu.roll(b, 4, 0))
        edge[t, 1] = c
        at = 6 * t
        tip[t] = jnp.where(
            row < 2,
            turn_rows(a, -at),
            jnp.where(four, turn_rows(b, 2 - at), turn_rows(c, 4 - at)),
        )


def turn_rows(x, by):
    return pltpu.roll(x, by % 8, 0) if by % 8 else x


def mirrored(x):
    place = lane_of(x.shape) % 8
    return jnp.where(place == 0, roll(x, -3), jnp.where(place == 1, roll(x, -1), x))


def wall_rates(layer, top, rows, wanted, jac, at_wall):
    cells, grads, smooths = [], [[], [], []], []
    shape = (rows // 8, 8, LANES)
    for v in range(VARS):
        c = layer[v, top : top + rows, :]
        reads = [
            [roll(c, -8 * k) for k in (-2, -1, 1, 2)],
            [layer[v, top + k : top + k + rows, :] for k in (-2, -1, 1, 2)],
        ]
        if at_wall:
            p1, p2 = roll(c, -1), roll(c, -2)
            reads.append([p1, c, p1, p2])
        else:
            reads.append([roll(c, -k) for k in (-2, -1, 1, 2)])
        near, far = None, None
        for d, (m2, m1, p1, p2) in enumerate(reads):
            grads[d].append(((m2 - p2) + 8.0 * (p1 - m1)).reshape(shape))
            near = (m1 + p1) if near is None else near + (m1 + p1)
            far = (m2 + p2) if far is None else far + (m2 + p2)
        smooths.append((-DISSIPATION * (far - 4.0 * near + 18.0 * c)).reshape(shape))
        cells.append(c)
    rates = []
    for u in range(wanted):
        total = smooths[u]
        for d in range(3):
            for v in range(VARS):
                total = total + jac[25 * d + 5 * u + v][None] * grads[d][v]
        rates.append(total.reshape(rows, LANES))
    return cells, rates


def wall_loads(span, n_span, packed, beside, edges, tips, layer, mid, faces, jac):
    group = lane_of((8, LANES)) // 8
    first, last = span == 0, span == n_span - 1

    def swing(x, when):
        return roll(x, LANES // 2) if when else x

    for v in range(VARS + 1):
        p, upper = v % 3, v >= 3
        low_edge = edges[0, 1] if p == 2 else turn_rows(edges[0, 0], 4 - 4 * p)
        high_edge = edges[1, 1] if p == 2 else turn_rows(edges[1, 0], 4 * p)
        tiles = [
            (turn_rows(tips[0], 6 - 2 * p), swing(low_edge, upper), turn_rows(tips[1], 6 - 2 * p)),
            (beside[0, p, 0:8], packed[v, 0:8], beside[1, p, 0:8]),
            (beside[0, p, 8:16], packed[v, 8:16], beside[1, p, 8:16]),
            (turn_rows(tips[2], -2 * p), swing(high_edge, upper), turn_rows(tips[3], -2 * p)),
        ]
        for t, (left, centre, right) in enumerate(tiles):
            left = jnp.where(first, 0.0, swing(left, not upper))
            right = jnp.where(last, 0.0, swing(right, not upper))
            whole = jnp.where(group < 4, left, jnp.where(group >= 12, right, centre))
            layer[v, 8 * t : 8 * t + 8, :] = whole
    span_group = lane_of((24, LANES)) // 8
    outside = (first & (span_group < 4)) | (last & (span_group >= 12))
    cells, rates = wall_rates(layer, 4, 24, VARS, jac, False)
    scale = DT_FLOW * layer[VARS, 4:28, :]
    for u in range(VARS):
        mid[u] = jnp.where(outside, 0.0, cells[u] + scale * rates[u])
    cells, rates = wall_rates(mid, 4, 16, 1, jac, True)
    scale = DT_FLOW * layer[VARS, 8:24, :]
    after = 0.5 * (layer[0, 8:24, :] + cells[0] + scale * rates[0])
    total = jnp.zeros((WRAP, LANES), jnp.float32)
    for s in range(SPAN):
        at = 8 * (s + 4) + 2
        total = total + faces[s] * jnp.broadcast_to(after[:, at : at + 1], (WRAP, LANES))
    return jnp.sum(total, axis=0, keepdims=True)


def kernel(
    n_span,
    n_wrap,
    n_norm,
    flow_hbm,
    volume_hbm,
    jac_hbm,
    area_hbm,
    map_hbm,
    contact_hbm,
    bending_hbm,
    mass_hbm,
    hardening_hbm,
    disp_hbm,
    vel_hbm,
    result,
    defl_ref,
    field1,
    field2,
    planes,
    volume,
    wall_send,
    wall_recv,
    edges,
    corr,
    jac,
    faces,
    area,
    stations,
    contact_v,
    beam_v,
    jac_held,
    loads_a,
    loads_b,
    loads_c,
    tally,
    wall_packed,
    wall_pairs,
    wall_beside,
    edge_put,
    edge_got,
    tip_put,
    tip_got,
    wall_layer,
    wall_mid,
    local_sem,
    send_sem,
    recv_sem,
    group_sem,
    wide_send_sem,
    wide_recv_sem,
):
    span, wrap, normal = lax.axis_index("span"), lax.axis_index("wrap"), lax.axis_index("normal")
    rows = 2
    cols = n_span // rows
    row, col = lax.div(span, cols), lax.rem(span, cols)
    zs, cores = cols // 2, 2
    z, core = lax.div(col, cores), lax.rem(col, cores)
    y_own = row * n_wrap + wrap

    inputs = [
        (flow_hbm, field1.at[:, 2 : 2 + SPAN, TOP : TOP + WRAP, :]),
        (volume_hbm, volume),
        (area_hbm, area),
        (map_hbm, stations),
        (contact_hbm, contact_v),
        (bending_hbm, beam_v.at[0]),
        (mass_hbm, beam_v.at[1]),
        (hardening_hbm, beam_v.at[2]),
        (disp_hbm, beam_v.at[3]),
        (vel_hbm, beam_v.at[4]),
        (jac_hbm, jac_held),
    ]
    reads = [pltpu.make_async_copy(a, b, local_sem.at[i]) for i, (a, b) in enumerate(inputs)]
    for read in reads[:2]:
        read.start()

    def turned(index, by, count):
        return lax.rem(index + (by + count), count)

    span_at = {by: turned(span, by, n_span) for by in (-1, 1)}
    wrap_at = [turned(wrap, by, n_wrap) for by in range(n_wrap)]
    norm_at = {by: turned(normal, by, n_norm) for by in (-1, 1)}
    row_at = [turned(row, by, rows) for by in range(rows)]
    z_at = [turned(z, by, zs) for by in range(zs)]
    core_at = [core, turned(core, 1, cores)]
    sides = [
        (span_at[-1], wrap, normal),
        (span_at[1], wrap, normal),
        (span, wrap_at[n_wrap - 1], normal),
        (span, wrap_at[1], normal),
        (span, wrap, norm_at[-1]),
        (span, wrap, norm_at[1]),
    ]
    barrier = pltpu.get_barrier_semaphore()

    def greet(target):
        pl.semaphore_signal(barrier, inc=1, device_id=target, device_id_type=MESH)

    corners = [(span_at[i], wrap_at[j], normal) for j in (n_wrap - 1, 1) for i in (-1, 1)]
    for side in sides:
        greet(side)

    def device(y, z, core, x):
        return (y[0] * cols + z * cores + core, y[1], x)

    here = (row, wrap)
    y_at = [(row_at[a], wrap_at[b]) for a in range(rows) for b in range(n_wrap)]
    y_far = sorted(range(1, rows * n_wrap), key=lambda k: -ring(2 * (k % n_wrap) + k // n_wrap, 2 * n_wrap))
    z_far = sorted(range(1, zs), key=lambda k: -ring(k, zs))
    beside_y = (1, n_wrap - 1)

    @pl.when(normal == 0)
    def _():
        for one in corners:
            greet(one)
        for k in y_far:
            if k not in beside_y:
                greet(device(y_at[k], z, core, 0))
        for k in z_far:
            greet(device(here, z_at[k], core, 0))

    @pl.when(normal != 0)
    def _():
        for k in range(cores):
            greet(device(here, z, core_at[k], 0))

    def copy(src, dst, slot, target):
        return pltpu.make_async_remote_copy(
            src_ref=src,
            dst_ref=dst,
            send_sem=send_sem.at[slot],
            recv_sem=recv_sem.at[slot],
            device_id=target,
            device_id_type=MESH,
        )

    def stage_copies(stage, field):
        cells = pl.ds(TOP, WRAP)
        base = 6 * stage
        pairs = [
            (field.at[:, 2:4, cells, :], planes.at[stage, 1]),
            (field.at[:, SPAN : 2 + SPAN, cells, :], planes.at[stage, 0]),
            (wall_send.at[stage, 0], wall_recv.at[stage, 0]),
            (wall_send.at[stage, 1], wall_recv.at[stage, 1]),
            (edges.at[stage, 0], edges.at[stage, 2]),
            (edges.at[stage, 0], edges.at[stage, 1]),
        ]
        return [copy(src, dst, base + i, sides[i]) for i, (src, dst) in enumerate(pairs)]

    def stage_wrap_rows(stage, field):
        for v in range(VARS):
            for r in range(2):
                wall_send[stage, 0, v, r] = field[v, 2 : 2 + SPAN, TOP + r, :]
                wall_send[stage, 1, v, r] = field[v, 2 : 2 + SPAN, TOP + WRAP - 2 + r, :]

    def stage_columns(stage):
        edge_terms(
            normal, n_norm, edges.at[stage, 0], edges.at[stage, 1], edges.at[stage, 2], jac, corr
        )

    for field in (field1, field2):
        for s in (0, 1, 2 + SPAN, 3 + SPAN):
            field[:, s, TOP : TOP + WRAP, :] = jnp.zeros((VARS, WRAP, LANES), jnp.float32)
        for r in (0, TOP + WRAP):
            field[:, 2 : 2 + SPAN, r : r + 8, :] = jnp.zeros((VARS, SPAN, 8, LANES), jnp.float32)

    wide = []
    for i, (src, dst, target) in enumerate(
        [
            (tip_put.at[0], tip_got.at[3], corners[0]),
            (tip_put.at[0], tip_got.at[2], corners[1]),
            (tip_put.at[1], tip_got.at[1], corners[2]),
            (tip_put.at[1], tip_got.at[0], corners[3]),
            (edge_put.at[0], edge_got.at[1], sides[2]),
            (edge_put.at[1], edge_got.at[0], sides[3]),
            (wall_pairs, wall_beside.at[1], sides[0]),
            (wall_pairs, wall_beside.at[0], sides[1]),
        ]
    ):
        wide.append(
            pltpu.make_async_remote_copy(
                src_ref=src,
                dst_ref=dst,
                send_sem=wide_send_sem.at[i],
                recv_sem=wide_recv_sem.at[i],
                device_id=target,
                device_id_type=MESH,
            )
        )

    empty = tuple(jnp.zeros((8, LANES), jnp.float32) for _ in range(VARS))

    reads[0].wait()
    reads[1].wait()

    @pl.when(normal == 0)
    def _():
        pack_wall(field1, volume, wall_packed)
        pair_wall(wall_packed, wall_pairs, edge_put, tip_put)

    at_wall = lax.div(n_norm - normal, n_norm)
    wall_peers = 4 + (len(y_at) - 1 - len(set(beside_y))) + (zs - 1) + cores * (n_norm - 1)
    pl.semaphore_wait(barrier, 6 + at_wall * wall_peers)

    @pl.when(normal == 0)
    def _():
        for one in wide:
            one.start()

    for read in reads[2:]:
        read.start()
    stage_wrap_rows(0, field1)

    def pack_first(s, packed):
        cells = [
            field1[v, s + 2, TOP : TOP + WRAP, :].reshape(2, 8, LANES) for v in range(VARS)
        ]
        return pack_plane(packed, cells, s)

    packed = lax.fori_loop(0, SPAN, pack_first, empty, unroll=True)
    for v in range(VARS):
        edges[0, 0, v] = packed[v]

    first = stage_copies(0, field1)
    for one in first:
        one.start()

    for read in reads[2:]:
        read.wait()
    for d in range(3):
        for u in range(VARS):
            for v in range(VARS):
                scaled = jac_held[u, d, v] * (-1.0 / 12.0)
                jac[25 * d + 5 * u + v] = jnp.full((8, LANES), scaled, jnp.float32)
    lane = lane_of((8, LANES))
    held = jnp.where(lane < LANES // 2, 2 * lane, 2 * lane - (LANES - 1))

    def group_copy(buffer, own, which, target):
        return pltpu.make_async_remote_copy(
            src_ref=buffer.at[own],
            dst_ref=buffer.at[own],
            send_sem=group_sem.at[2 * which],
            recv_sem=group_sem.at[2 * which + 1],
            device_id=target,
            device_id_type=MESH,
        )

    def added(ref):
        terms = [ref[i] for i in range(ref.shape[0])]
        while len(terms) > 1:
            terms = [sum(terms[i + 1 : i + 2], terms[i]) for i in range(0, len(terms), 2)]
        return terms[0]

    def take(ref, which):
        pltpu.make_async_copy(ref, ref, group_sem.at[which]).wait()

    def first_plane(s, carry):
        cells, rates = plane_rates(field1, s, jac)
        scale = DT_FLOW * volume[s].reshape(2, 8, LANES)
        for u in range(VARS):
            mid = cells[u] + scale * rates[u]
            field2[u, s + 2, TOP : TOP + WRAP, :] = mid.reshape(WRAP, LANES)
        return carry

    lax.fori_loop(0, SPAN, first_plane, 0)

    @pl.when(normal == 0)
    def _():
        row_id = lax.broadcasted_iota(jnp.int32, (WRAP, WRAP), 0)
        same = (row_id == lane_of((WRAP, WRAP))).astype(jnp.float32)

        def turned_over(x):
            return lax.dot_general(
                same, x, (((1,), (1,)), ((), ())), precision=lax.Precision.HIGHEST
            )

        weights = turned_over(area[...])
        places = turned_over(stations[...].astype(jnp.float32))
        aims = jnp.broadcast_to(held[0:1], (WRAP, LANES)).astype(jnp.float32)
        for s in range(SPAN):
            weight = jnp.broadcast_to(weights[:, s : s + 1], (WRAP, LANES))
            place = jnp.broadcast_to(places[:, s : s + 1], (WRAP, LANES))
            faces[s] = jnp.where(place == aims, weight, 0.0)
        for one in wide:
            one.wait_recv()
        loads_a[y_own] = wall_loads(
            span,
            n_span,
            wall_packed,
            wall_beside,
            edge_got,
            tip_got,
            wall_layer,
            wall_mid,
            faces,
            jac,
        )
        for k in y_far:
            group_copy(loads_a, y_own, 0, device(y_at[k], z, core, 0)).start()

    for one in first:
        one.wait_recv()
    stage_columns(0)

    def mid_plane(u, s, part):
        field2[u, s + 2, TOP : TOP + WRAP, :] += part

    def mid_row(u, r, part):
        field2[u, 2 : 2 + SPAN, TOP + r, :] += part

    def mid_cells(u, s, part):
        cells = field2[u, s + 2, TOP : TOP + WRAP, :].reshape(2, 8, LANES) + part
        field2[u, s + 2, TOP : TOP + WRAP, :] = cells.reshape(WRAP, LANES)
        return cells

    columns = add_ghosts(
        span,
        n_span,
        planes.at[0],
        wall_recv.at[0],
        corr,
        jac,
        volume,
        DT_FLOW,
        mid_plane,
        mid_row,
        mid_cells,
        pack_plane,
    )
    packed = lax.fori_loop(0, SPAN, lambda s, packed: columns(s, packed), empty, unroll=True)
    for v in range(VARS):
        edges[1, 0, v] = packed[v]

    stage_wrap_rows(1, field2)
    second = stage_copies(1, field2)
    for one in second:
        one.start()

    def permuted(x):
        full = jnp.broadcast_to(x, (8, LANES))
        return jnp.take_along_axis(full, held, axis=1)[0:1]

    bending, mass, hardening, disp, vel = [permuted(beam_v[i]) for i in range(5)]
    contact = permuted(contact_v[...])
    inertia = 2.0 * mass / (DT_BEAM * DT_BEAM)
    pull = CONTACT_STIFF * STOP_GAP
    push = jnp.where(contact == 1, pull, jnp.where(contact == 2, -pull, 0.0))
    steady = inertia * (disp + DT_BEAM * vel) + push
    base = inertia + jnp.where(contact > 0, CONTACT_STIFF, 0.0)
    be, bo = halves(bending)
    he, ho = halves(hardening)
    ge, go = halves(base)
    ue, uo = halves(disp)
    fe, fo = halves(steady)
    factors = factor(be, bo, ge + 3.0 * he * ue * ue, go + 3.0 * ho * uo * uo)
    @pl.when(normal == 0)
    def _():
        take(loads_a.at[1:], 1)
        loads_b[z] = added(loads_a)
        for k in z_far:
            group_copy(loads_b, z, 1, device(here, z_at[k], core, 0)).start()

    def second_plane(s, carry):
        cells, rates = plane_rates(field2, s, jac)
        scale = DT_FLOW * volume[s].reshape(2, 8, LANES)
        for u in range(VARS):
            start = field1[u, s + 2, TOP : TOP + WRAP, :].reshape(2, 8, LANES)
            after = 0.5 * (start + cells[u] + scale * rates[u])
            result[u, s] = after.reshape(WRAP, LANES)
        return carry

    lax.fori_loop(0, SPAN, second_plane, 0)

    @pl.when(normal == 0)
    def _():
        if zs > 1:
            take(loads_b.at[1:], 3)
        loads_c[core] = added(loads_b)
        for x in sorted(range(n_norm), key=lambda x: -ring(x, n_norm)):
            for k in range(cores):
                if x or k:
                    group_copy(loads_c, core, 2, device(here, z, core_at[k], x)).start()

    for one in second:
        one.wait_recv()
    stage_columns(1)

    def end_plane(u, s, part):
        result[u, s] += part

    def end_row(u, r, part):
        result[u, :, r, :] += part

    def end_cells(u, s, part):
        result[u, s] += part.reshape(WRAP, LANES)

    columns = add_ghosts(
        span,
        n_span,
        planes.at[1],
        wall_recv.at[1],
        corr,
        jac,
        volume,
        0.5 * DT_FLOW,
        end_plane,
        end_row,
        end_cells,
        lambda carry, cells, s: carry,
    )
    lax.fori_loop(0, SPAN, columns, 0, unroll=True)

    for one in first + second:
        one.wait_send()

    @pl.when(normal == 0)
    def _():
        for one in wide:
            one.wait_send()
        take(loads_a.at[1:], 0)
        if zs > 1:
            take(loads_b.at[1:], 2)
        take(tally, 4)

    @pl.when(normal == 0)
    def _():
        take(loads_c.at[1:], 5)

    @pl.when(normal != 0)
    def _():
        take(loads_c, 5)

    loads = added(loads_c)

    le, lo = halves(loads)
    fe, fo = fe + le, fo + lo
    for newton_step in range(NEWTON):
        if newton_step:
            factors = factor(be, bo, ge + 3.0 * he * ue * ue, go + 3.0 * ho * uo * uo)
        ue, uo = substitute(factors, *right_side(fe, fo, he, ho, ue, uo))
    both = jnp.where(lane_of((1, LANES)) < LANES // 2, ue, roll(uo, LANES // 2))
    back = (lane % 2) * (LANES // 2) + lane // 2
    full = jnp.broadcast_to(both, (8, LANES))
    defl_ref[...] = jnp.take_along_axis(full, back, axis=1)[0:1]


def hand_out(flow_ref, defl_ref, flow_out, defl_out, sem):
    copies = [
        pltpu.make_async_copy(flow_ref, flow_out, sem.at[0]),
        pltpu.make_async_copy(defl_ref, defl_out, sem.at[1]),
    ]
    for one in copies:
        one.start()
    for one in copies:
        one.wait()


def solution(mesh):
    n_span, n_wrap, n_norm = (mesh.shape[axis] for axis in ("span", "wrap", "normal"))
    zs, ys = n_span // 4, 2 * n_wrap
    f32 = jnp.float32

    def step(
        flow_state,
        inv_volume,
        flux_jacobians,
        area,
        station_map,
        contact,
        bending,
        mass,
        hardening,
        disp_old,
        vel_old,
    ):
        vectors = [
            x.reshape(1, STATIONS) for x in (contact, bending, mass, hardening, disp_old, vel_old)
        ]
        hbm, vmem = (pl.BlockSpec(memory_space=space) for space in (pltpu.HBM, pltpu.VMEM))
        operands = [flow_state, inv_volume, flux_jacobians.transpose(1, 0, 2), area, station_map]
        operands = [pltpu.with_memory_space_constraint(x, pltpu.HBM) for x in operands + vectors]
        flow_next, deflection = pl.pallas_call(
            functools.partial(kernel, n_span, n_wrap, n_norm),
            out_shape=(
                pltpu.VMEM(flow_state.shape, f32),
                pltpu.VMEM((1, STATIONS), f32),
            ),
            in_specs=[hbm] * len(operands),
            out_specs=(vmem, vmem),
            scratch_shapes=[
                pltpu.VMEM((VARS, SPAN + 4, WRAP + 16, LANES), f32),
                pltpu.VMEM((VARS, SPAN + 4, WRAP + 16, LANES), f32),
                pltpu.VMEM((2, 2, VARS, 2, WRAP, LANES), f32),
                pltpu.VMEM((SPAN, WRAP, LANES), f32),
                pltpu.VMEM((2, 2, VARS, 2, SPAN, LANES), f32),
                pltpu.VMEM((2, 2, VARS, 2, SPAN, LANES), f32),
                pltpu.VMEM((2, 3, VARS, 8, LANES), f32),
                pltpu.VMEM((VARS, 8, LANES), f32),
                pltpu.VMEM((75, 8, LANES), f32),
                pltpu.VMEM((SPAN, WRAP, LANES), f32),
                pltpu.VMEM((SPAN, WRAP), f32),
                pltpu.VMEM((SPAN, WRAP), jnp.int32),
                pltpu.VMEM((1, STATIONS), jnp.int32),
                pltpu.VMEM((5, 1, STATIONS), f32),
                pltpu.SMEM((VARS, 3, VARS), f32),
                pltpu.VMEM((ys, 1, LANES), f32),
                pltpu.VMEM((zs, 1, LANES), f32),
                pltpu.VMEM((2, 1, LANES), f32),
                pltpu.VMEM((2 * n_norm - 1, 1, LANES), f32),
                pltpu.VMEM((VARS + 1, WRAP, LANES), f32),
                pltpu.VMEM((3, WRAP, LANES), f32),
                pltpu.VMEM((2, 3, WRAP, LANES), f32),
                pltpu.VMEM((2, 2, 8, LANES), f32),
                pltpu.VMEM((2, 2, 8, LANES), f32),
                pltpu.VMEM((2, 8, LANES), f32),
                pltpu.VMEM((4, 8, LANES), f32),
                pltpu.VMEM((VARS + 1, WRAP + 16, LANES), f32),
                pltpu.VMEM((VARS, 24, LANES), f32),
                pltpu.SemaphoreType.DMA((11,)),
                pltpu.SemaphoreType.DMA((12,)),
                pltpu.SemaphoreType.DMA((12,)),
                pltpu.SemaphoreType.DMA((6,)),
                pltpu.SemaphoreType.DMA((8,)),
                pltpu.SemaphoreType.DMA((8,)),
            ],
            compiler_params=pltpu.CompilerParams(
                collective_id=0, has_side_effects=True, vmem_limit_bytes=32 * 1024 * 1024
            ),
            cost_estimate=pl.CostEstimate(
                flops=10_000_000, bytes_accessed=1_000_000, transcendentals=0
            ),
        )(*operands)
        flow_next, deflection = pl.pallas_call(
            hand_out,
            out_shape=(
                jax.ShapeDtypeStruct(flow_state.shape, f32),
                jax.ShapeDtypeStruct((1, STATIONS), f32),
            ),
            in_specs=(vmem, vmem),
            out_specs=(hbm, hbm),
            scratch_shapes=[pltpu.SemaphoreType.DMA((2,))],
        )(
            pltpu.with_memory_space_constraint(flow_next, pltpu.VMEM),
            pltpu.with_memory_space_constraint(deflection, pltpu.VMEM),
        )
        return flow_next, deflection.reshape(STATIONS)

    placed = (
        P(None, "span", "wrap", "normal"),
        P("span", "wrap", "normal"),
        P(),
        P("span", "wrap"),
        P("span", "wrap"),
    ) + (P(),) * 6
    return jax.shard_map(
        step,
        mesh=mesh,
        in_specs=placed,
        out_specs=(P(None, "span", "wrap", "normal"), P()),
        check_vma=False,
    )
```

```python
import functools

import jax
import jax.numpy as jnp
from jax import lax
from jax.experimental import pallas as pl
from jax.experimental.pallas import tpu as pltpu
from jax.sharding import PartitionSpec as P

MESH = pl.DeviceIdType.MESH
VARS = 5
STATIONS = 128
NEWTON = 3
DT_FLOW = 0.2
DISSIPATION = 0.03
DT_BEAM = 0.2
STOP_GAP = 0.5
CONTACT_STIFF = 40.0
SPAN, WRAP, LANES = 8, 16, 128
TOP = 8


def lane_of(shape):
    return lax.broadcasted_iota(jnp.int32, shape, len(shape) - 1)


def roll(x, shift):
    return pltpu.roll(x, shift % LANES if isinstance(shift, int) else shift, 1)


def factor(be, bo, diag_e, diag_o):
    lane = lane_of((1, LANES))
    half = LANES // 2
    valid, inner = lane < half, lane < half - 1
    bo_prev, be_next = roll(bo, 1), roll(be, -1)
    p = jnp.where(valid, 4.0 * be + bo_prev + bo + diag_e, 1.0)
    q = jnp.where(valid, -2.0 * (be + bo), 0.0)
    r = jnp.where(valid, 4.0 * bo + be + be_next + diag_o, 1.0)
    c11 = jnp.where(inner, bo, 0.0)
    c12 = jnp.zeros_like(bo)
    c21 = jnp.where(inner, -2.0 * (bo + be_next), 0.0)
    c22 = jnp.where(inner, be_next, 0.0)
    a11, a12, a21, a22 = roll(c11, 1), roll(c21, 1), c12, roll(c22, 1)
    levels = []
    step = 1
    while step < half:
        inv = 1.0 / (p * r - q * q)
        u11, u12 = c11 * r - c21 * q, c21 * p - c11 * q
        u21, u22 = c12 * r - c22 * q, c22 * p - c12 * q
        d11, d12 = a11 * r - a21 * q, a21 * p - a11 * q
        d21, d22 = a12 * r - a22 * q, a22 * p - a12 * q
        levels.append((step, inv, u11, u12, u21, u22, d11, d12, d21, d22))
        up = [
            (u11 * c11 + u12 * c21) * inv,
            (u11 * c12 + u12 * c22) * inv,
            (u21 * c12 + u22 * c22) * inv,
        ]
        down = [
            (d11 * a11 + d12 * a21) * inv,
            (d11 * a12 + d12 * a22) * inv,
            (d21 * a12 + d22 * a22) * inv,
        ]
        p = p - (roll(up[0], step) + roll(down[0], -step))
        q = q - (roll(up[1], step) + roll(down[1], -step))
        r = r - (roll(up[2], step) + roll(down[2], -step))
        if 2 * step < half:
            n11, n12 = -(d11 * c11 + d12 * c21) * inv, -(d11 * c12 + d12 * c22) * inv
            n21, n22 = -(d21 * c11 + d22 * c21) * inv, -(d21 * c12 + d22 * c22) * inv
            c11, c12 = roll(n11, -step), roll(n12, -step)
            c21, c22 = roll(n21, -step), roll(n22, -step)
            a11, a12 = roll(n11, step), roll(n21, step)
            a21, a22 = roll(n12, step), roll(n22, step)
        step *= 2
    return levels, (1.0 / (p * r - q * q), p, q, r)


def substitute(factors, e, o):
    levels, (inv, p, q, r) = factors
    for step, scale, u11, u12, u21, u22, d11, d12, d21, d22 in levels:
        e, o = (
            e - (roll((u11 * e + u12 * o) * scale, step) + roll((d11 * e + d12 * o) * scale, -step)),
            o - (roll((u21 * e + u22 * o) * scale, step) + roll((d21 * e + d22 * o) * scale, -step)),
        )
    return (r * e - q * o) * inv, (p * o - q * e) * inv


def right_side(fe, fo, he, ho, ue, uo):
    return fe + 2.0 * he * ue * ue * ue, fo + 2.0 * ho * uo * uo * uo


def halves(x):
    valid = lane_of((1, LANES)) < LANES // 2
    return jnp.where(valid, x, 0.0), jnp.where(valid, roll(x, LANES // 2), 0.0)


def ring(by, count):
    return min(by, count - by)


def pack_plane(packed, cells, s):
    slot = lane_of((8, LANES)) // 4
    new = []
    for v in range(VARS):
        have = packed[v]
        for t in range(2):
            k = 2 * s + t
            have = jnp.where(slot == k, roll(cells[v][t], 4 * k + 2), have)
        new.append(have)
    return tuple(new)


def edge_terms(normal, n_norm, own, left, right, jac, corr):
    lane = lane_of((8, LANES))
    place = lane % 4
    ends, smooths = [], []
    for v in range(VARS):
        mine = own[v]
        mirror = jnp.where(place == 0, roll(mine, -3), roll(mine, -1))
        low = jnp.where(normal == 0, mirror, left[v])
        high = jnp.where(normal == n_norm - 1, 0.0, right[v])
        delta = jnp.where(place < 2, roll(high - mine, -2), roll(low - mine, 2))
        near = jnp.where(place == 1, roll(delta, 1), jnp.where(place == 2, roll(delta, -1), 0.0))
        end = delta - 8.0 * near
        ends.append(jnp.where(place < 2, -end, end))
        smooths.append(delta - 4.0 * near)
    for u in range(VARS):
        total = -DISSIPATION * smooths[u]
        for v in range(VARS):
            total = total + jac[50 + 5 * u + v] * ends[v]
        corr[u] = total


def plane_rates(field, s, jac):
    cells, grads, smooths = [], [[], [], []], []
    for v in range(VARS):

        def at(ds, dw):
            return field[v, s + (2 + ds), TOP + dw : TOP + dw + WRAP, :]

        c = at(0, 0)
        reads = [
            [at(k, 0) for k in (-2, -1, 1, 2)],
            [at(0, k) for k in (-2, -1, 1, 2)],
            [roll(c, -k) for k in (-2, -1, 1, 2)],
        ]
        near, far = None, None
        for d, (m2, m1, p1, p2) in enumerate(reads):
            grads[d].append(((m2 - p2) + 8.0 * (p1 - m1)).reshape(2, 8, LANES))
            near = (m1 + p1) if near is None else near + (m1 + p1)
            far = (m2 + p2) if far is None else far + (m2 + p2)
        smooths.append((-DISSIPATION * (far - 4.0 * near + 18.0 * c)).reshape(2, 8, LANES))
        cells.append(c.reshape(2, 8, LANES))
    rates = []
    for u in range(VARS):
        total = smooths[u]
        for d in range(3):
            for v in range(VARS):
                total = total + jac[25 * d + 5 * u + v][None] * grads[d][v]
        rates.append(total)
    return cells, rates


def ghost_rates(direction, low, first, second, jac, shape):
    outer, inner = [], []
    for v in range(VARS):
        a, b = first(v), second(v)
        if low:
            outer.append((a - 8.0 * b, a - 4.0 * b))
            inner.append((b, b))
        else:
            outer.append((8.0 * a - b, b - 4.0 * a))
            inner.append((-a, a))
    fixes = []
    for layer in (outer, inner):
        grads = [g.reshape(shape) for g, _ in layer]
        layer_fixes = []
        for u in range(VARS):
            total = -DISSIPATION * layer[u][1].reshape(shape)
            for v in range(VARS):
                total = total + jac[25 * direction + 5 * u + v][None] * grads[v]
            layer_fixes.append(total)
        fixes.append(layer_fixes)
    return fixes


def add_ghosts(span, n_span, planes, rows, corr, jac, volume, factor_of, at_plane, at_row, at_cells, done):
    for low in (True, False):
        gone = span == (0 if low else n_span - 1)
        side = 0 if low else 1

        def ghost(layer):
            return lambda v: jnp.where(gone, 0.0, planes[side, v, layer])

        fixes = ghost_rates(0, low, ghost(0), ghost(1), jac, (2, 8, LANES))
        for s, fix in zip((0, 1) if low else (SPAN - 1, SPAN - 2), fixes):
            scale = factor_of * volume[s]
            for u in range(VARS):
                at_plane(u, s, scale * fix[u].reshape(WRAP, LANES))
    for low in (True, False):
        side = 1 if low else 0

        def ghost(layer):
            return lambda v: rows[side, v, layer]

        fixes = ghost_rates(1, low, ghost(0), ghost(1), jac, (1, 8, LANES))
        for r, fix in zip((0, 1) if low else (WRAP - 1, WRAP - 2), fixes):
            scale = factor_of * volume[:, r, :]
            for u in range(VARS):
                at_row(u, r, scale * fix[u].reshape(8, LANES))
    lane = lane_of((8, LANES))
    edge = (lane < 2) | (lane >= LANES - 2)

    def columns(s, carry):
        scale = factor_of * volume[s].reshape(2, 8, LANES)
        cells = []
        for u in range(VARS):
            ends = corr[u]
            fix = [
                jnp.where(edge, roll(ends, (2 * LANES - 2 - 4 * (2 * s + t)) % LANES), 0.0)
                for t in range(2)
            ]
            cells.append(at_cells(u, s, scale * jnp.stack(fix)))
        return done(carry, cells, s)

    return columns


def pack_wall(field, volume, packed):
    group = lane_of((8, LANES)) // 8
    for v in range(VARS + 1):
        for t in range(2):
            have = jnp.zeros((8, LANES), jnp.float32)
            for s in range(SPAN):
                if v < VARS:
                    tile = field[v, s + 2, TOP + 8 * t : TOP + 8 * t + 8, :]
                else:
                    tile = volume[s, 8 * t : 8 * t + 8, :]
                have = jnp.where(group == s + 4, roll(tile, 8 * (s + 4) + 2), have)
            packed[v, 8 * t : 8 * t + 8, :] = mirrored(have)


def pair_wall(packed, pairs, edge, tip):
    lane, row = lane_of((8, LANES)), lax.broadcasted_iota(jnp.int32, (8, LANES), 0)
    own = (lane >= LANES // 4) & (lane < 3 * LANES // 4)
    for p in range(3):
        for t in range(2):
            rows = slice(8 * t, 8 * t + 8)
            pairs[p, rows, :] = jnp.where(own, packed[p, rows, :], roll(packed[p + 3, rows, :], 64))
    for t in range(2):
        a, b, c = (pairs[p, 8 * t : 8 * t + 8, :] for p in range(3))
        four = row < 4
        edge[t, 0] = jnp.where(four, a if t == 0 else pltpu.roll(a, 4, 0), b if t else pltpu.roll(b, 4, 0))
        edge[t, 1] = c
        at = 6 * t
        tip[t] = jnp.where(
            row < 2,
            turn_rows(a, -at),
            jnp.where(four, turn_rows(b, 2 - at), turn_rows(c, 4 - at)),
        )


def turn_rows(x, by):
    return pltpu.roll(x, by % 8, 0) if by % 8 else x


def mirrored(x):
    place = lane_of(x.shape) % 8
    return jnp.where(place == 0, roll(x, -3), jnp.where(place == 1, roll(x, -1), x))


def wall_rates(layer, top, rows, wanted, jac, at_wall):
    cells, grads, smooths = [], [[], [], []], []
    shape = (rows // 8, 8, LANES)
    for v in range(VARS):
        c = layer[v, top : top + rows, :]
        reads = [
            [roll(c, -8 * k) for k in (-2, -1, 1, 2)],
            [layer[v, top + k : top + k + rows, :] for k in (-2, -1, 1, 2)],
        ]
        if at_wall:
            p1, p2 = roll(c, -1), roll(c, -2)
            reads.append([p1, c, p1, p2])
        else:
            reads.append([roll(c, -k) for k in (-2, -1, 1, 2)])
        near, far = None, None
        for d, (m2, m1, p1, p2) in enumerate(reads):
            grads[d].append(((m2 - p2) + 8.0 * (p1 - m1)).reshape(shape))
            near = (m1 + p1) if near is None else near + (m1 + p1)
            far = (m2 + p2) if far is None else far + (m2 + p2)
        smooths.append((-DISSIPATION * (far - 4.0 * near + 18.0 * c)).reshape(shape))
        cells.append(c)
    rates = []
    for u in range(wanted):
        total = smooths[u]
        for d in range(3):
            for v in range(VARS):
                total = total + jac[25 * d + 5 * u + v][None] * grads[d][v]
        rates.append(total.reshape(rows, LANES))
    return cells, rates


def wall_loads(span, n_span, packed, beside, edges, tips, layer, mid, faces, jac):
    group = lane_of((8, LANES)) // 8
    first, last = span == 0, span == n_span - 1

    def swing(x, when):
        return roll(x, LANES // 2) if when else x

    for v in range(VARS + 1):
        p, upper = v % 3, v >= 3
        low_edge = edges[0, 1] if p == 2 else turn_rows(edges[0, 0], 4 - 4 * p)
        high_edge = edges[1, 1] if p == 2 else turn_rows(edges[1, 0], 4 * p)
        tiles = [
            (turn_rows(tips[0], 6 - 2 * p), swing(low_edge, upper), turn_rows(tips[1], 6 - 2 * p)),
            (beside[0, p, 0:8], packed[v, 0:8], beside[1, p, 0:8]),
            (beside[0, p, 8:16], packed[v, 8:16], beside[1, p, 8:16]),
            (turn_rows(tips[2], -2 * p), swing(high_edge, upper), turn_rows(tips[3], -2 * p)),
        ]
        for t, (left, centre, right) in enumerate(tiles):
            left = jnp.where(first, 0.0, swing(left, not upper))
            right = jnp.where(last, 0.0, swing(right, not upper))
            whole = jnp.where(group < 4, left, jnp.where(group >= 12, right, centre))
            layer[v, 8 * t : 8 * t + 8, :] = whole
    span_group = lane_of((24, LANES)) // 8
    outside = (first & (span_group < 4)) | (last & (span_group >= 12))
    cells, rates = wall_rates(layer, 4, 24, VARS, jac, False)
    scale = DT_FLOW * layer[VARS, 4:28, :]
    for u in range(VARS):
        mid[u] = jnp.where(outside, 0.0, cells[u] + scale * rates[u])
    cells, rates = wall_rates(mid, 4, 16, 1, jac, True)
    scale = DT_FLOW * layer[VARS, 8:24, :]
    after = 0.5 * (layer[0, 8:24, :] + cells[0] + scale * rates[0])
    total = jnp.zeros((WRAP, LANES), jnp.float32)
    for s in range(SPAN):
        at = 8 * (s + 4) + 2
        total = total + faces[s] * jnp.broadcast_to(after[:, at : at + 1], (WRAP, LANES))
    return jnp.sum(total, axis=0, keepdims=True)


def kernel(
    n_span,
    n_wrap,
    n_norm,
    flow_hbm,
    volume_hbm,
    jac_hbm,
    area_hbm,
    map_hbm,
    contact_hbm,
    bending_hbm,
    mass_hbm,
    hardening_hbm,
    disp_hbm,
    vel_hbm,
    result,
    defl_ref,
    field1,
    field2,
    planes,
    volume,
    wall_send,
    wall_recv,
    edges,
    corr,
    jac,
    faces,
    area,
    stations,
    contact_v,
    beam_v,
    jac_held,
    loads_a,
    loads_b,
    loads_c,
    tally,
    wall_packed,
    wall_pairs,
    wall_beside,
    edge_put,
    edge_got,
    tip_put,
    tip_got,
    wall_layer,
    wall_mid,
    local_sem,
    send_sem,
    recv_sem,
    group_sem,
    wide_send_sem,
    wide_recv_sem,
):
    span, wrap, normal = lax.axis_index("span"), lax.axis_index("wrap"), lax.axis_index("normal")
    rows = 2
    cols = n_span // rows
    row, col = lax.div(span, cols), lax.rem(span, cols)
    zs, cores = cols // 2, 2
    z, core = lax.div(col, cores), lax.rem(col, cores)
    y_own = row * n_wrap + wrap

    inputs = [
        (flow_hbm, field1.at[:, 2 : 2 + SPAN, TOP : TOP + WRAP, :]),
        (volume_hbm, volume),
        (area_hbm, area),
        (map_hbm, stations),
        (contact_hbm, contact_v),
        (bending_hbm, beam_v.at[0]),
        (mass_hbm, beam_v.at[1]),
        (hardening_hbm, beam_v.at[2]),
        (disp_hbm, beam_v.at[3]),
        (vel_hbm, beam_v.at[4]),
        (jac_hbm, jac_held),
    ]
    reads = [pltpu.make_async_copy(a, b, local_sem.at[i]) for i, (a, b) in enumerate(inputs)]
    for read in reads[:2]:
        read.start()

    def turned(index, by, count):
        return lax.rem(index + (by + count), count)

    span_at = {by: turned(span, by, n_span) for by in (-1, 1)}
    wrap_at = [turned(wrap, by, n_wrap) for by in range(n_wrap)]
    norm_at = {by: turned(normal, by, n_norm) for by in (-1, 1)}
    row_at = [turned(row, by, rows) for by in range(rows)]
    z_at = [turned(z, by, zs) for by in range(zs)]
    core_at = [core, turned(core, 1, cores)]
    sides = [
        (span_at[-1], wrap, normal),
        (span_at[1], wrap, normal),
        (span, wrap_at[n_wrap - 1], normal),
        (span, wrap_at[1], normal),
        (span, wrap, norm_at[-1]),
        (span, wrap, norm_at[1]),
    ]
    barrier = pltpu.get_barrier_semaphore()

    def greet(target):
        pl.semaphore_signal(barrier, inc=1, device_id=target, device_id_type=MESH)

    corners = [(span_at[i], wrap_at[j], normal) for j in (n_wrap - 1, 1) for i in (-1, 1)]

    def device(y, z, core, x):
        return (y[0] * cols + z * cores + core, y[1], x)

    here = (row, wrap)
    y_at = [(row_at[a], wrap_at[b]) for a in range(rows) for b in range(n_wrap)]
    y_far = sorted(range(1, rows * n_wrap), key=lambda k: -ring(2 * (k % n_wrap) + k // n_wrap, 2 * n_wrap))
    z_far = sorted(range(1, zs), key=lambda k: -ring(k, zs))
    beside_y = (1, n_wrap - 1)

    @pl.when(normal == 0)
    def _():
        for k in z_far:
            greet(device(here, z_at[k], core, 0))
        for k in y_far:
            if k not in beside_y:
                greet(device(y_at[k], z, core, 0))
        for one in corners:
            greet(one)

    @pl.when(normal != 0)
    def _():
        for k in range(cores):
            greet(device(here, z, core_at[k], 0))

    for side in sides:
        greet(side)

    for read in reads[2:]:
        read.start()

    def copy(src, dst, slot, target):
        return pltpu.make_async_remote_copy(
            src_ref=src,
            dst_ref=dst,
            send_sem=send_sem.at[slot],
            recv_sem=recv_sem.at[slot],
            device_id=target,
            device_id_type=MESH,
        )

    def stage_copies(stage, field):
        cells = pl.ds(TOP, WRAP)
        base = 6 * stage
        pairs = [
            (field.at[:, 2:4, cells, :], planes.at[stage, 1]),
            (field.at[:, SPAN : 2 + SPAN, cells, :], planes.at[stage, 0]),
            (wall_send.at[stage, 0], wall_recv.at[stage, 0]),
            (wall_send.at[stage, 1], wall_recv.at[stage, 1]),
            (edges.at[stage, 0], edges.at[stage, 2]),
            (edges.at[stage, 0], edges.at[stage, 1]),
        ]
        return [copy(src, dst, base + i, sides[i]) for i, (src, dst) in enumerate(pairs)]

    def stage_wrap_rows(stage, field):
        for v in range(VARS):
            for r in range(2):
                wall_send[stage, 0, v, r] = field[v, 2 : 2 + SPAN, TOP + r, :]
                wall_send[stage, 1, v, r] = field[v, 2 : 2 + SPAN, TOP + WRAP - 2 + r, :]

    def stage_columns(stage):
        edge_terms(
            normal, n_norm, edges.at[stage, 0], edges.at[stage, 1], edges.at[stage, 2], jac, corr
        )

    for field in (field1, field2):
        for s in (0, 1, 2 + SPAN, 3 + SPAN):
            field[:, s, TOP : TOP + WRAP, :] = jnp.zeros((VARS, WRAP, LANES), jnp.float32)
        for r in (0, TOP + WRAP):
            field[:, 2 : 2 + SPAN, r : r + 8, :] = jnp.zeros((VARS, SPAN, 8, LANES), jnp.float32)

    wide = []
    for i, (src, dst, target) in enumerate(
        [
            (tip_put.at[0], tip_got.at[3], corners[0]),
            (tip_put.at[0], tip_got.at[2], corners[1]),
            (tip_put.at[1], tip_got.at[1], corners[2]),
            (tip_put.at[1], tip_got.at[0], corners[3]),
            (edge_put.at[0], edge_got.at[1], sides[2]),
            (edge_put.at[1], edge_got.at[0], sides[3]),
            (wall_pairs, wall_beside.at[1], sides[0]),
            (wall_pairs, wall_beside.at[0], sides[1]),
        ]
    ):
        wide.append(
            pltpu.make_async_remote_copy(
                src_ref=src,
                dst_ref=dst,
                send_sem=wide_send_sem.at[i],
                recv_sem=wide_recv_sem.at[i],
                device_id=target,
                device_id_type=MESH,
            )
        )

    empty = tuple(jnp.zeros((8, LANES), jnp.float32) for _ in range(VARS))

    reads[0].wait()
    reads[1].wait()

    @pl.when(normal == 0)
    def _():
        pack_wall(field1, volume, wall_packed)
        pair_wall(wall_packed, wall_pairs, edge_put, tip_put)

    stage_wrap_rows(0, field1)

    def pack_first(s, packed):
        cells = [
            field1[v, s + 2, TOP : TOP + WRAP, :].reshape(2, 8, LANES) for v in range(VARS)
        ]
        return pack_plane(packed, cells, s)

    packed = lax.fori_loop(0, SPAN, pack_first, empty, unroll=True)
    for v in range(VARS):
        edges[0, 0, v] = packed[v]

    for read in reads[2:]:
        read.wait()
    lane = lane_of((8, LANES))
    held = jnp.where(lane < LANES // 2, 2 * lane, 2 * lane - (LANES - 1))

    for d in range(3):
        for u in range(VARS):
            for v in range(VARS):
                scaled = jac_held[u, d, v] * (-1.0 / 12.0)
                jac[25 * d + 5 * u + v] = jnp.full((8, LANES), scaled, jnp.float32)
    def permuted(x):
        full = jnp.broadcast_to(x, (8, LANES))
        return jnp.take_along_axis(full, held, axis=1)[0:1]

    bending, mass, hardening, disp, vel = [permuted(beam_v[i]) for i in range(5)]
    contact = permuted(contact_v[...])
    inertia = 2.0 * mass / (DT_BEAM * DT_BEAM)
    pull = CONTACT_STIFF * STOP_GAP
    push = jnp.where(contact == 1, pull, jnp.where(contact == 2, -pull, 0.0))
    steady = inertia * (disp + DT_BEAM * vel) + push
    base = inertia + jnp.where(contact > 0, CONTACT_STIFF, 0.0)
    be, bo = halves(bending)
    he, ho = halves(hardening)
    ge, go = halves(base)
    ue, uo = halves(disp)
    fe, fo = halves(steady)
    factors = factor(be, bo, ge + 3.0 * he * ue * ue, go + 3.0 * ho * uo * uo)

    @pl.when(normal == 0)
    def _():
        row_id = lax.broadcasted_iota(jnp.int32, (WRAP, WRAP), 0)
        same = (row_id == lane_of((WRAP, WRAP))).astype(jnp.float32)

        def turned_over(x):
            return lax.dot_general(
                same, x, (((1,), (1,)), ((), ())), precision=lax.Precision.HIGHEST
            )

        weights = turned_over(area[...])
        places = turned_over(stations[...].astype(jnp.float32))
        aims = jnp.broadcast_to(held[0:1], (WRAP, LANES)).astype(jnp.float32)
        for s in range(SPAN):
            weight = jnp.broadcast_to(weights[:, s : s + 1], (WRAP, LANES))
            place = jnp.broadcast_to(places[:, s : s + 1], (WRAP, LANES))
            faces[s] = jnp.where(place == aims, weight, 0.0)

    at_wall = lax.div(n_norm - normal, n_norm)
    wall_peers = 4 + (len(y_at) - 1 - len(set(beside_y))) + (zs - 1) + cores * (n_norm - 1)
    pl.semaphore_wait(barrier, 6 + at_wall * wall_peers)

    @pl.when(normal == 0)
    def _():
        for one in wide:
            one.start()

    first = stage_copies(0, field1)
    for one in first:
        one.start()

    def group_copy(buffer, own, which, target):
        return pltpu.make_async_remote_copy(
            src_ref=buffer.at[own],
            dst_ref=buffer.at[own],
            send_sem=group_sem.at[2 * which],
            recv_sem=group_sem.at[2 * which + 1],
            device_id=target,
            device_id_type=MESH,
        )

    def added(ref):
        terms = [ref[i] for i in range(ref.shape[0])]
        while len(terms) > 1:
            terms = [sum(terms[i + 1 : i + 2], terms[i]) for i in range(0, len(terms), 2)]
        return terms[0]

    def take(ref, which):
        pltpu.make_async_copy(ref, ref, group_sem.at[which]).wait()

    def first_plane(s, carry):
        cells, rates = plane_rates(field1, s, jac)
        scale = DT_FLOW * volume[s].reshape(2, 8, LANES)
        for u in range(VARS):
            mid = cells[u] + scale * rates[u]
            field2[u, s + 2, TOP : TOP + WRAP, :] = mid.reshape(WRAP, LANES)
        return carry

    lax.fori_loop(0, SPAN, first_plane, 0)

    @pl.when(normal == 0)
    def _():
        for one in wide:
            one.wait_recv()
        loads_a[y_own] = wall_loads(
            span,
            n_span,
            wall_packed,
            wall_beside,
            edge_got,
            tip_got,
            wall_layer,
            wall_mid,
            faces,
            jac,
        )
        for k in y_far:
            group_copy(loads_a, y_own, 0, device(y_at[k], z, core, 0)).start()

    for one in first:
        one.wait_recv()
    stage_columns(0)

    def mid_plane(u, s, part):
        field2[u, s + 2, TOP : TOP + WRAP, :] += part

    def mid_row(u, r, part):
        field2[u, 2 : 2 + SPAN, TOP + r, :] += part

    def mid_cells(u, s, part):
        cells = field2[u, s + 2, TOP : TOP + WRAP, :].reshape(2, 8, LANES) + part
        field2[u, s + 2, TOP : TOP + WRAP, :] = cells.reshape(WRAP, LANES)
        return cells

    columns = add_ghosts(
        span,
        n_span,
        planes.at[0],
        wall_recv.at[0],
        corr,
        jac,
        volume,
        DT_FLOW,
        mid_plane,
        mid_row,
        mid_cells,
        pack_plane,
    )
    packed = lax.fori_loop(0, SPAN, lambda s, packed: columns(s, packed), empty, unroll=True)
    for v in range(VARS):
        edges[1, 0, v] = packed[v]

    stage_wrap_rows(1, field2)
    second = stage_copies(1, field2)
    for one in second:
        one.start()

    @pl.when(normal == 0)
    def _():
        take(loads_a.at[1:], 1)
        loads_b[z] = added(loads_a)
        for k in z_far:
            group_copy(loads_b, z, 1, device(here, z_at[k], core, 0)).start()

    def second_plane(s, carry):
        cells, rates = plane_rates(field2, s, jac)
        scale = DT_FLOW * volume[s].reshape(2, 8, LANES)
        for u in range(VARS):
            start = field1[u, s + 2, TOP : TOP + WRAP, :].reshape(2, 8, LANES)
            after = 0.5 * (start + cells[u] + scale * rates[u])
            result[u, s] = after.reshape(WRAP, LANES)
        return carry

    lax.fori_loop(0, SPAN, second_plane, 0)

    @pl.when(normal == 0)
    def _():
        if zs > 1:
            take(loads_b.at[1:], 3)
        loads_c[core] = added(loads_b)
        for x in sorted(range(n_norm), key=lambda x: -ring(x, n_norm)):
            for k in range(cores):
                if x or k:
                    group_copy(loads_c, core, 2, device(here, z, core_at[k], x)).start()

    for one in second:
        one.wait_recv()
    stage_columns(1)

    def end_plane(u, s, part):
        result[u, s] += part

    def end_row(u, r, part):
        result[u, :, r, :] += part

    def end_cells(u, s, part):
        result[u, s] += part.reshape(WRAP, LANES)

    columns = add_ghosts(
        span,
        n_span,
        planes.at[1],
        wall_recv.at[1],
        corr,
        jac,
        volume,
        0.5 * DT_FLOW,
        end_plane,
        end_row,
        end_cells,
        lambda carry, cells, s: carry,
    )
    lax.fori_loop(0, SPAN, columns, 0, unroll=True)

    for one in first + second:
        one.wait_send()

    @pl.when(normal == 0)
    def _():
        for one in wide:
            one.wait_send()
        take(loads_a.at[1:], 0)
        if zs > 1:
            take(loads_b.at[1:], 2)
        take(tally, 4)

    @pl.when(normal == 0)
    def _():
        take(loads_c.at[1:], 5)

    @pl.when(normal != 0)
    def _():
        take(loads_c, 5)

    loads = added(loads_c)

    le, lo = halves(loads)
    fe, fo = fe + le, fo + lo
    for newton_step in range(NEWTON):
        if newton_step:
            factors = factor(be, bo, ge + 3.0 * he * ue * ue, go + 3.0 * ho * uo * uo)
        ue, uo = substitute(factors, *right_side(fe, fo, he, ho, ue, uo))
    both = jnp.where(lane_of((1, LANES)) < LANES // 2, ue, roll(uo, LANES // 2))
    back = (lane % 2) * (LANES // 2) + lane // 2
    full = jnp.broadcast_to(both, (8, LANES))
    defl_ref[...] = jnp.take_along_axis(full, back, axis=1)[0:1]


def hand_out(flow_ref, defl_ref, flow_out, defl_out, sem):
    copies = [
        pltpu.make_async_copy(flow_ref, flow_out, sem.at[0]),
        pltpu.make_async_copy(defl_ref, defl_out, sem.at[1]),
    ]
    for one in copies:
        one.start()
    for one in copies:
        one.wait()


def solution(mesh):
    n_span, n_wrap, n_norm = (mesh.shape[axis] for axis in ("span", "wrap", "normal"))
    zs, ys = n_span // 4, 2 * n_wrap
    f32 = jnp.float32

    def step(
        flow_state,
        inv_volume,
        flux_jacobians,
        area,
        station_map,
        contact,
        bending,
        mass,
        hardening,
        disp_old,
        vel_old,
    ):
        vectors = [
            x.reshape(1, STATIONS) for x in (contact, bending, mass, hardening, disp_old, vel_old)
        ]
        hbm, vmem = (pl.BlockSpec(memory_space=space) for space in (pltpu.HBM, pltpu.VMEM))
        operands = [flow_state, inv_volume, flux_jacobians.transpose(1, 0, 2), area, station_map]
        operands = [pltpu.with_memory_space_constraint(x, pltpu.HBM) for x in operands + vectors]
        flow_next, deflection = pl.pallas_call(
            functools.partial(kernel, n_span, n_wrap, n_norm),
            out_shape=(
                pltpu.VMEM(flow_state.shape, f32),
                pltpu.VMEM((1, STATIONS), f32),
            ),
            in_specs=[hbm] * len(operands),
            out_specs=(vmem, vmem),
            scratch_shapes=[
                pltpu.VMEM((VARS, SPAN + 4, WRAP + 16, LANES), f32),
                pltpu.VMEM((VARS, SPAN + 4, WRAP + 16, LANES), f32),
                pltpu.VMEM((2, 2, VARS, 2, WRAP, LANES), f32),
                pltpu.VMEM((SPAN, WRAP, LANES), f32),
                pltpu.VMEM((2, 2, VARS, 2, SPAN, LANES), f32),
                pltpu.VMEM((2, 2, VARS, 2, SPAN, LANES), f32),
                pltpu.VMEM((2, 3, VARS, 8, LANES), f32),
                pltpu.VMEM((VARS, 8, LANES), f32),
                pltpu.VMEM((75, 8, LANES), f32),
                pltpu.VMEM((SPAN, WRAP, LANES), f32),
                pltpu.VMEM((SPAN, WRAP), f32),
                pltpu.VMEM((SPAN, WRAP), jnp.int32),
                pltpu.VMEM((1, STATIONS), jnp.int32),
                pltpu.VMEM((5, 1, STATIONS), f32),
                pltpu.SMEM((VARS, 3, VARS), f32),
                pltpu.VMEM((ys, 1, LANES), f32),
                pltpu.VMEM((zs, 1, LANES), f32),
                pltpu.VMEM((2, 1, LANES), f32),
                pltpu.VMEM((2 * n_norm - 1, 1, LANES), f32),
                pltpu.VMEM((VARS + 1, WRAP, LANES), f32),
                pltpu.VMEM((3, WRAP, LANES), f32),
                pltpu.VMEM((2, 3, WRAP, LANES), f32),
                pltpu.VMEM((2, 2, 8, LANES), f32),
                pltpu.VMEM((2, 2, 8, LANES), f32),
                pltpu.VMEM((2, 8, LANES), f32),
                pltpu.VMEM((4, 8, LANES), f32),
                pltpu.VMEM((VARS + 1, WRAP + 16, LANES), f32),
                pltpu.VMEM((VARS, 24, LANES), f32),
                pltpu.SemaphoreType.DMA((11,)),
                pltpu.SemaphoreType.DMA((12,)),
                pltpu.SemaphoreType.DMA((12,)),
                pltpu.SemaphoreType.DMA((6,)),
                pltpu.SemaphoreType.DMA((8,)),
                pltpu.SemaphoreType.DMA((8,)),
            ],
            compiler_params=pltpu.CompilerParams(
                collective_id=0, has_side_effects=True, vmem_limit_bytes=32 * 1024 * 1024
            ),
            cost_estimate=pl.CostEstimate(
                flops=10_000_000, bytes_accessed=1_000_000, transcendentals=0
            ),
        )(*operands)
        flow_next, deflection = pl.pallas_call(
            hand_out,
            out_shape=(
                jax.ShapeDtypeStruct(flow_state.shape, f32),
                jax.ShapeDtypeStruct((1, STATIONS), f32),
            ),
            in_specs=(vmem, vmem),
            out_specs=(hbm, hbm),
            scratch_shapes=[pltpu.SemaphoreType.DMA((2,))],
        )(
            pltpu.with_memory_space_constraint(flow_next, pltpu.VMEM),
            pltpu.with_memory_space_constraint(deflection, pltpu.VMEM),
        )
        return flow_next, deflection.reshape(STATIONS)

    placed = (
        P(None, "span", "wrap", "normal"),
        P("span", "wrap", "normal"),
        P(),
        P("span", "wrap"),
        P("span", "wrap"),
    ) + (P(),) * 6
    return jax.shard_map(
        step,
        mesh=mesh,
        in_specs=placed,
        out_specs=(P(None, "span", "wrap", "normal"), P()),
        check_vma=False,
    )
```

```python
import functools

import jax
import jax.numpy as jnp
from jax import lax
from jax.experimental import pallas as pl
from jax.experimental.pallas import tpu as pltpu
from jax.sharding import PartitionSpec as P

MESH = pl.DeviceIdType.MESH
VARS = 5
STATIONS = 128
NEWTON = 3
DT_FLOW = 0.2
DISSIPATION = 0.03
DT_BEAM = 0.2
STOP_GAP = 0.5
CONTACT_STIFF = 40.0
SPAN, WRAP, LANES = 8, 16, 128
TOP = 8


def lane_of(shape):
    return lax.broadcasted_iota(jnp.int32, shape, len(shape) - 1)


def roll(x, shift):
    return pltpu.roll(x, shift % LANES if isinstance(shift, int) else shift, 1)


def factor(be, bo, diag_e, diag_o):
    lane = lane_of((1, LANES))
    half = LANES // 2
    valid, inner = lane < half, lane < half - 1
    bo_prev, be_next = roll(bo, 1), roll(be, -1)
    p = jnp.where(valid, 4.0 * be + bo_prev + bo + diag_e, 1.0)
    q = jnp.where(valid, -2.0 * (be + bo), 0.0)
    r = jnp.where(valid, 4.0 * bo + be + be_next + diag_o, 1.0)
    c11 = jnp.where(inner, bo, 0.0)
    c12 = jnp.zeros_like(bo)
    c21 = jnp.where(inner, -2.0 * (bo + be_next), 0.0)
    c22 = jnp.where(inner, be_next, 0.0)
    a11, a12, a21, a22 = roll(c11, 1), roll(c21, 1), c12, roll(c22, 1)
    levels = []
    step = 1
    while step < half:
        inv = 1.0 / (p * r - q * q)
        u11, u12 = c11 * r - c21 * q, c21 * p - c11 * q
        u21, u22 = c12 * r - c22 * q, c22 * p - c12 * q
        d11, d12 = a11 * r - a21 * q, a21 * p - a11 * q
        d21, d22 = a12 * r - a22 * q, a22 * p - a12 * q
        levels.append((step, inv, u11, u12, u21, u22, d11, d12, d21, d22))
        up = [
            (u11 * c11 + u12 * c21) * inv,
            (u11 * c12 + u12 * c22) * inv,
            (u21 * c12 + u22 * c22) * inv,
        ]
        down = [
            (d11 * a11 + d12 * a21) * inv,
            (d11 * a12 + d12 * a22) * inv,
            (d21 * a12 + d22 * a22) * inv,
        ]
        p = p - (roll(up[0], step) + roll(down[0], -step))
        q = q - (roll(up[1], step) + roll(down[1], -step))
        r = r - (roll(up[2], step) + roll(down[2], -step))
        if 2 * step < half:
            n11, n12 = -(d11 * c11 + d12 * c21) * inv, -(d11 * c12 + d12 * c22) * inv
            n21, n22 = -(d21 * c11 + d22 * c21) * inv, -(d21 * c12 + d22 * c22) * inv
            c11, c12 = roll(n11, -step), roll(n12, -step)
            c21, c22 = roll(n21, -step), roll(n22, -step)
            a11, a12 = roll(n11, step), roll(n21, step)
            a21, a22 = roll(n12, step), roll(n22, step)
        step *= 2
    return levels, (1.0 / (p * r - q * q), p, q, r)


def substitute(factors, e, o):
    levels, (inv, p, q, r) = factors
    for step, scale, u11, u12, u21, u22, d11, d12, d21, d22 in levels:
        e, o = (
            e - (roll((u11 * e + u12 * o) * scale, step) + roll((d11 * e + d12 * o) * scale, -step)),
            o - (roll((u21 * e + u22 * o) * scale, step) + roll((d21 * e + d22 * o) * scale, -step)),
        )
    return (r * e - q * o) * inv, (p * o - q * e) * inv


def right_side(fe, fo, he, ho, ue, uo):
    return fe + 2.0 * he * ue * ue * ue, fo + 2.0 * ho * uo * uo * uo


def halves(x):
    valid = lane_of((1, LANES)) < LANES // 2
    return jnp.where(valid, x, 0.0), jnp.where(valid, roll(x, LANES // 2), 0.0)


def ring(by, count):
    return min(by, count - by)


def pack_plane(packed, cells, s):
    slot = lane_of((8, LANES)) // 4
    new = []
    for v in range(VARS):
        have = packed[v]
        for t in range(2):
            k = 2 * s + t
            have = jnp.where(slot == k, roll(cells[v][t], 4 * k + 2), have)
        new.append(have)
    return tuple(new)


def edge_terms(normal, n_norm, own, left, right, jac, corr):
    lane = lane_of((8, LANES))
    place = lane % 4
    ends, smooths = [], []
    for v in range(VARS):
        mine = own[v]
        mirror = jnp.where(place == 0, roll(mine, -3), roll(mine, -1))
        low = jnp.where(normal == 0, mirror, left[v])
        high = jnp.where(normal == n_norm - 1, 0.0, right[v])
        delta = jnp.where(place < 2, roll(high - mine, -2), roll(low - mine, 2))
        near = jnp.where(place == 1, roll(delta, 1), jnp.where(place == 2, roll(delta, -1), 0.0))
        end = delta - 8.0 * near
        ends.append(jnp.where(place < 2, -end, end))
        smooths.append(delta - 4.0 * near)
    for u in range(VARS):
        total = -DISSIPATION * smooths[u]
        for v in range(VARS):
            total = total + jac[50 + 5 * u + v] * ends[v]
        corr[u] = total


def plane_rates(field, s, jac):
    cells, grads, smooths = [], [[], [], []], []
    for v in range(VARS):

        def at(ds, dw):
            return field[v, s + (2 + ds), TOP + dw : TOP + dw + WRAP, :]

        c = at(0, 0)
        reads = [
            [at(k, 0) for k in (-2, -1, 1, 2)],
            [at(0, k) for k in (-2, -1, 1, 2)],
            [roll(c, -k) for k in (-2, -1, 1, 2)],
        ]
        near, far = None, None
        for d, (m2, m1, p1, p2) in enumerate(reads):
            grads[d].append(((m2 - p2) + 8.0 * (p1 - m1)).reshape(2, 8, LANES))
            near = (m1 + p1) if near is None else near + (m1 + p1)
            far = (m2 + p2) if far is None else far + (m2 + p2)
        smooths.append((-DISSIPATION * (far - 4.0 * near + 18.0 * c)).reshape(2, 8, LANES))
        cells.append(c.reshape(2, 8, LANES))
    rates = []
    for u in range(VARS):
        total = smooths[u]
        for d in range(3):
            for v in range(VARS):
                total = total + jac[25 * d + 5 * u + v][None] * grads[d][v]
        rates.append(total)
    return cells, rates


def ghost_rates(direction, low, first, second, jac, shape):
    outer, inner = [], []
    for v in range(VARS):
        a, b = first(v), second(v)
        if low:
            outer.append((a - 8.0 * b, a - 4.0 * b))
            inner.append((b, b))
        else:
            outer.append((8.0 * a - b, b - 4.0 * a))
            inner.append((-a, a))
    fixes = []
    for layer in (outer, inner):
        grads = [g.reshape(shape) for g, _ in layer]
        layer_fixes = []
        for u in range(VARS):
            total = -DISSIPATION * layer[u][1].reshape(shape)
            for v in range(VARS):
                total = total + jac[25 * direction + 5 * u + v][None] * grads[v]
            layer_fixes.append(total)
        fixes.append(layer_fixes)
    return fixes


def add_ghosts(span, n_span, planes, rows, corr, jac, volume, factor_of, at_plane, at_row, at_cells, done):
    for low in (True, False):
        gone = span == (0 if low else n_span - 1)
        side = 0 if low else 1

        def ghost(layer):
            return lambda v: jnp.where(gone, 0.0, planes[side, v, layer])

        fixes = ghost_rates(0, low, ghost(0), ghost(1), jac, (2, 8, LANES))
        for s, fix in zip((0, 1) if low else (SPAN - 1, SPAN - 2), fixes):
            scale = factor_of * volume[s]
            for u in range(VARS):
                at_plane(u, s, scale * fix[u].reshape(WRAP, LANES))
    for low in (True, False):
        side = 1 if low else 0

        def ghost(layer):
            return lambda v: rows[side, v, layer]

        fixes = ghost_rates(1, low, ghost(0), ghost(1), jac, (1, 8, LANES))
        for r, fix in zip((0, 1) if low else (WRAP - 1, WRAP - 2), fixes):
            scale = factor_of * volume[:, r, :]
            for u in range(VARS):
                at_row(u, r, scale * fix[u].reshape(8, LANES))
    lane = lane_of((8, LANES))
    edge = (lane < 2) | (lane >= LANES - 2)

    def columns(s, carry):
        scale = factor_of * volume[s].reshape(2, 8, LANES)
        cells = []
        for u in range(VARS):
            ends = corr[u]
            fix = [
                jnp.where(edge, roll(ends, (2 * LANES - 2 - 4 * (2 * s + t)) % LANES), 0.0)
                for t in range(2)
            ]
            cells.append(at_cells(u, s, scale * jnp.stack(fix)))
        return done(carry, cells, s)

    return columns


def pack_wall(field, volume, packed):
    group = lane_of((8, LANES)) // 8
    for v in range(VARS + 1):
        for t in range(2):
            have = jnp.zeros((8, LANES), jnp.float32)
            for s in range(SPAN):
                if v < VARS:
                    tile = field[v, s + 2, TOP + 8 * t : TOP + 8 * t + 8, :]
                else:
                    tile = volume[s, 8 * t : 8 * t + 8, :]
                have = jnp.where(group == s + 4, roll(tile, 8 * (s + 4) + 2), have)
            packed[v, 8 * t : 8 * t + 8, :] = mirrored(have)


def pair_wall(packed, pairs, edge, tip):
    lane, row = lane_of((8, LANES)), lax.broadcasted_iota(jnp.int32, (8, LANES), 0)
    own = (lane >= LANES // 4) & (lane < 3 * LANES // 4)
    for p in range(3):
        for t in range(2):
            rows = slice(8 * t, 8 * t + 8)
            pairs[p, rows, :] = jnp.where(own, packed[p, rows, :], roll(packed[p + 3, rows, :], 64))
    for t in range(2):
        a, b, c = (pairs[p, 8 * t : 8 * t + 8, :] for p in range(3))
        four = row < 4
        edge[t, 0] = jnp.where(four, a if t == 0 else pltpu.roll(a, 4, 0), b if t else pltpu.roll(b, 4, 0))
        edge[t, 1] = c
        at = 6 * t
        tip[t] = jnp.where(
            row < 2,
            turn_rows(a, -at),
            jnp.where(four, turn_rows(b, 2 - at), turn_rows(c, 4 - at)),
        )


def turn_rows(x, by):
    return pltpu.roll(x, by % 8, 0) if by % 8 else x


def mirrored(x):
    place = lane_of(x.shape) % 8
    return jnp.where(place == 0, roll(x, -3), jnp.where(place == 1, roll(x, -1), x))


def wall_rates(layer, top, rows, wanted, jac, at_wall):
    cells, grads, smooths = [], [[], [], []], []
    shape = (rows // 8, 8, LANES)
    for v in range(VARS):
        c = layer[v, top : top + rows, :]
        reads = [
            [roll(c, -8 * k) for k in (-2, -1, 1, 2)],
            [layer[v, top + k : top + k + rows, :] for k in (-2, -1, 1, 2)],
        ]
        if at_wall:
            p1, p2 = roll(c, -1), roll(c, -2)
            reads.append([p1, c, p1, p2])
        else:
            reads.append([roll(c, -k) for k in (-2, -1, 1, 2)])
        near, far = None, None
        for d, (m2, m1, p1, p2) in enumerate(reads):
            grads[d].append(((m2 - p2) + 8.0 * (p1 - m1)).reshape(shape))
            near = (m1 + p1) if near is None else near + (m1 + p1)
            far = (m2 + p2) if far is None else far + (m2 + p2)
        smooths.append((-DISSIPATION * (far - 4.0 * near + 18.0 * c)).reshape(shape))
        cells.append(c)
    rates = []
    for u in range(wanted):
        total = smooths[u]
        for d in range(3):
            for v in range(VARS):
                total = total + jac[25 * d + 5 * u + v][None] * grads[d][v]
        rates.append(total.reshape(rows, LANES))
    return cells, rates


def wall_loads(span, n_span, packed, beside, edges, tips, layer, mid, faces, jac):
    group = lane_of((8, LANES)) // 8
    first, last = span == 0, span == n_span - 1

    def swing(x, when):
        return roll(x, LANES // 2) if when else x

    for v in range(VARS + 1):
        p, upper = v % 3, v >= 3
        low_edge = edges[0, 1] if p == 2 else turn_rows(edges[0, 0], 4 - 4 * p)
        high_edge = edges[1, 1] if p == 2 else turn_rows(edges[1, 0], 4 * p)
        tiles = [
            (turn_rows(tips[0], 6 - 2 * p), swing(low_edge, upper), turn_rows(tips[1], 6 - 2 * p)),
            (beside[0, p, 0:8], packed[v, 0:8], beside[1, p, 0:8]),
            (beside[0, p, 8:16], packed[v, 8:16], beside[1, p, 8:16]),
            (turn_rows(tips[2], -2 * p), swing(high_edge, upper), turn_rows(tips[3], -2 * p)),
        ]
        for t, (left, centre, right) in enumerate(tiles):
            left = jnp.where(first, 0.0, swing(left, not upper))
            right = jnp.where(last, 0.0, swing(right, not upper))
            whole = jnp.where(group < 4, left, jnp.where(group >= 12, right, centre))
            layer[v, 8 * t : 8 * t + 8, :] = whole
    span_group = lane_of((24, LANES)) // 8
    outside = (first & (span_group < 4)) | (last & (span_group >= 12))
    cells, rates = wall_rates(layer, 4, 24, VARS, jac, False)
    scale = DT_FLOW * layer[VARS, 4:28, :]
    for u in range(VARS):
        mid[u] = jnp.where(outside, 0.0, cells[u] + scale * rates[u])
    cells, rates = wall_rates(mid, 4, 16, 1, jac, True)
    scale = DT_FLOW * layer[VARS, 8:24, :]
    after = 0.5 * (layer[0, 8:24, :] + cells[0] + scale * rates[0])
    total = jnp.zeros((WRAP, LANES), jnp.float32)
    for s in range(SPAN):
        at = 8 * (s + 4) + 2
        total = total + faces[s] * jnp.broadcast_to(after[:, at : at + 1], (WRAP, LANES))
    return jnp.sum(total, axis=0, keepdims=True)


def kernel(
    n_span,
    n_wrap,
    n_norm,
    flow_hbm,
    volume_hbm,
    jac_hbm,
    area_hbm,
    map_hbm,
    contact_hbm,
    bending_hbm,
    mass_hbm,
    hardening_hbm,
    disp_hbm,
    vel_hbm,
    result,
    defl_ref,
    field1,
    field2,
    planes,
    volume,
    wall_send,
    wall_recv,
    edges,
    corr,
    jac,
    faces,
    area,
    stations,
    contact_v,
    beam_v,
    jac_held,
    loads_a,
    loads_b,
    loads_c,
    tally,
    wall_packed,
    wall_pairs,
    wall_beside,
    edge_put,
    edge_got,
    tip_put,
    tip_got,
    wall_layer,
    wall_mid,
    local_sem,
    send_sem,
    recv_sem,
    group_sem,
    wide_send_sem,
    wide_recv_sem,
):
    span, wrap, normal = lax.axis_index("span"), lax.axis_index("wrap"), lax.axis_index("normal")
    rows = 2
    cols = n_span // rows
    row, col = lax.div(span, cols), lax.rem(span, cols)
    zs, cores = cols // 2, 2
    z, core = lax.div(col, cores), lax.rem(col, cores)
    y_own = row * n_wrap + wrap

    inputs = [
        (flow_hbm, field1.at[:, 2 : 2 + SPAN, TOP : TOP + WRAP, :]),
        (volume_hbm, volume),
        (area_hbm, area),
        (map_hbm, stations),
        (contact_hbm, contact_v),
        (bending_hbm, beam_v.at[0]),
        (mass_hbm, beam_v.at[1]),
        (hardening_hbm, beam_v.at[2]),
        (disp_hbm, beam_v.at[3]),
        (vel_hbm, beam_v.at[4]),
        (jac_hbm, jac_held),
    ]
    reads = [pltpu.make_async_copy(a, b, local_sem.at[i]) for i, (a, b) in enumerate(inputs)]
    for read in reads[:2]:
        read.start()

    def turned(index, by, count):
        return lax.rem(index + (by + count), count)

    span_at = {by: turned(span, by, n_span) for by in (-1, 1)}
    wrap_at = [turned(wrap, by, n_wrap) for by in range(n_wrap)]
    norm_at = {by: turned(normal, by, n_norm) for by in (-1, 1)}
    row_at = [turned(row, by, rows) for by in range(rows)]
    z_at = [turned(z, by, zs) for by in range(zs)]
    core_at = [core, turned(core, 1, cores)]
    sides = [
        (span_at[-1], wrap, normal),
        (span_at[1], wrap, normal),
        (span, wrap_at[n_wrap - 1], normal),
        (span, wrap_at[1], normal),
        (span, wrap, norm_at[-1]),
        (span, wrap, norm_at[1]),
    ]
    barrier = pltpu.get_barrier_semaphore()

    def greet(target):
        pl.semaphore_signal(barrier, inc=1, device_id=target, device_id_type=MESH)

    corners = [(span_at[i], wrap_at[j], normal) for j in (n_wrap - 1, 1) for i in (-1, 1)]

    def device(y, z, core, x):
        return (y[0] * cols + z * cores + core, y[1], x)

    here = (row, wrap)
    y_at = [(row_at[a], wrap_at[b]) for a in range(rows) for b in range(n_wrap)]
    y_far = sorted(range(1, rows * n_wrap), key=lambda k: -ring(2 * (k % n_wrap) + k // n_wrap, 2 * n_wrap))
    z_far = sorted(range(1, zs), key=lambda k: -ring(k, zs))
    beside_y = (1, n_wrap - 1)

    @pl.when(normal == 0)
    def _():
        for k in z_far:
            greet(device(here, z_at[k], core, 0))
        for k in y_far:
            if k not in beside_y:
                greet(device(y_at[k], z, core, 0))
        for one in corners:
            greet(one)

    @pl.when(normal != 0)
    def _():
        for k in range(cores):
            greet(device(here, z, core_at[k], 0))

    for side in sides:
        greet(side)

    for read in reads[2:]:
        read.start()

    def copy(src, dst, slot, target):
        return pltpu.make_async_remote_copy(
            src_ref=src,
            dst_ref=dst,
            send_sem=send_sem.at[slot],
            recv_sem=recv_sem.at[slot],
            device_id=target,
            device_id_type=MESH,
        )

    def stage_copies(stage, field):
        cells = pl.ds(TOP, WRAP)
        base = 6 * stage
        pairs = [
            (field.at[:, 2:4, cells, :], planes.at[stage, 1]),
            (field.at[:, SPAN : 2 + SPAN, cells, :], planes.at[stage, 0]),
            (wall_send.at[stage, 0], wall_recv.at[stage, 0]),
            (wall_send.at[stage, 1], wall_recv.at[stage, 1]),
            (edges.at[stage, 0], edges.at[stage, 2]),
            (edges.at[stage, 0], edges.at[stage, 1]),
        ]
        return [copy(src, dst, base + i, sides[i]) for i, (src, dst) in enumerate(pairs)]

    def stage_wrap_rows(stage, field):
        for v in range(VARS):
            for r in range(2):
                wall_send[stage, 0, v, r] = field[v, 2 : 2 + SPAN, TOP + r, :]
                wall_send[stage, 1, v, r] = field[v, 2 : 2 + SPAN, TOP + WRAP - 2 + r, :]

    def stage_columns(stage):
        edge_terms(
            normal, n_norm, edges.at[stage, 0], edges.at[stage, 1], edges.at[stage, 2], jac, corr
        )

    for field in (field1, field2):
        for s in (0, 1, 2 + SPAN, 3 + SPAN):
            field[:, s, TOP : TOP + WRAP, :] = jnp.zeros((VARS, WRAP, LANES), jnp.float32)
        for r in (0, TOP + WRAP):
            field[:, 2 : 2 + SPAN, r : r + 8, :] = jnp.zeros((VARS, SPAN, 8, LANES), jnp.float32)

    wide = []
    for i, (src, dst, target) in enumerate(
        [
            (tip_put.at[0], tip_got.at[3], corners[0]),
            (tip_put.at[0], tip_got.at[2], corners[1]),
            (tip_put.at[1], tip_got.at[1], corners[2]),
            (tip_put.at[1], tip_got.at[0], corners[3]),
            (edge_put.at[0], edge_got.at[1], sides[2]),
            (edge_put.at[1], edge_got.at[0], sides[3]),
            (wall_pairs, wall_beside.at[1], sides[0]),
            (wall_pairs, wall_beside.at[0], sides[1]),
        ]
    ):
        wide.append(
            pltpu.make_async_remote_copy(
                src_ref=src,
                dst_ref=dst,
                send_sem=wide_send_sem.at[i],
                recv_sem=wide_recv_sem.at[i],
                device_id=target,
                device_id_type=MESH,
            )
        )

    empty = tuple(jnp.zeros((8, LANES), jnp.float32) for _ in range(VARS))

    reads[0].wait()
    reads[1].wait()

    @pl.when(normal == 0)
    def _():
        pack_wall(field1, volume, wall_packed)
        pair_wall(wall_packed, wall_pairs, edge_put, tip_put)

    stage_wrap_rows(0, field1)

    def pack_first(s, packed):
        cells = [
            field1[v, s + 2, TOP : TOP + WRAP, :].reshape(2, 8, LANES) for v in range(VARS)
        ]
        return pack_plane(packed, cells, s)

    packed = lax.fori_loop(0, SPAN, pack_first, empty, unroll=True)
    for v in range(VARS):
        edges[0, 0, v] = packed[v]

    lane = lane_of((8, LANES))
    held = jnp.where(lane < LANES // 2, 2 * lane, 2 * lane - (LANES - 1))

    def prepare():
        for read in reads[2:]:
            read.wait()
        for d in range(3):
            for u in range(VARS):
                for v in range(VARS):
                    scaled = jac_held[u, d, v] * (-1.0 / 12.0)
                    jac[25 * d + 5 * u + v] = jnp.full((8, LANES), scaled, jnp.float32)

    @pl.when(normal == 0)
    def _():
        prepare()
        row_id = lax.broadcasted_iota(jnp.int32, (WRAP, WRAP), 0)
        same = (row_id == lane_of((WRAP, WRAP))).astype(jnp.float32)

        def turned_over(x):
            return lax.dot_general(
                same, x, (((1,), (1,)), ((), ())), precision=lax.Precision.HIGHEST
            )

        weights = turned_over(area[...])
        places = turned_over(stations[...].astype(jnp.float32))
        aims = jnp.broadcast_to(held[0:1], (WRAP, LANES)).astype(jnp.float32)
        for s in range(SPAN):
            weight = jnp.broadcast_to(weights[:, s : s + 1], (WRAP, LANES))
            place = jnp.broadcast_to(places[:, s : s + 1], (WRAP, LANES))
            faces[s] = jnp.where(place == aims, weight, 0.0)

    at_wall = lax.div(n_norm - normal, n_norm)
    wall_peers = 4 + (len(y_at) - 1 - len(set(beside_y))) + (zs - 1) + cores * (n_norm - 1)
    pl.semaphore_wait(barrier, 6 + at_wall * wall_peers)

    @pl.when(normal == 0)
    def _():
        for one in wide:
            one.start()

    first = stage_copies(0, field1)
    for one in first:
        one.start()

    @pl.when(normal != 0)
    def _():
        prepare()


    def group_copy(buffer, own, which, target):
        return pltpu.make_async_remote_copy(
            src_ref=buffer.at[own],
            dst_ref=buffer.at[own],
            send_sem=group_sem.at[2 * which],
            recv_sem=group_sem.at[2 * which + 1],
            device_id=target,
            device_id_type=MESH,
        )

    def added(ref):
        terms = [ref[i] for i in range(ref.shape[0])]
        while len(terms) > 1:
            terms = [sum(terms[i + 1 : i + 2], terms[i]) for i in range(0, len(terms), 2)]
        return terms[0]

    def take(ref, which):
        pltpu.make_async_copy(ref, ref, group_sem.at[which]).wait()

    def first_plane(s, carry):
        cells, rates = plane_rates(field1, s, jac)
        scale = DT_FLOW * volume[s].reshape(2, 8, LANES)
        for u in range(VARS):
            mid = cells[u] + scale * rates[u]
            field2[u, s + 2, TOP : TOP + WRAP, :] = mid.reshape(WRAP, LANES)
        return carry

    lax.fori_loop(0, SPAN, first_plane, 0)

    @pl.when(normal == 0)
    def _():
        for one in wide:
            one.wait_recv()
        loads_a[y_own] = wall_loads(
            span,
            n_span,
            wall_packed,
            wall_beside,
            edge_got,
            tip_got,
            wall_layer,
            wall_mid,
            faces,
            jac,
        )
        for k in y_far:
            group_copy(loads_a, y_own, 0, device(y_at[k], z, core, 0)).start()
        take(loads_a.at[1:], 1)
        loads_b[z] = added(loads_a)
        for k in z_far:
            group_copy(loads_b, z, 1, device(here, z_at[k], core, 0)).start()

    for one in first:
        one.wait_recv()
    stage_columns(0)

    def mid_plane(u, s, part):
        field2[u, s + 2, TOP : TOP + WRAP, :] += part

    def mid_row(u, r, part):
        field2[u, 2 : 2 + SPAN, TOP + r, :] += part

    def mid_cells(u, s, part):
        cells = field2[u, s + 2, TOP : TOP + WRAP, :].reshape(2, 8, LANES) + part
        field2[u, s + 2, TOP : TOP + WRAP, :] = cells.reshape(WRAP, LANES)
        return cells

    columns = add_ghosts(
        span,
        n_span,
        planes.at[0],
        wall_recv.at[0],
        corr,
        jac,
        volume,
        DT_FLOW,
        mid_plane,
        mid_row,
        mid_cells,
        pack_plane,
    )
    packed = lax.fori_loop(0, SPAN, lambda s, packed: columns(s, packed), empty, unroll=True)
    for v in range(VARS):
        edges[1, 0, v] = packed[v]

    stage_wrap_rows(1, field2)
    second = stage_copies(1, field2)
    for one in second:
        one.start()


    @pl.when(normal == 0)
    def _():
        if zs > 1:
            take(loads_b.at[1:], 3)
        loads_c[core] = added(loads_b)
        for x in sorted(range(n_norm), key=lambda x: -ring(x, n_norm)):
            for k in range(cores):
                if x or k:
                    group_copy(loads_c, core, 2, device(here, z, core_at[k], x)).start()

    def second_plane(s, carry):
        cells, rates = plane_rates(field2, s, jac)
        scale = DT_FLOW * volume[s].reshape(2, 8, LANES)
        for u in range(VARS):
            start = field1[u, s + 2, TOP : TOP + WRAP, :].reshape(2, 8, LANES)
            after = 0.5 * (start + cells[u] + scale * rates[u])
            result[u, s] = after.reshape(WRAP, LANES)
        return carry

    lax.fori_loop(0, SPAN, second_plane, 0)

    def permuted(x):
        full = jnp.broadcast_to(x, (8, LANES))
        return jnp.take_along_axis(full, held, axis=1)[0:1]

    bending, mass, hardening, disp, vel = [permuted(beam_v[i]) for i in range(5)]
    contact = permuted(contact_v[...])
    inertia = 2.0 * mass / (DT_BEAM * DT_BEAM)
    pull = CONTACT_STIFF * STOP_GAP
    push = jnp.where(contact == 1, pull, jnp.where(contact == 2, -pull, 0.0))
    steady = inertia * (disp + DT_BEAM * vel) + push
    base = inertia + jnp.where(contact > 0, CONTACT_STIFF, 0.0)
    be, bo = halves(bending)
    he, ho = halves(hardening)
    ge, go = halves(base)
    ue, uo = halves(disp)
    fe, fo = halves(steady)
    factors = factor(be, bo, ge + 3.0 * he * ue * ue, go + 3.0 * ho * uo * uo)

    for one in second:
        one.wait_recv()
    stage_columns(1)

    def end_plane(u, s, part):
        result[u, s] += part

    def end_row(u, r, part):
        result[u, :, r, :] += part

    def end_cells(u, s, part):
        result[u, s] += part.reshape(WRAP, LANES)

    columns = add_ghosts(
        span,
        n_span,
        planes.at[1],
        wall_recv.at[1],
        corr,
        jac,
        volume,
        0.5 * DT_FLOW,
        end_plane,
        end_row,
        end_cells,
        lambda carry, cells, s: carry,
    )
    lax.fori_loop(0, SPAN, columns, 0, unroll=True)

    for one in first + second:
        one.wait_send()

    @pl.when(normal == 0)
    def _():
        for one in wide:
            one.wait_send()
        take(loads_a.at[1:], 0)
        if zs > 1:
            take(loads_b.at[1:], 2)
        take(tally, 4)

    @pl.when(normal == 0)
    def _():
        take(loads_c.at[1:], 5)

    @pl.when(normal != 0)
    def _():
        take(loads_c, 5)

    loads = added(loads_c)

    le, lo = halves(loads)
    fe, fo = fe + le, fo + lo
    for newton_step in range(NEWTON):
        if newton_step:
            factors = factor(be, bo, ge + 3.0 * he * ue * ue, go + 3.0 * ho * uo * uo)
        ue, uo = substitute(factors, *right_side(fe, fo, he, ho, ue, uo))
    both = jnp.where(lane_of((1, LANES)) < LANES // 2, ue, roll(uo, LANES // 2))
    back = (lane % 2) * (LANES // 2) + lane // 2
    full = jnp.broadcast_to(both, (8, LANES))
    defl_ref[...] = jnp.take_along_axis(full, back, axis=1)[0:1]


def hand_out(flow_ref, defl_ref, flow_out, defl_out, sem):
    copies = [
        pltpu.make_async_copy(flow_ref, flow_out, sem.at[0]),
        pltpu.make_async_copy(defl_ref, defl_out, sem.at[1]),
    ]
    for one in copies:
        one.start()
    for one in copies:
        one.wait()


def solution(mesh):
    n_span, n_wrap, n_norm = (mesh.shape[axis] for axis in ("span", "wrap", "normal"))
    zs, ys = n_span // 4, 2 * n_wrap
    f32 = jnp.float32

    def step(
        flow_state,
        inv_volume,
        flux_jacobians,
        area,
        station_map,
        contact,
        bending,
        mass,
        hardening,
        disp_old,
        vel_old,
    ):
        vectors = [
            x.reshape(1, STATIONS) for x in (contact, bending, mass, hardening, disp_old, vel_old)
        ]
        hbm, vmem = (pl.BlockSpec(memory_space=space) for space in (pltpu.HBM, pltpu.VMEM))
        operands = [flow_state, inv_volume, flux_jacobians.transpose(1, 0, 2), area, station_map]
        operands = [pltpu.with_memory_space_constraint(x, pltpu.HBM) for x in operands + vectors]
        flow_next, deflection = pl.pallas_call(
            functools.partial(kernel, n_span, n_wrap, n_norm),
            out_shape=(
                pltpu.VMEM(flow_state.shape, f32),
                pltpu.VMEM((1, STATIONS), f32),
            ),
            in_specs=[hbm] * len(operands),
            out_specs=(vmem, vmem),
            scratch_shapes=[
                pltpu.VMEM((VARS, SPAN + 4, WRAP + 16, LANES), f32),
                pltpu.VMEM((VARS, SPAN + 4, WRAP + 16, LANES), f32),
                pltpu.VMEM((2, 2, VARS, 2, WRAP, LANES), f32),
                pltpu.VMEM((SPAN, WRAP, LANES), f32),
                pltpu.VMEM((2, 2, VARS, 2, SPAN, LANES), f32),
                pltpu.VMEM((2, 2, VARS, 2, SPAN, LANES), f32),
                pltpu.VMEM((2, 3, VARS, 8, LANES), f32),
                pltpu.VMEM((VARS, 8, LANES), f32),
                pltpu.VMEM((75, 8, LANES), f32),
                pltpu.VMEM((SPAN, WRAP, LANES), f32),
                pltpu.VMEM((SPAN, WRAP), f32),
                pltpu.VMEM((SPAN, WRAP), jnp.int32),
                pltpu.VMEM((1, STATIONS), jnp.int32),
                pltpu.VMEM((5, 1, STATIONS), f32),
                pltpu.SMEM((VARS, 3, VARS), f32),
                pltpu.VMEM((ys, 1, LANES), f32),
                pltpu.VMEM((zs, 1, LANES), f32),
                pltpu.VMEM((2, 1, LANES), f32),
                pltpu.VMEM((2 * n_norm - 1, 1, LANES), f32),
                pltpu.VMEM((VARS + 1, WRAP, LANES), f32),
                pltpu.VMEM((3, WRAP, LANES), f32),
                pltpu.VMEM((2, 3, WRAP, LANES), f32),
                pltpu.VMEM((2, 2, 8, LANES), f32),
                pltpu.VMEM((2, 2, 8, LANES), f32),
                pltpu.VMEM((2, 8, LANES), f32),
                pltpu.VMEM((4, 8, LANES), f32),
                pltpu.VMEM((VARS + 1, WRAP + 16, LANES), f32),
                pltpu.VMEM((VARS, 24, LANES), f32),
                pltpu.SemaphoreType.DMA((11,)),
                pltpu.SemaphoreType.DMA((12,)),
                pltpu.SemaphoreType.DMA((12,)),
                pltpu.SemaphoreType.DMA((6,)),
                pltpu.SemaphoreType.DMA((8,)),
                pltpu.SemaphoreType.DMA((8,)),
            ],
            compiler_params=pltpu.CompilerParams(
                collective_id=0, has_side_effects=True, vmem_limit_bytes=32 * 1024 * 1024
            ),
            cost_estimate=pl.CostEstimate(
                flops=10_000_000, bytes_accessed=1_000_000, transcendentals=0
            ),
        )(*operands)
        flow_next, deflection = pl.pallas_call(
            hand_out,
            out_shape=(
                jax.ShapeDtypeStruct(flow_state.shape, f32),
                jax.ShapeDtypeStruct((1, STATIONS), f32),
            ),
            in_specs=(vmem, vmem),
            out_specs=(hbm, hbm),
            scratch_shapes=[pltpu.SemaphoreType.DMA((2,))],
        )(
            pltpu.with_memory_space_constraint(flow_next, pltpu.VMEM),
            pltpu.with_memory_space_constraint(deflection, pltpu.VMEM),
        )
        return flow_next, deflection.reshape(STATIONS)

    placed = (
        P(None, "span", "wrap", "normal"),
        P("span", "wrap", "normal"),
        P(),
        P("span", "wrap"),
        P("span", "wrap"),
    ) + (P(),) * 6
    return jax.shard_map(
        step,
        mesh=mesh,
        in_specs=placed,
        out_specs=(P(None, "span", "wrap", "normal"), P()),
        check_vma=False,
    )
```

```python
import functools

import jax
import jax.numpy as jnp
from jax import lax
from jax.experimental import pallas as pl
from jax.experimental.pallas import tpu as pltpu
from jax.sharding import PartitionSpec as P

MESH = pl.DeviceIdType.MESH
VARS = 5
STATIONS = 128
NEWTON = 3
DT_FLOW = 0.2
DISSIPATION = 0.03
DT_BEAM = 0.2
STOP_GAP = 0.5
CONTACT_STIFF = 40.0
SPAN, WRAP, LANES = 8, 16, 128
TOP = 8


def lane_of(shape):
    return lax.broadcasted_iota(jnp.int32, shape, len(shape) - 1)


def roll(x, shift):
    return pltpu.roll(x, shift % LANES if isinstance(shift, int) else shift, 1)


def factor(be, bo, diag_e, diag_o):
    lane = lane_of((1, LANES))
    half = LANES // 2
    valid, inner = lane < half, lane < half - 1
    bo_prev, be_next = roll(bo, 1), roll(be, -1)
    p = jnp.where(valid, 4.0 * be + bo_prev + bo + diag_e, 1.0)
    q = jnp.where(valid, -2.0 * (be + bo), 0.0)
    r = jnp.where(valid, 4.0 * bo + be + be_next + diag_o, 1.0)
    c11 = jnp.where(inner, bo, 0.0)
    c12 = jnp.zeros_like(bo)
    c21 = jnp.where(inner, -2.0 * (bo + be_next), 0.0)
    c22 = jnp.where(inner, be_next, 0.0)
    a11, a12, a21, a22 = roll(c11, 1), roll(c21, 1), c12, roll(c22, 1)
    levels = []
    step = 1
    while step < half:
        inv = 1.0 / (p * r - q * q)
        u11, u12 = c11 * r - c21 * q, c21 * p - c11 * q
        u21, u22 = c12 * r - c22 * q, c22 * p - c12 * q
        d11, d12 = a11 * r - a21 * q, a21 * p - a11 * q
        d21, d22 = a12 * r - a22 * q, a22 * p - a12 * q
        levels.append((step, inv, u11, u12, u21, u22, d11, d12, d21, d22))
        up = [
            (u11 * c11 + u12 * c21) * inv,
            (u11 * c12 + u12 * c22) * inv,
            (u21 * c12 + u22 * c22) * inv,
        ]
        down = [
            (d11 * a11 + d12 * a21) * inv,
            (d11 * a12 + d12 * a22) * inv,
            (d21 * a12 + d22 * a22) * inv,
        ]
        p = p - (roll(up[0], step) + roll(down[0], -step))
        q = q - (roll(up[1], step) + roll(down[1], -step))
        r = r - (roll(up[2], step) + roll(down[2], -step))
        if 2 * step < half:
            n11, n12 = -(d11 * c11 + d12 * c21) * inv, -(d11 * c12 + d12 * c22) * inv
            n21, n22 = -(d21 * c11 + d22 * c21) * inv, -(d21 * c12 + d22 * c22) * inv
            c11, c12 = roll(n11, -step), roll(n12, -step)
            c21, c22 = roll(n21, -step), roll(n22, -step)
            a11, a12 = roll(n11, step), roll(n21, step)
            a21, a22 = roll(n12, step), roll(n22, step)
        step *= 2
    return levels, (1.0 / (p * r - q * q), p, q, r)


def substitute(factors, e, o):
    levels, (inv, p, q, r) = factors
    for step, scale, u11, u12, u21, u22, d11, d12, d21, d22 in levels:
        e, o = (
            e - (roll((u11 * e + u12 * o) * scale, step) + roll((d11 * e + d12 * o) * scale, -step)),
            o - (roll((u21 * e + u22 * o) * scale, step) + roll((d21 * e + d22 * o) * scale, -step)),
        )
    return (r * e - q * o) * inv, (p * o - q * e) * inv


def right_side(fe, fo, he, ho, ue, uo):
    return fe + 2.0 * he * ue * ue * ue, fo + 2.0 * ho * uo * uo * uo


def halves(x):
    valid = lane_of((1, LANES)) < LANES // 2
    return jnp.where(valid, x, 0.0), jnp.where(valid, roll(x, LANES // 2), 0.0)


def ring(by, count):
    return min(by, count - by)


def pack_plane(packed, cells, s):
    slot = lane_of((8, LANES)) // 4
    new = []
    for v in range(VARS):
        have = packed[v]
        for t in range(2):
            k = 2 * s + t
            have = jnp.where(slot == k, roll(cells[v][t], 4 * k + 2), have)
        new.append(have)
    return tuple(new)


def edge_terms(normal, n_norm, own, left, right, jac, corr):
    lane = lane_of((8, LANES))
    place = lane % 4
    ends, smooths = [], []
    for v in range(VARS):
        mine = own[v]
        mirror = jnp.where(place == 0, roll(mine, -3), roll(mine, -1))
        low = jnp.where(normal == 0, mirror, left[v])
        high = jnp.where(normal == n_norm - 1, 0.0, right[v])
        delta = jnp.where(place < 2, roll(high - mine, -2), roll(low - mine, 2))
        near = jnp.where(place == 1, roll(delta, 1), jnp.where(place == 2, roll(delta, -1), 0.0))
        end = delta - 8.0 * near
        ends.append(jnp.where(place < 2, -end, end))
        smooths.append(delta - 4.0 * near)
    for u in range(VARS):
        total = -DISSIPATION * smooths[u]
        for v in range(VARS):
            total = total + jac[50 + 5 * u + v] * ends[v]
        corr[u] = total


def plane_rates(field, s, jac):
    cells, grads, smooths = [], [[], [], []], []
    for v in range(VARS):

        def at(ds, dw):
            return field[v, s + (2 + ds), TOP + dw : TOP + dw + WRAP, :]

        c = at(0, 0)
        reads = [
            [at(k, 0) for k in (-2, -1, 1, 2)],
            [at(0, k) for k in (-2, -1, 1, 2)],
            [roll(c, -k) for k in (-2, -1, 1, 2)],
        ]
        near, far = None, None
        for d, (m2, m1, p1, p2) in enumerate(reads):
            grads[d].append(((m2 - p2) + 8.0 * (p1 - m1)).reshape(2, 8, LANES))
            near = (m1 + p1) if near is None else near + (m1 + p1)
            far = (m2 + p2) if far is None else far + (m2 + p2)
        smooths.append((-DISSIPATION * (far - 4.0 * near + 18.0 * c)).reshape(2, 8, LANES))
        cells.append(c.reshape(2, 8, LANES))
    rates = []
    for u in range(VARS):
        total = smooths[u]
        for d in range(3):
            for v in range(VARS):
                total = total + jac[25 * d + 5 * u + v][None] * grads[d][v]
        rates.append(total)
    return cells, rates


def ghost_rates(direction, low, first, second, jac, shape):
    outer, inner = [], []
    for v in range(VARS):
        a, b = first(v), second(v)
        if low:
            outer.append((a - 8.0 * b, a - 4.0 * b))
            inner.append((b, b))
        else:
            outer.append((8.0 * a - b, b - 4.0 * a))
            inner.append((-a, a))
    fixes = []
    for layer in (outer, inner):
        grads = [g.reshape(shape) for g, _ in layer]
        layer_fixes = []
        for u in range(VARS):
            total = -DISSIPATION * layer[u][1].reshape(shape)
            for v in range(VARS):
                total = total + jac[25 * direction + 5 * u + v][None] * grads[v]
            layer_fixes.append(total)
        fixes.append(layer_fixes)
    return fixes


def add_ghosts(span, n_span, planes, rows, corr, jac, volume, factor_of, at_plane, at_row, at_cells, done):
    for low in (True, False):
        gone = span == (0 if low else n_span - 1)
        side = 0 if low else 1

        def ghost(layer):
            return lambda v: jnp.where(gone, 0.0, planes[side, v, layer])

        fixes = ghost_rates(0, low, ghost(0), ghost(1), jac, (2, 8, LANES))
        for s, fix in zip((0, 1) if low else (SPAN - 1, SPAN - 2), fixes):
            scale = factor_of * volume[s]
            for u in range(VARS):
                at_plane(u, s, scale * fix[u].reshape(WRAP, LANES))
    for low in (True, False):
        side = 1 if low else 0

        def ghost(layer):
            return lambda v: rows[side, v, layer]

        fixes = ghost_rates(1, low, ghost(0), ghost(1), jac, (1, 8, LANES))
        for r, fix in zip((0, 1) if low else (WRAP - 1, WRAP - 2), fixes):
            scale = factor_of * volume[:, r, :]
            for u in range(VARS):
                at_row(u, r, scale * fix[u].reshape(8, LANES))
    lane = lane_of((8, LANES))
    edge = (lane < 2) | (lane >= LANES - 2)

    def columns(s, carry):
        scale = factor_of * volume[s].reshape(2, 8, LANES)
        cells = []
        for u in range(VARS):
            ends = corr[u]
            fix = [
                jnp.where(edge, roll(ends, (2 * LANES - 2 - 4 * (2 * s + t)) % LANES), 0.0)
                for t in range(2)
            ]
            cells.append(at_cells(u, s, scale * jnp.stack(fix)))
        return done(carry, cells, s)

    return columns


def pack_wall(field, volume, packed):
    group = lane_of((8, LANES)) // 8
    for v in range(VARS + 1):
        for t in range(2):
            have = jnp.zeros((8, LANES), jnp.float32)
            for s in range(SPAN):
                if v < VARS:
                    tile = field[v, s + 2, TOP + 8 * t : TOP + 8 * t + 8, :]
                else:
                    tile = volume[s, 8 * t : 8 * t + 8, :]
                have = jnp.where(group == s + 4, roll(tile, 8 * (s + 4) + 2), have)
            packed[v, 8 * t : 8 * t + 8, :] = mirrored(have)


def pair_wall(packed, pairs, edge, tip):
    lane, row = lane_of((8, LANES)), lax.broadcasted_iota(jnp.int32, (8, LANES), 0)
    own = (lane >= LANES // 4) & (lane < 3 * LANES // 4)
    for p in range(3):
        for t in range(2):
            rows = slice(8 * t, 8 * t + 8)
            pairs[p, rows, :] = jnp.where(own, packed[p, rows, :], roll(packed[p + 3, rows, :], 64))
    for t in range(2):
        a, b, c = (pairs[p, 8 * t : 8 * t + 8, :] for p in range(3))
        four = row < 4
        edge[t, 0] = jnp.where(four, a if t == 0 else pltpu.roll(a, 4, 0), b if t else pltpu.roll(b, 4, 0))
        edge[t, 1] = c
        at = 6 * t
        tip[t] = jnp.where(
            row < 2,
            turn_rows(a, -at),
            jnp.where(four, turn_rows(b, 2 - at), turn_rows(c, 4 - at)),
        )


def turn_rows(x, by):
    return pltpu.roll(x, by % 8, 0) if by % 8 else x


def mirrored(x):
    place = lane_of(x.shape) % 8
    return jnp.where(place == 0, roll(x, -3), jnp.where(place == 1, roll(x, -1), x))


def wall_rates(layer, top, rows, wanted, jac, at_wall):
    cells, grads, smooths = [], [[], [], []], []
    shape = (rows // 8, 8, LANES)
    for v in range(VARS):
        c = layer[v, top : top + rows, :]
        reads = [
            [roll(c, -8 * k) for k in (-2, -1, 1, 2)],
            [layer[v, top + k : top + k + rows, :] for k in (-2, -1, 1, 2)],
        ]
        if at_wall:
            p1, p2 = roll(c, -1), roll(c, -2)
            reads.append([p1, c, p1, p2])
        else:
            reads.append([roll(c, -k) for k in (-2, -1, 1, 2)])
        near, far = None, None
        for d, (m2, m1, p1, p2) in enumerate(reads):
            grads[d].append(((m2 - p2) + 8.0 * (p1 - m1)).reshape(shape))
            near = (m1 + p1) if near is None else near + (m1 + p1)
            far = (m2 + p2) if far is None else far + (m2 + p2)
        smooths.append((-DISSIPATION * (far - 4.0 * near + 18.0 * c)).reshape(shape))
        cells.append(c)
    rates = []
    for u in range(wanted):
        total = smooths[u]
        for d in range(3):
            for v in range(VARS):
                total = total + jac[25 * d + 5 * u + v][None] * grads[d][v]
        rates.append(total.reshape(rows, LANES))
    return cells, rates


def wall_loads(span, n_span, packed, beside, edges, tips, layer, mid, faces, jac):
    group = lane_of((8, LANES)) // 8
    first, last = span == 0, span == n_span - 1

    def swing(x, when):
        return roll(x, LANES // 2) if when else x

    for v in range(VARS + 1):
        p, upper = v % 3, v >= 3
        low_edge = edges[0, 1] if p == 2 else turn_rows(edges[0, 0], 4 - 4 * p)
        high_edge = edges[1, 1] if p == 2 else turn_rows(edges[1, 0], 4 * p)
        tiles = [
            (turn_rows(tips[0], 6 - 2 * p), swing(low_edge, upper), turn_rows(tips[1], 6 - 2 * p)),
            (beside[0, p, 0:8], packed[v, 0:8], beside[1, p, 0:8]),
            (beside[0, p, 8:16], packed[v, 8:16], beside[1, p, 8:16]),
            (turn_rows(tips[2], -2 * p), swing(high_edge, upper), turn_rows(tips[3], -2 * p)),
        ]
        for t, (left, centre, right) in enumerate(tiles):
            left = jnp.where(first, 0.0, swing(left, not upper))
            right = jnp.where(last, 0.0, swing(right, not upper))
            whole = jnp.where(group < 4, left, jnp.where(group >= 12, right, centre))
            layer[v, 8 * t : 8 * t + 8, :] = whole
    span_group = lane_of((24, LANES)) // 8
    outside = (first & (span_group < 4)) | (last & (span_group >= 12))
    cells, rates = wall_rates(layer, 4, 24, VARS, jac, False)
    scale = DT_FLOW * layer[VARS, 4:28, :]
    for u in range(VARS):
        mid[u] = jnp.where(outside, 0.0, cells[u] + scale * rates[u])
    cells, rates = wall_rates(mid, 4, 16, 1, jac, True)
    scale = DT_FLOW * layer[VARS, 8:24, :]
    after = 0.5 * (layer[0, 8:24, :] + cells[0] + scale * rates[0])
    total = jnp.zeros((WRAP, LANES), jnp.float32)
    for s in range(SPAN):
        at = 8 * (s + 4) + 2
        total = total + faces[s] * jnp.broadcast_to(after[:, at : at + 1], (WRAP, LANES))
    return jnp.sum(total, axis=0, keepdims=True)


def kernel(
    n_span,
    n_wrap,
    n_norm,
    flow_hbm,
    volume_hbm,
    jac_hbm,
    area_hbm,
    map_hbm,
    contact_hbm,
    bending_hbm,
    mass_hbm,
    hardening_hbm,
    disp_hbm,
    vel_hbm,
    result,
    defl_ref,
    field1,
    field2,
    planes,
    volume,
    wall_send,
    wall_recv,
    edges,
    corr,
    jac,
    faces,
    area,
    stations,
    contact_v,
    beam_v,
    jac_held,
    loads_a,
    loads_b,
    tally,
    wall_packed,
    wall_pairs,
    wall_beside,
    edge_put,
    edge_got,
    tip_put,
    tip_got,
    wall_layer,
    wall_mid,
    local_sem,
    send_sem,
    recv_sem,
    group_sem,
    wide_send_sem,
    wide_recv_sem,
):
    span, wrap, normal = lax.axis_index("span"), lax.axis_index("wrap"), lax.axis_index("normal")
    rows = 2
    cols = n_span // rows
    row, col = lax.div(span, cols), lax.rem(span, cols)
    zs, cores = cols // 2, 2
    z, core = lax.div(col, cores), lax.rem(col, cores)
    y_own = row * n_wrap + wrap

    inputs = [
        (flow_hbm, field1.at[:, 2 : 2 + SPAN, TOP : TOP + WRAP, :]),
        (volume_hbm, volume),
        (area_hbm, area),
        (map_hbm, stations),
        (contact_hbm, contact_v),
        (bending_hbm, beam_v.at[0]),
        (mass_hbm, beam_v.at[1]),
        (hardening_hbm, beam_v.at[2]),
        (disp_hbm, beam_v.at[3]),
        (vel_hbm, beam_v.at[4]),
        (jac_hbm, jac_held),
    ]
    reads = [pltpu.make_async_copy(a, b, local_sem.at[i]) for i, (a, b) in enumerate(inputs)]
    for read in reads[:2]:
        read.start()

    def turned(index, by, count):
        return lax.rem(index + (by + count), count)

    span_at = {by: turned(span, by, n_span) for by in (-1, 1)}
    wrap_at = [turned(wrap, by, n_wrap) for by in range(n_wrap)]
    norm_at = {by: turned(normal, by, n_norm) for by in (-1, 1)}
    row_at = [turned(row, by, rows) for by in range(rows)]
    z_at = [turned(z, by, zs) for by in range(zs)]
    core_at = [core, turned(core, 1, cores)]
    sides = [
        (span_at[-1], wrap, normal),
        (span_at[1], wrap, normal),
        (span, wrap_at[n_wrap - 1], normal),
        (span, wrap_at[1], normal),
        (span, wrap, norm_at[-1]),
        (span, wrap, norm_at[1]),
    ]
    barrier = pltpu.get_barrier_semaphore()

    def greet(target):
        pl.semaphore_signal(barrier, inc=1, device_id=target, device_id_type=MESH)

    corners = [(span_at[i], wrap_at[j], normal) for j in (n_wrap - 1, 1) for i in (-1, 1)]

    def device(y, z, core, x):
        return (y[0] * cols + z * cores + core, y[1], x)

    here = (row, wrap)
    y_at = [(row_at[a], wrap_at[b]) for a in range(rows) for b in range(n_wrap)]
    y_far = sorted(range(1, rows * n_wrap), key=lambda k: -ring(2 * (k % n_wrap) + k // n_wrap, 2 * n_wrap))
    z_far = sorted(range(1, zs), key=lambda k: -ring(k, zs))
    beside_y = (1, n_wrap - 1)

    @pl.when(normal == 0)
    def _():
        for k in z_far:
            for c in range(cores):
                greet(device(here, z_at[k], core_at[c], 0))
        for k in y_far:
            if k not in beside_y:
                greet(device(y_at[k], z, core, 0))
        for one in corners:
            greet(one)

    @pl.when(normal != 0)
    def _():
        for k in y_far + [0]:
            greet(device(y_at[k], z, core, 0))

    for side in sides:
        greet(side)

    for read in reads[2:]:
        read.start()

    def copy(src, dst, slot, target):
        return pltpu.make_async_remote_copy(
            src_ref=src,
            dst_ref=dst,
            send_sem=send_sem.at[slot],
            recv_sem=recv_sem.at[slot],
            device_id=target,
            device_id_type=MESH,
        )

    def stage_copies(stage, field):
        cells = pl.ds(TOP, WRAP)
        base = 6 * stage
        pairs = [
            (field.at[:, 2:4, cells, :], planes.at[stage, 1]),
            (field.at[:, SPAN : 2 + SPAN, cells, :], planes.at[stage, 0]),
            (wall_send.at[stage, 0], wall_recv.at[stage, 0]),
            (wall_send.at[stage, 1], wall_recv.at[stage, 1]),
            (edges.at[stage, 0], edges.at[stage, 2]),
            (edges.at[stage, 0], edges.at[stage, 1]),
        ]
        return [copy(src, dst, base + i, sides[i]) for i, (src, dst) in enumerate(pairs)]

    def stage_wrap_rows(stage, field):
        for v in range(VARS):
            for r in range(2):
                wall_send[stage, 0, v, r] = field[v, 2 : 2 + SPAN, TOP + r, :]
                wall_send[stage, 1, v, r] = field[v, 2 : 2 + SPAN, TOP + WRAP - 2 + r, :]

    def stage_columns(stage):
        edge_terms(
            normal, n_norm, edges.at[stage, 0], edges.at[stage, 1], edges.at[stage, 2], jac, corr
        )

    for field in (field1, field2):
        for s in (0, 1, 2 + SPAN, 3 + SPAN):
            field[:, s, TOP : TOP + WRAP, :] = jnp.zeros((VARS, WRAP, LANES), jnp.float32)
        for r in (0, TOP + WRAP):
            field[:, 2 : 2 + SPAN, r : r + 8, :] = jnp.zeros((VARS, SPAN, 8, LANES), jnp.float32)

    wide = []
    for i, (src, dst, target) in enumerate(
        [
            (tip_put.at[0], tip_got.at[3], corners[0]),
            (tip_put.at[0], tip_got.at[2], corners[1]),
            (tip_put.at[1], tip_got.at[1], corners[2]),
            (tip_put.at[1], tip_got.at[0], corners[3]),
            (edge_put.at[0], edge_got.at[1], sides[2]),
            (edge_put.at[1], edge_got.at[0], sides[3]),
            (wall_pairs, wall_beside.at[1], sides[0]),
            (wall_pairs, wall_beside.at[0], sides[1]),
        ]
    ):
        wide.append(
            pltpu.make_async_remote_copy(
                src_ref=src,
                dst_ref=dst,
                send_sem=wide_send_sem.at[i],
                recv_sem=wide_recv_sem.at[i],
                device_id=target,
                device_id_type=MESH,
            )
        )

    empty = tuple(jnp.zeros((8, LANES), jnp.float32) for _ in range(VARS))

    reads[0].wait()
    reads[1].wait()

    @pl.when(normal == 0)
    def _():
        pack_wall(field1, volume, wall_packed)
        pair_wall(wall_packed, wall_pairs, edge_put, tip_put)

    stage_wrap_rows(0, field1)

    def pack_first(s, packed):
        cells = [
            field1[v, s + 2, TOP : TOP + WRAP, :].reshape(2, 8, LANES) for v in range(VARS)
        ]
        return pack_plane(packed, cells, s)

    packed = lax.fori_loop(0, SPAN, pack_first, empty, unroll=True)
    for v in range(VARS):
        edges[0, 0, v] = packed[v]

    lane = lane_of((8, LANES))
    held = jnp.where(lane < LANES // 2, 2 * lane, 2 * lane - (LANES - 1))

    def prepare():
        for read in reads[2:]:
            read.wait()
        for d in range(3):
            for u in range(VARS):
                for v in range(VARS):
                    scaled = jac_held[u, d, v] * (-1.0 / 12.0)
                    jac[25 * d + 5 * u + v] = jnp.full((8, LANES), scaled, jnp.float32)

    @pl.when(normal == 0)
    def _():
        prepare()
        row_id = lax.broadcasted_iota(jnp.int32, (WRAP, WRAP), 0)
        same = (row_id == lane_of((WRAP, WRAP))).astype(jnp.float32)

        def turned_over(x):
            return lax.dot_general(
                same, x, (((1,), (1,)), ((), ())), precision=lax.Precision.HIGHEST
            )

        weights = turned_over(area[...])
        places = turned_over(stations[...].astype(jnp.float32))
        aims = jnp.broadcast_to(held[0:1], (WRAP, LANES)).astype(jnp.float32)
        for s in range(SPAN):
            weight = jnp.broadcast_to(weights[:, s : s + 1], (WRAP, LANES))
            place = jnp.broadcast_to(places[:, s : s + 1], (WRAP, LANES))
            faces[s] = jnp.where(place == aims, weight, 0.0)

    at_wall = lax.div(n_norm - normal, n_norm)
    wall_peers = 4 + cores * (zs - 1) + (len(y_at) * n_norm - 1 - len(set(beside_y)))
    pl.semaphore_wait(barrier, 6 + at_wall * wall_peers)

    @pl.when(normal == 0)
    def _():
        for one in wide:
            one.start()

    first = stage_copies(0, field1)
    for one in first:
        one.start()

    @pl.when(normal != 0)
    def _():
        prepare()


    def group_copy(buffer, own, which, target):
        return pltpu.make_async_remote_copy(
            src_ref=buffer.at[own],
            dst_ref=buffer.at[own],
            send_sem=group_sem.at[2 * which],
            recv_sem=group_sem.at[2 * which + 1],
            device_id=target,
            device_id_type=MESH,
        )

    def added(ref):
        terms = [ref[i] for i in range(ref.shape[0])]
        while len(terms) > 1:
            terms = [sum(terms[i + 1 : i + 2], terms[i]) for i in range(0, len(terms), 2)]
        return terms[0]

    def take(ref, which):
        pltpu.make_async_copy(ref, ref, group_sem.at[which]).wait()

    def first_plane(s, carry):
        cells, rates = plane_rates(field1, s, jac)
        scale = DT_FLOW * volume[s].reshape(2, 8, LANES)
        for u in range(VARS):
            mid = cells[u] + scale * rates[u]
            field2[u, s + 2, TOP : TOP + WRAP, :] = mid.reshape(WRAP, LANES)
        return carry

    lax.fori_loop(0, SPAN, first_plane, 0)

    @pl.when(normal == 0)
    def _():
        for one in wide:
            one.wait_recv()
        loads_a[col] = wall_loads(
            span,
            n_span,
            wall_packed,
            wall_beside,
            edge_got,
            tip_got,
            wall_layer,
            wall_mid,
            faces,
            jac,
        )
        for k in z_far + [0]:
            for c in range(cores):
                if k or c:
                    group_copy(loads_a, col, 0, device(here, z_at[k], core_at[c], 0)).start()

    for one in first:
        one.wait_recv()
    stage_columns(0)

    def mid_plane(u, s, part):
        field2[u, s + 2, TOP : TOP + WRAP, :] += part

    def mid_row(u, r, part):
        field2[u, 2 : 2 + SPAN, TOP + r, :] += part

    def mid_cells(u, s, part):
        cells = field2[u, s + 2, TOP : TOP + WRAP, :].reshape(2, 8, LANES) + part
        field2[u, s + 2, TOP : TOP + WRAP, :] = cells.reshape(WRAP, LANES)
        return cells

    columns = add_ghosts(
        span,
        n_span,
        planes.at[0],
        wall_recv.at[0],
        corr,
        jac,
        volume,
        DT_FLOW,
        mid_plane,
        mid_row,
        mid_cells,
        pack_plane,
    )
    packed = lax.fori_loop(0, SPAN, lambda s, packed: columns(s, packed), empty, unroll=True)
    for v in range(VARS):
        edges[1, 0, v] = packed[v]

    stage_wrap_rows(1, field2)
    second = stage_copies(1, field2)
    for one in second:
        one.start()


    @pl.when(normal == 0)
    def _():
        take(loads_a.at[1:], 1)
        loads_b[y_own] = added(loads_a)
        for x in sorted(range(n_norm), key=lambda x: -ring(x, n_norm)):
            for k in y_far + [0]:
                if x or k:
                    group_copy(loads_b, y_own, 1, device(y_at[k], z, core, x)).start()

    def second_plane(s, carry):
        cells, rates = plane_rates(field2, s, jac)
        scale = DT_FLOW * volume[s].reshape(2, 8, LANES)
        for u in range(VARS):
            start = field1[u, s + 2, TOP : TOP + WRAP, :].reshape(2, 8, LANES)
            after = 0.5 * (start + cells[u] + scale * rates[u])
            result[u, s] = after.reshape(WRAP, LANES)
        return carry

    lax.fori_loop(0, SPAN, second_plane, 0)

    def permuted(x):
        full = jnp.broadcast_to(x, (8, LANES))
        return jnp.take_along_axis(full, held, axis=1)[0:1]

    bending, mass, hardening, disp, vel = [permuted(beam_v[i]) for i in range(5)]
    contact = permuted(contact_v[...])
    inertia = 2.0 * mass / (DT_BEAM * DT_BEAM)
    pull = CONTACT_STIFF * STOP_GAP
    push = jnp.where(contact == 1, pull, jnp.where(contact == 2, -pull, 0.0))
    steady = inertia * (disp + DT_BEAM * vel) + push
    base = inertia + jnp.where(contact > 0, CONTACT_STIFF, 0.0)
    be, bo = halves(bending)
    he, ho = halves(hardening)
    ge, go = halves(base)
    ue, uo = halves(disp)
    fe, fo = halves(steady)
    factors = factor(be, bo, ge + 3.0 * he * ue * ue, go + 3.0 * ho * uo * uo)

    for one in second:
        one.wait_recv()
    stage_columns(1)

    def end_plane(u, s, part):
        result[u, s] += part

    def end_row(u, r, part):
        result[u, :, r, :] += part

    def end_cells(u, s, part):
        result[u, s] += part.reshape(WRAP, LANES)

    columns = add_ghosts(
        span,
        n_span,
        planes.at[1],
        wall_recv.at[1],
        corr,
        jac,
        volume,
        0.5 * DT_FLOW,
        end_plane,
        end_row,
        end_cells,
        lambda carry, cells, s: carry,
    )
    lax.fori_loop(0, SPAN, columns, 0, unroll=True)

    for one in first + second:
        one.wait_send()

    @pl.when(normal == 0)
    def _():
        for one in wide:
            one.wait_send()
        take(loads_a.at[1:], 0)
        take(tally, 2)

    @pl.when(normal == 0)
    def _():
        take(loads_b.at[1:], 3)

    @pl.when(normal != 0)
    def _():
        take(loads_b, 3)

    loads = added(loads_b)

    le, lo = halves(loads)
    fe, fo = fe + le, fo + lo
    for newton_step in range(NEWTON):
        if newton_step:
            factors = factor(be, bo, ge + 3.0 * he * ue * ue, go + 3.0 * ho * uo * uo)
        ue, uo = substitute(factors, *right_side(fe, fo, he, ho, ue, uo))
    both = jnp.where(lane_of((1, LANES)) < LANES // 2, ue, roll(uo, LANES // 2))
    back = (lane % 2) * (LANES // 2) + lane // 2
    full = jnp.broadcast_to(both, (8, LANES))
    defl_ref[...] = jnp.take_along_axis(full, back, axis=1)[0:1]


def hand_out(flow_ref, defl_ref, flow_out, defl_out, sem):
    copies = [
        pltpu.make_async_copy(flow_ref, flow_out, sem.at[0]),
        pltpu.make_async_copy(defl_ref, defl_out, sem.at[1]),
    ]
    for one in copies:
        one.start()
    for one in copies:
        one.wait()


def solution(mesh):
    n_span, n_wrap, n_norm = (mesh.shape[axis] for axis in ("span", "wrap", "normal"))
    zs, ys = n_span // 4, 2 * n_wrap
    f32 = jnp.float32

    def step(
        flow_state,
        inv_volume,
        flux_jacobians,
        area,
        station_map,
        contact,
        bending,
        mass,
        hardening,
        disp_old,
        vel_old,
    ):
        vectors = [
            x.reshape(1, STATIONS) for x in (contact, bending, mass, hardening, disp_old, vel_old)
        ]
        hbm, vmem = (pl.BlockSpec(memory_space=space) for space in (pltpu.HBM, pltpu.VMEM))
        operands = [flow_state, inv_volume, flux_jacobians.transpose(1, 0, 2), area, station_map]
        operands = [pltpu.with_memory_space_constraint(x, pltpu.HBM) for x in operands + vectors]
        flow_next, deflection = pl.pallas_call(
            functools.partial(kernel, n_span, n_wrap, n_norm),
            out_shape=(
                pltpu.VMEM(flow_state.shape, f32),
                pltpu.VMEM((1, STATIONS), f32),
            ),
            in_specs=[hbm] * len(operands),
            out_specs=(vmem, vmem),
            scratch_shapes=[
                pltpu.VMEM((VARS, SPAN + 4, WRAP + 16, LANES), f32),
                pltpu.VMEM((VARS, SPAN + 4, WRAP + 16, LANES), f32),
                pltpu.VMEM((2, 2, VARS, 2, WRAP, LANES), f32),
                pltpu.VMEM((SPAN, WRAP, LANES), f32),
                pltpu.VMEM((2, 2, VARS, 2, SPAN, LANES), f32),
                pltpu.VMEM((2, 2, VARS, 2, SPAN, LANES), f32),
                pltpu.VMEM((2, 3, VARS, 8, LANES), f32),
                pltpu.VMEM((VARS, 8, LANES), f32),
                pltpu.VMEM((75, 8, LANES), f32),
                pltpu.VMEM((SPAN, WRAP, LANES), f32),
                pltpu.VMEM((SPAN, WRAP), f32),
                pltpu.VMEM((SPAN, WRAP), jnp.int32),
                pltpu.VMEM((1, STATIONS), jnp.int32),
                pltpu.VMEM((5, 1, STATIONS), f32),
                pltpu.SMEM((VARS, 3, VARS), f32),
                pltpu.VMEM((2 * zs, 1, LANES), f32),
                pltpu.VMEM((ys, 1, LANES), f32),
                pltpu.VMEM((ys * n_norm - 1, 1, LANES), f32),
                pltpu.VMEM((VARS + 1, WRAP, LANES), f32),
                pltpu.VMEM((3, WRAP, LANES), f32),
                pltpu.VMEM((2, 3, WRAP, LANES), f32),
                pltpu.VMEM((2, 2, 8, LANES), f32),
                pltpu.VMEM((2, 2, 8, LANES), f32),
                pltpu.VMEM((2, 8, LANES), f32),
                pltpu.VMEM((4, 8, LANES), f32),
                pltpu.VMEM((VARS + 1, WRAP + 16, LANES), f32),
                pltpu.VMEM((VARS, 24, LANES), f32),
                pltpu.SemaphoreType.DMA((11,)),
                pltpu.SemaphoreType.DMA((12,)),
                pltpu.SemaphoreType.DMA((12,)),
                pltpu.SemaphoreType.DMA((4,)),
                pltpu.SemaphoreType.DMA((8,)),
                pltpu.SemaphoreType.DMA((8,)),
            ],
            compiler_params=pltpu.CompilerParams(
                collective_id=0, has_side_effects=True, vmem_limit_bytes=32 * 1024 * 1024
            ),
            cost_estimate=pl.CostEstimate(
                flops=10_000_000, bytes_accessed=1_000_000, transcendentals=0
            ),
        )(*operands)
        flow_next, deflection = pl.pallas_call(
            hand_out,
            out_shape=(
                jax.ShapeDtypeStruct(flow_state.shape, f32),
                jax.ShapeDtypeStruct((1, STATIONS), f32),
            ),
            in_specs=(vmem, vmem),
            out_specs=(hbm, hbm),
            scratch_shapes=[pltpu.SemaphoreType.DMA((2,))],
        )(
            pltpu.with_memory_space_constraint(flow_next, pltpu.VMEM),
            pltpu.with_memory_space_constraint(deflection, pltpu.VMEM),
        )
        return flow_next, deflection.reshape(STATIONS)

    placed = (
        P(None, "span", "wrap", "normal"),
        P("span", "wrap", "normal"),
        P(),
        P("span", "wrap"),
        P("span", "wrap"),
    ) + (P(),) * 6
    return jax.shard_map(
        step,
        mesh=mesh,
        in_specs=placed,
        out_specs=(P(None, "span", "wrap", "normal"), P()),
        check_vma=False,
    )
```

```python
import functools

import jax
import jax.numpy as jnp
from jax import lax
from jax.experimental import pallas as pl
from jax.experimental.pallas import tpu as pltpu
from jax.sharding import PartitionSpec as P

MESH = pl.DeviceIdType.MESH
VARS = 5
STATIONS = 128
NEWTON = 3
LEVELS = 6
DT_FLOW = 0.2
DISSIPATION = 0.03
DT_BEAM = 0.2
STOP_GAP = 0.5
CONTACT_STIFF = 40.0
SPAN, WRAP, LANES = 8, 16, 128
TOP = 8


def lane_of(shape):
    return lax.broadcasted_iota(jnp.int32, shape, len(shape) - 1)


def roll(x, shift):
    return pltpu.roll(x, shift % LANES if isinstance(shift, int) else shift, 1)


def factor(be, bo, diag_e, diag_o):
    lane = lane_of((1, LANES))
    half = LANES // 2
    valid, inner = lane < half, lane < half - 1
    bo_prev, be_next = roll(bo, 1), roll(be, -1)
    p = jnp.where(valid, 4.0 * be + bo_prev + bo + diag_e, 1.0)
    q = jnp.where(valid, -2.0 * (be + bo), 0.0)
    r = jnp.where(valid, 4.0 * bo + be + be_next + diag_o, 1.0)
    c11 = jnp.where(inner, bo, 0.0)
    c12 = jnp.zeros_like(bo)
    c21 = jnp.where(inner, -2.0 * (bo + be_next), 0.0)
    c22 = jnp.where(inner, be_next, 0.0)
    a11, a12, a21, a22 = roll(c11, 1), roll(c21, 1), c12, roll(c22, 1)
    levels = []
    step = 1
    while step < half:
        inv = 1.0 / (p * r - q * q)
        u11, u12 = c11 * r - c21 * q, c21 * p - c11 * q
        u21, u22 = c12 * r - c22 * q, c22 * p - c12 * q
        d11, d12 = a11 * r - a21 * q, a21 * p - a11 * q
        d21, d22 = a12 * r - a22 * q, a22 * p - a12 * q
        levels.append((step, inv, u11, u12, u21, u22, d11, d12, d21, d22))
        up = [
            (u11 * c11 + u12 * c21) * inv,
            (u11 * c12 + u12 * c22) * inv,
            (u21 * c12 + u22 * c22) * inv,
        ]
        down = [
            (d11 * a11 + d12 * a21) * inv,
            (d11 * a12 + d12 * a22) * inv,
            (d21 * a12 + d22 * a22) * inv,
        ]
        p = p - (roll(up[0], step) + roll(down[0], -step))
        q = q - (roll(up[1], step) + roll(down[1], -step))
        r = r - (roll(up[2], step) + roll(down[2], -step))
        if 2 * step < half:
            n11, n12 = -(d11 * c11 + d12 * c21) * inv, -(d11 * c12 + d12 * c22) * inv
            n21, n22 = -(d21 * c11 + d22 * c21) * inv, -(d21 * c12 + d22 * c22) * inv
            c11, c12 = roll(n11, -step), roll(n12, -step)
            c21, c22 = roll(n21, -step), roll(n22, -step)
            a11, a12 = roll(n11, step), roll(n21, step)
            a21, a22 = roll(n12, step), roll(n22, step)
        step *= 2
    return levels, (1.0 / (p * r - q * q), p, q, r)


def substitute(factors, e, o):
    levels, (inv, p, q, r) = factors
    for step, scale, u11, u12, u21, u22, d11, d12, d21, d22 in levels:
        e, o = (
            e - (roll((u11 * e + u12 * o) * scale, step) + roll((d11 * e + d12 * o) * scale, -step)),
            o - (roll((u21 * e + u22 * o) * scale, step) + roll((d21 * e + d22 * o) * scale, -step)),
        )
    return (r * e - q * o) * inv, (p * o - q * e) * inv


def right_side(fe, fo, he, ho, ue, uo):
    return fe + 2.0 * he * ue * ue * ue, fo + 2.0 * ho * uo * uo * uo


def halves(x):
    valid = lane_of((1, LANES)) < LANES // 2
    return jnp.where(valid, x, 0.0), jnp.where(valid, roll(x, LANES // 2), 0.0)


def ring(by, count):
    return min(by, count - by)


def pack_plane(packed, cells, s):
    slot = lane_of((8, LANES)) // 4
    new = []
    for v in range(VARS):
        have = packed[v]
        for t in range(2):
            k = 2 * s + t
            have = jnp.where(slot == k, roll(cells[v][t], 4 * k + 2), have)
        new.append(have)
    return tuple(new)


def edge_terms(normal, n_norm, own, left, right, jac, corr):
    lane = lane_of((8, LANES))
    place = lane % 4
    ends, smooths = [], []
    for v in range(VARS):
        mine = own[v]
        mirror = jnp.where(place == 0, roll(mine, -3), roll(mine, -1))
        low = jnp.where(normal == 0, mirror, left[v])
        high = jnp.where(normal == n_norm - 1, 0.0, right[v])
        delta = jnp.where(place < 2, roll(high - mine, -2), roll(low - mine, 2))
        near = jnp.where(place == 1, roll(delta, 1), jnp.where(place == 2, roll(delta, -1), 0.0))
        end = delta - 8.0 * near
        ends.append(jnp.where(place < 2, -end, end))
        smooths.append(delta - 4.0 * near)
    for u in range(VARS):
        total = -DISSIPATION * smooths[u]
        for v in range(VARS):
            total = total + jac[50 + 5 * u + v] * ends[v]
        corr[u] = total


def plane_rates(field, s, jac):
    cells, grads, smooths = [], [[], [], []], []
    for v in range(VARS):

        def at(ds, dw):
            return field[v, s + (2 + ds), TOP + dw : TOP + dw + WRAP, :]

        c = at(0, 0)
        reads = [
            [at(k, 0) for k in (-2, -1, 1, 2)],
            [at(0, k) for k in (-2, -1, 1, 2)],
            [roll(c, -k) for k in (-2, -1, 1, 2)],
        ]
        near, far = None, None
        for d, (m2, m1, p1, p2) in enumerate(reads):
            grads[d].append(((m2 - p2) + 8.0 * (p1 - m1)).reshape(2, 8, LANES))
            near = (m1 + p1) if near is None else near + (m1 + p1)
            far = (m2 + p2) if far is None else far + (m2 + p2)
        smooths.append((-DISSIPATION * (far - 4.0 * near + 18.0 * c)).reshape(2, 8, LANES))
        cells.append(c.reshape(2, 8, LANES))
    rates = []
    for u in range(VARS):
        total = smooths[u]
        for d in range(3):
            for v in range(VARS):
                total = total + jac[25 * d + 5 * u + v][None] * grads[d][v]
        rates.append(total)
    return cells, rates


def in_pairs(plane):
    return lambda i, carry: plane(2 * i + 1, plane(2 * i, carry))


def ghost_rates(direction, low, first, second, jac, shape):
    outer, inner = [], []
    for v in range(VARS):
        a, b = first(v), second(v)
        if low:
            outer.append((a - 8.0 * b, a - 4.0 * b))
            inner.append((b, b))
        else:
            outer.append((8.0 * a - b, b - 4.0 * a))
            inner.append((-a, a))
    fixes = []
    for layer in (outer, inner):
        grads = [g.reshape(shape) for g, _ in layer]
        layer_fixes = []
        for u in range(VARS):
            total = -DISSIPATION * layer[u][1].reshape(shape)
            for v in range(VARS):
                total = total + jac[25 * direction + 5 * u + v][None] * grads[v]
            layer_fixes.append(total)
        fixes.append(layer_fixes)
    return fixes


def add_ghosts(span, n_span, planes, rows, corr, jac, volume, factor_of, at_plane, at_row, at_cells, done):
    for low in (True, False):
        gone = span == (0 if low else n_span - 1)
        side = 0 if low else 1

        def ghost(layer):
            return lambda v: jnp.where(gone, 0.0, planes[side, v, layer])

        fixes = ghost_rates(0, low, ghost(0), ghost(1), jac, (2, 8, LANES))
        for s, fix in zip((0, 1) if low else (SPAN - 1, SPAN - 2), fixes):
            scale = factor_of * volume[s]
            for u in range(VARS):
                at_plane(u, s, scale * fix[u].reshape(WRAP, LANES))
    for low in (True, False):
        side = 1 if low else 0

        def ghost(layer):
            return lambda v: rows[side, v, layer]

        fixes = ghost_rates(1, low, ghost(0), ghost(1), jac, (1, 8, LANES))
        for r, fix in zip((0, 1) if low else (WRAP - 1, WRAP - 2), fixes):
            scale = factor_of * volume[:, r, :]
            for u in range(VARS):
                at_row(u, r, scale * fix[u].reshape(8, LANES))
    lane = lane_of((8, LANES))
    edge = (lane < 2) | (lane >= LANES - 2)

    def columns(s, carry):
        scale = factor_of * volume[s].reshape(2, 8, LANES)
        cells = []
        for u in range(VARS):
            ends = corr[u]
            fix = [
                jnp.where(edge, roll(ends, (2 * LANES - 2 - 4 * (2 * s + t)) % LANES), 0.0)
                for t in range(2)
            ]
            cells.append(at_cells(u, s, scale * jnp.stack(fix)))
        return done(carry, cells, s)

    return columns


def pack_wall(field, volume, packed):
    group = lane_of((8, LANES)) // 8
    for v in range(VARS + 1):
        for t in range(2):
            have = jnp.zeros((8, LANES), jnp.float32)
            for s in range(SPAN):
                if v < VARS:
                    tile = field[v, s + 2, TOP + 8 * t : TOP + 8 * t + 8, :]
                else:
                    tile = volume[s, 8 * t : 8 * t + 8, :]
                have = jnp.where(group == s + 4, roll(tile, 8 * (s + 4) + 2), have)
            packed[v, 8 * t : 8 * t + 8, :] = mirrored(have)


def pair_wall(packed, pairs, edge, tip):
    lane, row = lane_of((8, LANES)), lax.broadcasted_iota(jnp.int32, (8, LANES), 0)
    own = (lane >= LANES // 4) & (lane < 3 * LANES // 4)
    for p in range(3):
        for t in range(2):
            rows = slice(8 * t, 8 * t + 8)
            pairs[p, rows, :] = jnp.where(own, packed[p, rows, :], roll(packed[p + 3, rows, :], 64))
    for t in range(2):
        a, b, c = (pairs[p, 8 * t : 8 * t + 8, :] for p in range(3))
        four = row < 4
        edge[t, 0] = jnp.where(four, a if t == 0 else pltpu.roll(a, 4, 0), b if t else pltpu.roll(b, 4, 0))
        edge[t, 1] = c
        at = 6 * t
        tip[t] = jnp.where(
            row < 2,
            turn_rows(a, -at),
            jnp.where(four, turn_rows(b, 2 - at), turn_rows(c, 4 - at)),
        )


def turn_rows(x, by):
    return pltpu.roll(x, by % 8, 0) if by % 8 else x


def mirrored(x):
    place = lane_of(x.shape) % 8
    return jnp.where(place == 0, roll(x, -3), jnp.where(place == 1, roll(x, -1), x))


def wall_rates(layer, top, rows, wanted, jac, at_wall):
    cells, grads, smooths = [], [[], [], []], []
    shape = (rows // 8, 8, LANES)
    for v in range(VARS):
        c = layer[v, top : top + rows, :]
        reads = [
            [roll(c, -8 * k) for k in (-2, -1, 1, 2)],
            [layer[v, top + k : top + k + rows, :] for k in (-2, -1, 1, 2)],
        ]
        if at_wall:
            p1, p2 = roll(c, -1), roll(c, -2)
            reads.append([p1, c, p1, p2])
        else:
            reads.append([roll(c, -k) for k in (-2, -1, 1, 2)])
        near, far = None, None
        for d, (m2, m1, p1, p2) in enumerate(reads):
            grads[d].append(((m2 - p2) + 8.0 * (p1 - m1)).reshape(shape))
            near = (m1 + p1) if near is None else near + (m1 + p1)
            far = (m2 + p2) if far is None else far + (m2 + p2)
        smooths.append((-DISSIPATION * (far - 4.0 * near + 18.0 * c)).reshape(shape))
        cells.append(c)
    rates = []
    for u in range(wanted):
        total = smooths[u]
        for d in range(3):
            for v in range(VARS):
                total = total + jac[25 * d + 5 * u + v][None] * grads[d][v]
        rates.append(total.reshape(rows, LANES))
    return cells, rates


def wall_loads(span, n_span, packed, beside, edges, tips, layer, mid, faces, jac):
    group = lane_of((8, LANES)) // 8
    first, last = span == 0, span == n_span - 1

    def swing(x, when):
        return roll(x, LANES // 2) if when else x

    for v in range(VARS + 1):
        p, upper = v % 3, v >= 3
        low_edge = edges[0, 1] if p == 2 else turn_rows(edges[0, 0], 4 - 4 * p)
        high_edge = edges[1, 1] if p == 2 else turn_rows(edges[1, 0], 4 * p)
        tiles = [
            (turn_rows(tips[0], 6 - 2 * p), swing(low_edge, upper), turn_rows(tips[1], 6 - 2 * p)),
            (beside[0, p, 0:8], packed[v, 0:8], beside[1, p, 0:8]),
            (beside[0, p, 8:16], packed[v, 8:16], beside[1, p, 8:16]),
            (turn_rows(tips[2], -2 * p), swing(high_edge, upper), turn_rows(tips[3], -2 * p)),
        ]
        for t, (left, centre, right) in enumerate(tiles):
            left = jnp.where(first, 0.0, swing(left, not upper))
            right = jnp.where(last, 0.0, swing(right, not upper))
            whole = jnp.where(group < 4, left, jnp.where(group >= 12, right, centre))
            layer[v, 8 * t : 8 * t + 8, :] = whole
    span_group = lane_of((24, LANES)) // 8
    outside = (first & (span_group < 4)) | (last & (span_group >= 12))
    cells, rates = wall_rates(layer, 4, 24, VARS, jac, False)
    scale = DT_FLOW * layer[VARS, 4:28, :]
    for u in range(VARS):
        mid[u] = jnp.where(outside, 0.0, cells[u] + scale * rates[u])
    cells, rates = wall_rates(mid, 4, 16, 1, jac, True)
    scale = DT_FLOW * layer[VARS, 8:24, :]
    after = 0.5 * (layer[0, 8:24, :] + cells[0] + scale * rates[0])
    total = jnp.zeros((WRAP, LANES), jnp.float32)
    for s in range(SPAN):
        at = 8 * (s + 4) + 2
        total = total + faces[s] * jnp.broadcast_to(after[:, at : at + 1], (WRAP, LANES))
    return jnp.sum(total, axis=0, keepdims=True)


def kernel(
    n_span,
    n_wrap,
    n_norm,
    flow_hbm,
    volume_hbm,
    jac_hbm,
    area_hbm,
    map_hbm,
    contact_hbm,
    bending_hbm,
    mass_hbm,
    hardening_hbm,
    disp_hbm,
    vel_hbm,
    result,
    defl_ref,
    field1,
    field2,
    planes,
    volume,
    wall_send,
    wall_recv,
    edges,
    corr,
    jac,
    faces,
    area,
    stations,
    contact_v,
    beam_v,
    jac_held,
    beam_held,
    loads_a,
    loads_b,
    tally,
    wall_packed,
    wall_pairs,
    wall_beside,
    edge_put,
    edge_got,
    tip_put,
    tip_got,
    wall_layer,
    wall_mid,
    local_sem,
    send_sem,
    recv_sem,
    group_sem,
    wide_send_sem,
    wide_recv_sem,
):
    span, wrap, normal = lax.axis_index("span"), lax.axis_index("wrap"), lax.axis_index("normal")
    rows = 2
    cols = n_span // rows
    row, col = lax.div(span, cols), lax.rem(span, cols)
    zs, cores = cols // 2, 2
    z, core = lax.div(col, cores), lax.rem(col, cores)
    y_own = row * n_wrap + wrap

    inputs = [
        (flow_hbm, field1.at[:, 2 : 2 + SPAN, TOP : TOP + WRAP, :]),
        (volume_hbm, volume),
        (area_hbm, area),
        (map_hbm, stations),
        (contact_hbm, contact_v),
        (bending_hbm, beam_v.at[0]),
        (mass_hbm, beam_v.at[1]),
        (hardening_hbm, beam_v.at[2]),
        (disp_hbm, beam_v.at[3]),
        (vel_hbm, beam_v.at[4]),
        (jac_hbm, jac_held),
    ]
    reads = [pltpu.make_async_copy(a, b, local_sem.at[i]) for i, (a, b) in enumerate(inputs)]
    for read in reads[:2]:
        read.start()

    def turned(index, by, count):
        return lax.rem(index + (by + count), count)

    span_at = {by: turned(span, by, n_span) for by in (-1, 1)}
    wrap_at = [turned(wrap, by, n_wrap) for by in range(n_wrap)]
    norm_at = {by: turned(normal, by, n_norm) for by in (-1, 1)}
    row_at = [turned(row, by, rows) for by in range(rows)]
    z_at = [turned(z, by, zs) for by in range(zs)]
    core_at = [core, turned(core, 1, cores)]
    sides = [
        (span_at[-1], wrap, normal),
        (span_at[1], wrap, normal),
        (span, wrap_at[n_wrap - 1], normal),
        (span, wrap_at[1], normal),
        (span, wrap, norm_at[-1]),
        (span, wrap, norm_at[1]),
    ]
    barrier = pltpu.get_barrier_semaphore()

    def greet(target):
        pl.semaphore_signal(barrier, inc=1, device_id=target, device_id_type=MESH)

    corners = [(span_at[i], wrap_at[j], normal) for j in (n_wrap - 1, 1) for i in (-1, 1)]

    def device(y, z, core, x):
        return (y[0] * cols + z * cores + core, y[1], x)

    here = (row, wrap)
    y_at = [(row_at[a], wrap_at[b]) for a in range(rows) for b in range(n_wrap)]
    y_far = sorted(range(1, rows * n_wrap), key=lambda k: -ring(2 * (k % n_wrap) + k // n_wrap, 2 * n_wrap))
    z_far = sorted(range(1, zs), key=lambda k: -ring(k, zs))
    beside_y = (1, n_wrap - 1)

    @pl.when(normal == 0)
    def _():
        for k in z_far:
            for c in range(cores):
                greet(device(here, z_at[k], core_at[c], 0))
        for k in y_far:
            if k not in beside_y:
                greet(device(y_at[k], z, core, 0))
        for one in corners:
            greet(one)

    @pl.when(normal != 0)
    def _():
        for k in y_far + [0]:
            greet(device(y_at[k], z, core, 0))

    for side in sides:
        greet(side)

    for read in reads[2:]:
        read.start()

    def copy(src, dst, slot, target):
        return pltpu.make_async_remote_copy(
            src_ref=src,
            dst_ref=dst,
            send_sem=send_sem.at[slot],
            recv_sem=recv_sem.at[slot],
            device_id=target,
            device_id_type=MESH,
        )

    def stage_copies(stage, field):
        cells = pl.ds(TOP, WRAP)
        base = 6 * stage
        pairs = [
            (field.at[:, 2:4, cells, :], planes.at[stage, 1]),
            (field.at[:, SPAN : 2 + SPAN, cells, :], planes.at[stage, 0]),
            (wall_send.at[stage, 0], wall_recv.at[stage, 0]),
            (wall_send.at[stage, 1], wall_recv.at[stage, 1]),
            (edges.at[stage, 0], edges.at[stage, 2]),
            (edges.at[stage, 0], edges.at[stage, 1]),
        ]
        return [copy(src, dst, base + i, sides[i]) for i, (src, dst) in enumerate(pairs)]

    def stage_wrap_rows(stage, field):
        for v in range(VARS):
            for r in range(2):
                wall_send[stage, 0, v, r] = field[v, 2 : 2 + SPAN, TOP + r, :]
                wall_send[stage, 1, v, r] = field[v, 2 : 2 + SPAN, TOP + WRAP - 2 + r, :]

    def stage_columns(stage):
        edge_terms(
            normal, n_norm, edges.at[stage, 0], edges.at[stage, 1], edges.at[stage, 2], jac, corr
        )

    for field in (field1, field2):
        for s in (0, 1, 2 + SPAN, 3 + SPAN):
            field[:, s, TOP : TOP + WRAP, :] = jnp.zeros((VARS, WRAP, LANES), jnp.float32)
        for r in (0, TOP + WRAP):
            field[:, 2 : 2 + SPAN, r : r + 8, :] = jnp.zeros((VARS, SPAN, 8, LANES), jnp.float32)

    wide = []
    for i, (src, dst, target) in enumerate(
        [
            (tip_put.at[0], tip_got.at[3], corners[0]),
            (tip_put.at[0], tip_got.at[2], corners[1]),
            (tip_put.at[1], tip_got.at[1], corners[2]),
            (tip_put.at[1], tip_got.at[0], corners[3]),
            (edge_put.at[0], edge_got.at[1], sides[2]),
            (edge_put.at[1], edge_got.at[0], sides[3]),
            (wall_pairs, wall_beside.at[1], sides[0]),
            (wall_pairs, wall_beside.at[0], sides[1]),
        ]
    ):
        wide.append(
            pltpu.make_async_remote_copy(
                src_ref=src,
                dst_ref=dst,
                send_sem=wide_send_sem.at[i],
                recv_sem=wide_recv_sem.at[i],
                device_id=target,
                device_id_type=MESH,
            )
        )

    empty = tuple(jnp.zeros((8, LANES), jnp.float32) for _ in range(VARS))

    reads[0].wait()
    reads[1].wait()

    @pl.when(normal == 0)
    def _():
        pack_wall(field1, volume, wall_packed)
        pair_wall(wall_packed, wall_pairs, edge_put, tip_put)

    stage_wrap_rows(0, field1)

    def pack_first(s, packed):
        cells = [
            field1[v, s + 2, TOP : TOP + WRAP, :].reshape(2, 8, LANES) for v in range(VARS)
        ]
        return pack_plane(packed, cells, s)

    packed = lax.fori_loop(0, SPAN, pack_first, empty, unroll=True)
    for v in range(VARS):
        edges[0, 0, v] = packed[v]

    lane = lane_of((8, LANES))
    held = jnp.where(lane < LANES // 2, 2 * lane, 2 * lane - (LANES - 1))

    def prepare():
        for read in reads[2:]:
            read.wait()
        for d in range(3):
            for u in range(VARS):
                for v in range(VARS):
                    scaled = jac_held[u, d, v] * (-1.0 / 12.0)
                    jac[25 * d + 5 * u + v] = jnp.full((8, LANES), scaled, jnp.float32)

    def prepare_beam():
        def permuted(x):
            full = jnp.broadcast_to(x, (8, LANES))
            return jnp.take_along_axis(full, held, axis=1)[0:1]

        bending, mass, hardening, disp, vel = [permuted(beam_v[i]) for i in range(5)]
        contact = permuted(contact_v[...])
        inertia = 2.0 * mass / (DT_BEAM * DT_BEAM)
        pull = CONTACT_STIFF * STOP_GAP
        push = jnp.where(contact == 1, pull, jnp.where(contact == 2, -pull, 0.0))
        steady = inertia * (disp + DT_BEAM * vel) + push
        base = inertia + jnp.where(contact > 0, CONTACT_STIFF, 0.0)
        be, bo = halves(bending)
        he, ho = halves(hardening)
        ge, go = halves(base)
        ue, uo = halves(disp)
        fe, fo = halves(steady)
        factors = factor(be, bo, ge + 3.0 * he * ue * ue, go + 3.0 * ho * uo * uo)
        levels, last = factors
        kept = [x for level in levels for x in level[1:]] + list(last)
        kept += [be, bo, ge, go, he, ho, ue, uo, fe, fo]
        for i, x in enumerate(kept):
            beam_held[i] = x

    @pl.when(normal == 0)
    def _():
        prepare()
        prepare_beam()
        row_id = lax.broadcasted_iota(jnp.int32, (WRAP, WRAP), 0)
        same = (row_id == lane_of((WRAP, WRAP))).astype(jnp.float32)

        def turned_over(x):
            return lax.dot_general(
                same, x, (((1,), (1,)), ((), ())), precision=lax.Precision.HIGHEST
            )

        weights = turned_over(area[...])
        places = turned_over(stations[...].astype(jnp.float32))
        aims = jnp.broadcast_to(held[0:1], (WRAP, LANES)).astype(jnp.float32)
        for s in range(SPAN):
            weight = jnp.broadcast_to(weights[:, s : s + 1], (WRAP, LANES))
            place = jnp.broadcast_to(places[:, s : s + 1], (WRAP, LANES))
            faces[s] = jnp.where(place == aims, weight, 0.0)

    at_wall = lax.div(n_norm - normal, n_norm)
    wall_peers = 4 + cores * (zs - 1) + (len(y_at) * n_norm - 1 - len(set(beside_y)))
    pl.semaphore_wait(barrier, 6 + at_wall * wall_peers)

    @pl.when(normal == 0)
    def _():
        for one in wide:
            one.start()

    first = stage_copies(0, field1)

    @pl.when(normal != 0)
    def _():
        for one in first:
            one.start()
        prepare()


    def group_copy(buffer, own, which, target):
        return pltpu.make_async_remote_copy(
            src_ref=buffer.at[own],
            dst_ref=buffer.at[own],
            send_sem=group_sem.at[2 * which],
            recv_sem=group_sem.at[2 * which + 1],
            device_id=target,
            device_id_type=MESH,
        )

    def added(ref):
        terms = [ref[i] for i in range(ref.shape[0])]
        while len(terms) > 1:
            terms = [sum(terms[i + 1 : i + 2], terms[i]) for i in range(0, len(terms), 2)]
        return terms[0]

    def take(ref, which):
        pltpu.make_async_copy(ref, ref, group_sem.at[which]).wait()

    def first_plane(s, carry):
        cells, rates = plane_rates(field1, s, jac)
        scale = DT_FLOW * volume[s].reshape(2, 8, LANES)
        for u in range(VARS):
            mid = cells[u] + scale * rates[u]
            field2[u, s + 2, TOP : TOP + WRAP, :] = mid.reshape(WRAP, LANES)
        return carry

    lax.fori_loop(0, SPAN // 2, in_pairs(first_plane), 0)

    @pl.when(normal == 0)
    def _():
        for one in first:
            one.start()
        for one in wide:
            one.wait_recv()
        loads_a[col] = wall_loads(
            span,
            n_span,
            wall_packed,
            wall_beside,
            edge_got,
            tip_got,
            wall_layer,
            wall_mid,
            faces,
            jac,
        )
        for k in z_far + [0]:
            for c in range(cores):
                if k or c:
                    group_copy(loads_a, col, 0, device(here, z_at[k], core_at[c], 0)).start()

    for one in first:
        one.wait_recv()
    stage_columns(0)

    def mid_plane(u, s, part):
        field2[u, s + 2, TOP : TOP + WRAP, :] += part

    def mid_row(u, r, part):
        field2[u, 2 : 2 + SPAN, TOP + r, :] += part

    def mid_cells(u, s, part):
        cells = field2[u, s + 2, TOP : TOP + WRAP, :].reshape(2, 8, LANES) + part
        field2[u, s + 2, TOP : TOP + WRAP, :] = cells.reshape(WRAP, LANES)
        return cells

    columns = add_ghosts(
        span,
        n_span,
        planes.at[0],
        wall_recv.at[0],
        corr,
        jac,
        volume,
        DT_FLOW,
        mid_plane,
        mid_row,
        mid_cells,
        pack_plane,
    )
    packed = lax.fori_loop(0, SPAN, lambda s, packed: columns(s, packed), empty, unroll=True)
    for v in range(VARS):
        edges[1, 0, v] = packed[v]

    stage_wrap_rows(1, field2)
    second = stage_copies(1, field2)
    for one in second:
        one.start()


    @pl.when(normal != 0)
    def _():
        prepare_beam()

    for one in first:
        one.wait_send()

    @pl.when(normal == 0)
    def _():
        for one in wide:
            one.wait_send()
        take(loads_a.at[1:], 1)
        loads_b[y_own] = added(loads_a)
        for x in sorted(range(n_norm), key=lambda x: -ring(x, n_norm)):
            for k in y_far + [0]:
                if x or k:
                    group_copy(loads_b, y_own, 1, device(y_at[k], z, core, x)).start()

    def second_plane(s, carry):
        cells, rates = plane_rates(field2, s, jac)
        scale = DT_FLOW * volume[s].reshape(2, 8, LANES)
        for u in range(VARS):
            start = field1[u, s + 2, TOP : TOP + WRAP, :].reshape(2, 8, LANES)
            after = 0.5 * (start + cells[u] + scale * rates[u])
            result[u, s] = after.reshape(WRAP, LANES)
        return carry

    lax.fori_loop(0, SPAN // 2, in_pairs(second_plane), 0)

    for one in second:
        one.wait_recv()
    stage_columns(1)

    def end_plane(u, s, part):
        result[u, s] += part

    def end_row(u, r, part):
        result[u, :, r, :] += part

    def end_cells(u, s, part):
        result[u, s] += part.reshape(WRAP, LANES)

    columns = add_ghosts(
        span,
        n_span,
        planes.at[1],
        wall_recv.at[1],
        corr,
        jac,
        volume,
        0.5 * DT_FLOW,
        end_plane,
        end_row,
        end_cells,
        lambda carry, cells, s: carry,
    )
    lax.fori_loop(0, SPAN, columns, 0, unroll=True)

    for one in second:
        one.wait_send()

    @pl.when(normal == 0)
    def _():
        take(loads_a.at[1:], 0)
        take(tally, 2)

    @pl.when(normal == 0)
    def _():
        take(loads_b.at[1:], 3)

    @pl.when(normal != 0)
    def _():
        take(loads_b, 3)

    loads = added(loads_b)
    kept = [beam_held[i] for i in range(9 * LEVELS + 14)]
    levels = [(2**i, *kept[9 * i : 9 * i + 9]) for i in range(LEVELS)]
    factors = (levels, tuple(kept[9 * LEVELS : 9 * LEVELS + 4]))
    be, bo, ge, go, he, ho, ue, uo, fe, fo = kept[9 * LEVELS + 4 :]
    le, lo = halves(loads)
    fe, fo = fe + le, fo + lo
    for newton_step in range(NEWTON):
        if newton_step:
            factors = factor(be, bo, ge + 3.0 * he * ue * ue, go + 3.0 * ho * uo * uo)
        ue, uo = substitute(factors, *right_side(fe, fo, he, ho, ue, uo))
    both = jnp.where(lane_of((1, LANES)) < LANES // 2, ue, roll(uo, LANES // 2))
    back = (lane % 2) * (LANES // 2) + lane // 2
    full = jnp.broadcast_to(both, (8, LANES))
    defl_ref[...] = jnp.take_along_axis(full, back, axis=1)[0:1]


def hand_out(flow_ref, defl_ref, flow_out, defl_out, sem):
    copies = [
        pltpu.make_async_copy(flow_ref, flow_out, sem.at[0]),
        pltpu.make_async_copy(defl_ref, defl_out, sem.at[1]),
    ]
    for one in copies:
        one.start()
    for one in copies:
        one.wait()


def solution(mesh):
    n_span, n_wrap, n_norm = (mesh.shape[axis] for axis in ("span", "wrap", "normal"))
    zs, ys = n_span // 4, 2 * n_wrap
    f32 = jnp.float32

    def step(
        flow_state,
        inv_volume,
        flux_jacobians,
        area,
        station_map,
        contact,
        bending,
        mass,
        hardening,
        disp_old,
        vel_old,
    ):
        vectors = [
            x.reshape(1, STATIONS) for x in (contact, bending, mass, hardening, disp_old, vel_old)
        ]
        hbm, vmem = (pl.BlockSpec(memory_space=space) for space in (pltpu.HBM, pltpu.VMEM))
        operands = [flow_state, inv_volume, flux_jacobians.transpose(1, 0, 2), area, station_map]
        operands = [pltpu.with_memory_space_constraint(x, pltpu.HBM) for x in operands + vectors]
        flow_next, deflection = pl.pallas_call(
            functools.partial(kernel, n_span, n_wrap, n_norm),
            out_shape=(
                pltpu.VMEM(flow_state.shape, f32),
                pltpu.VMEM((1, STATIONS), f32),
            ),
            in_specs=[hbm] * len(operands),
            out_specs=(vmem, vmem),
            scratch_shapes=[
                pltpu.VMEM((VARS, SPAN + 4, WRAP + 16, LANES), f32),
                pltpu.VMEM((VARS, SPAN + 4, WRAP + 16, LANES), f32),
                pltpu.VMEM((2, 2, VARS, 2, WRAP, LANES), f32),
                pltpu.VMEM((SPAN, WRAP, LANES), f32),
                pltpu.VMEM((2, 2, VARS, 2, SPAN, LANES), f32),
                pltpu.VMEM((2, 2, VARS, 2, SPAN, LANES), f32),
                pltpu.VMEM((2, 3, VARS, 8, LANES), f32),
                pltpu.VMEM((VARS, 8, LANES), f32),
                pltpu.VMEM((75, 8, LANES), f32),
                pltpu.VMEM((SPAN, WRAP, LANES), f32),
                pltpu.VMEM((SPAN, WRAP), f32),
                pltpu.VMEM((SPAN, WRAP), jnp.int32),
                pltpu.VMEM((1, STATIONS), jnp.int32),
                pltpu.VMEM((5, 1, STATIONS), f32),
                pltpu.SMEM((VARS, 3, VARS), f32),
                pltpu.VMEM((9 * LEVELS + 14, 1, LANES), f32),
                pltpu.VMEM((2 * zs, 1, LANES), f32),
                pltpu.VMEM((ys, 1, LANES), f32),
                pltpu.VMEM((ys * n_norm - 1, 1, LANES), f32),
                pltpu.VMEM((VARS + 1, WRAP, LANES), f32),
                pltpu.VMEM((3, WRAP, LANES), f32),
                pltpu.VMEM((2, 3, WRAP, LANES), f32),
                pltpu.VMEM((2, 2, 8, LANES), f32),
                pltpu.VMEM((2, 2, 8, LANES), f32),
                pltpu.VMEM((2, 8, LANES), f32),
                pltpu.VMEM((4, 8, LANES), f32),
                pltpu.VMEM((VARS + 1, WRAP + 16, LANES), f32),
                pltpu.VMEM((VARS, 24, LANES), f32),
                pltpu.SemaphoreType.DMA((11,)),
                pltpu.SemaphoreType.DMA((12,)),
                pltpu.SemaphoreType.DMA((12,)),
                pltpu.SemaphoreType.DMA((4,)),
                pltpu.SemaphoreType.DMA((8,)),
                pltpu.SemaphoreType.DMA((8,)),
            ],
            compiler_params=pltpu.CompilerParams(
                collective_id=0, has_side_effects=True, vmem_limit_bytes=32 * 1024 * 1024
            ),
            cost_estimate=pl.CostEstimate(
                flops=10_000_000, bytes_accessed=1_000_000, transcendentals=0
            ),
        )(*operands)
        flow_next, deflection = pl.pallas_call(
            hand_out,
            out_shape=(
                jax.ShapeDtypeStruct(flow_state.shape, f32),
                jax.ShapeDtypeStruct((1, STATIONS), f32),
            ),
            in_specs=(vmem, vmem),
            out_specs=(hbm, hbm),
            scratch_shapes=[pltpu.SemaphoreType.DMA((2,))],
        )(
            pltpu.with_memory_space_constraint(flow_next, pltpu.VMEM),
            pltpu.with_memory_space_constraint(deflection, pltpu.VMEM),
        )
        return flow_next, deflection.reshape(STATIONS)

    placed = (
        P(None, "span", "wrap", "normal"),
        P("span", "wrap", "normal"),
        P(),
        P("span", "wrap"),
        P("span", "wrap"),
    ) + (P(),) * 6
    return jax.shard_map(
        step,
        mesh=mesh,
        in_specs=placed,
        out_specs=(P(None, "span", "wrap", "normal"), P()),
        check_vma=False,
    )
```

```python
import functools

import jax
import jax.numpy as jnp
from jax import lax
from jax.experimental import pallas as pl
from jax.experimental.pallas import tpu as pltpu
from jax.sharding import PartitionSpec as P

MESH = pl.DeviceIdType.MESH
VARS = 5
STATIONS = 128
NEWTON = 3
LEVELS = 6
DT_FLOW = 0.2
DISSIPATION = 0.03
DT_BEAM = 0.2
STOP_GAP = 0.5
CONTACT_STIFF = 40.0
SPAN, WRAP, LANES = 8, 16, 128
TOP = 8


def lane_of(shape):
    return lax.broadcasted_iota(jnp.int32, shape, len(shape) - 1)


def roll(x, shift):
    return pltpu.roll(x, shift % LANES if isinstance(shift, int) else shift, 1)


def factor(be, bo, diag_e, diag_o):
    lane = lane_of((1, LANES))
    half = LANES // 2
    valid, inner = lane < half, lane < half - 1
    bo_prev, be_next = roll(bo, 1), roll(be, -1)
    p = jnp.where(valid, 4.0 * be + bo_prev + bo + diag_e, 1.0)
    q = jnp.where(valid, -2.0 * (be + bo), 0.0)
    r = jnp.where(valid, 4.0 * bo + be + be_next + diag_o, 1.0)
    c11 = jnp.where(inner, bo, 0.0)
    c12 = jnp.zeros_like(bo)
    c21 = jnp.where(inner, -2.0 * (bo + be_next), 0.0)
    c22 = jnp.where(inner, be_next, 0.0)
    a11, a12, a21, a22 = roll(c11, 1), roll(c21, 1), c12, roll(c22, 1)
    levels = []
    step = 1
    while step < half:
        inv = 1.0 / (p * r - q * q)
        u11, u12 = c11 * r - c21 * q, c21 * p - c11 * q
        u21, u22 = c12 * r - c22 * q, c22 * p - c12 * q
        d11, d12 = a11 * r - a21 * q, a21 * p - a11 * q
        d21, d22 = a12 * r - a22 * q, a22 * p - a12 * q
        levels.append((step, inv, u11, u12, u21, u22, d11, d12, d21, d22))
        up = [
            (u11 * c11 + u12 * c21) * inv,
            (u11 * c12 + u12 * c22) * inv,
            (u21 * c12 + u22 * c22) * inv,
        ]
        down = [
            (d11 * a11 + d12 * a21) * inv,
            (d11 * a12 + d12 * a22) * inv,
            (d21 * a12 + d22 * a22) * inv,
        ]
        p = p - (roll(up[0], step) + roll(down[0], -step))
        q = q - (roll(up[1], step) + roll(down[1], -step))
        r = r - (roll(up[2], step) + roll(down[2], -step))
        if 2 * step < half:
            n11, n12 = -(d11 * c11 + d12 * c21) * inv, -(d11 * c12 + d12 * c22) * inv
            n21, n22 = -(d21 * c11 + d22 * c21) * inv, -(d21 * c12 + d22 * c22) * inv
            c11, c12 = roll(n11, -step), roll(n12, -step)
            c21, c22 = roll(n21, -step), roll(n22, -step)
            a11, a12 = roll(n11, step), roll(n21, step)
            a21, a22 = roll(n12, step), roll(n22, step)
        step *= 2
    return levels, (1.0 / (p * r - q * q), p, q, r)


def substitute(factors, e, o):
    levels, (inv, p, q, r) = factors
    for step, scale, u11, u12, u21, u22, d11, d12, d21, d22 in levels:
        e, o = (
            e - (roll((u11 * e + u12 * o) * scale, step) + roll((d11 * e + d12 * o) * scale, -step)),
            o - (roll((u21 * e + u22 * o) * scale, step) + roll((d21 * e + d22 * o) * scale, -step)),
        )
    return (r * e - q * o) * inv, (p * o - q * e) * inv


def right_side(fe, fo, he, ho, ue, uo):
    return fe + 2.0 * he * ue * ue * ue, fo + 2.0 * ho * uo * uo * uo


def halves(x):
    valid = lane_of((1, LANES)) < LANES // 2
    return jnp.where(valid, x, 0.0), jnp.where(valid, roll(x, LANES // 2), 0.0)


def ring(by, count):
    return min(by, count - by)


def pack_plane(packed, cells, s):
    slot = lane_of((8, LANES)) // 4
    new = []
    for v in range(VARS):
        have = packed[v]
        for t in range(2):
            k = 2 * s + t
            have = jnp.where(slot == k, roll(cells[v][t], 4 * k + 2), have)
        new.append(have)
    return tuple(new)


def edge_terms(normal, n_norm, own, left, right, jac, corr):
    lane = lane_of((8, LANES))
    place = lane % 4
    ends, smooths = [], []
    for v in range(VARS):
        mine = own[v]
        mirror = jnp.where(place == 0, roll(mine, -3), roll(mine, -1))
        low = jnp.where(normal == 0, mirror, left[v])
        high = jnp.where(normal == n_norm - 1, 0.0, right[v])
        delta = jnp.where(place < 2, roll(high - mine, -2), roll(low - mine, 2))
        near = jnp.where(place == 1, roll(delta, 1), jnp.where(place == 2, roll(delta, -1), 0.0))
        end = delta - 8.0 * near
        ends.append(jnp.where(place < 2, -end, end))
        smooths.append(delta - 4.0 * near)
    for u in range(VARS):
        total = -DISSIPATION * smooths[u]
        for v in range(VARS):
            total = total + jac[50 + 5 * u + v] * ends[v]
        corr[u] = total


def plane_rates(field, s, jac):
    cells, grads, smooths = [], [[], [], []], []
    for v in range(VARS):

        def at(ds, dw):
            return field[v, s + (2 + ds), TOP + dw : TOP + dw + WRAP, :]

        c = at(0, 0)
        reads = [
            [at(k, 0) for k in (-2, -1, 1, 2)],
            [at(0, k) for k in (-2, -1, 1, 2)],
            [roll(c, -k) for k in (-2, -1, 1, 2)],
        ]
        near, far = None, None
        for d, (m2, m1, p1, p2) in enumerate(reads):
            grads[d].append(((m2 - p2) + 8.0 * (p1 - m1)).reshape(2, 8, LANES))
            near = (m1 + p1) if near is None else near + (m1 + p1)
            far = (m2 + p2) if far is None else far + (m2 + p2)
        smooths.append((-DISSIPATION * (far - 4.0 * near + 18.0 * c)).reshape(2, 8, LANES))
        cells.append(c.reshape(2, 8, LANES))
    rates = []
    for u in range(VARS):
        total = smooths[u]
        for d in range(3):
            for v in range(VARS):
                total = total + jac[25 * d + 5 * u + v][None] * grads[d][v]
        rates.append(total)
    return cells, rates


def in_fours(plane):
    def four(i, carry):
        for j in range(4):
            carry = plane(4 * i + j, carry)
        return carry

    return four


def ghost_rates(direction, low, first, second, jac, shape):
    outer, inner = [], []
    for v in range(VARS):
        a, b = first(v), second(v)
        if low:
            outer.append((a - 8.0 * b, a - 4.0 * b))
            inner.append((b, b))
        else:
            outer.append((8.0 * a - b, b - 4.0 * a))
            inner.append((-a, a))
    fixes = []
    for layer in (outer, inner):
        grads = [g.reshape(shape) for g, _ in layer]
        layer_fixes = []
        for u in range(VARS):
            total = -DISSIPATION * layer[u][1].reshape(shape)
            for v in range(VARS):
                total = total + jac[25 * direction + 5 * u + v][None] * grads[v]
            layer_fixes.append(total)
        fixes.append(layer_fixes)
    return fixes


def add_ghosts(span, n_span, planes, rows, corr, jac, volume, factor_of, at_plane, at_row, at_cells, done):
    for low in (True, False):
        gone = span == (0 if low else n_span - 1)
        side = 0 if low else 1

        def ghost(layer):
            return lambda v: jnp.where(gone, 0.0, planes[side, v, layer])

        fixes = ghost_rates(0, low, ghost(0), ghost(1), jac, (2, 8, LANES))
        for s, fix in zip((0, 1) if low else (SPAN - 1, SPAN - 2), fixes):
            scale = factor_of * volume[s]
            for u in range(VARS):
                at_plane(u, s, scale * fix[u].reshape(WRAP, LANES))
    for low in (True, False):
        side = 1 if low else 0

        def ghost(layer):
            return lambda v: rows[side, v, layer]

        fixes = ghost_rates(1, low, ghost(0), ghost(1), jac, (1, 8, LANES))
        for r, fix in zip((0, 1) if low else (WRAP - 1, WRAP - 2), fixes):
            scale = factor_of * volume[:, r, :]
            for u in range(VARS):
                at_row(u, r, scale * fix[u].reshape(8, LANES))
    lane = lane_of((8, LANES))
    edge = (lane < 2) | (lane >= LANES - 2)

    def columns(s, carry):
        scale = factor_of * volume[s].reshape(2, 8, LANES)
        cells = []
        for u in range(VARS):
            ends = corr[u]
            fix = [
                jnp.where(edge, roll(ends, (2 * LANES - 2 - 4 * (2 * s + t)) % LANES), 0.0)
                for t in range(2)
            ]
            cells.append(at_cells(u, s, scale * jnp.stack(fix)))
        return done(carry, cells, s)

    return columns


def pack_wall(field, volume, packed):
    group = lane_of((8, LANES)) // 8
    for v in range(VARS + 1):
        for t in range(2):
            have = jnp.zeros((8, LANES), jnp.float32)
            for s in range(SPAN):
                if v < VARS:
                    tile = field[v, s + 2, TOP + 8 * t : TOP + 8 * t + 8, :]
                else:
                    tile = volume[s, 8 * t : 8 * t + 8, :]
                have = jnp.where(group == s + 4, roll(tile, 8 * (s + 4) + 2), have)
            packed[v, 8 * t : 8 * t + 8, :] = mirrored(have)


def pair_wall(packed, pairs, edge, tip):
    lane, row = lane_of((8, LANES)), lax.broadcasted_iota(jnp.int32, (8, LANES), 0)
    own = (lane >= LANES // 4) & (lane < 3 * LANES // 4)
    for p in range(3):
        for t in range(2):
            rows = slice(8 * t, 8 * t + 8)
            pairs[p, rows, :] = jnp.where(own, packed[p, rows, :], roll(packed[p + 3, rows, :], 64))
    for t in range(2):
        a, b, c = (pairs[p, 8 * t : 8 * t + 8, :] for p in range(3))
        four = row < 4
        edge[t, 0] = jnp.where(four, a if t == 0 else pltpu.roll(a, 4, 0), b if t else pltpu.roll(b, 4, 0))
        edge[t, 1] = c
        at = 6 * t
        tip[t] = jnp.where(
            row < 2,
            turn_rows(a, -at),
            jnp.where(four, turn_rows(b, 2 - at), turn_rows(c, 4 - at)),
        )


def turn_rows(x, by):
    return pltpu.roll(x, by % 8, 0) if by % 8 else x


def mirrored(x):
    place = lane_of(x.shape) % 8
    return jnp.where(place == 0, roll(x, -3), jnp.where(place == 1, roll(x, -1), x))


def wall_rates(layer, top, rows, wanted, jac, at_wall):
    cells, grads, smooths = [], [[], [], []], []
    shape = (rows // 8, 8, LANES)
    for v in range(VARS):
        c = layer[v, top : top + rows, :]
        reads = [
            [roll(c, -8 * k) for k in (-2, -1, 1, 2)],
            [layer[v, top + k : top + k + rows, :] for k in (-2, -1, 1, 2)],
        ]
        if at_wall:
            p1, p2 = roll(c, -1), roll(c, -2)
            reads.append([p1, c, p1, p2])
        else:
            reads.append([roll(c, -k) for k in (-2, -1, 1, 2)])
        near, far = None, None
        for d, (m2, m1, p1, p2) in enumerate(reads):
            grads[d].append(((m2 - p2) + 8.0 * (p1 - m1)).reshape(shape))
            near = (m1 + p1) if near is None else near + (m1 + p1)
            far = (m2 + p2) if far is None else far + (m2 + p2)
        smooths.append((-DISSIPATION * (far - 4.0 * near + 18.0 * c)).reshape(shape))
        cells.append(c)
    rates = []
    for u in range(wanted):
        total = smooths[u]
        for d in range(3):
            for v in range(VARS):
                total = total + jac[25 * d + 5 * u + v][None] * grads[d][v]
        rates.append(total.reshape(rows, LANES))
    return cells, rates


def wall_loads(span, n_span, packed, beside, edges, tips, layer, mid, faces, jac):
    group = lane_of((8, LANES)) // 8
    first, last = span == 0, span == n_span - 1

    def swing(x, when):
        return roll(x, LANES // 2) if when else x

    for v in range(VARS + 1):
        p, upper = v % 3, v >= 3
        low_edge = edges[0, 1] if p == 2 else turn_rows(edges[0, 0], 4 - 4 * p)
        high_edge = edges[1, 1] if p == 2 else turn_rows(edges[1, 0], 4 * p)
        tiles = [
            (turn_rows(tips[0], 6 - 2 * p), swing(low_edge, upper), turn_rows(tips[1], 6 - 2 * p)),
            (beside[0, p, 0:8], packed[v, 0:8], beside[1, p, 0:8]),
            (beside[0, p, 8:16], packed[v, 8:16], beside[1, p, 8:16]),
            (turn_rows(tips[2], -2 * p), swing(high_edge, upper), turn_rows(tips[3], -2 * p)),
        ]
        for t, (left, centre, right) in enumerate(tiles):
            left = jnp.where(first, 0.0, swing(left, not upper))
            right = jnp.where(last, 0.0, swing(right, not upper))
            whole = jnp.where(group < 4, left, jnp.where(group >= 12, right, centre))
            layer[v, 8 * t : 8 * t + 8, :] = whole
    span_group = lane_of((24, LANES)) // 8
    outside = (first & (span_group < 4)) | (last & (span_group >= 12))
    cells, rates = wall_rates(layer, 4, 24, VARS, jac, False)
    scale = DT_FLOW * layer[VARS, 4:28, :]
    for u in range(VARS):
        mid[u] = jnp.where(outside, 0.0, cells[u] + scale * rates[u])
    cells, rates = wall_rates(mid, 4, 16, 1, jac, True)
    scale = DT_FLOW * layer[VARS, 8:24, :]
    after = 0.5 * (layer[0, 8:24, :] + cells[0] + scale * rates[0])
    total = jnp.zeros((WRAP, LANES), jnp.float32)
    for s in range(SPAN):
        at = 8 * (s + 4) + 2
        total = total + faces[s] * jnp.broadcast_to(after[:, at : at + 1], (WRAP, LANES))
    return jnp.sum(total, axis=0, keepdims=True)


def kernel(
    n_span,
    n_wrap,
    n_norm,
    flow_hbm,
    volume_hbm,
    jac_hbm,
    area_hbm,
    map_hbm,
    contact_hbm,
    bending_hbm,
    mass_hbm,
    hardening_hbm,
    disp_hbm,
    vel_hbm,
    result,
    defl_ref,
    field1,
    field2,
    planes,
    volume,
    wall_send,
    wall_recv,
    edges,
    corr,
    jac,
    faces,
    area,
    stations,
    contact_v,
    beam_v,
    jac_held,
    beam_held,
    loads_a,
    loads_b,
    tally,
    wall_packed,
    wall_pairs,
    wall_beside,
    edge_put,
    edge_got,
    tip_put,
    tip_got,
    wall_layer,
    wall_mid,
    local_sem,
    send_sem,
    recv_sem,
    group_sem,
    wide_send_sem,
    wide_recv_sem,
):
    span, wrap, normal = lax.axis_index("span"), lax.axis_index("wrap"), lax.axis_index("normal")
    rows = 2
    cols = n_span // rows
    row, col = lax.div(span, cols), lax.rem(span, cols)
    zs, cores = cols // 2, 2
    z, core = lax.div(col, cores), lax.rem(col, cores)
    y_own = row * n_wrap + wrap

    inputs = [
        (flow_hbm, field1.at[:, 2 : 2 + SPAN, TOP : TOP + WRAP, :]),
        (volume_hbm, volume),
        (area_hbm, area),
        (map_hbm, stations),
        (contact_hbm, contact_v),
        (bending_hbm, beam_v.at[0]),
        (mass_hbm, beam_v.at[1]),
        (hardening_hbm, beam_v.at[2]),
        (disp_hbm, beam_v.at[3]),
        (vel_hbm, beam_v.at[4]),
        (jac_hbm, jac_held),
    ]
    reads = [pltpu.make_async_copy(a, b, local_sem.at[i]) for i, (a, b) in enumerate(inputs)]
    for read in reads[:2]:
        read.start()

    def turned(index, by, count):
        return lax.rem(index + (by + count), count)

    span_at = {by: turned(span, by, n_span) for by in (-1, 1)}
    wrap_at = [turned(wrap, by, n_wrap) for by in range(n_wrap)]
    norm_at = {by: turned(normal, by, n_norm) for by in (-1, 1)}
    row_at = [turned(row, by, rows) for by in range(rows)]
    z_at = [turned(z, by, zs) for by in range(zs)]
    core_at = [core, turned(core, 1, cores)]
    sides = [
        (span_at[-1], wrap, normal),
        (span_at[1], wrap, normal),
        (span, wrap_at[n_wrap - 1], normal),
        (span, wrap_at[1], normal),
        (span, wrap, norm_at[-1]),
        (span, wrap, norm_at[1]),
    ]
    barrier = pltpu.get_barrier_semaphore()

    def greet(target):
        pl.semaphore_signal(barrier, inc=1, device_id=target, device_id_type=MESH)

    corners = [(span_at[i], wrap_at[j], normal) for j in (n_wrap - 1, 1) for i in (-1, 1)]

    def device(y, z, core, x):
        return (y[0] * cols + z * cores + core, y[1], x)

    here = (row, wrap)
    y_at = [(row_at[a], wrap_at[b]) for a in range(rows) for b in range(n_wrap)]
    y_far = sorted(range(1, rows * n_wrap), key=lambda k: -ring(2 * (k % n_wrap) + k // n_wrap, 2 * n_wrap))
    z_far = sorted(range(1, zs), key=lambda k: -ring(k, zs))
    beside_y = (1, n_wrap - 1)

    @pl.when(normal == 0)
    def _():
        for k in z_far:
            for c in range(cores):
                greet(device(here, z_at[k], core_at[c], 0))
        for k in y_far:
            if k not in beside_y:
                greet(device(y_at[k], z, core, 0))
        for one in corners:
            greet(one)

    @pl.when(normal != 0)
    def _():
        for k in y_far + [0]:
            greet(device(y_at[k], z, core, 0))

    for side in sides:
        greet(side)

    for read in reads[2:]:
        read.start()

    def copy(src, dst, slot, target):
        return pltpu.make_async_remote_copy(
            src_ref=src,
            dst_ref=dst,
            send_sem=send_sem.at[slot],
            recv_sem=recv_sem.at[slot],
            device_id=target,
            device_id_type=MESH,
        )

    def stage_copies(stage, field):
        cells = pl.ds(TOP, WRAP)
        base = 6 * stage
        pairs = [
            (field.at[:, 2:4, cells, :], planes.at[stage, 1]),
            (field.at[:, SPAN : 2 + SPAN, cells, :], planes.at[stage, 0]),
            (wall_send.at[stage, 0], wall_recv.at[stage, 0]),
            (wall_send.at[stage, 1], wall_recv.at[stage, 1]),
            (edges.at[stage, 0], edges.at[stage, 2]),
            (edges.at[stage, 0], edges.at[stage, 1]),
        ]
        return [copy(src, dst, base + i, sides[i]) for i, (src, dst) in enumerate(pairs)]

    def stage_wrap_rows(stage, field):
        for v in range(VARS):
            for r in range(2):
                wall_send[stage, 0, v, r] = field[v, 2 : 2 + SPAN, TOP + r, :]
                wall_send[stage, 1, v, r] = field[v, 2 : 2 + SPAN, TOP + WRAP - 2 + r, :]

    def stage_columns(stage):
        edge_terms(
            normal, n_norm, edges.at[stage, 0], edges.at[stage, 1], edges.at[stage, 2], jac, corr
        )

    for field in (field1, field2):
        for s in (0, 1, 2 + SPAN, 3 + SPAN):
            field[:, s, TOP : TOP + WRAP, :] = jnp.zeros((VARS, WRAP, LANES), jnp.float32)
        for r in (0, TOP + WRAP):
            field[:, 2 : 2 + SPAN, r : r + 8, :] = jnp.zeros((VARS, SPAN, 8, LANES), jnp.float32)

    wide = []
    for i, (src, dst, target) in enumerate(
        [
            (tip_put.at[0], tip_got.at[3], corners[0]),
            (tip_put.at[0], tip_got.at[2], corners[1]),
            (tip_put.at[1], tip_got.at[1], corners[2]),
            (tip_put.at[1], tip_got.at[0], corners[3]),
            (edge_put.at[0], edge_got.at[1], sides[2]),
            (edge_put.at[1], edge_got.at[0], sides[3]),
            (wall_pairs, wall_beside.at[1], sides[0]),
            (wall_pairs, wall_beside.at[0], sides[1]),
        ]
    ):
        wide.append(
            pltpu.make_async_remote_copy(
                src_ref=src,
                dst_ref=dst,
                send_sem=wide_send_sem.at[i],
                recv_sem=wide_recv_sem.at[i],
                device_id=target,
                device_id_type=MESH,
            )
        )

    empty = tuple(jnp.zeros((8, LANES), jnp.float32) for _ in range(VARS))

    reads[0].wait()
    reads[1].wait()

    @pl.when(normal == 0)
    def _():
        pack_wall(field1, volume, wall_packed)
        pair_wall(wall_packed, wall_pairs, edge_put, tip_put)

    stage_wrap_rows(0, field1)

    def pack_first(s, packed):
        cells = [
            field1[v, s + 2, TOP : TOP + WRAP, :].reshape(2, 8, LANES) for v in range(VARS)
        ]
        return pack_plane(packed, cells, s)

    packed = lax.fori_loop(0, SPAN, pack_first, empty, unroll=True)
    for v in range(VARS):
        edges[0, 0, v] = packed[v]

    lane = lane_of((8, LANES))
    held = jnp.where(lane < LANES // 2, 2 * lane, 2 * lane - (LANES - 1))

    def prepare():
        for read in reads[2:]:
            read.wait()
        for d in range(3):
            for u in range(VARS):
                for v in range(VARS):
                    scaled = jac_held[u, d, v] * (-1.0 / 12.0)
                    jac[25 * d + 5 * u + v] = jnp.full((8, LANES), scaled, jnp.float32)

    def prepare_beam():
        def permuted(x):
            full = jnp.broadcast_to(x, (8, LANES))
            return jnp.take_along_axis(full, held, axis=1)[0:1]

        bending, mass, hardening, disp, vel = [permuted(beam_v[i]) for i in range(5)]
        contact = permuted(contact_v[...])
        inertia = 2.0 * mass / (DT_BEAM * DT_BEAM)
        pull = CONTACT_STIFF * STOP_GAP
        push = jnp.where(contact == 1, pull, jnp.where(contact == 2, -pull, 0.0))
        steady = inertia * (disp + DT_BEAM * vel) + push
        base = inertia + jnp.where(contact > 0, CONTACT_STIFF, 0.0)
        be, bo = halves(bending)
        he, ho = halves(hardening)
        ge, go = halves(base)
        ue, uo = halves(disp)
        fe, fo = halves(steady)
        factors = factor(be, bo, ge + 3.0 * he * ue * ue, go + 3.0 * ho * uo * uo)
        levels, last = factors
        kept = [x for level in levels for x in level[1:]] + list(last)
        kept += [be, bo, ge, go, he, ho, ue, uo, fe, fo]
        for i, x in enumerate(kept):
            beam_held[i] = x

    @pl.when(normal == 0)
    def _():
        prepare()
        prepare_beam()
        row_id = lax.broadcasted_iota(jnp.int32, (WRAP, WRAP), 0)
        same = (row_id == lane_of((WRAP, WRAP))).astype(jnp.float32)

        def turned_over(x):
            return lax.dot_general(
                same, x, (((1,), (1,)), ((), ())), precision=lax.Precision.HIGHEST
            )

        weights = turned_over(area[...])
        places = turned_over(stations[...].astype(jnp.float32))
        aims = jnp.broadcast_to(held[0:1], (WRAP, LANES)).astype(jnp.float32)
        for s in range(SPAN):
            weight = jnp.broadcast_to(weights[:, s : s + 1], (WRAP, LANES))
            place = jnp.broadcast_to(places[:, s : s + 1], (WRAP, LANES))
            faces[s] = jnp.where(place == aims, weight, 0.0)

    at_wall = lax.div(n_norm - normal, n_norm)
    wall_peers = 4 + cores * (zs - 1) + (len(y_at) * n_norm - 1 - len(set(beside_y)))
    pl.semaphore_wait(barrier, 6 + at_wall * wall_peers)

    @pl.when(normal == 0)
    def _():
        for one in wide:
            one.start()

    first = stage_copies(0, field1)

    for one in first:
        one.start()

    @pl.when(normal != 0)
    def _():
        prepare()


    def group_copy(buffer, own, which, target):
        return pltpu.make_async_remote_copy(
            src_ref=buffer.at[own],
            dst_ref=buffer.at[own],
            send_sem=group_sem.at[2 * which],
            recv_sem=group_sem.at[2 * which + 1],
            device_id=target,
            device_id_type=MESH,
        )

    def added(ref):
        terms = [ref[i] for i in range(ref.shape[0])]
        while len(terms) > 1:
            terms = [sum(terms[i + 1 : i + 2], terms[i]) for i in range(0, len(terms), 2)]
        return terms[0]

    def take(ref, which):
        pltpu.make_async_copy(ref, ref, group_sem.at[which]).wait()

    def first_plane(s, carry):
        cells, rates = plane_rates(field1, s, jac)
        scale = DT_FLOW * volume[s].reshape(2, 8, LANES)
        for u in range(VARS):
            mid = cells[u] + scale * rates[u]
            field2[u, s + 2, TOP : TOP + WRAP, :] = mid.reshape(WRAP, LANES)
        return carry

    lax.fori_loop(0, SPAN // 4, in_fours(first_plane), 0)

    @pl.when(normal == 0)
    def _():
        for one in wide:
            one.wait_recv()
        loads_a[col] = wall_loads(
            span,
            n_span,
            wall_packed,
            wall_beside,
            edge_got,
            tip_got,
            wall_layer,
            wall_mid,
            faces,
            jac,
        )
        for k in z_far + [0]:
            for c in range(cores):
                if k or c:
                    group_copy(loads_a, col, 0, device(here, z_at[k], core_at[c], 0)).start()

    for one in first:
        one.wait_recv()
    stage_columns(0)

    def mid_plane(u, s, part):
        field2[u, s + 2, TOP : TOP + WRAP, :] += part

    def mid_row(u, r, part):
        field2[u, 2 : 2 + SPAN, TOP + r, :] += part

    def mid_cells(u, s, part):
        cells = field2[u, s + 2, TOP : TOP + WRAP, :].reshape(2, 8, LANES) + part
        field2[u, s + 2, TOP : TOP + WRAP, :] = cells.reshape(WRAP, LANES)
        return cells

    columns = add_ghosts(
        span,
        n_span,
        planes.at[0],
        wall_recv.at[0],
        corr,
        jac,
        volume,
        DT_FLOW,
        mid_plane,
        mid_row,
        mid_cells,
        pack_plane,
    )
    packed = lax.fori_loop(0, SPAN, lambda s, packed: columns(s, packed), empty, unroll=True)
    for v in range(VARS):
        edges[1, 0, v] = packed[v]

    stage_wrap_rows(1, field2)
    second = stage_copies(1, field2)
    for one in second:
        one.start()


    @pl.when(normal != 0)
    def _():
        prepare_beam()

    for one in first:
        one.wait_send()

    @pl.when(normal == 0)
    def _():
        for one in wide:
            one.wait_send()
        take(loads_a.at[1:], 1)
        loads_b[y_own] = added(loads_a)
        for x in sorted(range(n_norm), key=lambda x: -ring(x, n_norm)):
            for k in y_far + [0]:
                if x or k:
                    group_copy(loads_b, y_own, 1, device(y_at[k], z, core, x)).start()

    def second_plane(s, carry):
        cells, rates = plane_rates(field2, s, jac)
        scale = DT_FLOW * volume[s].reshape(2, 8, LANES)
        for u in range(VARS):
            start = field1[u, s + 2, TOP : TOP + WRAP, :].reshape(2, 8, LANES)
            after = 0.5 * (start + cells[u] + scale * rates[u])
            result[u, s] = after.reshape(WRAP, LANES)
        return carry

    lax.fori_loop(0, SPAN // 4, in_fours(second_plane), 0)

    for one in second:
        one.wait_recv()
    stage_columns(1)

    def end_plane(u, s, part):
        result[u, s] += part

    def end_row(u, r, part):
        result[u, :, r, :] += part

    def end_cells(u, s, part):
        result[u, s] += part.reshape(WRAP, LANES)

    columns = add_ghosts(
        span,
        n_span,
        planes.at[1],
        wall_recv.at[1],
        corr,
        jac,
        volume,
        0.5 * DT_FLOW,
        end_plane,
        end_row,
        end_cells,
        lambda carry, cells, s: carry,
    )
    lax.fori_loop(0, SPAN, columns, 0, unroll=True)

    for one in second:
        one.wait_send()

    @pl.when(normal == 0)
    def _():
        take(loads_a.at[1:], 0)
        take(tally, 2)

    @pl.when(normal == 0)
    def _():
        take(loads_b.at[1:], 3)

    @pl.when(normal != 0)
    def _():
        take(loads_b, 3)

    loads = added(loads_b)
    kept = [beam_held[i] for i in range(9 * LEVELS + 14)]
    levels = [(2**i, *kept[9 * i : 9 * i + 9]) for i in range(LEVELS)]
    factors = (levels, tuple(kept[9 * LEVELS : 9 * LEVELS + 4]))
    be, bo, ge, go, he, ho, ue, uo, fe, fo = kept[9 * LEVELS + 4 :]
    le, lo = halves(loads)
    fe, fo = fe + le, fo + lo
    for newton_step in range(NEWTON):
        if newton_step:
            factors = factor(be, bo, ge + 3.0 * he * ue * ue, go + 3.0 * ho * uo * uo)
        ue, uo = substitute(factors, *right_side(fe, fo, he, ho, ue, uo))
    both = jnp.where(lane_of((1, LANES)) < LANES // 2, ue, roll(uo, LANES // 2))
    back = (lane % 2) * (LANES // 2) + lane // 2
    full = jnp.broadcast_to(both, (8, LANES))
    defl_ref[...] = jnp.take_along_axis(full, back, axis=1)[0:1]


def hand_out(flow_ref, defl_ref, flow_out, defl_out, sem):
    copies = [
        pltpu.make_async_copy(flow_ref, flow_out, sem.at[0]),
        pltpu.make_async_copy(defl_ref, defl_out, sem.at[1]),
    ]
    for one in copies:
        one.start()
    for one in copies:
        one.wait()


def solution(mesh):
    n_span, n_wrap, n_norm = (mesh.shape[axis] for axis in ("span", "wrap", "normal"))
    zs, ys = n_span // 4, 2 * n_wrap
    f32 = jnp.float32

    def step(
        flow_state,
        inv_volume,
        flux_jacobians,
        area,
        station_map,
        contact,
        bending,
        mass,
        hardening,
        disp_old,
        vel_old,
    ):
        vectors = [
            x.reshape(1, STATIONS) for x in (contact, bending, mass, hardening, disp_old, vel_old)
        ]
        hbm, vmem = (pl.BlockSpec(memory_space=space) for space in (pltpu.HBM, pltpu.VMEM))
        operands = [flow_state, inv_volume, flux_jacobians.transpose(1, 0, 2), area, station_map]
        operands = [pltpu.with_memory_space_constraint(x, pltpu.HBM) for x in operands + vectors]
        flow_next, deflection = pl.pallas_call(
            functools.partial(kernel, n_span, n_wrap, n_norm),
            out_shape=(
                pltpu.VMEM(flow_state.shape, f32),
                pltpu.VMEM((1, STATIONS), f32),
            ),
            in_specs=[hbm] * len(operands),
            out_specs=(vmem, vmem),
            scratch_shapes=[
                pltpu.VMEM((VARS, SPAN + 4, WRAP + 16, LANES), f32),
                pltpu.VMEM((VARS, SPAN + 4, WRAP + 16, LANES), f32),
                pltpu.VMEM((2, 2, VARS, 2, WRAP, LANES), f32),
                pltpu.VMEM((SPAN, WRAP, LANES), f32),
                pltpu.VMEM((2, 2, VARS, 2, SPAN, LANES), f32),
                pltpu.VMEM((2, 2, VARS, 2, SPAN, LANES), f32),
                pltpu.VMEM((2, 3, VARS, 8, LANES), f32),
                pltpu.VMEM((VARS, 8, LANES), f32),
                pltpu.VMEM((75, 8, LANES), f32),
                pltpu.VMEM((SPAN, WRAP, LANES), f32),
                pltpu.VMEM((SPAN, WRAP), f32),
                pltpu.VMEM((SPAN, WRAP), jnp.int32),
                pltpu.VMEM((1, STATIONS), jnp.int32),
                pltpu.VMEM((5, 1, STATIONS), f32),
                pltpu.SMEM((VARS, 3, VARS), f32),
                pltpu.VMEM((9 * LEVELS + 14, 1, LANES), f32),
                pltpu.VMEM((2 * zs, 1, LANES), f32),
                pltpu.VMEM((ys, 1, LANES), f32),
                pltpu.VMEM((ys * n_norm - 1, 1, LANES), f32),
                pltpu.VMEM((VARS + 1, WRAP, LANES), f32),
                pltpu.VMEM((3, WRAP, LANES), f32),
                pltpu.VMEM((2, 3, WRAP, LANES), f32),
                pltpu.VMEM((2, 2, 8, LANES), f32),
                pltpu.VMEM((2, 2, 8, LANES), f32),
                pltpu.VMEM((2, 8, LANES), f32),
                pltpu.VMEM((4, 8, LANES), f32),
                pltpu.VMEM((VARS + 1, WRAP + 16, LANES), f32),
                pltpu.VMEM((VARS, 24, LANES), f32),
                pltpu.SemaphoreType.DMA((11,)),
                pltpu.SemaphoreType.DMA((12,)),
                pltpu.SemaphoreType.DMA((12,)),
                pltpu.SemaphoreType.DMA((4,)),
                pltpu.SemaphoreType.DMA((8,)),
                pltpu.SemaphoreType.DMA((8,)),
            ],
            compiler_params=pltpu.CompilerParams(
                collective_id=0, has_side_effects=True, vmem_limit_bytes=32 * 1024 * 1024
            ),
            cost_estimate=pl.CostEstimate(
                flops=10_000_000, bytes_accessed=1_000_000, transcendentals=0
            ),
        )(*operands)
        flow_next, deflection = pl.pallas_call(
            hand_out,
            out_shape=(
                jax.ShapeDtypeStruct(flow_state.shape, f32),
                jax.ShapeDtypeStruct((1, STATIONS), f32),
            ),
            in_specs=(vmem, vmem),
            out_specs=(hbm, hbm),
            scratch_shapes=[pltpu.SemaphoreType.DMA((2,))],
        )(
            pltpu.with_memory_space_constraint(flow_next, pltpu.VMEM),
            pltpu.with_memory_space_constraint(deflection, pltpu.VMEM),
        )
        return flow_next, deflection.reshape(STATIONS)

    placed = (
        P(None, "span", "wrap", "normal"),
        P("span", "wrap", "normal"),
        P(),
        P("span", "wrap"),
        P("span", "wrap"),
    ) + (P(),) * 6
    return jax.shard_map(
        step,
        mesh=mesh,
        in_specs=placed,
        out_specs=(P(None, "span", "wrap", "normal"), P()),
        check_vma=False,
    )
```

```python
import functools

import jax
import jax.numpy as jnp
from jax import lax
from jax.experimental import pallas as pl
from jax.experimental.pallas import tpu as pltpu
from jax.sharding import PartitionSpec as P

MESH = pl.DeviceIdType.MESH
VARS = 5
STATIONS = 128
NEWTON = 3
LEVELS = 6
DT_FLOW = 0.2
DISSIPATION = 0.03
DT_BEAM = 0.2
STOP_GAP = 0.5
CONTACT_STIFF = 40.0
SPAN, WRAP, LANES = 8, 16, 128
TOP = 8


def lane_of(shape):
    return lax.broadcasted_iota(jnp.int32, shape, len(shape) - 1)


def roll(x, shift):
    return pltpu.roll(x, shift % LANES if isinstance(shift, int) else shift, 1)


def factor(be, bo, diag_e, diag_o):
    lane = lane_of((1, LANES))
    half = LANES // 2
    valid, inner = lane < half, lane < half - 1
    bo_prev, be_next = roll(bo, 1), roll(be, -1)
    p = jnp.where(valid, 4.0 * be + bo_prev + bo + diag_e, 1.0)
    q = jnp.where(valid, -2.0 * (be + bo), 0.0)
    r = jnp.where(valid, 4.0 * bo + be + be_next + diag_o, 1.0)
    c11 = jnp.where(inner, bo, 0.0)
    c12 = jnp.zeros_like(bo)
    c21 = jnp.where(inner, -2.0 * (bo + be_next), 0.0)
    c22 = jnp.where(inner, be_next, 0.0)
    a11, a12, a21, a22 = roll(c11, 1), roll(c21, 1), c12, roll(c22, 1)
    levels = []
    step = 1
    while step < half:
        inv = 1.0 / (p * r - q * q)
        u11, u12 = c11 * r - c21 * q, c21 * p - c11 * q
        u21, u22 = c12 * r - c22 * q, c22 * p - c12 * q
        d11, d12 = a11 * r - a21 * q, a21 * p - a11 * q
        d21, d22 = a12 * r - a22 * q, a22 * p - a12 * q
        levels.append((step, inv, u11, u12, u21, u22, d11, d12, d21, d22))
        up = [
            (u11 * c11 + u12 * c21) * inv,
            (u11 * c12 + u12 * c22) * inv,
            (u21 * c12 + u22 * c22) * inv,
        ]
        down = [
            (d11 * a11 + d12 * a21) * inv,
            (d11 * a12 + d12 * a22) * inv,
            (d21 * a12 + d22 * a22) * inv,
        ]
        p = p - (roll(up[0], step) + roll(down[0], -step))
        q = q - (roll(up[1], step) + roll(down[1], -step))
        r = r - (roll(up[2], step) + roll(down[2], -step))
        if 2 * step < half:
            n11, n12 = -(d11 * c11 + d12 * c21) * inv, -(d11 * c12 + d12 * c22) * inv
            n21, n22 = -(d21 * c11 + d22 * c21) * inv, -(d21 * c12 + d22 * c22) * inv
            c11, c12 = roll(n11, -step), roll(n12, -step)
            c21, c22 = roll(n21, -step), roll(n22, -step)
            a11, a12 = roll(n11, step), roll(n21, step)
            a21, a22 = roll(n12, step), roll(n22, step)
        step *= 2
    return levels, (1.0 / (p * r - q * q), p, q, r)


def substitute(factors, e, o):
    levels, (inv, p, q, r) = factors
    for step, scale, u11, u12, u21, u22, d11, d12, d21, d22 in levels:
        e, o = (
            e - (roll((u11 * e + u12 * o) * scale, step) + roll((d11 * e + d12 * o) * scale, -step)),
            o - (roll((u21 * e + u22 * o) * scale, step) + roll((d21 * e + d22 * o) * scale, -step)),
        )
    return (r * e - q * o) * inv, (p * o - q * e) * inv


def right_side(fe, fo, he, ho, ue, uo):
    return fe + 2.0 * he * ue * ue * ue, fo + 2.0 * ho * uo * uo * uo


def halves(x):
    valid = lane_of((1, LANES)) < LANES // 2
    return jnp.where(valid, x, 0.0), jnp.where(valid, roll(x, LANES // 2), 0.0)


def ring(by, count):
    return min(by, count - by)


def pack_plane(packed, cells, s):
    slot = lane_of((8, LANES)) // 4
    new = []
    for v in range(VARS):
        have = packed[v]
        for t in range(2):
            k = 2 * s + t
            have = jnp.where(slot == k, roll(cells[v][t], 4 * k + 2), have)
        new.append(have)
    return tuple(new)


def edge_terms(normal, n_norm, own, left, right, jac, corr):
    lane = lane_of((8, LANES))
    place = lane % 4
    ends, smooths = [], []
    for v in range(VARS):
        mine = own[v]
        mirror = jnp.where(place == 0, roll(mine, -3), roll(mine, -1))
        low = jnp.where(normal == 0, mirror, left[v])
        high = jnp.where(normal == n_norm - 1, 0.0, right[v])
        delta = jnp.where(place < 2, roll(high - mine, -2), roll(low - mine, 2))
        near = jnp.where(place == 1, roll(delta, 1), jnp.where(place == 2, roll(delta, -1), 0.0))
        end = delta - 8.0 * near
        ends.append(jnp.where(place < 2, -end, end))
        smooths.append(delta - 4.0 * near)
    for u in range(VARS):
        total = -DISSIPATION * smooths[u]
        for v in range(VARS):
            total = total + jac[50 + 5 * u + v] * ends[v]
        corr[u] = total


def plane_rates(field, s, jac):
    cells, grads, smooths = [], [[], [], []], []
    for v in range(VARS):

        def at(ds, dw):
            return field[v, s + (2 + ds), TOP + dw : TOP + dw + WRAP, :]

        c = at(0, 0)
        reads = [
            [at(k, 0) for k in (-2, -1, 1, 2)],
            [at(0, k) for k in (-2, -1, 1, 2)],
            [roll(c, -k) for k in (-2, -1, 1, 2)],
        ]
        near, far = None, None
        for d, (m2, m1, p1, p2) in enumerate(reads):
            grads[d].append(((m2 - p2) + 8.0 * (p1 - m1)).reshape(2, 8, LANES))
            near = (m1 + p1) if near is None else near + (m1 + p1)
            far = (m2 + p2) if far is None else far + (m2 + p2)
        smooths.append((-DISSIPATION * (far - 4.0 * near + 18.0 * c)).reshape(2, 8, LANES))
        cells.append(c.reshape(2, 8, LANES))
    rates = []
    for u in range(VARS):
        total = smooths[u]
        for d in range(3):
            for v in range(VARS):
                total = total + jac[25 * d + 5 * u + v][None] * grads[d][v]
        rates.append(total)
    return cells, rates


def in_fours(plane):
    def four(i, carry):
        for j in range(4):
            carry = plane(4 * i + j, carry)
        return carry

    return four


def ghost_rates(direction, low, first, second, jac, shape):
    outer, inner = [], []
    for v in range(VARS):
        a, b = first(v), second(v)
        if low:
            outer.append((a - 8.0 * b, a - 4.0 * b))
            inner.append((b, b))
        else:
            outer.append((8.0 * a - b, b - 4.0 * a))
            inner.append((-a, a))
    fixes = []
    for layer in (outer, inner):
        grads = [g.reshape(shape) for g, _ in layer]
        layer_fixes = []
        for u in range(VARS):
            total = -DISSIPATION * layer[u][1].reshape(shape)
            for v in range(VARS):
                total = total + jac[25 * direction + 5 * u + v][None] * grads[v]
            layer_fixes.append(total)
        fixes.append(layer_fixes)
    return fixes


def add_ghosts(span, n_span, planes, rows, corr, jac, volume, factor_of, at_plane, at_row, at_cells, done):
    for low in (True, False):
        gone = span == (0 if low else n_span - 1)
        side = 0 if low else 1

        def ghost(layer):
            return lambda v: jnp.where(gone, 0.0, planes[side, v, layer])

        fixes = ghost_rates(0, low, ghost(0), ghost(1), jac, (2, 8, LANES))
        for s, fix in zip((0, 1) if low else (SPAN - 1, SPAN - 2), fixes):
            scale = factor_of * volume[s]
            for u in range(VARS):
                at_plane(u, s, scale * fix[u].reshape(WRAP, LANES))
    for low in (True, False):
        side = 1 if low else 0

        def ghost(layer):
            return lambda v: rows[side, v, layer]

        fixes = ghost_rates(1, low, ghost(0), ghost(1), jac, (1, 8, LANES))
        for r, fix in zip((0, 1) if low else (WRAP - 1, WRAP - 2), fixes):
            scale = factor_of * volume[:, r, :]
            for u in range(VARS):
                at_row(u, r, scale * fix[u].reshape(8, LANES))
    lane = lane_of((8, LANES))
    edge = (lane < 2) | (lane >= LANES - 2)

    def columns(s, carry):
        scale = factor_of * volume[s].reshape(2, 8, LANES)
        cells = []
        for u in range(VARS):
            ends = corr[u]
            fix = [
                jnp.where(edge, roll(ends, (2 * LANES - 2 - 4 * (2 * s + t)) % LANES), 0.0)
                for t in range(2)
            ]
            cells.append(at_cells(u, s, scale * jnp.stack(fix)))
        return done(carry, cells, s)

    return columns


def pack_wall(field, volume, packed):
    group = lane_of((8, LANES)) // 8
    for v in range(VARS + 1):
        for t in range(2):
            have = jnp.zeros((8, LANES), jnp.float32)
            for s in range(SPAN):
                if v < VARS:
                    tile = field[v, s + 2, TOP + 8 * t : TOP + 8 * t + 8, :]
                else:
                    tile = volume[s, 8 * t : 8 * t + 8, :]
                have = jnp.where(group == s + 4, roll(tile, 8 * (s + 4) + 2), have)
            packed[v, 8 * t : 8 * t + 8, :] = mirrored(have)


def pair_wall(packed, pairs, edge, tip):
    lane, row = lane_of((8, LANES)), lax.broadcasted_iota(jnp.int32, (8, LANES), 0)
    own = (lane >= LANES // 4) & (lane < 3 * LANES // 4)
    for p in range(3):
        for t in range(2):
            rows = slice(8 * t, 8 * t + 8)
            pairs[p, rows, :] = jnp.where(own, packed[p, rows, :], roll(packed[p + 3, rows, :], 64))
    for t in range(2):
        a, b, c = (pairs[p, 8 * t : 8 * t + 8, :] for p in range(3))
        four = row < 4
        edge[t, 0] = jnp.where(four, a if t == 0 else pltpu.roll(a, 4, 0), b if t else pltpu.roll(b, 4, 0))
        edge[t, 1] = c
        at = 6 * t
        tip[t] = jnp.where(
            row < 2,
            turn_rows(a, -at),
            jnp.where(four, turn_rows(b, 2 - at), turn_rows(c, 4 - at)),
        )


def turn_rows(x, by):
    return pltpu.roll(x, by % 8, 0) if by % 8 else x


def mirrored(x):
    place = lane_of(x.shape) % 8
    return jnp.where(place == 0, roll(x, -3), jnp.where(place == 1, roll(x, -1), x))


def wall_rates(layer, top, rows, wanted, jac, at_wall):
    cells, grads, smooths = [], [[], [], []], []
    shape = (rows // 8, 8, LANES)
    for v in range(VARS):
        c = layer[v, top : top + rows, :]
        reads = [
            [roll(c, -8 * k) for k in (-2, -1, 1, 2)],
            [layer[v, top + k : top + k + rows, :] for k in (-2, -1, 1, 2)],
        ]
        if at_wall:
            p1, p2 = roll(c, -1), roll(c, -2)
            reads.append([p1, c, p1, p2])
        else:
            reads.append([roll(c, -k) for k in (-2, -1, 1, 2)])
        near, far = None, None
        for d, (m2, m1, p1, p2) in enumerate(reads):
            grads[d].append(((m2 - p2) + 8.0 * (p1 - m1)).reshape(shape))
            near = (m1 + p1) if near is None else near + (m1 + p1)
            far = (m2 + p2) if far is None else far + (m2 + p2)
        smooths.append((-DISSIPATION * (far - 4.0 * near + 18.0 * c)).reshape(shape))
        cells.append(c)
    rates = []
    for u in range(wanted):
        total = smooths[u]
        for d in range(3):
            for v in range(VARS):
                total = total + jac[25 * d + 5 * u + v][None] * grads[d][v]
        rates.append(total.reshape(rows, LANES))
    return cells, rates


def wall_loads(span, n_span, packed, beside, edges, tips, layer, mid, faces, jac):
    group = lane_of((8, LANES)) // 8
    first, last = span == 0, span == n_span - 1

    def swing(x, when):
        return roll(x, LANES // 2) if when else x

    for v in range(VARS + 1):
        p, upper = v % 3, v >= 3
        low_edge = edges[0, 1] if p == 2 else turn_rows(edges[0, 0], 4 - 4 * p)
        high_edge = edges[1, 1] if p == 2 else turn_rows(edges[1, 0], 4 * p)
        tiles = [
            (turn_rows(tips[0], 6 - 2 * p), swing(low_edge, upper), turn_rows(tips[1], 6 - 2 * p)),
            (beside[0, p, 0:8], packed[v, 0:8], beside[1, p, 0:8]),
            (beside[0, p, 8:16], packed[v, 8:16], beside[1, p, 8:16]),
            (turn_rows(tips[2], -2 * p), swing(high_edge, upper), turn_rows(tips[3], -2 * p)),
        ]
        for t, (left, centre, right) in enumerate(tiles):
            left = jnp.where(first, 0.0, swing(left, not upper))
            right = jnp.where(last, 0.0, swing(right, not upper))
            whole = jnp.where(group < 4, left, jnp.where(group >= 12, right, centre))
            layer[v, 8 * t : 8 * t + 8, :] = whole
    span_group = lane_of((24, LANES)) // 8
    outside = (first & (span_group < 4)) | (last & (span_group >= 12))
    cells, rates = wall_rates(layer, 4, 24, VARS, jac, False)
    scale = DT_FLOW * layer[VARS, 4:28, :]
    for u in range(VARS):
        mid[u] = jnp.where(outside, 0.0, cells[u] + scale * rates[u])
    cells, rates = wall_rates(mid, 4, 16, 1, jac, True)
    scale = DT_FLOW * layer[VARS, 8:24, :]
    after = 0.5 * (layer[0, 8:24, :] + cells[0] + scale * rates[0])
    total = jnp.zeros((WRAP, LANES), jnp.float32)
    for s in range(SPAN):
        at = 8 * (s + 4) + 2
        total = total + faces[s] * jnp.broadcast_to(after[:, at : at + 1], (WRAP, LANES))
    return jnp.sum(total, axis=0, keepdims=True)


def kernel(
    n_span,
    n_wrap,
    n_norm,
    flow_hbm,
    volume_hbm,
    jac_hbm,
    area_hbm,
    map_hbm,
    contact_hbm,
    bending_hbm,
    mass_hbm,
    hardening_hbm,
    disp_hbm,
    vel_hbm,
    result,
    defl_ref,
    field1,
    field2,
    planes,
    volume,
    wall_send,
    wall_recv,
    edges,
    corr,
    jac,
    faces,
    area,
    stations,
    contact_v,
    beam_v,
    jac_held,
    beam_held,
    loads_a,
    loads_b,
    tally,
    wall_packed,
    wall_pairs,
    wall_beside,
    edge_put,
    edge_got,
    tip_put,
    tip_got,
    wall_layer,
    wall_mid,
    local_sem,
    send_sem,
    recv_sem,
    group_sem,
    wide_send_sem,
    wide_recv_sem,
):
    span, wrap, normal = lax.axis_index("span"), lax.axis_index("wrap"), lax.axis_index("normal")
    rows = 2
    cols = n_span // rows
    row, col = lax.div(span, cols), lax.rem(span, cols)
    zs, cores = cols // 2, 2
    z, core = lax.div(col, cores), lax.rem(col, cores)
    y_own = row * n_wrap + wrap

    inputs = [
        (flow_hbm, field1.at[:, 2 : 2 + SPAN, TOP : TOP + WRAP, :]),
        (volume_hbm, volume),
        (area_hbm, area),
        (map_hbm, stations),
        (contact_hbm, contact_v),
        (bending_hbm, beam_v.at[0]),
        (mass_hbm, beam_v.at[1]),
        (hardening_hbm, beam_v.at[2]),
        (disp_hbm, beam_v.at[3]),
        (vel_hbm, beam_v.at[4]),
        (jac_hbm, jac_held),
    ]
    reads = [pltpu.make_async_copy(a, b, local_sem.at[i]) for i, (a, b) in enumerate(inputs)]
    for read in reads[:2]:
        read.start()

    def turned(index, by, count):
        return lax.rem(index + (by + count), count)

    span_at = {by: turned(span, by, n_span) for by in (-1, 1)}
    wrap_at = [turned(wrap, by, n_wrap) for by in range(n_wrap)]
    norm_at = {by: turned(normal, by, n_norm) for by in (-1, 1)}
    row_at = [turned(row, by, rows) for by in range(rows)]
    z_at = [turned(z, by, zs) for by in range(zs)]
    core_at = [core, turned(core, 1, cores)]
    sides = [
        (span_at[-1], wrap, normal),
        (span_at[1], wrap, normal),
        (span, wrap_at[n_wrap - 1], normal),
        (span, wrap_at[1], normal),
        (span, wrap, norm_at[-1]),
        (span, wrap, norm_at[1]),
    ]
    barrier = pltpu.get_barrier_semaphore()

    def greet(target):
        pl.semaphore_signal(barrier, inc=1, device_id=target, device_id_type=MESH)

    corners = [(span_at[i], wrap_at[j], normal) for j in (n_wrap - 1, 1) for i in (-1, 1)]

    def device(y, z, core, x):
        return (y[0] * cols + z * cores + core, y[1], x)

    here = (row, wrap)
    y_at = [(row_at[a], wrap_at[b]) for a in range(rows) for b in range(n_wrap)]
    y_far = sorted(range(1, rows * n_wrap), key=lambda k: -ring(2 * (k % n_wrap) + k // n_wrap, 2 * n_wrap))
    z_far = sorted(range(1, zs), key=lambda k: -ring(k, zs))
    beside_y = (1, n_wrap - 1)

    @pl.when(normal == 0)
    def _():
        for k in z_far:
            for c in range(cores):
                greet(device(here, z_at[k], core_at[c], 0))
        for k in y_far:
            if k not in beside_y:
                greet(device(y_at[k], z, core, 0))
        for one in corners:
            greet(one)

    @pl.when(normal != 0)
    def _():
        for k in y_far + [0]:
            greet(device(y_at[k], z, core, 0))

    for side in sides:
        greet(side)

    for read in reads[2:]:
        read.start()

    def copy(src, dst, slot, target):
        return pltpu.make_async_remote_copy(
            src_ref=src,
            dst_ref=dst,
            send_sem=send_sem.at[slot],
            recv_sem=recv_sem.at[slot],
            device_id=target,
            device_id_type=MESH,
        )

    def stage_copies(stage, field):
        cells = pl.ds(TOP, WRAP)
        base = 6 * stage
        pairs = [
            (field.at[:, 2:4, cells, :], planes.at[stage, 1]),
            (field.at[:, SPAN : 2 + SPAN, cells, :], planes.at[stage, 0]),
            (wall_send.at[stage, 0], wall_recv.at[stage, 0]),
            (wall_send.at[stage, 1], wall_recv.at[stage, 1]),
            (edges.at[stage, 0], edges.at[stage, 2]),
            (edges.at[stage, 0], edges.at[stage, 1]),
        ]
        return [copy(src, dst, base + i, sides[i]) for i, (src, dst) in enumerate(pairs)]

    def stage_wrap_rows(stage, field):
        for v in range(VARS):
            for r in range(2):
                wall_send[stage, 0, v, r] = field[v, 2 : 2 + SPAN, TOP + r, :]
                wall_send[stage, 1, v, r] = field[v, 2 : 2 + SPAN, TOP + WRAP - 2 + r, :]

    def stage_columns(stage):
        edge_terms(
            normal, n_norm, edges.at[stage, 0], edges.at[stage, 1], edges.at[stage, 2], jac, corr
        )

    for field in (field1, field2):
        for s in (0, 1, 2 + SPAN, 3 + SPAN):
            field[:, s, TOP : TOP + WRAP, :] = jnp.zeros((VARS, WRAP, LANES), jnp.float32)
        for r in (0, TOP + WRAP):
            field[:, 2 : 2 + SPAN, r : r + 8, :] = jnp.zeros((VARS, SPAN, 8, LANES), jnp.float32)

    wide = []
    for i, (src, dst, target) in enumerate(
        [
            (tip_put.at[0], tip_got.at[3], corners[0]),
            (tip_put.at[0], tip_got.at[2], corners[1]),
            (tip_put.at[1], tip_got.at[1], corners[2]),
            (tip_put.at[1], tip_got.at[0], corners[3]),
            (edge_put.at[0], edge_got.at[1], sides[2]),
            (edge_put.at[1], edge_got.at[0], sides[3]),
            (wall_pairs, wall_beside.at[1], sides[0]),
            (wall_pairs, wall_beside.at[0], sides[1]),
        ]
    ):
        wide.append(
            pltpu.make_async_remote_copy(
                src_ref=src,
                dst_ref=dst,
                send_sem=wide_send_sem.at[i],
                recv_sem=wide_recv_sem.at[i],
                device_id=target,
                device_id_type=MESH,
            )
        )

    empty = tuple(jnp.zeros((8, LANES), jnp.float32) for _ in range(VARS))

    reads[0].wait()
    reads[1].wait()

    @pl.when(normal == 0)
    def _():
        pack_wall(field1, volume, wall_packed)
        pair_wall(wall_packed, wall_pairs, edge_put, tip_put)

    stage_wrap_rows(0, field1)

    def pack_first(s, packed):
        cells = [
            field1[v, s + 2, TOP : TOP + WRAP, :].reshape(2, 8, LANES) for v in range(VARS)
        ]
        return pack_plane(packed, cells, s)

    packed = lax.fori_loop(0, SPAN, pack_first, empty, unroll=True)
    for v in range(VARS):
        edges[0, 0, v] = packed[v]

    lane = lane_of((8, LANES))
    held = jnp.where(lane < LANES // 2, 2 * lane, 2 * lane - (LANES - 1))

    def prepare():
        for read in reads[2:]:
            read.wait()
        for d in range(3):
            for u in range(VARS):
                for v in range(VARS):
                    scaled = jac_held[u, d, v] * (-1.0 / 12.0)
                    jac[25 * d + 5 * u + v] = jnp.full((8, LANES), scaled, jnp.float32)

    def prepare_beam():
        def permuted(x):
            full = jnp.broadcast_to(x, (8, LANES))
            return jnp.take_along_axis(full, held, axis=1)[0:1]

        bending, mass, hardening, disp, vel = [permuted(beam_v[i]) for i in range(5)]
        contact = permuted(contact_v[...])
        inertia = 2.0 * mass / (DT_BEAM * DT_BEAM)
        pull = CONTACT_STIFF * STOP_GAP
        push = jnp.where(contact == 1, pull, jnp.where(contact == 2, -pull, 0.0))
        steady = inertia * (disp + DT_BEAM * vel) + push
        base = inertia + jnp.where(contact > 0, CONTACT_STIFF, 0.0)
        be, bo = halves(bending)
        he, ho = halves(hardening)
        ge, go = halves(base)
        ue, uo = halves(disp)
        fe, fo = halves(steady)
        factors = factor(be, bo, ge + 3.0 * he * ue * ue, go + 3.0 * ho * uo * uo)
        levels, last = factors
        kept = [x for level in levels for x in level[1:]] + list(last)
        kept += [be, bo, ge, go, he, ho, ue, uo, fe, fo]
        for i, x in enumerate(kept):
            beam_held[i] = x

    @pl.when(normal == 0)
    def _():
        prepare()

    at_wall = lax.div(n_norm - normal, n_norm)
    wall_peers = 4 + cores * (zs - 1) + (len(y_at) * n_norm - 1 - len(set(beside_y)))
    pl.semaphore_wait(barrier, 6 + at_wall * wall_peers)

    @pl.when(normal == 0)
    def _():
        for one in wide:
            one.start()

    first = stage_copies(0, field1)

    @pl.when(normal != 0)
    def _():
        for one in first:
            one.start()
        prepare()


    def group_copy(buffer, own, which, target):
        return pltpu.make_async_remote_copy(
            src_ref=buffer.at[own],
            dst_ref=buffer.at[own],
            send_sem=group_sem.at[2 * which],
            recv_sem=group_sem.at[2 * which + 1],
            device_id=target,
            device_id_type=MESH,
        )

    def added(ref):
        terms = [ref[i] for i in range(ref.shape[0])]
        while len(terms) > 1:
            terms = [sum(terms[i + 1 : i + 2], terms[i]) for i in range(0, len(terms), 2)]
        return terms[0]

    def take(ref, which):
        pltpu.make_async_copy(ref, ref, group_sem.at[which]).wait()

    def first_plane(s, carry):
        cells, rates = plane_rates(field1, s, jac)
        scale = DT_FLOW * volume[s].reshape(2, 8, LANES)
        for u in range(VARS):
            mid = cells[u] + scale * rates[u]
            field2[u, s + 2, TOP : TOP + WRAP, :] = mid.reshape(WRAP, LANES)
        return carry

    lax.fori_loop(0, SPAN // 4, in_fours(first_plane), 0)

    @pl.when(normal == 0)
    def _():
        for one in first:
            one.start()
        row_id = lax.broadcasted_iota(jnp.int32, (WRAP, WRAP), 0)
        same = (row_id == lane_of((WRAP, WRAP))).astype(jnp.float32)

        def turned_over(x):
            return lax.dot_general(
                same, x, (((1,), (1,)), ((), ())), precision=lax.Precision.HIGHEST
            )

        weights = turned_over(area[...])
        places = turned_over(stations[...].astype(jnp.float32))
        aims = jnp.broadcast_to(held[0:1], (WRAP, LANES)).astype(jnp.float32)
        for s in range(SPAN):
            weight = jnp.broadcast_to(weights[:, s : s + 1], (WRAP, LANES))
            place = jnp.broadcast_to(places[:, s : s + 1], (WRAP, LANES))
            faces[s] = jnp.where(place == aims, weight, 0.0)
        for one in wide:
            one.wait_recv()
        loads_a[col] = wall_loads(
            span,
            n_span,
            wall_packed,
            wall_beside,
            edge_got,
            tip_got,
            wall_layer,
            wall_mid,
            faces,
            jac,
        )
        for k in z_far + [0]:
            for c in range(cores):
                if k or c:
                    group_copy(loads_a, col, 0, device(here, z_at[k], core_at[c], 0)).start()

    for one in first:
        one.wait_recv()
    stage_columns(0)

    def mid_plane(u, s, part):
        field2[u, s + 2, TOP : TOP + WRAP, :] += part

    def mid_row(u, r, part):
        field2[u, 2 : 2 + SPAN, TOP + r, :] += part

    def mid_cells(u, s, part):
        cells = field2[u, s + 2, TOP : TOP + WRAP, :].reshape(2, 8, LANES) + part
        field2[u, s + 2, TOP : TOP + WRAP, :] = cells.reshape(WRAP, LANES)
        return cells

    columns = add_ghosts(
        span,
        n_span,
        planes.at[0],
        wall_recv.at[0],
        corr,
        jac,
        volume,
        DT_FLOW,
        mid_plane,
        mid_row,
        mid_cells,
        pack_plane,
    )
    packed = lax.fori_loop(0, SPAN, lambda s, packed: columns(s, packed), empty, unroll=True)
    for v in range(VARS):
        edges[1, 0, v] = packed[v]

    stage_wrap_rows(1, field2)
    second = stage_copies(1, field2)
    for one in second:
        one.start()


    for one in first:
        one.wait_send()

    @pl.when(normal == 0)
    def _():
        for one in wide:
            one.wait_send()
        take(loads_a.at[1:], 1)
        loads_b[y_own] = added(loads_a)
        for x in sorted(range(n_norm), key=lambda x: -ring(x, n_norm)):
            for k in y_far + [0]:
                if x or k:
                    group_copy(loads_b, y_own, 1, device(y_at[k], z, core, x)).start()

    def second_plane(s, carry):
        cells, rates = plane_rates(field2, s, jac)
        scale = DT_FLOW * volume[s].reshape(2, 8, LANES)
        for u in range(VARS):
            start = field1[u, s + 2, TOP : TOP + WRAP, :].reshape(2, 8, LANES)
            after = 0.5 * (start + cells[u] + scale * rates[u])
            result[u, s] = after.reshape(WRAP, LANES)
        return carry

    lax.fori_loop(0, SPAN // 4, in_fours(second_plane), 0)

    prepare_beam()
    for one in second:
        one.wait_recv()
    stage_columns(1)

    def end_plane(u, s, part):
        result[u, s] += part

    def end_row(u, r, part):
        result[u, :, r, :] += part

    def end_cells(u, s, part):
        result[u, s] += part.reshape(WRAP, LANES)

    columns = add_ghosts(
        span,
        n_span,
        planes.at[1],
        wall_recv.at[1],
        corr,
        jac,
        volume,
        0.5 * DT_FLOW,
        end_plane,
        end_row,
        end_cells,
        lambda carry, cells, s: carry,
    )
    lax.fori_loop(0, SPAN, columns, 0, unroll=True)

    for one in second:
        one.wait_send()

    @pl.when(normal == 0)
    def _():
        take(loads_a.at[1:], 0)
        take(tally, 2)

    @pl.when(normal == 0)
    def _():
        take(loads_b.at[1:], 3)

    @pl.when(normal != 0)
    def _():
        take(loads_b, 3)

    loads = added(loads_b)
    kept = [beam_held[i] for i in range(9 * LEVELS + 14)]
    levels = [(2**i, *kept[9 * i : 9 * i + 9]) for i in range(LEVELS)]
    factors = (levels, tuple(kept[9 * LEVELS : 9 * LEVELS + 4]))
    be, bo, ge, go, he, ho, ue, uo, fe, fo = kept[9 * LEVELS + 4 :]
    le, lo = halves(loads)
    fe, fo = fe + le, fo + lo
    for newton_step in range(NEWTON):
        if newton_step:
            factors = factor(be, bo, ge + 3.0 * he * ue * ue, go + 3.0 * ho * uo * uo)
        ue, uo = substitute(factors, *right_side(fe, fo, he, ho, ue, uo))
    both = jnp.where(lane_of((1, LANES)) < LANES // 2, ue, roll(uo, LANES // 2))
    back = (lane % 2) * (LANES // 2) + lane // 2
    full = jnp.broadcast_to(both, (8, LANES))
    defl_ref[...] = jnp.take_along_axis(full, back, axis=1)[0:1]


def hand_out(flow_ref, defl_ref, flow_out, defl_out, sem):
    copies = [
        pltpu.make_async_copy(flow_ref, flow_out, sem.at[0]),
        pltpu.make_async_copy(defl_ref, defl_out, sem.at[1]),
    ]
    for one in copies:
        one.start()
    for one in copies:
        one.wait()


def solution(mesh):
    n_span, n_wrap, n_norm = (mesh.shape[axis] for axis in ("span", "wrap", "normal"))
    zs, ys = n_span // 4, 2 * n_wrap
    f32 = jnp.float32

    def step(
        flow_state,
        inv_volume,
        flux_jacobians,
        area,
        station_map,
        contact,
        bending,
        mass,
        hardening,
        disp_old,
        vel_old,
    ):
        vectors = [
            x.reshape(1, STATIONS) for x in (contact, bending, mass, hardening, disp_old, vel_old)
        ]
        hbm, vmem = (pl.BlockSpec(memory_space=space) for space in (pltpu.HBM, pltpu.VMEM))
        operands = [flow_state, inv_volume, flux_jacobians.transpose(1, 0, 2), area, station_map]
        operands = [pltpu.with_memory_space_constraint(x, pltpu.HBM) for x in operands + vectors]
        flow_next, deflection = pl.pallas_call(
            functools.partial(kernel, n_span, n_wrap, n_norm),
            out_shape=(
                pltpu.VMEM(flow_state.shape, f32),
                pltpu.VMEM((1, STATIONS), f32),
            ),
            in_specs=[hbm] * len(operands),
            out_specs=(vmem, vmem),
            scratch_shapes=[
                pltpu.VMEM((VARS, SPAN + 4, WRAP + 16, LANES), f32),
                pltpu.VMEM((VARS, SPAN + 4, WRAP + 16, LANES), f32),
                pltpu.VMEM((2, 2, VARS, 2, WRAP, LANES), f32),
                pltpu.VMEM((SPAN, WRAP, LANES), f32),
                pltpu.VMEM((2, 2, VARS, 2, SPAN, LANES), f32),
                pltpu.VMEM((2, 2, VARS, 2, SPAN, LANES), f32),
                pltpu.VMEM((2, 3, VARS, 8, LANES), f32),
                pltpu.VMEM((VARS, 8, LANES), f32),
                pltpu.VMEM((75, 8, LANES), f32),
                pltpu.VMEM((SPAN, WRAP, LANES), f32),
                pltpu.VMEM((SPAN, WRAP), f32),
                pltpu.VMEM((SPAN, WRAP), jnp.int32),
                pltpu.VMEM((1, STATIONS), jnp.int32),
                pltpu.VMEM((5, 1, STATIONS), f32),
                pltpu.SMEM((VARS, 3, VARS), f32),
                pltpu.VMEM((9 * LEVELS + 14, 1, LANES), f32),
                pltpu.VMEM((2 * zs, 1, LANES), f32),
                pltpu.VMEM((ys, 1, LANES), f32),
                pltpu.VMEM((ys * n_norm - 1, 1, LANES), f32),
                pltpu.VMEM((VARS + 1, WRAP, LANES), f32),
                pltpu.VMEM((3, WRAP, LANES), f32),
                pltpu.VMEM((2, 3, WRAP, LANES), f32),
                pltpu.VMEM((2, 2, 8, LANES), f32),
                pltpu.VMEM((2, 2, 8, LANES), f32),
                pltpu.VMEM((2, 8, LANES), f32),
                pltpu.VMEM((4, 8, LANES), f32),
                pltpu.VMEM((VARS + 1, WRAP + 16, LANES), f32),
                pltpu.VMEM((VARS, 24, LANES), f32),
                pltpu.SemaphoreType.DMA((11,)),
                pltpu.SemaphoreType.DMA((12,)),
                pltpu.SemaphoreType.DMA((12,)),
                pltpu.SemaphoreType.DMA((4,)),
                pltpu.SemaphoreType.DMA((8,)),
                pltpu.SemaphoreType.DMA((8,)),
            ],
            compiler_params=pltpu.CompilerParams(
                collective_id=0, has_side_effects=True, vmem_limit_bytes=32 * 1024 * 1024
            ),
            cost_estimate=pl.CostEstimate(
                flops=10_000_000, bytes_accessed=1_000_000, transcendentals=0
            ),
        )(*operands)
        flow_next, deflection = pl.pallas_call(
            hand_out,
            out_shape=(
                jax.ShapeDtypeStruct(flow_state.shape, f32),
                jax.ShapeDtypeStruct((1, STATIONS), f32),
            ),
            in_specs=(vmem, vmem),
            out_specs=(hbm, hbm),
            scratch_shapes=[pltpu.SemaphoreType.DMA((2,))],
        )(
            pltpu.with_memory_space_constraint(flow_next, pltpu.VMEM),
            pltpu.with_memory_space_constraint(deflection, pltpu.VMEM),
        )
        return flow_next, deflection.reshape(STATIONS)

    placed = (
        P(None, "span", "wrap", "normal"),
        P("span", "wrap", "normal"),
        P(),
        P("span", "wrap"),
        P("span", "wrap"),
    ) + (P(),) * 6
    return jax.shard_map(
        step,
        mesh=mesh,
        in_specs=placed,
        out_specs=(P(None, "span", "wrap", "normal"), P()),
        check_vma=False,
    )
```

```python
import functools

import jax
import jax.numpy as jnp
from jax import lax
from jax.experimental import pallas as pl
from jax.experimental.pallas import tpu as pltpu
from jax.sharding import PartitionSpec as P

MESH = pl.DeviceIdType.MESH
VARS = 5
STATIONS = 128
NEWTON = 3
LEVELS = 6
DT_FLOW = 0.2
DISSIPATION = 0.03
DT_BEAM = 0.2
STOP_GAP = 0.5
CONTACT_STIFF = 40.0
SPAN, WRAP, LANES = 8, 16, 128
TOP = 8


def lane_of(shape):
    return lax.broadcasted_iota(jnp.int32, shape, len(shape) - 1)


def roll(x, shift):
    return pltpu.roll(x, shift % LANES if isinstance(shift, int) else shift, 1)


def factor(be, bo, diag_e, diag_o):
    lane = lane_of((1, LANES))
    half = LANES // 2
    valid, inner = lane < half, lane < half - 1
    bo_prev, be_next = roll(bo, 1), roll(be, -1)
    p = jnp.where(valid, 4.0 * be + bo_prev + bo + diag_e, 1.0)
    q = jnp.where(valid, -2.0 * (be + bo), 0.0)
    r = jnp.where(valid, 4.0 * bo + be + be_next + diag_o, 1.0)
    c11 = jnp.where(inner, bo, 0.0)
    c12 = jnp.zeros_like(bo)
    c21 = jnp.where(inner, -2.0 * (bo + be_next), 0.0)
    c22 = jnp.where(inner, be_next, 0.0)
    a11, a12, a21, a22 = roll(c11, 1), roll(c21, 1), c12, roll(c22, 1)
    levels = []
    step = 1
    while step < half:
        inv = 1.0 / (p * r - q * q)
        u11, u12 = c11 * r - c21 * q, c21 * p - c11 * q
        u21, u22 = c12 * r - c22 * q, c22 * p - c12 * q
        d11, d12 = a11 * r - a21 * q, a21 * p - a11 * q
        d21, d22 = a12 * r - a22 * q, a22 * p - a12 * q
        levels.append((step, inv, u11, u12, u21, u22, d11, d12, d21, d22))
        up = [
            (u11 * c11 + u12 * c21) * inv,
            (u11 * c12 + u12 * c22) * inv,
            (u21 * c12 + u22 * c22) * inv,
        ]
        down = [
            (d11 * a11 + d12 * a21) * inv,
            (d11 * a12 + d12 * a22) * inv,
            (d21 * a12 + d22 * a22) * inv,
        ]
        p = p - (roll(up[0], step) + roll(down[0], -step))
        q = q - (roll(up[1], step) + roll(down[1], -step))
        r = r - (roll(up[2], step) + roll(down[2], -step))
        if 2 * step < half:
            n11, n12 = -(d11 * c11 + d12 * c21) * inv, -(d11 * c12 + d12 * c22) * inv
            n21, n22 = -(d21 * c11 + d22 * c21) * inv, -(d21 * c12 + d22 * c22) * inv
            c11, c12 = roll(n11, -step), roll(n12, -step)
            c21, c22 = roll(n21, -step), roll(n22, -step)
            a11, a12 = roll(n11, step), roll(n21, step)
            a21, a22 = roll(n12, step), roll(n22, step)
        step *= 2
    return levels, (1.0 / (p * r - q * q), p, q, r)


def substitute(factors, e, o):
    levels, (inv, p, q, r) = factors
    for step, scale, u11, u12, u21, u22, d11, d12, d21, d22 in levels:
        e, o = (
            e - (roll((u11 * e + u12 * o) * scale, step) + roll((d11 * e + d12 * o) * scale, -step)),
            o - (roll((u21 * e + u22 * o) * scale, step) + roll((d21 * e + d22 * o) * scale, -step)),
        )
    return (r * e - q * o) * inv, (p * o - q * e) * inv


def right_side(fe, fo, he, ho, ue, uo):
    return fe + 2.0 * he * ue * ue * ue, fo + 2.0 * ho * uo * uo * uo


def halves(x):
    valid = lane_of((1, LANES)) < LANES // 2
    return jnp.where(valid, x, 0.0), jnp.where(valid, roll(x, LANES // 2), 0.0)


def ring(by, count):
    return min(by, count - by)


def pack_plane(packed, cells, s):
    slot = lane_of((8, LANES)) // 4
    new = []
    for v in range(VARS):
        have = packed[v]
        for t in range(2):
            k = 2 * s + t
            have = jnp.where(slot == k, roll(cells[v][t], 4 * k + 2), have)
        new.append(have)
    return tuple(new)


def edge_terms(normal, n_norm, own, left, right, jac, corr):
    lane = lane_of((8, LANES))
    place = lane % 4
    ends, smooths = [], []
    for v in range(VARS):
        mine = own[v]
        mirror = jnp.where(place == 0, roll(mine, -3), roll(mine, -1))
        low = jnp.where(normal == 0, mirror, left[v])
        high = jnp.where(normal == n_norm - 1, 0.0, right[v])
        delta = jnp.where(place < 2, roll(high - mine, -2), roll(low - mine, 2))
        near = jnp.where(place == 1, roll(delta, 1), jnp.where(place == 2, roll(delta, -1), 0.0))
        end = delta - 8.0 * near
        ends.append(jnp.where(place < 2, -end, end))
        smooths.append(delta - 4.0 * near)
    for u in range(VARS):
        total = -DISSIPATION * smooths[u]
        for v in range(VARS):
            total = total + jac[50 + 5 * u + v] * ends[v]
        corr[u] = total


def plane_rates(field, s, jac):
    cells, grads, smooths = [], [[], [], []], []
    for v in range(VARS):

        def at(ds, dw):
            return field[v, s + (2 + ds), TOP + dw : TOP + dw + WRAP, :]

        c = at(0, 0)
        reads = [
            [at(k, 0) for k in (-2, -1, 1, 2)],
            [at(0, k) for k in (-2, -1, 1, 2)],
            [roll(c, -k) for k in (-2, -1, 1, 2)],
        ]
        near, far = None, None
        for d, (m2, m1, p1, p2) in enumerate(reads):
            grads[d].append(((m2 - p2) + 8.0 * (p1 - m1)).reshape(2, 8, LANES))
            near = (m1 + p1) if near is None else near + (m1 + p1)
            far = (m2 + p2) if far is None else far + (m2 + p2)
        smooths.append((-DISSIPATION * (far - 4.0 * near + 18.0 * c)).reshape(2, 8, LANES))
        cells.append(c.reshape(2, 8, LANES))
    rates = []
    for u in range(VARS):
        total = smooths[u]
        for d in range(3):
            for v in range(VARS):
                total = total + jac[25 * d + 5 * u + v][None] * grads[d][v]
        rates.append(total)
    return cells, rates


def in_pairs(plane):
    return lambda i, carry: plane(2 * i + 1, plane(2 * i, carry))


def ghost_rates(direction, low, first, second, jac, shape):
    outer, inner = [], []
    for v in range(VARS):
        a, b = first(v), second(v)
        if low:
            outer.append((a - 8.0 * b, a - 4.0 * b))
            inner.append((b, b))
        else:
            outer.append((8.0 * a - b, b - 4.0 * a))
            inner.append((-a, a))
    fixes = []
    for layer in (outer, inner):
        grads = [g.reshape(shape) for g, _ in layer]
        layer_fixes = []
        for u in range(VARS):
            total = -DISSIPATION * layer[u][1].reshape(shape)
            for v in range(VARS):
                total = total + jac[25 * direction + 5 * u + v][None] * grads[v]
            layer_fixes.append(total)
        fixes.append(layer_fixes)
    return fixes


def add_ghosts(span, n_span, planes, rows, corr, jac, volume, factor_of, at_plane, at_row, at_cells, done):
    for low in (True, False):
        gone = span == (0 if low else n_span - 1)
        side = 0 if low else 1

        def ghost(layer):
            return lambda v: jnp.where(gone, 0.0, planes[side, v, layer])

        fixes = ghost_rates(0, low, ghost(0), ghost(1), jac, (2, 8, LANES))
        for s, fix in zip((0, 1) if low else (SPAN - 1, SPAN - 2), fixes):
            scale = factor_of * volume[s]
            for u in range(VARS):
                at_plane(u, s, scale * fix[u].reshape(WRAP, LANES))
    for low in (True, False):
        side = 1 if low else 0

        def ghost(layer):
            return lambda v: rows[side, v, layer]

        fixes = ghost_rates(1, low, ghost(0), ghost(1), jac, (1, 8, LANES))
        for r, fix in zip((0, 1) if low else (WRAP - 1, WRAP - 2), fixes):
            scale = factor_of * volume[:, r, :]
            for u in range(VARS):
                at_row(u, r, scale * fix[u].reshape(8, LANES))
    lane = lane_of((8, LANES))
    edge = (lane < 2) | (lane >= LANES - 2)

    def columns(s, carry):
        scale = factor_of * volume[s].reshape(2, 8, LANES)
        cells = []
        for u in range(VARS):
            ends = corr[u]
            fix = [
                jnp.where(edge, roll(ends, (2 * LANES - 2 - 4 * (2 * s + t)) % LANES), 0.0)
                for t in range(2)
            ]
            cells.append(at_cells(u, s, scale * jnp.stack(fix)))
        return done(carry, cells, s)

    return columns


def pack_wall(field, volume, packed):
    group = lane_of((8, LANES)) // 8
    for v in range(VARS + 1):
        for t in range(2):
            have = jnp.zeros((8, LANES), jnp.float32)
            for s in range(SPAN):
                if v < VARS:
                    tile = field[v, s + 2, TOP + 8 * t : TOP + 8 * t + 8, :]
                else:
                    tile = volume[s, 8 * t : 8 * t + 8, :]
                have = jnp.where(group == s + 4, roll(tile, 8 * (s + 4) + 2), have)
            packed[v, 8 * t : 8 * t + 8, :] = mirrored(have)


def pair_wall(packed, pairs, edge, tip):
    lane, row = lane_of((8, LANES)), lax.broadcasted_iota(jnp.int32, (8, LANES), 0)
    own = (lane >= LANES // 4) & (lane < 3 * LANES // 4)
    for p in range(3):
        for t in range(2):
            rows = slice(8 * t, 8 * t + 8)
            pairs[p, rows, :] = jnp.where(own, packed[p, rows, :], roll(packed[p + 3, rows, :], 64))
    for t in range(2):
        a, b, c = (pairs[p, 8 * t : 8 * t + 8, :] for p in range(3))
        four = row < 4
        edge[t, 0] = jnp.where(four, a if t == 0 else pltpu.roll(a, 4, 0), b if t else pltpu.roll(b, 4, 0))
        edge[t, 1] = c
        at = 6 * t
        tip[t] = jnp.where(
            row < 2,
            turn_rows(a, -at),
            jnp.where(four, turn_rows(b, 2 - at), turn_rows(c, 4 - at)),
        )


def turn_rows(x, by):
    return pltpu.roll(x, by % 8, 0) if by % 8 else x


def mirrored(x):
    place = lane_of(x.shape) % 8
    return jnp.where(place == 0, roll(x, -3), jnp.where(place == 1, roll(x, -1), x))


def wall_rates(layer, top, rows, wanted, jac, at_wall):
    cells, grads, smooths = [], [[], [], []], []
    shape = (rows // 8, 8, LANES)
    for v in range(VARS):
        c = layer[v, top : top + rows, :]
        reads = [
            [roll(c, -8 * k) for k in (-2, -1, 1, 2)],
            [layer[v, top + k : top + k + rows, :] for k in (-2, -1, 1, 2)],
        ]
        if at_wall:
            p1, p2 = roll(c, -1), roll(c, -2)
            reads.append([p1, c, p1, p2])
        else:
            reads.append([roll(c, -k) for k in (-2, -1, 1, 2)])
        near, far = None, None
        for d, (m2, m1, p1, p2) in enumerate(reads):
            grads[d].append(((m2 - p2) + 8.0 * (p1 - m1)).reshape(shape))
            near = (m1 + p1) if near is None else near + (m1 + p1)
            far = (m2 + p2) if far is None else far + (m2 + p2)
        smooths.append((-DISSIPATION * (far - 4.0 * near + 18.0 * c)).reshape(shape))
        cells.append(c)
    rates = []
    for u in range(wanted):
        total = smooths[u]
        for d in range(3):
            for v in range(VARS):
                total = total + jac[25 * d + 5 * u + v][None] * grads[d][v]
        rates.append(total.reshape(rows, LANES))
    return cells, rates


def wall_loads(span, n_span, packed, beside, edges, tips, layer, mid, faces, jac):
    group = lane_of((8, LANES)) // 8
    first, last = span == 0, span == n_span - 1

    def swing(x, when):
        return roll(x, LANES // 2) if when else x

    for v in range(VARS + 1):
        p, upper = v % 3, v >= 3
        low_edge = edges[0, 1] if p == 2 else turn_rows(edges[0, 0], 4 - 4 * p)
        high_edge = edges[1, 1] if p == 2 else turn_rows(edges[1, 0], 4 * p)
        tiles = [
            (turn_rows(tips[0], 6 - 2 * p), swing(low_edge, upper), turn_rows(tips[1], 6 - 2 * p)),
            (beside[0, p, 0:8], packed[v, 0:8], beside[1, p, 0:8]),
            (beside[0, p, 8:16], packed[v, 8:16], beside[1, p, 8:16]),
            (turn_rows(tips[2], -2 * p), swing(high_edge, upper), turn_rows(tips[3], -2 * p)),
        ]
        for t, (left, centre, right) in enumerate(tiles):
            left = jnp.where(first, 0.0, swing(left, not upper))
            right = jnp.where(last, 0.0, swing(right, not upper))
            whole = jnp.where(group < 4, left, jnp.where(group >= 12, right, centre))
            layer[v, 8 * t : 8 * t + 8, :] = whole
    span_group = lane_of((24, LANES)) // 8
    outside = (first & (span_group < 4)) | (last & (span_group >= 12))
    cells, rates = wall_rates(layer, 4, 24, VARS, jac, False)
    scale = DT_FLOW * layer[VARS, 4:28, :]
    for u in range(VARS):
        mid[u] = jnp.where(outside, 0.0, cells[u] + scale * rates[u])
    cells, rates = wall_rates(mid, 4, 16, 1, jac, True)
    scale = DT_FLOW * layer[VARS, 8:24, :]
    after = 0.5 * (layer[0, 8:24, :] + cells[0] + scale * rates[0])
    total = jnp.zeros((WRAP, LANES), jnp.float32)
    for s in range(SPAN):
        at = 8 * (s + 4) + 2
        total = total + faces[s] * jnp.broadcast_to(after[:, at : at + 1], (WRAP, LANES))
    return jnp.sum(total, axis=0, keepdims=True)


def kernel(
    n_span,
    n_wrap,
    n_norm,
    flow_hbm,
    volume_hbm,
    jac_hbm,
    area_hbm,
    map_hbm,
    contact_hbm,
    bending_hbm,
    mass_hbm,
    hardening_hbm,
    disp_hbm,
    vel_hbm,
    result,
    defl_ref,
    field1,
    field2,
    planes,
    volume,
    wall_send,
    wall_recv,
    edges,
    corr,
    jac,
    faces,
    area,
    stations,
    contact_v,
    beam_v,
    jac_held,
    beam_held,
    loads_a,
    loads_b,
    tally,
    wall_packed,
    wall_pairs,
    wall_beside,
    edge_put,
    edge_got,
    tip_put,
    tip_got,
    wall_layer,
    wall_mid,
    local_sem,
    send_sem,
    recv_sem,
    group_sem,
    wide_send_sem,
    wide_recv_sem,
):
    span, wrap, normal = lax.axis_index("span"), lax.axis_index("wrap"), lax.axis_index("normal")
    rows = 2
    cols = n_span // rows
    row, col = lax.div(span, cols), lax.rem(span, cols)
    zs, cores = cols // 2, 2
    z, core = lax.div(col, cores), lax.rem(col, cores)
    y_own = row * n_wrap + wrap

    inputs = [
        (flow_hbm, field1.at[:, 2 : 2 + SPAN, TOP : TOP + WRAP, :]),
        (volume_hbm, volume),
        (area_hbm, area),
        (map_hbm, stations),
        (contact_hbm, contact_v),
        (bending_hbm, beam_v.at[0]),
        (mass_hbm, beam_v.at[1]),
        (hardening_hbm, beam_v.at[2]),
        (disp_hbm, beam_v.at[3]),
        (vel_hbm, beam_v.at[4]),
        (jac_hbm, jac_held),
    ]
    reads = [pltpu.make_async_copy(a, b, local_sem.at[i]) for i, (a, b) in enumerate(inputs)]
    for read in reads[:2]:
        read.start()

    def turned(index, by, count):
        return lax.rem(index + (by + count), count)

    span_at = {by: turned(span, by, n_span) for by in (-1, 1)}
    wrap_at = [turned(wrap, by, n_wrap) for by in range(n_wrap)]
    norm_at = {by: turned(normal, by, n_norm) for by in (-1, 1)}
    row_at = [turned(row, by, rows) for by in range(rows)]
    z_at = [turned(z, by, zs) for by in range(zs)]
    core_at = [core, turned(core, 1, cores)]
    sides = [
        (span_at[-1], wrap, normal),
        (span_at[1], wrap, normal),
        (span, wrap_at[n_wrap - 1], normal),
        (span, wrap_at[1], normal),
        (span, wrap, norm_at[-1]),
        (span, wrap, norm_at[1]),
    ]
    barrier = pltpu.get_barrier_semaphore()

    def greet(target):
        pl.semaphore_signal(barrier, inc=1, device_id=target, device_id_type=MESH)

    corners = [(span_at[i], wrap_at[j], normal) for j in (n_wrap - 1, 1) for i in (-1, 1)]

    def device(y, z, core, x):
        return (y[0] * cols + z * cores + core, y[1], x)

    here = (row, wrap)
    y_at = [(row_at[a], wrap_at[b]) for a in range(rows) for b in range(n_wrap)]
    y_far = sorted(range(1, rows * n_wrap), key=lambda k: -ring(2 * (k % n_wrap) + k // n_wrap, 2 * n_wrap))
    z_far = sorted(range(1, zs), key=lambda k: -ring(k, zs))
    beside_y = (1, n_wrap - 1)

    @pl.when(normal == 0)
    def _():
        for k in z_far:
            for c in range(cores):
                greet(device(here, z_at[k], core_at[c], 0))
        for k in y_far:
            if k not in beside_y:
                greet(device(y_at[k], z, core, 0))
        for one in corners:
            greet(one)

    @pl.when(normal != 0)
    def _():
        for k in y_far + [0]:
            greet(device(y_at[k], z, core, 0))

    for side in sides:
        greet(side)

    for read in reads[2:]:
        read.start()

    def copy(src, dst, slot, target):
        return pltpu.make_async_remote_copy(
            src_ref=src,
            dst_ref=dst,
            send_sem=send_sem.at[slot],
            recv_sem=recv_sem.at[slot],
            device_id=target,
            device_id_type=MESH,
        )

    def stage_copies(stage, field):
        cells = pl.ds(TOP, WRAP)
        base = 6 * stage
        pairs = [
            (field.at[:, 2:4, cells, :], planes.at[stage, 1]),
            (field.at[:, SPAN : 2 + SPAN, cells, :], planes.at[stage, 0]),
            (wall_send.at[stage, 0], wall_recv.at[stage, 0]),
            (wall_send.at[stage, 1], wall_recv.at[stage, 1]),
            (edges.at[stage, 0], edges.at[stage, 2]),
            (edges.at[stage, 0], edges.at[stage, 1]),
        ]
        return [copy(src, dst, base + i, sides[i]) for i, (src, dst) in enumerate(pairs)]

    def stage_wrap_rows(stage, field):
        for v in range(VARS):
            for r in range(2):
                wall_send[stage, 0, v, r] = field[v, 2 : 2 + SPAN, TOP + r, :]
                wall_send[stage, 1, v, r] = field[v, 2 : 2 + SPAN, TOP + WRAP - 2 + r, :]

    def stage_columns(stage):
        edge_terms(
            normal, n_norm, edges.at[stage, 0], edges.at[stage, 1], edges.at[stage, 2], jac, corr
        )

    for field in (field1, field2):
        for s in (0, 1, 2 + SPAN, 3 + SPAN):
            field[:, s, TOP : TOP + WRAP, :] = jnp.zeros((VARS, WRAP, LANES), jnp.float32)
        for r in (0, TOP + WRAP):
            field[:, 2 : 2 + SPAN, r : r + 8, :] = jnp.zeros((VARS, SPAN, 8, LANES), jnp.float32)

    wide = []
    for i, (src, dst, target) in enumerate(
        [
            (tip_put.at[0], tip_got.at[3], corners[0]),
            (tip_put.at[0], tip_got.at[2], corners[1]),
            (tip_put.at[1], tip_got.at[1], corners[2]),
            (tip_put.at[1], tip_got.at[0], corners[3]),
            (edge_put.at[0], edge_got.at[1], sides[2]),
            (edge_put.at[1], edge_got.at[0], sides[3]),
            (wall_pairs, wall_beside.at[1], sides[0]),
            (wall_pairs, wall_beside.at[0], sides[1]),
        ]
    ):
        wide.append(
            pltpu.make_async_remote_copy(
                src_ref=src,
                dst_ref=dst,
                send_sem=wide_send_sem.at[i],
                recv_sem=wide_recv_sem.at[i],
                device_id=target,
                device_id_type=MESH,
            )
        )

    empty = tuple(jnp.zeros((8, LANES), jnp.float32) for _ in range(VARS))

    reads[0].wait()
    reads[1].wait()

    @pl.when(normal == 0)
    def _():
        pack_wall(field1, volume, wall_packed)
        pair_wall(wall_packed, wall_pairs, edge_put, tip_put)

    stage_wrap_rows(0, field1)

    def pack_first(s, packed):
        cells = [
            field1[v, s + 2, TOP : TOP + WRAP, :].reshape(2, 8, LANES) for v in range(VARS)
        ]
        return pack_plane(packed, cells, s)

    packed = lax.fori_loop(0, SPAN, pack_first, empty, unroll=True)
    for v in range(VARS):
        edges[0, 0, v] = packed[v]

    lane = lane_of((8, LANES))
    held = jnp.where(lane < LANES // 2, 2 * lane, 2 * lane - (LANES - 1))

    def prepare():
        for read in reads[2:]:
            read.wait()
        for d in range(3):
            for u in range(VARS):
                for v in range(VARS):
                    scaled = jac_held[u, d, v] * (-1.0 / 12.0)
                    jac[25 * d + 5 * u + v] = jnp.full((8, LANES), scaled, jnp.float32)

    def prepare_beam():
        def permuted(x):
            full = jnp.broadcast_to(x, (8, LANES))
            return jnp.take_along_axis(full, held, axis=1)[0:1]

        bending, mass, hardening, disp, vel = [permuted(beam_v[i]) for i in range(5)]
        contact = permuted(contact_v[...])
        inertia = 2.0 * mass / (DT_BEAM * DT_BEAM)
        pull = CONTACT_STIFF * STOP_GAP
        push = jnp.where(contact == 1, pull, jnp.where(contact == 2, -pull, 0.0))
        steady = inertia * (disp + DT_BEAM * vel) + push
        base = inertia + jnp.where(contact > 0, CONTACT_STIFF, 0.0)
        be, bo = halves(bending)
        he, ho = halves(hardening)
        ge, go = halves(base)
        ue, uo = halves(disp)
        fe, fo = halves(steady)
        factors = factor(be, bo, ge + 3.0 * he * ue * ue, go + 3.0 * ho * uo * uo)
        levels, last = factors
        kept = [x for level in levels for x in level[1:]] + list(last)
        kept += [be, bo, ge, go, he, ho, ue, uo, fe, fo]
        for i, x in enumerate(kept):
            beam_held[i] = x

    @pl.when(normal == 0)
    def _():
        prepare()
        prepare_beam()
        row_id = lax.broadcasted_iota(jnp.int32, (WRAP, WRAP), 0)
        same = (row_id == lane_of((WRAP, WRAP))).astype(jnp.float32)

        def turned_over(x):
            return lax.dot_general(
                same, x, (((1,), (1,)), ((), ())), precision=lax.Precision.HIGHEST
            )

        weights = turned_over(area[...])
        places = turned_over(stations[...].astype(jnp.float32))
        aims = jnp.broadcast_to(held[0:1], (WRAP, LANES)).astype(jnp.float32)
        for s in range(SPAN):
            weight = jnp.broadcast_to(weights[:, s : s + 1], (WRAP, LANES))
            place = jnp.broadcast_to(places[:, s : s + 1], (WRAP, LANES))
            faces[s] = jnp.where(place == aims, weight, 0.0)

    at_wall = lax.div(n_norm - normal, n_norm)
    wall_peers = 4 + cores * (zs - 1) + (len(y_at) * n_norm - 1 - len(set(beside_y)))
    pl.semaphore_wait(barrier, 6 + at_wall * wall_peers)

    @pl.when(normal == 0)
    def _():
        for one in wide:
            one.start()

    first = stage_copies(0, field1)

    for one in first[:2] + first[4:]:
        one.start()

    @pl.when(normal != 0)
    def _():
        for one in first[2:4]:
            one.start()
        prepare()


    def group_copy(buffer, own, which, target):
        return pltpu.make_async_remote_copy(
            src_ref=buffer.at[own],
            dst_ref=buffer.at[own],
            send_sem=group_sem.at[2 * which],
            recv_sem=group_sem.at[2 * which + 1],
            device_id=target,
            device_id_type=MESH,
        )

    def added(ref):
        terms = [ref[i] for i in range(ref.shape[0])]
        while len(terms) > 1:
            terms = [sum(terms[i + 1 : i + 2], terms[i]) for i in range(0, len(terms), 2)]
        return terms[0]

    def take(ref, which):
        pltpu.make_async_copy(ref, ref, group_sem.at[which]).wait()

    def first_plane(s, carry):
        cells, rates = plane_rates(field1, s, jac)
        scale = DT_FLOW * volume[s].reshape(2, 8, LANES)
        for u in range(VARS):
            mid = cells[u] + scale * rates[u]
            field2[u, s + 2, TOP : TOP + WRAP, :] = mid.reshape(WRAP, LANES)
        return carry

    lax.fori_loop(0, SPAN // 2, in_pairs(first_plane), 0)

    @pl.when(normal == 0)
    def _():
        for one in first[2:4]:
            one.start()
        for one in wide:
            one.wait_recv()
        loads_a[col] = wall_loads(
            span,
            n_span,
            wall_packed,
            wall_beside,
            edge_got,
            tip_got,
            wall_layer,
            wall_mid,
            faces,
            jac,
        )
        for k in z_far + [0]:
            for c in range(cores):
                if k or c:
                    group_copy(loads_a, col, 0, device(here, z_at[k], core_at[c], 0)).start()

    for one in first:
        one.wait_recv()
    stage_columns(0)

    def mid_plane(u, s, part):
        field2[u, s + 2, TOP : TOP + WRAP, :] += part

    def mid_row(u, r, part):
        field2[u, 2 : 2 + SPAN, TOP + r, :] += part

    def mid_cells(u, s, part):
        cells = field2[u, s + 2, TOP : TOP + WRAP, :].reshape(2, 8, LANES) + part
        field2[u, s + 2, TOP : TOP + WRAP, :] = cells.reshape(WRAP, LANES)
        return cells

    columns = add_ghosts(
        span,
        n_span,
        planes.at[0],
        wall_recv.at[0],
        corr,
        jac,
        volume,
        DT_FLOW,
        mid_plane,
        mid_row,
        mid_cells,
        pack_plane,
    )
    packed = lax.fori_loop(0, SPAN, lambda s, packed: columns(s, packed), empty, unroll=True)
    for v in range(VARS):
        edges[1, 0, v] = packed[v]

    stage_wrap_rows(1, field2)
    second = stage_copies(1, field2)
    for one in second:
        one.start()


    @pl.when(normal != 0)
    def _():
        prepare_beam()

    for one in first:
        one.wait_send()

    @pl.when(normal == 0)
    def _():
        for one in wide:
            one.wait_send()
        take(loads_a.at[1:], 1)
        loads_b[y_own] = added(loads_a)
        for x in sorted(range(n_norm), key=lambda x: -ring(x, n_norm)):
            for k in y_far + [0]:
                if x or k:
                    group_copy(loads_b, y_own, 1, device(y_at[k], z, core, x)).start()

    def second_plane(s, carry):
        cells, rates = plane_rates(field2, s, jac)
        scale = DT_FLOW * volume[s].reshape(2, 8, LANES)
        for u in range(VARS):
            start = field1[u, s + 2, TOP : TOP + WRAP, :].reshape(2, 8, LANES)
            after = 0.5 * (start + cells[u] + scale * rates[u])
            result[u, s] = after.reshape(WRAP, LANES)
        return carry

    lax.fori_loop(0, SPAN // 2, in_pairs(second_plane), 0)

    for one in second:
        one.wait_recv()
    stage_columns(1)

    def end_plane(u, s, part):
        result[u, s] += part

    def end_row(u, r, part):
        result[u, :, r, :] += part

    def end_cells(u, s, part):
        result[u, s] += part.reshape(WRAP, LANES)

    columns = add_ghosts(
        span,
        n_span,
        planes.at[1],
        wall_recv.at[1],
        corr,
        jac,
        volume,
        0.5 * DT_FLOW,
        end_plane,
        end_row,
        end_cells,
        lambda carry, cells, s: carry,
    )
    lax.fori_loop(0, SPAN, columns, 0, unroll=True)

    for one in second:
        one.wait_send()

    @pl.when(normal == 0)
    def _():
        take(loads_a.at[1:], 0)
        take(tally, 2)

    @pl.when(normal == 0)
    def _():
        take(loads_b.at[1:], 3)

    @pl.when(normal != 0)
    def _():
        take(loads_b, 3)

    loads = added(loads_b)
    kept = [beam_held[i] for i in range(9 * LEVELS + 14)]
    levels = [(2**i, *kept[9 * i : 9 * i + 9]) for i in range(LEVELS)]
    factors = (levels, tuple(kept[9 * LEVELS : 9 * LEVELS + 4]))
    be, bo, ge, go, he, ho, ue, uo, fe, fo = kept[9 * LEVELS + 4 :]
    le, lo = halves(loads)
    fe, fo = fe + le, fo + lo
    for newton_step in range(NEWTON):
        if newton_step:
            factors = factor(be, bo, ge + 3.0 * he * ue * ue, go + 3.0 * ho * uo * uo)
        ue, uo = substitute(factors, *right_side(fe, fo, he, ho, ue, uo))
    both = jnp.where(lane_of((1, LANES)) < LANES // 2, ue, roll(uo, LANES // 2))
    back = (lane % 2) * (LANES // 2) + lane // 2
    full = jnp.broadcast_to(both, (8, LANES))
    defl_ref[...] = jnp.take_along_axis(full, back, axis=1)[0:1]


def hand_out(flow_ref, defl_ref, flow_out, defl_out, sem):
    copies = [
        pltpu.make_async_copy(flow_ref, flow_out, sem.at[0]),
        pltpu.make_async_copy(defl_ref, defl_out, sem.at[1]),
    ]
    for one in copies:
        one.start()
    for one in copies:
        one.wait()


def solution(mesh):
    n_span, n_wrap, n_norm = (mesh.shape[axis] for axis in ("span", "wrap", "normal"))
    zs, ys = n_span // 4, 2 * n_wrap
    f32 = jnp.float32

    def step(
        flow_state,
        inv_volume,
        flux_jacobians,
        area,
        station_map,
        contact,
        bending,
        mass,
        hardening,
        disp_old,
        vel_old,
    ):
        vectors = [
            x.reshape(1, STATIONS) for x in (contact, bending, mass, hardening, disp_old, vel_old)
        ]
        hbm, vmem = (pl.BlockSpec(memory_space=space) for space in (pltpu.HBM, pltpu.VMEM))
        operands = [flow_state, inv_volume, flux_jacobians.transpose(1, 0, 2), area, station_map]
        operands = [pltpu.with_memory_space_constraint(x, pltpu.HBM) for x in operands + vectors]
        flow_next, deflection = pl.pallas_call(
            functools.partial(kernel, n_span, n_wrap, n_norm),
            out_shape=(
                pltpu.VMEM(flow_state.shape, f32),
                pltpu.VMEM((1, STATIONS), f32),
            ),
            in_specs=[hbm] * len(operands),
            out_specs=(vmem, vmem),
            scratch_shapes=[
                pltpu.VMEM((VARS, SPAN + 4, WRAP + 16, LANES), f32),
                pltpu.VMEM((VARS, SPAN + 4, WRAP + 16, LANES), f32),
                pltpu.VMEM((2, 2, VARS, 2, WRAP, LANES), f32),
                pltpu.VMEM((SPAN, WRAP, LANES), f32),
                pltpu.VMEM((2, 2, VARS, 2, SPAN, LANES), f32),
                pltpu.VMEM((2, 2, VARS, 2, SPAN, LANES), f32),
                pltpu.VMEM((2, 3, VARS, 8, LANES), f32),
                pltpu.VMEM((VARS, 8, LANES), f32),
                pltpu.VMEM((75, 8, LANES), f32),
                pltpu.VMEM((SPAN, WRAP, LANES), f32),
                pltpu.VMEM((SPAN, WRAP), f32),
                pltpu.VMEM((SPAN, WRAP), jnp.int32),
                pltpu.VMEM((1, STATIONS), jnp.int32),
                pltpu.VMEM((5, 1, STATIONS), f32),
                pltpu.SMEM((VARS, 3, VARS), f32),
                pltpu.VMEM((9 * LEVELS + 14, 1, LANES), f32),
                pltpu.VMEM((2 * zs, 1, LANES), f32),
                pltpu.VMEM((ys, 1, LANES), f32),
                pltpu.VMEM((ys * n_norm - 1, 1, LANES), f32),
                pltpu.VMEM((VARS + 1, WRAP, LANES), f32),
                pltpu.VMEM((3, WRAP, LANES), f32),
                pltpu.VMEM((2, 3, WRAP, LANES), f32),
                pltpu.VMEM((2, 2, 8, LANES), f32),
                pltpu.VMEM((2, 2, 8, LANES), f32),
                pltpu.VMEM((2, 8, LANES), f32),
                pltpu.VMEM((4, 8, LANES), f32),
                pltpu.VMEM((VARS + 1, WRAP + 16, LANES), f32),
                pltpu.VMEM((VARS, 24, LANES), f32),
                pltpu.SemaphoreType.DMA((11,)),
                pltpu.SemaphoreType.DMA((12,)),
                pltpu.SemaphoreType.DMA((12,)),
                pltpu.SemaphoreType.DMA((4,)),
                pltpu.SemaphoreType.DMA((8,)),
                pltpu.SemaphoreType.DMA((8,)),
            ],
            compiler_params=pltpu.CompilerParams(
                collective_id=0, has_side_effects=True, vmem_limit_bytes=32 * 1024 * 1024
            ),
            cost_estimate=pl.CostEstimate(
                flops=10_000_000, bytes_accessed=1_000_000, transcendentals=0
            ),
        )(*operands)
        flow_next, deflection = pl.pallas_call(
            hand_out,
            out_shape=(
                jax.ShapeDtypeStruct(flow_state.shape, f32),
                jax.ShapeDtypeStruct((1, STATIONS), f32),
            ),
            in_specs=(vmem, vmem),
            out_specs=(hbm, hbm),
            scratch_shapes=[pltpu.SemaphoreType.DMA((2,))],
        )(
            pltpu.with_memory_space_constraint(flow_next, pltpu.VMEM),
            pltpu.with_memory_space_constraint(deflection, pltpu.VMEM),
        )
        return flow_next, deflection.reshape(STATIONS)

    placed = (
        P(None, "span", "wrap", "normal"),
        P("span", "wrap", "normal"),
        P(),
        P("span", "wrap"),
        P("span", "wrap"),
    ) + (P(),) * 6
    return jax.shard_map(
        step,
        mesh=mesh,
        in_specs=placed,
        out_specs=(P(None, "span", "wrap", "normal"), P()),
        check_vma=False,
    )
```
